128 devices in a mesh: fy: 8 (over y, core), fx: 16 (over x, z).
Axes of the slice: x: 4, y: 4, z: 4, core: 2. Of those that a mesh axis runs over, the one named last changes fastest.
Arguments:
- sky_image: float32 [8, 2048, 4096], P(None, 'fy', 'fx'), may hold values from 0 to 2
- vis_tiles: bfloat16 [2048, 2, 256, 256], P(('fy', 'fx')), may hold values from -6 to 6
- tile_dest: int32 [2048, 1], P(('fy', 'fx')), may hold values from 0 to 15; in each aligned block of 16 rows (0 to 15, 16 to 31, ...) at most 2 rows name the same one
- tile_chan: int32 [2048], P(('fy', 'fx')), may hold values from 0 to 7
- tile_count: int32 [2048], P(('fy', 'fx')), may hold values from 1 to 255
- thresholds: bfloat16 [8, 8, 2048, 4096], P(None, None, 'fy', 'fx'), may hold values from 0.0099487305 to 1
Outputs:
- new_image: float32 [8, 2048, 4096], P(None, 'fy', 'fx')
The draws below stay inside these ranges and needn't reach their ends.
Inputs may be any that keep to these rules, and one draw needn't show every extreme that they name: `tile_dest`: of the tiles of one device, at most 2 name one facet column, and some device has exactly 2 naming one.
All inputs are finite; a program needn't handle non-finite values.
Results may differ from the reference program's by a relative error of at most 0.0073.
Values may be sent and summed in bfloat16 or wider, within the bound.
A program may use at most 192 MiB of HBM per device.

```python
import math
import jax
import jax.numpy as jnp
import numpy as np
from jax import lax

CHANNELS = 8
SIDE = 256
BASES = 8
TILES_DEV = 16
CAPACITY = 2
TILES_ALL = 2048
IMG_ROWS = 2048
IMG_COLS = 4096
N_FY = 8
N_FX = 16


def with_ends(values, stream_key, smallest, largest):
    extent = values.shape
    index_at = [jax.random.randint(jax.random.fold_in(stream_key, axis), (), 0, extent[axis]) for axis in range(len(extent))]
    values = values.at[tuple(index_at)].set(smallest)
    longest = extent.index(max(extent))
    index_at[longest] = (index_at[longest] + 1) % extent[longest]
    return values.at[tuple(index_at)].set(largest)


def shard_levels(key, extent, pieces, low, high):
    def one(dim, blocks):
        steps = jax.random.uniform(jax.random.fold_in(jax.random.fold_in(key, 6), dim), (blocks,), jnp.float32, low / len(pieces), high / len(pieces))
        return jnp.repeat(jnp.exp(steps), extent[dim] // blocks).reshape((-1,) + (1,) * (len(extent) - dim - 1))

    level = one(*pieces[0])
    for cut in pieces[1:]:
        level = level * one(*cut)
    return level


def deal_out(rng, own, number, rows, amount, top, limit, slope):
    sequence = jax.random.permutation(rng, amount)
    heavy_load, ordinary = shares(amount, rows * top, limit, slope, True), shares(amount, rows * top, limit, slope, False)
    places = jnp.arange(amount)

    def named(sizes, offset_by):
        used = int((sizes > 0).sum())
        fixed = max(1, used // 4)
        passed = fixed + (places - fixed + offset_by * (used - fixed)) % max(1, amount - fixed)
        return jnp.zeros((amount,), jnp.int32).at[sequence[jnp.where(places < fixed, places, passed)]].set(jnp.asarray(sizes, jnp.int32))

    sizes = jnp.where(number % 4 == 0, named(heavy_load, number // 4), named(ordinary, number - number // 4 - 1))
    mixed = jax.random.permutation(jax.random.fold_in(own, 3), amount)
    source_of, taker = mixed[0:amount // 2 * 2:2], mixed[1:amount // 2 * 2:2]
    margin = jnp.minimum(sizes[source_of] - 1, limit - sizes[taker]) // 2
    margin = jnp.where((source_of == sequence[0]) | (taker == sequence[0]) | (sizes[taker] == 0), 0, jnp.maximum(margin, 0))
    passed = jax.random.randint(jax.random.fold_in(own, 4), (amount // 2,), 0, 1 << 20) % (margin + 1)
    sizes = sizes.at[source_of].add(-passed).at[taker].add(passed)
    items = jnp.searchsorted(jnp.cumsum(sizes), jnp.arange(rows * top), side="right").astype(jnp.int32)
    listing = items.reshape(top, rows).T
    listing = listing[jax.random.permutation(jax.random.fold_in(own, 1), rows)]
    offset_by = jax.random.randint(jax.random.fold_in(own, 2), (rows, 1), 0, top)
    return jnp.take_along_axis(listing, (jnp.arange(top)[None, :] + offset_by) % top, axis=1)


def shares(amount, total, most, slope, full):
    portions = [(1 << 20) // math.isqrt(standing ** slope) + 1 for standing in range(1, amount + 1)]
    largest = most if full else min(most, max(-(-total // amount), total * portions[0] // sum(portions)))
    least = 1 if total - largest >= amount - 1 else 0
    holding, surplus = [largest] + [least] * (amount - 1), total - largest - least * (amount - 1)
    while surplus > 0:
        free = [i for i in range(1, amount) if holding[i] < largest] or [i for i in range(1, amount) if holding[i] < most]
        whole, budget = sum([portions[i] for i in free]), surplus
        for i in free:
            more = min(most - holding[i], max(1, budget * portions[i] // whole), surplus)
            holding[i] = holding[i] + more
            surplus = surplus - more
    return np.array(holding)


def gaussian(rng, shape, spread, most, cuts=(), kind=jnp.bfloat16):
    loudness = shard_levels(rng, shape, cuts, -0.22, 0.18) if cuts else 1.0
    drawn = jax.random.normal(rng, shape, jnp.float32) * spread * loudness
    return jnp.minimum(jnp.maximum(drawn, -most), most).astype(kind)


def setup_inputs(seed: int = 0) -> dict:
    seeds = jax.random.split(jax.random.key(seed), 7)
    sky_image = jnp.clip(2.0 * jax.random.uniform(seeds[0], (CHANNELS, IMG_ROWS, IMG_COLS), jnp.float32) ** shard_levels(seeds[0], (CHANNELS, IMG_ROWS, IMG_COLS), ((1, 8), (2, 16)), -0.2, 0.2), 0.0, 2.0)
    vis_tiles = gaussian(seeds[1], (TILES_ALL, 2, SIDE, SIDE), 1.0, 6.0, ((0, 128),))
    tile_dest_keys = jax.random.split(jax.random.fold_in(seeds[2], 1), TILES_ALL // TILES_DEV)
    tile_dest_turns = jax.random.permutation(jax.random.fold_in(seeds[2], 3), TILES_ALL // TILES_DEV)
    tile_dest = jax.vmap(lambda own, number: deal_out(jax.random.fold_in(seeds[2], 2), own, number, TILES_DEV, N_FX, 1, CAPACITY, 2))(tile_dest_keys, tile_dest_turns).reshape((TILES_ALL, 1))
    tile_chan = with_ends(jax.random.randint(seeds[3], (TILES_ALL,), 0, CHANNELS), jax.random.fold_in(seeds[3], 1), 0, CHANNELS - 1).astype(jnp.int32)
    tile_count = with_ends(jax.random.randint(seeds[4], (TILES_ALL,), 1, 256), jax.random.fold_in(seeds[4], 1), 1, 255).astype(jnp.int32)
    thresholds = jnp.clip(jnp.exp(math.log(1.0) - 4.61031033 * jax.random.uniform(seeds[5], (BASES, CHANNELS, IMG_ROWS, IMG_COLS), jnp.float32) ** shard_levels(seeds[5], (BASES, CHANNELS, IMG_ROWS, IMG_COLS), ((2, 8), (3, 16)), -0.2, 0.2)), 0.0099487305, 1.0).astype(jnp.bfloat16)
    return {"sky_image": sky_image, "vis_tiles": vis_tiles, "tile_dest": tile_dest, "tile_chan": tile_chan, "tile_count": tile_count, "thresholds": thresholds}


daubechies_taps = [[0.7071067811865476, 0.7071067811865476], [0.48296291314469025, 0.836516303737469, 0.22414386804185735, -0.12940952255092145], [0.3326705529509569, 0.8068915093133388, 0.4598775021193313, -0.13501102001039084, -0.08544127388224149, 0.035226291882100656], [0.23037781330885523, 0.7148465705525415, 0.6308807679295904, -0.02798376941698385, -0.18703481171888114, 0.030841381835986965, 0.032883011666982945, -0.010597401784997278], [0.160102397974125, 0.6038292697974729, 0.7243085284385744, 0.13842814590110342, -0.24229488706619015, -0.03224486958502952, 0.07757149384006515, -0.006241490213011705, -0.012580751999015526, 0.003335725285001549], [0.11154074335008017, 0.4946238903983854, 0.7511339080215775, 0.3152503517092432, -0.22626469396516913, -0.12976686756709563, 0.09750160558707936, 0.02752286553001629, -0.031582039318031156, 0.0005538422009938016, 0.004777257511010651, -0.00107730108499558], [0.07785205408506236, 0.39653931948230575, 0.7291320908465551, 0.4697822874053586, -0.14390600392910627, -0.22403618499416572, 0.07130921926705004, 0.0806126091510659, -0.03802993693503463, -0.01657454163101562, 0.012550998556013784, 0.00042957797300470274, -0.0018016407039998328, 0.0003537138000010399], [0.05441584224308161, 0.3128715909144659, 0.6756307362980128, 0.5853546836548691, -0.015829105256023893, -0.2840155429624281, 0.00047248457399797254, 0.128747426620186, -0.01736930100202211, -0.04408825393106472, 0.013981027917015516, 0.008746094047015655, -0.00487035299301066, -0.0003917403729959771, 0.0006754494059985568, -0.00011747678400228192]]

def daubechies_bank():
    low_rows = np.zeros((8, 16))
    high_rows = np.zeros((8, 16))
    for degree in range(1, 9):
        filter_taps = np.array(daubechies_taps[degree - 1])
        filter_taps = filter_taps * math.sqrt(2.0) / np.sum(filter_taps)
        length = 2 * degree
        low_rows[degree - 1, :length] = filter_taps
        high_rows[degree - 1, :length] = [(-1.0) ** position * filter_taps[length - 1 - position] for position in range(length)]
    return (low_rows, high_rows)

def band_table(filter_taps, offsets):
    picks = (offsets[:, :, None] == jnp.arange(16, dtype=jnp.int32)[None, None, :]).astype(jnp.float32)
    return jnp.einsum('bj,rcj->brc', filter_taps, picks, precision=lax.Precision.HIGHEST)

def wavelet_tables(facet_side):
    low_bank, high_bank = daubechies_bank()
    lows = jnp.asarray(low_bank, jnp.float32).astype(jnp.bfloat16).astype(jnp.float32)
    highs = jnp.asarray(high_bank, jnp.float32).astype(jnp.bfloat16).astype(jnp.float32)
    half_side = facet_side // 2
    quarter = facet_side // 4
    cells_ext = jnp.arange(facet_side + 48, dtype=jnp.int32)
    coarse_ext = jnp.arange(half_side + 16, dtype=jnp.int32)
    approx_rows = jnp.arange(half_side + 16, dtype=jnp.int32)
    detail_rows = jnp.arange(half_side, dtype=jnp.int32)
    second_rows = jnp.arange(quarter, dtype=jnp.int32)
    analysis_one = jnp.concatenate([band_table(lows, cells_ext[None, :] - 2 * approx_rows[:, None]), band_table(highs, cells_ext[None, :] - 2 * detail_rows[:, None])], axis=1)
    analysis_two = jnp.concatenate([band_table(lows, coarse_ext[None, :] - 2 * second_rows[:, None]), band_table(highs, coarse_ext[None, :] - 2 * second_rows[:, None])], axis=1)
    up_rows = jnp.arange(half_side + 8, dtype=jnp.int32)
    up_cols = jnp.arange(quarter + 16, dtype=jnp.int32)
    offset_two = up_rows[:, None] - 2 * up_cols[None, :] + 24
    synthesis_two = jnp.concatenate([band_table(lows, offset_two), band_table(highs, offset_two)], axis=2)
    cell_rows = jnp.arange(facet_side, dtype=jnp.int32)
    offset_one = cell_rows[:, None] - 2 * up_rows[None, :] + 16
    synthesis_one = jnp.concatenate([band_table(lows, offset_one), band_table(highs, offset_one)], axis=2)
    return (analysis_one.astype(jnp.bfloat16), analysis_two.astype(jnp.bfloat16), synthesis_two.astype(jnp.bfloat16), synthesis_one.astype(jnp.bfloat16))

def fourier_tables(facet_side):
    grid = jnp.arange(facet_side, dtype=jnp.int32)[:, None] * jnp.arange(facet_side, dtype=jnp.int32)[None, :] % facet_side
    angle = grid.astype(jnp.float32) * (2.0 * math.pi / facet_side)
    scale = 1.0 / math.sqrt(facet_side)
    return ((jnp.cos(angle) * scale).astype(jnp.bfloat16), (jnp.sin(angle) * scale).astype(jnp.bfloat16))

def rounded(values):
    return lax.optimization_barrier(values.astype(jnp.bfloat16)).astype(jnp.float32)

def analyze_last(values, analysis_one, analysis_two):
    length = values.shape[-1]
    blocks = values.reshape(values.shape[:-1] + (length // SIDE, SIDE))
    next_rows = jnp.roll(blocks, -1, axis=-2)[..., :48]
    extended = jnp.concatenate([blocks, next_rows], axis=-1)
    level_one = jnp.einsum('...n,rn->...r', extended, analysis_one, precision=lax.Precision.HIGHEST)
    split_at = SIDE // 2 + 16
    approx = rounded(level_one[..., :split_at])
    level_two = jnp.einsum('...m,rm->...r', approx, analysis_two, precision=lax.Precision.HIGHEST)
    joined = jnp.concatenate([level_two, level_one[..., split_at:]], axis=-1)
    return joined.reshape(values.shape)

def synth_last(values, synthesis_two, synthesis_one):
    length = values.shape[-1]
    quarter = SIDE // 4
    half_side = SIDE // 2
    blocks = values.reshape(values.shape[:-1] + (length // SIDE, SIDE))
    behind = jnp.roll(blocks, 1, axis=-2)
    coarse = jnp.concatenate([behind[..., quarter - 16:quarter], blocks[..., :quarter], behind[..., half_side - 16:half_side], blocks[..., quarter:half_side]], axis=-1)
    approx = rounded(jnp.einsum('...m,km->...k', coarse, synthesis_two, precision=lax.Precision.HIGHEST))
    fine_part = jnp.concatenate([approx, behind[..., SIDE - 8:], blocks[..., half_side:]], axis=-1)
    joined = jnp.einsum('...k,nk->...n', fine_part, synthesis_one, precision=lax.Precision.HIGHEST)
    return joined.reshape(values.shape)

def reference(sky_image, vis_tiles, tile_dest, tile_chan, tile_count, thresholds):
    weight = tile_count.astype(jnp.float32) / 64.0
    tile_ids = jnp.arange(TILES_ALL, dtype=jnp.int32)
    facet = tile_ids // (N_FX * TILES_DEV) * N_FX + tile_dest[:, 0]
    segment = (facet * CHANNELS + tile_chan).astype(jnp.int32)
    groups = N_FY * N_FX * CHANNELS
    gathered = jax.ops.segment_sum(weight[:, None, None, None] * vis_tiles.astype(jnp.float32), segment, num_segments=groups)
    totals = jax.ops.segment_sum(weight, segment, num_segments=groups)
    gathered = gathered.reshape(N_FY, N_FX, CHANNELS, 2, SIDE, SIDE).transpose(3, 2, 0, 4, 1, 5)
    totals = totals.reshape(N_FY, N_FX, CHANNELS).transpose(2, 0, 1)[:, :, None, :, None]
    cosine_b, sine_b = fourier_tables(SIDE)
    cosine = cosine_b.astype(jnp.float32)
    sine_table = sine_b.astype(jnp.float32)
    high = lax.Precision.HIGHEST
    facets = rounded(sky_image).reshape(CHANNELS, N_FY, SIDE, N_FX, SIDE)
    half_re = rounded(jnp.einsum('cfyhx,xv->cfyhv', facets, cosine, precision=high))
    half_im = rounded(-jnp.einsum('cfyhx,xv->cfyhv', facets, sine_table, precision=high))
    model_re = jnp.einsum('uy,cfyhv->cfuhv', cosine, half_re, precision=high) + jnp.einsum('uy,cfyhv->cfuhv', sine_table, half_im, precision=high)
    model_im = jnp.einsum('uy,cfyhv->cfuhv', cosine, half_im, precision=high) - jnp.einsum('uy,cfyhv->cfuhv', sine_table, half_re, precision=high)
    resid_re = rounded(totals * model_re - gathered[0])
    resid_im = rounded(totals * model_im - gathered[1])
    back_re = rounded(jnp.einsum('uy,cfuhv->cfyhv', cosine, resid_re, precision=high) - jnp.einsum('uy,cfuhv->cfyhv', sine_table, resid_im, precision=high))
    back_im = rounded(jnp.einsum('uy,cfuhv->cfyhv', cosine, resid_im, precision=high) + jnp.einsum('uy,cfuhv->cfyhv', sine_table, resid_re, precision=high))
    gradient = jnp.einsum('cfyhv,xv->cfyhx', back_re, cosine, precision=high) - jnp.einsum('cfyhv,xv->cfyhx', back_im, sine_table, precision=high)
    stepped = rounded(sky_image - (gradient / (1.0 + totals)).reshape(CHANNELS, IMG_ROWS, IMG_COLS))
    tables = [table.astype(jnp.float32) for table in wavelet_tables(SIDE)]

    def per_basis(running, basis_index):
        analysis_one = tables[0][basis_index]
        analysis_two = tables[1][basis_index]
        synthesis_two = tables[2][basis_index]
        synthesis_one = tables[3][basis_index]
        row_section = rounded(analyze_last(jnp.swapaxes(stepped, 1, 2), analysis_one, analysis_two))
        row_section = jnp.swapaxes(row_section, 1, 2)
        coefficient = analyze_last(row_section, analysis_one, analysis_two)
        limits = thresholds[basis_index].astype(jnp.float32)
        shrunk = rounded(jnp.sign(coefficient) * jnp.maximum(jnp.abs(coefficient) - limits, 0.0))
        col_section = rounded(synth_last(shrunk, synthesis_two, synthesis_one))
        cell_terms = jnp.swapaxes(synth_last(jnp.swapaxes(col_section, 1, 2), synthesis_two, synthesis_one), 1, 2)
        return (running + cell_terms, None)
    start = jnp.zeros((CHANNELS, IMG_ROWS, IMG_COLS), jnp.float32)
    summed, unused = lax.scan(per_basis, start, jnp.arange(BASES, dtype=jnp.int32))
    return jnp.maximum(summed / BASES, 0.0)
```

```python
import functools
import math

import jax
import jax.numpy as jnp
import ml_dtypes
import numpy as np
from jax import lax
from jax.experimental import pallas as pl
from jax.experimental.pallas import tpu as pltpu
from jax.sharding import PartitionSpec as P

daubechies_taps = [
    [0.7071067811865476, 0.7071067811865476],
    [0.48296291314469025, 0.836516303737469, 0.22414386804185735, -0.12940952255092145],
    [
        0.3326705529509569,
        0.8068915093133388,
        0.4598775021193313,
        -0.13501102001039084,
        -0.08544127388224149,
        0.035226291882100656,
    ],
    [
        0.23037781330885523,
        0.7148465705525415,
        0.6308807679295904,
        -0.02798376941698385,
        -0.18703481171888114,
        0.030841381835986965,
        0.032883011666982945,
        -0.010597401784997278,
    ],
    [
        0.160102397974125,
        0.6038292697974729,
        0.7243085284385744,
        0.13842814590110342,
        -0.24229488706619015,
        -0.03224486958502952,
        0.07757149384006515,
        -0.006241490213011705,
        -0.012580751999015526,
        0.003335725285001549,
    ],
    [
        0.11154074335008017,
        0.4946238903983854,
        0.7511339080215775,
        0.3152503517092432,
        -0.22626469396516913,
        -0.12976686756709563,
        0.09750160558707936,
        0.02752286553001629,
        -0.031582039318031156,
        0.0005538422009938016,
        0.004777257511010651,
        -0.00107730108499558,
    ],
    [
        0.07785205408506236,
        0.39653931948230575,
        0.7291320908465551,
        0.4697822874053586,
        -0.14390600392910627,
        -0.22403618499416572,
        0.07130921926705004,
        0.0806126091510659,
        -0.03802993693503463,
        -0.01657454163101562,
        0.012550998556013784,
        0.00042957797300470274,
        -0.0018016407039998328,
        0.0003537138000010399,
    ],
    [
        0.05441584224308161,
        0.3128715909144659,
        0.6756307362980128,
        0.5853546836548691,
        -0.015829105256023893,
        -0.2840155429624281,
        0.00047248457399797254,
        0.128747426620186,
        -0.01736930100202211,
        -0.04408825393106472,
        0.013981027917015516,
        0.008746094047015655,
        -0.00487035299301066,
        -0.0003917403729959771,
        0.0006754494059985568,
        -0.00011747678400228192,
    ],
]


SIDE = 256
CH = 8
BASES = 8
HALO = 48
BF = jnp.bfloat16
F32 = jnp.float32
SEGMENTS = ((48, 64), (112, 128), (240, 256))
SEG_ROWS = 48


def rounded(table):
    return np.asarray(table, np.float32).astype(ml_dtypes.bfloat16)


def composite_tables():
    full = np.zeros((BASES, SIDE, SIDE + HALO))
    for degree in range(1, 9):
        taps = np.array(daubechies_taps[degree - 1])
        taps = taps * math.sqrt(2.0) / np.sum(taps)
        length = 2 * degree
        low = np.zeros(16)
        high = np.zeros(16)
        low[:length] = taps
        high[:length] = [(-1.0) ** j * taps[length - 1 - j] for j in range(length)]
        low = rounded(low).astype(np.float64)
        high = rounded(high).astype(np.float64)
        level_low = np.zeros((144, SIDE + HALO))
        level_high = np.zeros((128, SIDE + HALO))
        for k in range(144):
            level_low[k, 2 * k : 2 * k + 16] = low[: min(16, SIDE + HALO - 2 * k)]
        for k in range(128):
            level_high[k, 2 * k : 2 * k + 16] = high
        second = np.zeros((128, 144))
        for m in range(64):
            second[m, 2 * m : 2 * m + 16] = low
            second[64 + m, 2 * m : 2 * m + 16] = high
        full[degree - 1, :128] = second @ level_low
        full[degree - 1, 128:] = level_high
    return rounded(full).astype(np.float32)


@functools.lru_cache(maxsize=1)
def tables():
    full = composite_tables()
    main = full[:, :, :SIDE]
    over = full[:, :, SIDE:]
    seg = np.concatenate([np.arange(a, b) for a, b in SEGMENTS])
    assert not np.any(np.delete(over, seg, axis=1))
    flat = main.reshape(BASES * SIDE, SIDE)
    out = {"t_cols": flat.T}
    keep = np.setdiff1d(np.arange(SIDE), seg)
    out["inner_rows"] = main[:, keep].reshape(BASES * len(keep), SIDE)
    out["outer_rows"] = full[:, seg].reshape(BASES * SEG_ROWS, SIDE + HALO)
    analyse = np.zeros((BASES, SIDE + 128, SIDE), np.float32)
    analyse[:, : SIDE + HALO] = full.transpose(0, 2, 1)
    out["analyse"] = analyse
    select = np.zeros((BASES * SIDE, 128), np.float32)
    synthesise = np.zeros((BASES, SIDE + 128, SIDE), np.float32)
    synthesise[:, :SIDE] = main
    at = 0
    for b in range(BASES):
        for k in np.nonzero(np.any(over[b] != 0, axis=1))[0]:
            select[b * SIDE + k, at] = 1.0
            synthesise[b, SIDE + at, :HALO] = over[b, k]
            at += 1
    assert at <= 128 and not np.any(over[0])
    out["select"] = select
    out["synthesise"] = synthesise
    top = np.zeros((HALO, 3, BASES - 1, 16), np.float32)
    for i, (a, b) in enumerate(SEGMENTS):
        top[:, i] = over[1:, a:b].transpose(2, 0, 1)
    out["top"] = top.reshape(HALO, 3 * (BASES - 1) * 16)
    grid = np.arange(SIDE)[:, None] * np.arange(SIDE)[None, :] % SIDE
    angle = grid * (2.0 * math.pi / SIDE)
    cosine = rounded(np.cos(angle) / math.sqrt(SIDE)).astype(np.float64)
    sine = rounded(np.sin(angle) / math.sqrt(SIDE)).astype(np.float64)
    out["fourier"] = np.block([[cosine, sine], [-sine, cosine]])
    out["back"] = np.concatenate([cosine, -sine], axis=1)
    out["excess"] = cosine @ cosine + sine @ sine - np.eye(SIDE)
    return {name: rounded(table) for name, table in out.items()}


TABLES = ("t_cols", "inner_rows", "outer_rows", "analyse", "select", "synthesise", "top")


NEAR = ((1, 0), (3, 0), (0, 1), (0, 3), (1, 1), (1, 3), (3, 1), (3, 3))
FAR = ((2, 0), (0, 2), (2, 1), (2, 3), (1, 2), (3, 2), (2, 2))
THROUGH = (
    ((1, 0), (3, 0)),
    ((0, 1), (0, 3)),
    ((1, 1), (3, 1)),
    ((1, 3), (3, 3)),
    ((1, 1), (1, 3)),
    ((3, 1), (3, 3)),
    ((1, 1), (3, 3)),
)


def choose(j, values):
    out = jnp.int32(values[0])
    for i, value in enumerate(values):
        out = jnp.where(j == i, jnp.int32(value), out)
    return out


def dot(a, b):
    return jnp.dot(a, b, preferred_element_type=F32)


def exchange_kernel(
    n_fx,
    dest_ref,
    chan_ref,
    count_ref,
    fourier,
    back,
    excess,
    sky_hbm,
    vis_hbm,
    stepped,
    columns,
    vis,
    sky,
    model,
    sending,
    arrived,
    relay,
    share_ref,
    shares,
    kron,
    load_sem,
    tile_send,
    tile_recv,
    relay_send,
    relay_recv,
    share_send,
    share_recv,
):
    fx = lax.axis_index("fx")
    n_z = 4
    n_x = n_fx // n_z
    my_x, my_z = fx // n_z, fx % n_z

    def at(dx, dz):
        return (my_x + dx) % n_x * n_z + (my_z + dz) % n_z

    def peer(k):
        return at(k // n_z, k % n_z)

    load_vis = pltpu.make_async_copy(vis_hbm, vis, load_sem.at[0])
    load_sky = pltpu.make_async_copy(sky_hbm, sky, load_sem.at[1])
    load_vis.start()
    load_sky.start()

    barrier = pltpu.get_barrier_semaphore()

    def greet(k, carry):
        pl.semaphore_signal(
            barrier, inc=1, device_id={"fx": peer(k)}, device_id_type=pl.DeviceIdType.MESH
        )
        return carry

    lax.fori_loop(1, n_fx, greet, 0)
    pl.semaphore_wait(barrier, n_fx - 1)

    def share_copy(to, source):
        return pltpu.make_async_remote_copy(
            src_ref=share_ref.at[to],
            dst_ref=shares.at[source],
            send_sem=share_send.at[to],
            recv_sem=share_recv.at[source],
            device_id={"fx": to},
            device_id_type=pl.DeviceIdType.MESH,
        )

    def near(j):
        return choose(j, [o[0] for o in NEAR]), choose(j, [o[1] for o in NEAR])

    def far(j):
        return choose(j, [o[0] for o in FAR]), choose(j, [o[1] for o in FAR])

    def through(j, r):
        return (
            choose(j, [o[r][0] for o in THROUGH]),
            choose(j, [o[r][1] for o in THROUGH]),
        )

    def near_copy(j):
        return pltpu.make_async_remote_copy(
            src_ref=sending.at[len(FAR) + j],
            dst_ref=arrived.at[fx],
            send_sem=tile_send.at[len(FAR) + j, 0],
            recv_sem=tile_recv.at[fx, 0],
            device_id={"fx": at(*near(j))},
            device_id_type=pl.DeviceIdType.MESH,
        )

    def far_copy(j, r):
        return pltpu.make_async_remote_copy(
            src_ref=sending.at[j, r],
            dst_ref=relay.at[j, r],
            send_sem=tile_send.at[j, r],
            recv_sem=relay_recv.at[j, r],
            device_id={"fx": at(*through(j, r))},
            device_id_type=pl.DeviceIdType.MESH,
        )

    def relay_copy(j, r):
        end, mid = far(j), through(j, r)
        source = at(4 - mid[0], 4 - mid[1])
        return pltpu.make_async_remote_copy(
            src_ref=relay.at[j, r],
            dst_ref=arrived.at[source, r],
            send_sem=relay_send.at[j, r],
            recv_sem=tile_recv.at[source, r],
            device_id={"fx": at(end[0] + 4 - mid[0], end[1] + 4 - mid[1])},
            device_id_type=pl.DeviceIdType.MESH,
        )

    def near_arrival(j):
        dx, dz = near(j)
        source = at(4 - dx, 4 - dz)
        return pltpu.make_async_remote_copy(
            src_ref=arrived.at[source],
            dst_ref=arrived.at[source],
            send_sem=tile_send.at[0, 0],
            recv_sem=tile_recv.at[source, 0],
            device_id={"fx": source},
            device_id_type=pl.DeviceIdType.MESH,
        )

    def far_arrival(j, r):
        dx, dz = far(j)
        source = at(4 - dx, 4 - dz)
        return pltpu.make_async_remote_copy(
            src_ref=arrived.at[source, r],
            dst_ref=arrived.at[source, r],
            send_sem=tile_send.at[0, 0],
            recv_sem=tile_recv.at[source, r],
            device_id={"fx": source},
            device_id_type=pl.DeviceIdType.MESH,
        )

    tiles = vis_hbm.shape[0]
    row = lax.broadcasted_iota(jnp.int32, (8, 128), 0)
    lane = lax.broadcasted_iota(jnp.int32, (8, 128), 1)

    def slots_for(to):
        found = jnp.int32(0)
        picked = [(jnp.int32(0), jnp.int32(0), jnp.int32(0))] * 2
        for i in range(tiles):
            match = dest_ref[i, 0] == to
            for r in range(2):
                here = match & (found == r)
                new = (jnp.int32(i), count_ref[i], chan_ref[i])
                picked[r] = tuple(jnp.where(here, a, b) for a, b in zip(new, picked[r]))
            found = found + jnp.where(match, 1, 0)
        return [(tile, count.astype(F32) * (1.0 / 64.0), chan) for tile, count, chan in picked]

    def share_rows(slots):
        total = jnp.zeros((8, 128), F32)
        for r, (_, weight, chan) in enumerate(slots):
            total = total + jnp.where((row == r) & (lane == chan), weight, 0.0)
        return total

    load_vis.wait()

    def planes(slots):
        spectra = [jnp.concatenate([vis[t, 0], vis[t, 1]], axis=1) for t, _, _ in slots]
        both = dot(jnp.concatenate(spectra, axis=0), fourier[...]).astype(BF)
        stacked = [
            jnp.concatenate(
                [both[i * SIDE : (i + 1) * SIDE, :SIDE], both[i * SIDE : (i + 1) * SIDE, SIDE:]],
                axis=0,
            )
            for i in range(2)
        ]
        flat = dot(back[...], jnp.concatenate(stacked, axis=1))
        return [
            (flat[:, i * SIDE : (i + 1) * SIDE] * slots[i][1]).astype(BF) for i in range(2)
        ]

    def prepare(to, place):
        slots = slots_for(to)
        share_ref[to] = share_rows(slots)
        share_copy(to, fx).start()
        sending[place, 0], sending[place, 1] = planes(slots)

    def send_far(j, carry):
        prepare(at(*far(j)), j)
        far_copy(j, 0).start()
        far_copy(j, 1).start()
        return carry

    lax.fori_loop(0, len(FAR), send_far, 0)

    def send_near(j, carry):
        prepare(at(*near(j)), len(FAR) + j)
        near_copy(j).start()

        @pl.when(j >= 1)
        def _():
            for r in range(2):
                far_copy(j - 1, r).wait_recv()
                relay_copy(j - 1, r).start()

        return carry

    lax.fori_loop(0, len(NEAR), send_near, 0)
    own = slots_for(fx)
    shares[fx] = share_rows(own)
    arrived[fx, 0], arrived[fx, 1] = planes(own)

    load_sky.wait()

    def there_and_back(c, carry):
        pixels = sky[c].astype(BF)
        half = pixels.astype(F32) + dot(excess[...], pixels)
        model[c] = half + dot(half.astype(BF), excess[...])
        return carry

    lax.fori_loop(0, CH, there_and_back, 0)

    def wait_share(k, carry):
        share_copy(peer(k), peer(k)).wait_recv()
        return carry

    lax.fori_loop(1, n_fx, wait_share, 0)
    slots = n_fx * 2
    wide = slots * 16
    all_shares = shares[...].reshape(n_fx * 8, 128)
    members = jnp.where(all_shares > 0, 1.0, 0.0).astype(BF)
    spread = (
        lax.broadcasted_iota(jnp.int32, (CH * 16, 128), 0) // 16
        == lax.broadcasted_iota(jnp.int32, (CH * 16, 128), 1)
    )
    spread = jnp.where(spread, 1.0, 0.0).astype(BF)
    by_source = lax.dot_general(
        spread, members, (((1,), (1,)), ((), ())), preferred_element_type=F32
    ).astype(BF)
    weights = lax.dot_general(
        spread, all_shares.astype(BF), (((1,), (1,)), ((), ())), preferred_element_type=F32
    )
    totals = jnp.sum(weights, axis=1, keepdims=True)
    src_row = lax.broadcasted_iota(jnp.int32, (n_fx * 8, wide), 0)
    dst_col = lax.broadcasted_iota(jnp.int32, (n_fx * 8, wide), 1)
    widen = (src_row // 8 == dst_col // 32) & (src_row % 8 == dst_col // 16 % 2)
    widened = dot(by_source, jnp.where(widen, 1.0, 0.0).astype(BF))
    diagonal = (
        lax.broadcasted_iota(jnp.int32, (CH * 16, wide), 0) % 16
        == lax.broadcasted_iota(jnp.int32, (CH * 16, wide), 1) % 16
    )
    kron[...] = jnp.where(diagonal, widened, 0.0).astype(BF)
    scale = 1.0 / (1.0 + totals)

    def wait_near(j, carry):
        near_arrival(j).wait_recv()
        return carry

    def wait_far(j, carry):
        for r in range(2):
            far_arrival(j, r).wait_recv()
        return carry

    lax.fori_loop(0, len(NEAR), wait_near, 0)
    lax.fori_loop(0, len(FAR), wait_far, 0)

    def combine(g, carry):
        rows = pl.ds(pl.multiple_of(g * 16, 16), 16)
        gathered = dot(kron[...], arrived[:, :, rows, :].reshape(wide, SIDE))
        pixels = sky[:, rows, :].reshape(CH * 16, SIDE)
        there = model[:, rows, :].reshape(CH * 16, SIDE)
        new = pixels - (totals * there - gathered) * scale
        new = new.reshape(CH // 2, 2, 16, SIDE)
        stepped[:, rows, :] = new.reshape(CH, 16, SIDE).astype(BF)
        low = lax.broadcasted_iota(jnp.int32, (CH // 2, 16, 128), 2) < 64
        second = pltpu.roll(new[:, 1, :, :128].reshape(CH // 2 * 16, 128), 64, 1)
        pair = jnp.where(low, new[:, 0, :, :128], second.reshape(CH // 2, 16, 128))
        columns[:, rows, :] = pair.astype(BF)
        return carry

    lax.fori_loop(0, SIDE // 16, combine, 0)

    def finish_shares(k, carry):
        share_copy(peer(k), fx).wait_send()
        return carry

    def finish_near(j, carry):
        near_copy(j).wait_send()
        return carry

    def finish_far(j, carry):
        for r in range(2):
            far_copy(j, r).wait_send()
            relay_copy(j, r).wait_send()
        return carry

    lax.fori_loop(1, n_fx, finish_shares, 0)
    lax.fori_loop(0, len(NEAR), finish_near, 0)
    lax.fori_loop(0, len(FAR), finish_far, 0)


def wavelet_kernel(
    n_fy,
    n_fx,
    t_cols,
    inner_rows,
    outer_rows,
    analysis,
    select,
    synthesis,
    top,
    stepped,
    columns,
    thr_hbm,
    out_hbm,
    thr,
    below,
    beside,
    corner,
    side,
    row_sec,
    shrunk,
    edge,
    edge_left,
    col_sec,
    edge_top,
    result,
    load_sem,
    halo_send,
    halo_recv,
    edge_send,
    edge_recv,
    rows_send,
    rows_recv,
    out_sem,
):
    fy = lax.axis_index("fy")
    fx = lax.axis_index("fx")
    up, down = (fy + n_fy - 1) % n_fy, (fy + 1) % n_fy
    prev, nxt = (fx + n_fx - 1) % n_fx, (fx + 1) % n_fx

    load_thr = pltpu.make_async_copy(thr_hbm, thr, load_sem.at[0])
    load_thr.start()
    barrier = pltpu.get_barrier_semaphore()
    for where in (
        {"fy": up},
        {"fy": down},
        {"fx": prev},
        {"fx": nxt},
        {"fy": up, "fx": prev},
        {"fy": down, "fx": nxt},
    ):
        pl.semaphore_signal(barrier, inc=1, device_id=where, device_id_type=pl.DeviceIdType.MESH)
    pl.semaphore_wait(barrier, 6)

    def halo_copy(i):
        source = (stepped.at[:, :HALO, :], columns, columns.at[:, :HALO, :])[i]
        target = (below, beside, corner)[i]
        where = ({"fy": up}, {"fx": prev}, {"fy": up, "fx": prev})[i]
        return pltpu.make_async_remote_copy(
            src_ref=source,
            dst_ref=target,
            send_sem=halo_send.at[i],
            recv_sem=halo_recv.at[i],
            device_id=where,
            device_id_type=pl.DeviceIdType.MESH,
        )

    for i in range(3):
        halo_copy(i).start()
    load_thr.wait()
    for i in range(3):
        halo_copy(i).wait_recv()

    def edge_copy(p):
        return pltpu.make_async_remote_copy(
            src_ref=edge.at[p],
            dst_ref=edge_left.at[p],
            send_sem=edge_send.at[p],
            recv_sem=edge_recv.at[p],
            device_id={"fx": nxt},
            device_id_type=pl.DeviceIdType.MESH,
        )

    def rows_copy(p, i):
        return pltpu.make_async_remote_copy(
            src_ref=col_sec.at[p, 1:, SEGMENTS[i][0] : SEGMENTS[i][1], :],
            dst_ref=edge_top.at[p, i],
            send_sem=rows_send.at[p, i],
            recv_sem=rows_recv.at[p, i],
            device_id={"fy": down},
            device_id_type=pl.DeviceIdType.MESH,
        )

    def out_copy(p):
        pair = pl.ds(2 * p, 2)
        return pltpu.make_async_copy(result.at[pair], out_hbm.at[pair], out_sem.at[p])

    for p in range(CH // 2):
        whole = jnp.concatenate([beside[p], corner[p]], axis=0)
        turned = pltpu.roll(whole.astype(F32), 64, 1).astype(BF)
        side[p] = jnp.concatenate([whole, turned], axis=1)

    inner = SIDE - SEG_ROWS

    def analyse(p):
        first = 2 * p
        near = jnp.concatenate([stepped[first], stepped[first + 1], side[p, :SIDE]], axis=1)
        far = jnp.concatenate([below[first], below[first + 1], side[p, SIDE:]], axis=1)
        tall = jnp.concatenate([near, far], axis=0)

        def keep(b, begin, end, values):
            values = values.astype(BF)
            for h in range(2):
                row_sec[b, h, begin:end, :SIDE] = values[:, h * SIDE : (h + 1) * SIDE]
                row_sec[b, h, begin:end, SIDE:] = values[
                    :, 2 * SIDE + h * 128 : 2 * SIDE + (h + 1) * 128
                ]

        for b in range(BASES):
            r = dot(inner_rows[b * inner : (b + 1) * inner], near)
            at = 0
            begin = 0
            for a, e in SEGMENTS:
                keep(b, begin, a, r[at : at + a - begin])
                at += a - begin
                begin = e
        r = dot(outer_rows[...], tall)
        for b in range(BASES):
            for i, (a, e) in enumerate(SEGMENTS):
                at = b * SEG_ROWS + i * 16
                keep(b, a, e, r[at : at + 16])
        for b in range(BASES):
            lanes = slice(b * SIDE, (b + 1) * SIDE)
            coefficient = dot(row_sec[b].reshape(2 * SIDE, SIDE + 128), analysis[b])
            limit = thr[b, pl.ds(first, 2)].reshape(2 * SIDE, SIDE).astype(F32)
            kept = coefficient - jnp.clip(coefficient, -limit, limit)
            shrunk[:, lanes] = kept.astype(BF)
        edge[p] = dot(shrunk[...], select[...]).astype(BF)
        edge_copy(p).start()

    def synthesise_columns(p):
        edge_copy(p).wait_recv()
        for b in range(BASES):
            lanes = slice(b * SIDE, (b + 1) * SIDE)
            with_edge = jnp.concatenate([shrunk[:, lanes], edge_left[p]], axis=1)
            r = dot(with_edge, synthesis[b]).astype(BF)
            col_sec[p, b, :, :SIDE] = r[:SIDE]
            col_sec[p, b, :, SIDE:] = r[SIDE:]
        for i in range(3):
            rows_copy(p, i).start()

    def synthesise_rows(p, carry):
        for i in range(3):
            rows_copy(p, i).wait_recv()
        r = dot(t_cols[...], col_sec[p].reshape(BASES * SIDE, 2 * SIDE))
        t = dot(top[...], edge_top[p].reshape(3 * (BASES - 1) * 16, 2 * SIDE))
        for h in range(2):
            lanes = slice(h * SIDE, (h + 1) * SIDE)
            result[2 * p + h, :HALO] = r[:HALO, lanes] + t[:, lanes]
            result[2 * p + h, HALO:] = r[HALO:, lanes]
        out_copy(p).start()
        return carry

    def step(p, carry):
        @pl.when(p >= 1)
        def _():
            synthesise_columns(p - 1)

        @pl.when(p < CH // 2)
        def _():
            analyse(p)

        return carry

    lax.fori_loop(0, CH // 2 + 1, step, 0)
    lax.fori_loop(0, CH // 2, synthesise_rows, 0)

    for i in range(3):
        halo_copy(i).wait_send()

    def finish(p, carry):
        edge_copy(p).wait_send()
        for i in range(3):
            rows_copy(p, i).wait_send()
        out_copy(p).wait()
        return carry

    lax.fori_loop(0, CH // 2, finish, 0)


def per_device(n_fy, n_fx, sky_image, vis_tiles, tile_dest, tile_chan, tile_count, thresholds):
    made = {name: jnp.asarray(table) for name, table in tables().items()}
    smem = pl.BlockSpec(memory_space=pltpu.SMEM)
    vmem = pl.BlockSpec(memory_space=pltpu.VMEM)
    anywhere = pl.BlockSpec(memory_space=pl.ANY)
    dma = pltpu.SemaphoreType.DMA
    tiles = vis_tiles.shape[0]
    stepped, columns = pl.pallas_call(
        functools.partial(exchange_kernel, n_fx),
        out_shape=(
            jax.ShapeDtypeStruct((CH, SIDE, SIDE), BF),
            jax.ShapeDtypeStruct((CH // 2, SIDE, 128), BF),
        ),
        in_specs=[smem] * 3 + [vmem] * 3 + [anywhere] * 2,
        out_specs=[vmem] * 2,
        scratch_shapes=[
            pltpu.VMEM((tiles, 2, SIDE, SIDE), BF),
            pltpu.VMEM((CH, SIDE, SIDE), F32),
            pltpu.VMEM((CH, SIDE, SIDE), F32),
            pltpu.VMEM((n_fx, 2, SIDE, SIDE), BF),
            pltpu.VMEM((n_fx, 2, SIDE, SIDE), BF),
            pltpu.VMEM((len(FAR), 2, SIDE, SIDE), BF),
            pltpu.VMEM((n_fx, 8, 128), F32),
            pltpu.VMEM((n_fx, 8, 128), F32),
            pltpu.VMEM((CH * 16, n_fx * 32), BF),
            dma((2,)),
            dma((n_fx, 2)),
            dma((n_fx, 2)),
            dma((len(FAR), 2)),
            dma((len(FAR), 2)),
            dma((n_fx,)),
            dma((n_fx,)),
        ],
        compiler_params=pltpu.CompilerParams(
            collective_id=0, has_side_effects=True, vmem_limit_bytes=58 * 1024 * 1024
        ),
    )(
        tile_dest,
        tile_chan,
        tile_count,
        made["fourier"],
        made["back"],
        made["excess"],
        sky_image,
        vis_tiles,
    )
    summed = pl.pallas_call(
        functools.partial(wavelet_kernel, n_fy, n_fx),
        out_shape=jax.ShapeDtypeStruct((CH, SIDE, SIDE), F32),
        in_specs=[vmem] * (len(TABLES) + 2) + [anywhere],
        out_specs=anywhere,
        scratch_shapes=[
            pltpu.VMEM((BASES, CH, SIDE, SIDE), BF),
            pltpu.VMEM((CH, HALO, SIDE), BF),
            pltpu.VMEM((CH // 2, SIDE, 128), BF),
            pltpu.VMEM((CH // 2, HALO, 128), BF),
            pltpu.VMEM((CH // 2, SIDE + HALO, SIDE), BF),
            pltpu.VMEM((BASES, 2, SIDE, SIDE + 128), BF),
            pltpu.VMEM((2 * SIDE, BASES * SIDE), BF),
            pltpu.VMEM((CH // 2, 2 * SIDE, 128), BF),
            pltpu.VMEM((CH // 2, 2 * SIDE, 128), BF),
            pltpu.VMEM((CH // 2, BASES, SIDE, 2 * SIDE), BF),
            pltpu.VMEM((CH // 2, 3, BASES - 1, 16, 2 * SIDE), BF),
            pltpu.VMEM((CH, SIDE, SIDE), F32),
            dma((1,)),
            dma((3,)),
            dma((3,)),
            dma((CH // 2,)),
            dma((CH // 2,)),
            dma((CH // 2, 3)),
            dma((CH // 2, 3)),
            dma((CH // 2,)),
        ],
        compiler_params=pltpu.CompilerParams(
            collective_id=1, has_side_effects=True, vmem_limit_bytes=58 * 1024 * 1024
        ),
    )(*[made[name] for name in TABLES], stepped, columns, thresholds)
    return jnp.maximum(summed * (1.0 / BASES), 0.0)


def solution(mesh):
    in_specs = (
        P(None, "fy", "fx"),
        P(("fy", "fx"), None, None, None),
        P(("fy", "fx"), None),
        P(("fy", "fx")),
        P(("fy", "fx")),
        P(None, None, "fy", "fx"),
    )
    out_specs = P(None, "fy", "fx")
    return jax.shard_map(
        functools.partial(per_device, mesh.shape["fy"], mesh.shape["fx"]),
        mesh=mesh,
        in_specs=in_specs,
        out_specs=out_specs,
        check_vma=False,
    )
```

```python
import functools
import math

import jax
import jax.numpy as jnp
import ml_dtypes
import numpy as np
from jax import lax
from jax.experimental import pallas as pl
from jax.experimental.pallas import tpu as pltpu
from jax.sharding import PartitionSpec as P

daubechies_taps = [
    [0.7071067811865476, 0.7071067811865476],
    [0.48296291314469025, 0.836516303737469, 0.22414386804185735, -0.12940952255092145],
    [
        0.3326705529509569,
        0.8068915093133388,
        0.4598775021193313,
        -0.13501102001039084,
        -0.08544127388224149,
        0.035226291882100656,
    ],
    [
        0.23037781330885523,
        0.7148465705525415,
        0.6308807679295904,
        -0.02798376941698385,
        -0.18703481171888114,
        0.030841381835986965,
        0.032883011666982945,
        -0.010597401784997278,
    ],
    [
        0.160102397974125,
        0.6038292697974729,
        0.7243085284385744,
        0.13842814590110342,
        -0.24229488706619015,
        -0.03224486958502952,
        0.07757149384006515,
        -0.006241490213011705,
        -0.012580751999015526,
        0.003335725285001549,
    ],
    [
        0.11154074335008017,
        0.4946238903983854,
        0.7511339080215775,
        0.3152503517092432,
        -0.22626469396516913,
        -0.12976686756709563,
        0.09750160558707936,
        0.02752286553001629,
        -0.031582039318031156,
        0.0005538422009938016,
        0.004777257511010651,
        -0.00107730108499558,
    ],
    [
        0.07785205408506236,
        0.39653931948230575,
        0.7291320908465551,
        0.4697822874053586,
        -0.14390600392910627,
        -0.22403618499416572,
        0.07130921926705004,
        0.0806126091510659,
        -0.03802993693503463,
        -0.01657454163101562,
        0.012550998556013784,
        0.00042957797300470274,
        -0.0018016407039998328,
        0.0003537138000010399,
    ],
    [
        0.05441584224308161,
        0.3128715909144659,
        0.6756307362980128,
        0.5853546836548691,
        -0.015829105256023893,
        -0.2840155429624281,
        0.00047248457399797254,
        0.128747426620186,
        -0.01736930100202211,
        -0.04408825393106472,
        0.013981027917015516,
        0.008746094047015655,
        -0.00487035299301066,
        -0.0003917403729959771,
        0.0006754494059985568,
        -0.00011747678400228192,
    ],
]


SIDE = 256
CH = 8
BASES = 8
HALO = 48
BF = jnp.bfloat16
F32 = jnp.float32
SEGMENTS = ((48, 64), (112, 128), (240, 256))
SEG_ROWS = 48


def rounded(table):
    return np.asarray(table, np.float32).astype(ml_dtypes.bfloat16)


def composite_tables():
    full = np.zeros((BASES, SIDE, SIDE + HALO))
    for degree in range(1, 9):
        taps = np.array(daubechies_taps[degree - 1])
        taps = taps * math.sqrt(2.0) / np.sum(taps)
        length = 2 * degree
        low = np.zeros(16)
        high = np.zeros(16)
        low[:length] = taps
        high[:length] = [(-1.0) ** j * taps[length - 1 - j] for j in range(length)]
        low = rounded(low).astype(np.float64)
        high = rounded(high).astype(np.float64)
        level_low = np.zeros((144, SIDE + HALO))
        level_high = np.zeros((128, SIDE + HALO))
        for k in range(144):
            level_low[k, 2 * k : 2 * k + 16] = low[: min(16, SIDE + HALO - 2 * k)]
        for k in range(128):
            level_high[k, 2 * k : 2 * k + 16] = high
        second = np.zeros((128, 144))
        for m in range(64):
            second[m, 2 * m : 2 * m + 16] = low
            second[64 + m, 2 * m : 2 * m + 16] = high
        full[degree - 1, :128] = second @ level_low
        full[degree - 1, 128:] = level_high
    return rounded(full).astype(np.float32)


@functools.lru_cache(maxsize=1)
def tables():
    full = composite_tables()
    main = full[:, :, :SIDE]
    over = full[:, :, SIDE:]
    seg = np.concatenate([np.arange(a, b) for a, b in SEGMENTS])
    assert not np.any(np.delete(over, seg, axis=1))
    flat = main.reshape(BASES * SIDE, SIDE)
    out = {"t_cols": flat.T}
    out["inner_rows"] = main[:, np.setdiff1d(np.arange(SIDE), seg)]
    out["outer_rows"] = full[:, seg]
    analyse = np.zeros((BASES, SIDE + 128, SIDE), np.float32)
    analyse[:, : SIDE + HALO] = full.transpose(0, 2, 1)
    out["analyse"] = analyse
    select = np.zeros((BASES * SIDE, 128), np.float32)
    synthesise = np.zeros((BASES, SIDE + 128, SIDE), np.float32)
    synthesise[:, :SIDE] = main
    at = 0
    for b in range(BASES):
        for k in np.nonzero(np.any(over[b] != 0, axis=1))[0]:
            select[b * SIDE + k, at] = 1.0
            synthesise[b, SIDE + at, :HALO] = over[b, k]
            at += 1
    assert at <= 128 and not np.any(over[0])
    out["select"] = select
    out["synthesise"] = synthesise
    top = np.zeros((HALO, 3, BASES - 1, 16), np.float32)
    for i, (a, b) in enumerate(SEGMENTS):
        top[:, i] = over[1:, a:b].transpose(2, 0, 1)
    out["top"] = top.reshape(HALO, 3 * (BASES - 1) * 16)
    grid = np.arange(SIDE)[:, None] * np.arange(SIDE)[None, :] % SIDE
    angle = grid * (2.0 * math.pi / SIDE)
    cosine = rounded(np.cos(angle) / math.sqrt(SIDE)).astype(np.float64)
    sine = rounded(np.sin(angle) / math.sqrt(SIDE)).astype(np.float64)
    out["fourier"] = np.block([[cosine, sine], [-sine, cosine]])
    out["back"] = np.concatenate([cosine, -sine], axis=1)
    out["excess"] = cosine @ cosine + sine @ sine - np.eye(SIDE)
    return {name: rounded(table) for name, table in out.items()}


TABLES = ("t_cols", "inner_rows", "outer_rows", "analyse", "select", "synthesise", "top")


NEAR = ((1, 0), (3, 0), (0, 1), (0, 3), (1, 1), (1, 3), (3, 1), (3, 3))
FAR = ((2, 0), (0, 2), (2, 1), (2, 3), (1, 2), (3, 2), (2, 2))
THROUGH = (
    ((1, 0), (3, 0)),
    ((0, 1), (0, 3)),
    ((1, 1), (3, 1)),
    ((1, 3), (3, 3)),
    ((1, 1), (1, 3)),
    ((3, 1), (3, 3)),
    ((1, 1), (3, 3)),
)


def choose(j, values):
    out = jnp.int32(values[0])
    for i, value in enumerate(values):
        out = jnp.where(j == i, jnp.int32(value), out)
    return out


def dot(a, b):
    return jnp.dot(a, b, preferred_element_type=F32)


def exchange_kernel(
    n_fx,
    dest_ref,
    chan_ref,
    count_ref,
    fourier,
    back,
    excess,
    sky_hbm,
    vis_hbm,
    stepped,
    columns,
    vis,
    sky,
    model,
    sending,
    arrived,
    relay,
    half,
    share_ref,
    shares,
    kron,
    load_sem,
    tile_send,
    tile_recv,
    relay_send,
    relay_recv,
    share_send,
    share_recv,
):
    fx = lax.axis_index("fx")
    n_z = 4
    n_x = n_fx // n_z
    my_x, my_z = fx // n_z, fx % n_z

    def at(dx, dz):
        return (my_x + dx) % n_x * n_z + (my_z + dz) % n_z

    def peer(k):
        return at(k // n_z, k % n_z)

    load_vis = pltpu.make_async_copy(vis_hbm, vis, load_sem.at[0])
    load_sky = pltpu.make_async_copy(sky_hbm, sky, load_sem.at[1])
    load_vis.start()
    load_sky.start()

    barrier = pltpu.get_barrier_semaphore()

    def greet(k, carry):
        pl.semaphore_signal(
            barrier, inc=1, device_id={"fx": peer(k)}, device_id_type=pl.DeviceIdType.MESH
        )
        return carry

    lax.fori_loop(1, n_fx, greet, 0)
    pl.semaphore_wait(barrier, n_fx - 1)

    def share_copy(to, source):
        return pltpu.make_async_remote_copy(
            src_ref=share_ref.at[to],
            dst_ref=shares.at[source],
            send_sem=share_send.at[to],
            recv_sem=share_recv.at[source],
            device_id={"fx": to},
            device_id_type=pl.DeviceIdType.MESH,
        )

    def near(j):
        return choose(j, [o[0] for o in NEAR]), choose(j, [o[1] for o in NEAR])

    def far(j):
        return choose(j, [o[0] for o in FAR]), choose(j, [o[1] for o in FAR])

    def through(j, r):
        return (
            choose(j, [o[r][0] for o in THROUGH]),
            choose(j, [o[r][1] for o in THROUGH]),
        )

    def near_copy(j):
        return pltpu.make_async_remote_copy(
            src_ref=sending.at[len(FAR) + j],
            dst_ref=arrived.at[fx],
            send_sem=tile_send.at[len(FAR) + j, 0],
            recv_sem=tile_recv.at[fx, 0],
            device_id={"fx": at(*near(j))},
            device_id_type=pl.DeviceIdType.MESH,
        )

    def far_copy(j, r):
        return pltpu.make_async_remote_copy(
            src_ref=sending.at[j, r],
            dst_ref=relay.at[j, r],
            send_sem=tile_send.at[j, r],
            recv_sem=relay_recv.at[j, r],
            device_id={"fx": at(*through(j, r))},
            device_id_type=pl.DeviceIdType.MESH,
        )

    def relay_copy(j, r):
        end, mid = far(j), through(j, r)
        source = at(4 - mid[0], 4 - mid[1])
        return pltpu.make_async_remote_copy(
            src_ref=relay.at[j, r],
            dst_ref=arrived.at[source, r],
            send_sem=relay_send.at[j, r],
            recv_sem=tile_recv.at[source, r],
            device_id={"fx": at(end[0] + 4 - mid[0], end[1] + 4 - mid[1])},
            device_id_type=pl.DeviceIdType.MESH,
        )

    def near_arrival(j):
        dx, dz = near(j)
        source = at(4 - dx, 4 - dz)
        return pltpu.make_async_remote_copy(
            src_ref=arrived.at[source],
            dst_ref=arrived.at[source],
            send_sem=tile_send.at[0, 0],
            recv_sem=tile_recv.at[source, 0],
            device_id={"fx": source},
            device_id_type=pl.DeviceIdType.MESH,
        )

    def far_arrival(j, r):
        dx, dz = far(j)
        source = at(4 - dx, 4 - dz)
        return pltpu.make_async_remote_copy(
            src_ref=arrived.at[source, r],
            dst_ref=arrived.at[source, r],
            send_sem=tile_send.at[0, 0],
            recv_sem=tile_recv.at[source, r],
            device_id={"fx": source},
            device_id_type=pl.DeviceIdType.MESH,
        )

    tiles = vis_hbm.shape[0]
    row = lax.broadcasted_iota(jnp.int32, (8, 128), 0)
    lane = lax.broadcasted_iota(jnp.int32, (8, 128), 1)

    def slots_for(to):
        found = jnp.int32(0)
        picked = [(jnp.int32(0), jnp.int32(0), jnp.int32(0))] * 2
        for i in range(tiles):
            match = dest_ref[i] == to
            for r in range(2):
                here = match & (found == r)
                new = (jnp.int32(i), count_ref[i], chan_ref[i])
                picked[r] = tuple(jnp.where(here, a, b) for a, b in zip(new, picked[r]))
            found = found + jnp.where(match, 1, 0)
        return [(tile, count.astype(F32) * (1.0 / 64.0), chan) for tile, count, chan in picked]

    def share_rows(slots):
        total = jnp.zeros((8, 128), F32)
        for r, (_, weight, chan) in enumerate(slots):
            total = total + jnp.where((row == r) & (lane == chan), weight, 0.0)
        return total

    load_vis.wait()

    def planes(slots):
        for i, (t, _, _) in enumerate(slots):
            spectrum = jnp.concatenate([vis[t, 0], vis[t, 1]], axis=1)
            for part in range(2):
                half[i, part * SIDE : (part + 1) * SIDE] = dot(
                    spectrum, fourier[:, part * SIDE : (part + 1) * SIDE]
                ).astype(BF)
        return [(dot(back[...], half[i]) * slots[i][1]).astype(BF) for i in range(2)]

    def prepare(to, place):
        slots = slots_for(to)
        share_ref[to] = share_rows(slots)
        share_copy(to, fx).start()
        sending[place, 0], sending[place, 1] = planes(slots)

    def send_far(j, carry):
        prepare(at(*far(j)), j)
        far_copy(j, 0).start()
        far_copy(j, 1).start()
        return carry

    lax.fori_loop(0, len(FAR), send_far, 0)

    def send_near(j, carry):
        prepare(at(*near(j)), len(FAR) + j)
        near_copy(j).start()

        @pl.when(j >= 1)
        def _():
            for r in range(2):
                far_copy(j - 1, r).wait_recv()
                relay_copy(j - 1, r).start()

        return carry

    lax.fori_loop(0, len(NEAR), send_near, 0)
    own = slots_for(fx)
    shares[fx] = share_rows(own)
    arrived[fx, 0], arrived[fx, 1] = planes(own)

    load_sky.wait()

    def there_and_back(c, carry):
        pixels = sky[c].astype(BF)
        once = pixels.astype(F32) + dot(excess[...], pixels)
        model[c] = once + dot(once.astype(BF), excess[...])
        return carry

    lax.fori_loop(0, CH, there_and_back, 0)

    def wait_share(k, carry):
        share_copy(peer(k), peer(k)).wait_recv()
        return carry

    lax.fori_loop(1, n_fx, wait_share, 0)
    slots = n_fx * 2
    wide = slots * 16
    all_shares = shares[...].reshape(n_fx * 8, 128)
    members = jnp.where(all_shares > 0, 1.0, 0.0).astype(BF)
    spread = (
        lax.broadcasted_iota(jnp.int32, (CH * 16, 128), 0) // 16
        == lax.broadcasted_iota(jnp.int32, (CH * 16, 128), 1)
    )
    spread = jnp.where(spread, 1.0, 0.0).astype(BF)
    by_source = lax.dot_general(
        spread, members, (((1,), (1,)), ((), ())), preferred_element_type=F32
    ).astype(BF)
    weights = lax.dot_general(
        spread, all_shares.astype(BF), (((1,), (1,)), ((), ())), preferred_element_type=F32
    )
    totals = jnp.sum(weights, axis=1, keepdims=True)
    src_row = lax.broadcasted_iota(jnp.int32, (n_fx * 8, wide), 0)
    dst_col = lax.broadcasted_iota(jnp.int32, (n_fx * 8, wide), 1)
    widen = (src_row // 8 == dst_col // 32) & (src_row % 8 == dst_col // 16 % 2)
    widened = dot(by_source, jnp.where(widen, 1.0, 0.0).astype(BF))
    diagonal = (
        lax.broadcasted_iota(jnp.int32, (CH * 16, wide), 0) % 16
        == lax.broadcasted_iota(jnp.int32, (CH * 16, wide), 1) % 16
    )
    kron[...] = jnp.where(diagonal, widened, 0.0).astype(BF)
    scale = 1.0 / (1.0 + totals)

    def wait_near(j, carry):
        near_arrival(j).wait_recv()
        return carry

    def wait_far(j, carry):
        for r in range(2):
            far_arrival(j, r).wait_recv()
        return carry

    lax.fori_loop(0, len(NEAR), wait_near, 0)
    lax.fori_loop(0, len(FAR), wait_far, 0)

    def combine(g, carry):
        rows = pl.ds(pl.multiple_of(g * 16, 16), 16)
        gathered = dot(kron[...], arrived[:, :, rows, :].reshape(wide, SIDE))
        pixels = sky[:, rows, :].reshape(CH * 16, SIDE)
        there = model[:, rows, :].reshape(CH * 16, SIDE)
        new = pixels - (totals * there - gathered) * scale
        new = new.reshape(CH // 2, 2, 16, SIDE)
        stepped[:, rows, :] = new.reshape(CH, 16, SIDE).astype(BF)
        low = lax.broadcasted_iota(jnp.int32, (CH // 2, 16, 128), 2) < 64
        second = pltpu.roll(new[:, 1, :, :128].reshape(CH // 2 * 16, 128), 64, 1)
        pair = jnp.where(low, new[:, 0, :, :128], second.reshape(CH // 2, 16, 128))
        columns[:, rows, :] = pair.astype(BF)
        return carry

    lax.fori_loop(0, SIDE // 16, combine, 0)

    def finish_shares(k, carry):
        share_copy(peer(k), fx).wait_send()
        return carry

    def finish_near(j, carry):
        near_copy(j).wait_send()
        return carry

    def finish_far(j, carry):
        for r in range(2):
            far_copy(j, r).wait_send()
            relay_copy(j, r).wait_send()
        return carry

    lax.fori_loop(1, n_fx, finish_shares, 0)
    lax.fori_loop(0, len(NEAR), finish_near, 0)
    lax.fori_loop(0, len(FAR), finish_far, 0)


def wavelet_kernel(
    n_fy,
    n_fx,
    t_cols,
    inner_rows,
    outer_rows,
    analysis,
    select,
    synthesis,
    top,
    stepped,
    columns,
    thr_hbm,
    result,
    thr,
    below,
    beside,
    corner,
    side,
    row_sec,
    shrunk,
    edge,
    edge_left,
    col_sec,
    edge_top,
    load_sem,
    halo_send,
    halo_recv,
    edge_send,
    edge_recv,
    rows_send,
    rows_recv,
):
    fy = lax.axis_index("fy")
    fx = lax.axis_index("fx")
    up, down = (fy + n_fy - 1) % n_fy, (fy + 1) % n_fy
    prev, nxt = (fx + n_fx - 1) % n_fx, (fx + 1) % n_fx

    load_thr = pltpu.make_async_copy(thr_hbm, thr, load_sem.at[0])
    load_thr.start()
    barrier = pltpu.get_barrier_semaphore()
    for where in (
        {"fy": up},
        {"fy": down},
        {"fx": prev},
        {"fx": nxt},
        {"fy": up, "fx": prev},
        {"fy": down, "fx": nxt},
    ):
        pl.semaphore_signal(barrier, inc=1, device_id=where, device_id_type=pl.DeviceIdType.MESH)
    pl.semaphore_wait(barrier, 6)

    def halo_copy(i):
        source = (stepped.at[:, :HALO, :], columns, columns.at[:, :HALO, :])[i]
        target = (below, beside, corner)[i]
        where = ({"fy": up}, {"fx": prev}, {"fy": up, "fx": prev})[i]
        return pltpu.make_async_remote_copy(
            src_ref=source,
            dst_ref=target,
            send_sem=halo_send.at[i],
            recv_sem=halo_recv.at[i],
            device_id=where,
            device_id_type=pl.DeviceIdType.MESH,
        )

    for i in range(3):
        halo_copy(i).start()
    load_thr.wait()
    for i in range(3):
        halo_copy(i).wait_recv()

    def edge_copy(p):
        return pltpu.make_async_remote_copy(
            src_ref=edge.at[p],
            dst_ref=edge_left.at[p],
            send_sem=edge_send.at[p],
            recv_sem=edge_recv.at[p],
            device_id={"fx": nxt},
            device_id_type=pl.DeviceIdType.MESH,
        )

    def rows_copy(p, i):
        return pltpu.make_async_remote_copy(
            src_ref=col_sec.at[p, 1:, SEGMENTS[i][0] : SEGMENTS[i][1], :],
            dst_ref=edge_top.at[p, i],
            send_sem=rows_send.at[p, i],
            recv_sem=rows_recv.at[p, i],
            device_id={"fy": down},
            device_id_type=pl.DeviceIdType.MESH,
        )

    for p in range(CH // 2):
        whole = jnp.concatenate([beside[p], corner[p]], axis=0)
        turned = pltpu.roll(whole.astype(F32), 64, 1).astype(BF)
        side[p] = jnp.concatenate([whole, turned], axis=1)

    def analyse(p):
        first = 2 * p
        near = jnp.concatenate([stepped[first], stepped[first + 1], side[p, :SIDE]], axis=1)
        far = jnp.concatenate([below[first], below[first + 1], side[p, SIDE:]], axis=1)
        tall = jnp.concatenate([near, far], axis=0)

        def keep(b, begin, end, values):
            values = values.astype(BF)
            for h in range(2):
                row_sec[b, h, begin:end, :SIDE] = values[:, h * SIDE : (h + 1) * SIDE]
                row_sec[b, h, begin:end, SIDE:] = values[
                    :, 2 * SIDE + h * 128 : 2 * SIDE + (h + 1) * 128
                ]

        def rows_of(b, carry):
            r = dot(inner_rows[b], near)
            at = 0
            begin = 0
            for a, e in SEGMENTS:
                keep(b, begin, a, r[at : at + a - begin])
                at += a - begin
                begin = e
            r = dot(outer_rows[b], tall)
            for i, (a, e) in enumerate(SEGMENTS):
                keep(b, a, e, r[i * 16 : (i + 1) * 16])
            return carry

        lax.fori_loop(0, BASES, rows_of, 0)

        def columns_of(b, carry):
            lanes = pl.ds(pl.multiple_of(b * SIDE, SIDE), SIDE)
            coefficient = dot(row_sec[b].reshape(2 * SIDE, SIDE + 128), analysis[b])
            limit = thr[b, pl.ds(first, 2)].reshape(2 * SIDE, SIDE).astype(F32)
            kept = coefficient - jnp.clip(coefficient, -limit, limit)
            shrunk[:, lanes] = kept.astype(BF)
            return carry

        lax.fori_loop(0, BASES, columns_of, 0)
        edge[p] = dot(shrunk[...], select[...]).astype(BF)
        edge_copy(p).start()

    def synthesise_columns(p):
        edge_copy(p).wait_recv()
        edges = edge_left[p]

        def columns_of(b, carry):
            lanes = pl.ds(pl.multiple_of(b * SIDE, SIDE), SIDE)
            with_edge = jnp.concatenate([shrunk[:, lanes], edges], axis=1)
            r = dot(with_edge, synthesis[b]).astype(BF)
            col_sec[p, b, :, :SIDE] = r[:SIDE]
            col_sec[p, b, :, SIDE:] = r[SIDE:]
            return carry

        lax.fori_loop(0, BASES, columns_of, 0)
        for i in range(3):
            rows_copy(p, i).start()

    def synthesise_rows(p, carry):
        for i in range(3):
            rows_copy(p, i).wait_recv()
        r = dot(t_cols[...], col_sec[p].reshape(BASES * SIDE, 2 * SIDE))
        t = dot(top[...], edge_top[p].reshape(3 * (BASES - 1) * 16, 2 * SIDE))
        for h in range(2):
            lanes = slice(h * SIDE, (h + 1) * SIDE)
            result[2 * p + h, :HALO] = r[:HALO, lanes] + t[:, lanes]
            result[2 * p + h, HALO:] = r[HALO:, lanes]
        return carry

    def step(p, carry):
        @pl.when(p >= 1)
        def _():
            synthesise_columns(p - 1)

        @pl.when(p < CH // 2)
        def _():
            analyse(p)

        return carry

    lax.fori_loop(0, CH // 2 + 1, step, 0)
    lax.fori_loop(0, CH // 2, synthesise_rows, 0)

    for i in range(3):
        halo_copy(i).wait_send()

    def finish(p, carry):
        edge_copy(p).wait_send()
        for i in range(3):
            rows_copy(p, i).wait_send()
        return carry

    lax.fori_loop(0, CH // 2, finish, 0)


def per_device(n_fy, n_fx, sky_image, vis_tiles, tile_dest, tile_chan, tile_count, thresholds):
    made = {name: jnp.asarray(table) for name, table in tables().items()}
    smem = pl.BlockSpec(memory_space=pltpu.SMEM)
    vmem = pl.BlockSpec(memory_space=pltpu.VMEM)
    anywhere = pl.BlockSpec(memory_space=pl.ANY)
    dma = pltpu.SemaphoreType.DMA
    tiles = vis_tiles.shape[0]
    stepped, columns = pl.pallas_call(
        functools.partial(exchange_kernel, n_fx),
        out_shape=(
            jax.ShapeDtypeStruct((CH, SIDE, SIDE), BF),
            jax.ShapeDtypeStruct((CH // 2, SIDE, 128), BF),
        ),
        in_specs=[smem] * 3 + [vmem] * 3 + [anywhere] * 2,
        out_specs=[vmem] * 2,
        scratch_shapes=[
            pltpu.VMEM((tiles, 2, SIDE, SIDE), BF),
            pltpu.VMEM((CH, SIDE, SIDE), F32),
            pltpu.VMEM((CH, SIDE, SIDE), F32),
            pltpu.VMEM((n_fx, 2, SIDE, SIDE), BF),
            pltpu.VMEM((n_fx, 2, SIDE, SIDE), BF),
            pltpu.VMEM((len(FAR), 2, SIDE, SIDE), BF),
            pltpu.VMEM((2, 2 * SIDE, SIDE), BF),
            pltpu.VMEM((n_fx, 8, 128), F32),
            pltpu.VMEM((n_fx, 8, 128), F32),
            pltpu.VMEM((CH * 16, n_fx * 32), BF),
            dma((2,)),
            dma((n_fx, 2)),
            dma((n_fx, 2)),
            dma((len(FAR), 2)),
            dma((len(FAR), 2)),
            dma((n_fx,)),
            dma((n_fx,)),
        ],
        compiler_params=pltpu.CompilerParams(
            collective_id=0, has_side_effects=True, vmem_limit_bytes=58 * 1024 * 1024
        ),
    )(
        tile_dest.reshape(tiles),
        tile_chan,
        tile_count,
        made["fourier"],
        made["back"],
        made["excess"],
        sky_image,
        vis_tiles,
    )
    summed = pl.pallas_call(
        functools.partial(wavelet_kernel, n_fy, n_fx),
        out_shape=pltpu.VMEM((CH, SIDE, SIDE), F32),
        in_specs=[vmem] * (len(TABLES) + 2) + [anywhere],
        scratch_shapes=[
            pltpu.VMEM((BASES, CH, SIDE, SIDE), BF),
            pltpu.VMEM((CH, HALO, SIDE), BF),
            pltpu.VMEM((CH // 2, SIDE, 128), BF),
            pltpu.VMEM((CH // 2, HALO, 128), BF),
            pltpu.VMEM((CH // 2, SIDE + HALO, SIDE), BF),
            pltpu.VMEM((BASES, 2, SIDE, SIDE + 128), BF),
            pltpu.VMEM((2 * SIDE, BASES * SIDE), BF),
            pltpu.VMEM((CH // 2, 2 * SIDE, 128), BF),
            pltpu.VMEM((CH // 2, 2 * SIDE, 128), BF),
            pltpu.VMEM((CH // 2, BASES, SIDE, 2 * SIDE), BF),
            pltpu.VMEM((CH // 2, 3, BASES - 1, 16, 2 * SIDE), BF),
            dma((1,)),
            dma((3,)),
            dma((3,)),
            dma((CH // 2,)),
            dma((CH // 2,)),
            dma((CH // 2, 3)),
            dma((CH // 2, 3)),
        ],
        compiler_params=pltpu.CompilerParams(
            collective_id=1, has_side_effects=True, vmem_limit_bytes=58 * 1024 * 1024
        ),
    )(*[made[name] for name in TABLES], stepped, columns, thresholds)
    return jnp.maximum(summed * (1.0 / BASES), 0.0)


def solution(mesh):
    in_specs = (
        P(None, "fy", "fx"),
        P(("fy", "fx"), None, None, None),
        P(("fy", "fx"), None),
        P(("fy", "fx")),
        P(("fy", "fx")),
        P(None, None, "fy", "fx"),
    )
    out_specs = P(None, "fy", "fx")
    return jax.shard_map(
        functools.partial(per_device, mesh.shape["fy"], mesh.shape["fx"]),
        mesh=mesh,
        in_specs=in_specs,
        out_specs=out_specs,
        check_vma=False,
    )
```

```python
import functools
import math

import jax
import jax.numpy as jnp
import ml_dtypes
import numpy as np
from jax import lax
from jax.experimental import pallas as pl
from jax.experimental.pallas import tpu as pltpu
from jax.sharding import PartitionSpec as P

daubechies_taps = [
    [0.7071067811865476, 0.7071067811865476],
    [0.48296291314469025, 0.836516303737469, 0.22414386804185735, -0.12940952255092145],
    [
        0.3326705529509569,
        0.8068915093133388,
        0.4598775021193313,
        -0.13501102001039084,
        -0.08544127388224149,
        0.035226291882100656,
    ],
    [
        0.23037781330885523,
        0.7148465705525415,
        0.6308807679295904,
        -0.02798376941698385,
        -0.18703481171888114,
        0.030841381835986965,
        0.032883011666982945,
        -0.010597401784997278,
    ],
    [
        0.160102397974125,
        0.6038292697974729,
        0.7243085284385744,
        0.13842814590110342,
        -0.24229488706619015,
        -0.03224486958502952,
        0.07757149384006515,
        -0.006241490213011705,
        -0.012580751999015526,
        0.003335725285001549,
    ],
    [
        0.11154074335008017,
        0.4946238903983854,
        0.7511339080215775,
        0.3152503517092432,
        -0.22626469396516913,
        -0.12976686756709563,
        0.09750160558707936,
        0.02752286553001629,
        -0.031582039318031156,
        0.0005538422009938016,
        0.004777257511010651,
        -0.00107730108499558,
    ],
    [
        0.07785205408506236,
        0.39653931948230575,
        0.7291320908465551,
        0.4697822874053586,
        -0.14390600392910627,
        -0.22403618499416572,
        0.07130921926705004,
        0.0806126091510659,
        -0.03802993693503463,
        -0.01657454163101562,
        0.012550998556013784,
        0.00042957797300470274,
        -0.0018016407039998328,
        0.0003537138000010399,
    ],
    [
        0.05441584224308161,
        0.3128715909144659,
        0.6756307362980128,
        0.5853546836548691,
        -0.015829105256023893,
        -0.2840155429624281,
        0.00047248457399797254,
        0.128747426620186,
        -0.01736930100202211,
        -0.04408825393106472,
        0.013981027917015516,
        0.008746094047015655,
        -0.00487035299301066,
        -0.0003917403729959771,
        0.0006754494059985568,
        -0.00011747678400228192,
    ],
]


SIDE = 256
CH = 8
BASES = 8
HALO = 48
BF = jnp.bfloat16
F32 = jnp.float32
WIDE = SIDE + 128
TALL = SIDE + HALO


def rounded(table):
    return np.asarray(table, np.float32).astype(ml_dtypes.bfloat16)


def composite_tables():
    full = np.zeros((BASES, SIDE, SIDE + HALO))
    for degree in range(1, 9):
        taps = np.array(daubechies_taps[degree - 1])
        taps = taps * math.sqrt(2.0) / np.sum(taps)
        length = 2 * degree
        low = np.zeros(16)
        high = np.zeros(16)
        low[:length] = taps
        high[:length] = [(-1.0) ** j * taps[length - 1 - j] for j in range(length)]
        low = rounded(low).astype(np.float64)
        high = rounded(high).astype(np.float64)
        level_low = np.zeros((144, SIDE + HALO))
        level_high = np.zeros((128, SIDE + HALO))
        for k in range(144):
            level_low[k, 2 * k : 2 * k + 16] = low[: min(16, SIDE + HALO - 2 * k)]
        for k in range(128):
            level_high[k, 2 * k : 2 * k + 16] = high
        second = np.zeros((128, 144))
        for m in range(64):
            second[m, 2 * m : 2 * m + 16] = low
            second[64 + m, 2 * m : 2 * m + 16] = high
        full[degree - 1, :128] = second @ level_low
        full[degree - 1, 128:] = level_high
    return rounded(full).astype(np.float32)


@functools.lru_cache(maxsize=1)
def tables():
    full = composite_tables()
    wide = np.concatenate([full, np.zeros((BASES, SIDE, 128 - HALO), np.float32)], axis=2)
    out = {"rows": full, "columns": wide}
    grid = np.arange(SIDE)[:, None] * np.arange(SIDE)[None, :] % SIDE
    angle = grid * (2.0 * math.pi / SIDE)
    cosine = rounded(np.cos(angle) / math.sqrt(SIDE)).astype(np.float64)
    sine = rounded(np.sin(angle) / math.sqrt(SIDE)).astype(np.float64)
    out["fourier"] = np.block([[cosine, sine], [-sine, cosine]])
    out["back"] = np.concatenate([cosine, -sine], axis=1)
    out["excess"] = cosine @ cosine + sine @ sine - np.eye(SIDE)
    return {name: rounded(table) for name, table in out.items()}


NEAR = ((1, 0), (3, 0), (0, 1), (0, 3), (1, 1), (1, 3), (3, 1), (3, 3))
FAR = ((2, 0), (0, 2), (2, 1), (2, 3), (1, 2), (3, 2), (2, 2))
THROUGH = (
    ((1, 0), (3, 0)),
    ((0, 1), (0, 3)),
    ((1, 1), (3, 1)),
    ((1, 3), (3, 3)),
    ((1, 1), (1, 3)),
    ((3, 1), (3, 3)),
    ((1, 1), (3, 3)),
)


def choose(j, values):
    out = jnp.int32(values[0])
    for i, value in enumerate(values):
        out = jnp.where(j == i, jnp.int32(value), out)
    return out


def dot(a, b):
    return jnp.dot(a, b, preferred_element_type=F32)


def exchange_kernel(
    n_fy,
    n_fx,
    dest_ref,
    chan_ref,
    count_ref,
    fourier,
    back,
    excess,
    sky_hbm,
    vis_hbm,
    extended,
    vis,
    sky,
    model,
    sending,
    arrived,
    relay,
    half,
    share_ref,
    shares,
    kron,
    columns,
    beside,
    corner,
    load_sem,
    tile_send,
    tile_recv,
    relay_send,
    relay_recv,
    share_send,
    share_recv,
    halo_send,
    halo_recv,
):
    fy = lax.axis_index("fy")
    fx = lax.axis_index("fx")
    n_z = 4
    n_x = n_fx // n_z
    my_x, my_z = fx // n_z, fx % n_z

    def at(dx, dz):
        return (my_x + dx) % n_x * n_z + (my_z + dz) % n_z

    def peer(k):
        return at(k // n_z, k % n_z)

    load_vis = pltpu.make_async_copy(vis_hbm, vis, load_sem.at[0])
    load_sky = pltpu.make_async_copy(sky_hbm, sky, load_sem.at[1])
    load_vis.start()
    load_sky.start()

    barrier = pltpu.get_barrier_semaphore()

    def greet(k, carry):
        pl.semaphore_signal(
            barrier, inc=1, device_id={"fx": peer(k)}, device_id_type=pl.DeviceIdType.MESH
        )
        return carry

    lax.fori_loop(1, n_fx, greet, 0)
    up, down = (fy + n_fy - 1) % n_fy, (fy + 1) % n_fy
    prev, nxt = (fx + n_fx - 1) % n_fx, (fx + 1) % n_fx
    for where in ({"fy": up}, {"fy": down}, {"fy": up, "fx": prev}, {"fy": down, "fx": nxt}):
        pl.semaphore_signal(barrier, inc=1, device_id=where, device_id_type=pl.DeviceIdType.MESH)
    pl.semaphore_wait(barrier, n_fx - 1 + 4)

    def share_copy(to, source):
        return pltpu.make_async_remote_copy(
            src_ref=share_ref.at[to],
            dst_ref=shares.at[source],
            send_sem=share_send.at[to],
            recv_sem=share_recv.at[source],
            device_id={"fx": to},
            device_id_type=pl.DeviceIdType.MESH,
        )

    def near(j):
        return choose(j, [o[0] for o in NEAR]), choose(j, [o[1] for o in NEAR])

    def far(j):
        return choose(j, [o[0] for o in FAR]), choose(j, [o[1] for o in FAR])

    def through(j, r):
        return (
            choose(j, [o[r][0] for o in THROUGH]),
            choose(j, [o[r][1] for o in THROUGH]),
        )

    def near_copy(j):
        return pltpu.make_async_remote_copy(
            src_ref=sending.at[len(FAR) + j],
            dst_ref=arrived.at[fx],
            send_sem=tile_send.at[len(FAR) + j, 0],
            recv_sem=tile_recv.at[fx, 0],
            device_id={"fx": at(*near(j))},
            device_id_type=pl.DeviceIdType.MESH,
        )

    def far_copy(j, r):
        return pltpu.make_async_remote_copy(
            src_ref=sending.at[j, r],
            dst_ref=relay.at[j, r],
            send_sem=tile_send.at[j, r],
            recv_sem=relay_recv.at[j, r],
            device_id={"fx": at(*through(j, r))},
            device_id_type=pl.DeviceIdType.MESH,
        )

    def relay_copy(j, r):
        end, mid = far(j), through(j, r)
        source = at(4 - mid[0], 4 - mid[1])
        return pltpu.make_async_remote_copy(
            src_ref=relay.at[j, r],
            dst_ref=arrived.at[source, r],
            send_sem=relay_send.at[j, r],
            recv_sem=tile_recv.at[source, r],
            device_id={"fx": at(end[0] + 4 - mid[0], end[1] + 4 - mid[1])},
            device_id_type=pl.DeviceIdType.MESH,
        )

    def near_arrival(j):
        dx, dz = near(j)
        source = at(4 - dx, 4 - dz)
        return pltpu.make_async_remote_copy(
            src_ref=arrived.at[source],
            dst_ref=arrived.at[source],
            send_sem=tile_send.at[0, 0],
            recv_sem=tile_recv.at[source, 0],
            device_id={"fx": source},
            device_id_type=pl.DeviceIdType.MESH,
        )

    def far_arrival(j, r):
        dx, dz = far(j)
        source = at(4 - dx, 4 - dz)
        return pltpu.make_async_remote_copy(
            src_ref=arrived.at[source, r],
            dst_ref=arrived.at[source, r],
            send_sem=tile_send.at[0, 0],
            recv_sem=tile_recv.at[source, r],
            device_id={"fx": source},
            device_id_type=pl.DeviceIdType.MESH,
        )

    tiles = vis_hbm.shape[0]
    row = lax.broadcasted_iota(jnp.int32, (8, 128), 0)
    lane = lax.broadcasted_iota(jnp.int32, (8, 128), 1)

    def slots_for(to):
        found = jnp.int32(0)
        picked = [(jnp.int32(0), jnp.int32(0), jnp.int32(0))] * 2
        for i in range(tiles):
            match = dest_ref[i] == to
            for r in range(2):
                here = match & (found == r)
                new = (jnp.int32(i), count_ref[i], chan_ref[i])
                picked[r] = tuple(jnp.where(here, a, b) for a, b in zip(new, picked[r]))
            found = found + jnp.where(match, 1, 0)
        return [(tile, count.astype(F32) * (1.0 / 64.0), chan) for tile, count, chan in picked]

    def share_rows(slots):
        total = jnp.zeros((8, 128), F32)
        for r, (_, weight, chan) in enumerate(slots):
            total = total + jnp.where((row == r) & (lane == chan), weight, 0.0)
        return total

    load_vis.wait()

    def planes(slots):
        for i, (t, _, _) in enumerate(slots):
            spectrum = jnp.concatenate([vis[t, 0], vis[t, 1]], axis=1)
            for part in range(2):
                half[i, part * SIDE : (part + 1) * SIDE] = dot(
                    spectrum, fourier[:, part * SIDE : (part + 1) * SIDE]
                ).astype(BF)
        return [(dot(back[...], half[i]) * slots[i][1]).astype(BF) for i in range(2)]

    def prepare(to, place):
        slots = slots_for(to)
        share_ref[to] = share_rows(slots)
        share_copy(to, fx).start()
        sending[place, 0], sending[place, 1] = planes(slots)

    def send_far(j, carry):
        prepare(at(*far(j)), j)
        far_copy(j, 0).start()
        far_copy(j, 1).start()
        return carry

    lax.fori_loop(0, len(FAR), send_far, 0)

    def send_near(j, carry):
        prepare(at(*near(j)), len(FAR) + j)
        near_copy(j).start()

        @pl.when(j >= 1)
        def _():
            for r in range(2):
                far_copy(j - 1, r).wait_recv()
                relay_copy(j - 1, r).start()

        return carry

    lax.fori_loop(0, len(NEAR), send_near, 0)
    own = slots_for(fx)
    shares[fx] = share_rows(own)
    arrived[fx, 0], arrived[fx, 1] = planes(own)

    load_sky.wait()

    def there_and_back(c, carry):
        pixels = sky[c].astype(BF)
        once = pixels.astype(F32) + dot(excess[...], pixels)
        model[c] = once + dot(once.astype(BF), excess[...])
        return carry

    lax.fori_loop(0, CH, there_and_back, 0)

    def wait_share(k, carry):
        share_copy(peer(k), peer(k)).wait_recv()
        return carry

    lax.fori_loop(1, n_fx, wait_share, 0)
    slots = n_fx * 2
    wide = slots * 16
    all_shares = shares[...].reshape(n_fx * 8, 128)
    members = jnp.where(all_shares > 0, 1.0, 0.0).astype(BF)
    spread = (
        lax.broadcasted_iota(jnp.int32, (CH * 16, 128), 0) // 16
        == lax.broadcasted_iota(jnp.int32, (CH * 16, 128), 1)
    )
    spread = jnp.where(spread, 1.0, 0.0).astype(BF)
    by_source = lax.dot_general(
        spread, members, (((1,), (1,)), ((), ())), preferred_element_type=F32
    ).astype(BF)
    weights = lax.dot_general(
        spread, all_shares.astype(BF), (((1,), (1,)), ((), ())), preferred_element_type=F32
    )
    totals = jnp.sum(weights, axis=1, keepdims=True)
    src_row = lax.broadcasted_iota(jnp.int32, (n_fx * 8, wide), 0)
    dst_col = lax.broadcasted_iota(jnp.int32, (n_fx * 8, wide), 1)
    widen = (src_row // 8 == dst_col // 32) & (src_row % 8 == dst_col // 16 % 2)
    widened = dot(by_source, jnp.where(widen, 1.0, 0.0).astype(BF))
    diagonal = (
        lax.broadcasted_iota(jnp.int32, (CH * 16, wide), 0) % 16
        == lax.broadcasted_iota(jnp.int32, (CH * 16, wide), 1) % 16
    )
    kron[...] = jnp.where(diagonal, widened, 0.0).astype(BF)
    scale = 1.0 / (1.0 + totals)

    def wait_near(j, carry):
        near_arrival(j).wait_recv()
        return carry

    def wait_far(j, carry):
        for r in range(2):
            far_arrival(j, r).wait_recv()
        return carry

    lax.fori_loop(0, len(NEAR), wait_near, 0)
    lax.fori_loop(0, len(FAR), wait_far, 0)

    def combine(g, carry):
        rows = pl.ds(pl.multiple_of(g * 16, 16), 16)
        gathered = dot(kron[...], arrived[:, :, rows, :].reshape(wide, SIDE))
        pixels = sky[:, rows, :].reshape(CH * 16, SIDE)
        there = model[:, rows, :].reshape(CH * 16, SIDE)
        new = pixels - (totals * there - gathered) * scale
        new = new.reshape(CH // 2, 2, 16, SIDE)
        extended[:, rows, :SIDE] = new.reshape(CH, 16, SIDE).astype(BF)
        low = lax.broadcasted_iota(jnp.int32, (CH // 2, 16, 128), 2) < 64
        second = pltpu.roll(new[:, 1, :, :128].reshape(CH // 2 * 16, 128), 64, 1)
        pair = jnp.where(low, new[:, 0, :, :128], second.reshape(CH // 2, 16, 128))
        columns[:, rows, :] = pair.astype(BF)
        return carry

    lax.fori_loop(0, SIDE // 16, combine, 0)

    def halo_copy(i):
        source = (extended.at[:, :HALO, :SIDE], columns, columns.at[:, :HALO, :])[i]
        target = (extended.at[:, SIDE:, :SIDE], beside, corner)[i]
        where = ({"fy": up}, {"fx": prev}, {"fy": up, "fx": prev})[i]
        return pltpu.make_async_remote_copy(
            src_ref=source,
            dst_ref=target,
            send_sem=halo_send.at[i],
            recv_sem=halo_recv.at[i],
            device_id=where,
            device_id_type=pl.DeviceIdType.MESH,
        )

    for i in range(3):
        halo_copy(i).start()
    for i in range(1, 3):
        halo_copy(i).wait_recv()

    def place(p, carry):
        for source, begin, end in ((beside, 0, SIDE), (corner, SIDE, TALL)):
            first = source[p]
            extended[2 * p, begin:end, SIDE:] = first
            extended[2 * p + 1, begin:end, SIDE:] = pltpu.roll(first.astype(F32), 64, 1).astype(BF)
        return carry

    lax.fori_loop(0, CH // 2, place, 0)
    halo_copy(0).wait_recv()

    def finish_shares(k, carry):
        share_copy(peer(k), fx).wait_send()
        return carry

    def finish_near(j, carry):
        near_copy(j).wait_send()
        return carry

    def finish_far(j, carry):
        for r in range(2):
            far_copy(j, r).wait_send()
            relay_copy(j, r).wait_send()
        return carry

    lax.fori_loop(1, n_fx, finish_shares, 0)
    lax.fori_loop(0, len(NEAR), finish_near, 0)
    lax.fori_loop(0, len(FAR), finish_far, 0)
    for i in range(3):
        halo_copy(i).wait_send()


def passed(value, axes, to):
    sizes = [lax.axis_size(a) for a in axes]
    pairs = []
    for i in np.ndindex(*sizes):
        j = [(a + b) % n for a, b, n in zip(i, to, sizes)]
        pairs.append((int(np.ravel_multi_index(i, sizes)), int(np.ravel_multi_index(j, sizes))))
    return lax.ppermute(value, axes if len(axes) > 1 else axes[0], pairs)


def per_device(n_fy, n_fx, sky_image, vis_tiles, tile_dest, tile_chan, tile_count, thresholds):
    made = {name: jnp.asarray(table) for name, table in tables().items()}
    smem = pl.BlockSpec(memory_space=pltpu.SMEM)
    vmem = pl.BlockSpec(memory_space=pltpu.VMEM)
    anywhere = pl.BlockSpec(memory_space=pl.ANY)
    dma = pltpu.SemaphoreType.DMA
    tiles = vis_tiles.shape[0]
    extended = pl.pallas_call(
        functools.partial(exchange_kernel, n_fy, n_fx),
        out_shape=jax.ShapeDtypeStruct((CH, TALL, WIDE), BF),
        in_specs=[smem] * 3 + [vmem] * 3 + [anywhere] * 2,
        out_specs=vmem,
        scratch_shapes=[
            pltpu.VMEM((tiles, 2, SIDE, SIDE), BF),
            pltpu.VMEM((CH, SIDE, SIDE), F32),
            pltpu.VMEM((CH, SIDE, SIDE), F32),
            pltpu.VMEM((n_fx, 2, SIDE, SIDE), BF),
            pltpu.VMEM((n_fx, 2, SIDE, SIDE), BF),
            pltpu.VMEM((len(FAR), 2, SIDE, SIDE), BF),
            pltpu.VMEM((2, 2 * SIDE, SIDE), BF),
            pltpu.VMEM((n_fx, 8, 128), F32),
            pltpu.VMEM((n_fx, 8, 128), F32),
            pltpu.VMEM((CH * 16, n_fx * 32), BF),
            pltpu.VMEM((CH // 2, SIDE, 128), BF),
            pltpu.VMEM((CH // 2, SIDE, 128), BF),
            pltpu.VMEM((CH // 2, HALO, 128), BF),
            dma((2,)),
            dma((n_fx, 2)),
            dma((n_fx, 2)),
            dma((len(FAR), 2)),
            dma((len(FAR), 2)),
            dma((n_fx,)),
            dma((n_fx,)),
            dma((3,)),
            dma((3,)),
        ],
        compiler_params=pltpu.CompilerParams(
            collective_id=0, has_side_effects=True, vmem_limit_bytes=58 * 1024 * 1024
        ),
    )(
        tile_dest.reshape(tiles),
        tile_chan,
        tile_count,
        made["fourier"],
        made["back"],
        made["excess"],
        sky_image,
        vis_tiles,
    )
    rows, columns = made["rows"], made["columns"]
    row_sec = jnp.einsum("bkn,cnx->bckx", rows, extended, preferred_element_type=F32).astype(BF)
    coefficient = jnp.einsum("bcyx,bkx->bcyk", row_sec, columns, preferred_element_type=F32)
    limits = thresholds.astype(F32)
    shrunk = (coefficient - jnp.clip(coefficient, -limits, limits)).astype(BF)
    col_sec = jnp.einsum("bcyk,bkx->bcyx", shrunk, columns, preferred_element_type=F32).astype(BF)
    cells = jnp.einsum("bkn,bckx->cnx", rows, col_sec, preferred_element_type=F32)
    spill = cells.astype(BF)
    from_left = passed(spill[:, :SIDE, SIDE:TALL], ("fx",), (1,)).astype(F32)
    from_above = passed(spill[:, SIDE:, :SIDE], ("fy",), (1,)).astype(F32)
    from_corner = passed(spill[:, SIDE:, SIDE:TALL], ("fy", "fx"), (1, 1)).astype(F32)
    left = jnp.pad(from_left, ((0, 0), (0, 0), (0, SIDE - HALO)))
    above = jnp.pad(from_above, ((0, 0), (0, SIDE - HALO), (0, 0)))
    corner = jnp.pad(from_corner, ((0, 0), (0, SIDE - HALO), (0, SIDE - HALO)))
    summed = cells[:, :SIDE, :SIDE] + left + above + corner
    return jnp.maximum(summed * (1.0 / BASES), 0.0)


def solution(mesh):
    in_specs = (
        P(None, "fy", "fx"),
        P(("fy", "fx"), None, None, None),
        P(("fy", "fx"), None),
        P(("fy", "fx")),
        P(("fy", "fx")),
        P(None, None, "fy", "fx"),
    )
    out_specs = P(None, "fy", "fx")
    return jax.shard_map(
        functools.partial(per_device, mesh.shape["fy"], mesh.shape["fx"]),
        mesh=mesh,
        in_specs=in_specs,
        out_specs=out_specs,
        check_vma=False,
    )
```

```python
import functools
import math

import jax
import jax.numpy as jnp
import ml_dtypes
import numpy as np
from jax import lax
from jax.experimental import pallas as pl
from jax.experimental.pallas import tpu as pltpu
from jax.sharding import PartitionSpec as P

daubechies_taps = [
    [0.7071067811865476, 0.7071067811865476],
    [0.48296291314469025, 0.836516303737469, 0.22414386804185735, -0.12940952255092145],
    [
        0.3326705529509569,
        0.8068915093133388,
        0.4598775021193313,
        -0.13501102001039084,
        -0.08544127388224149,
        0.035226291882100656,
    ],
    [
        0.23037781330885523,
        0.7148465705525415,
        0.6308807679295904,
        -0.02798376941698385,
        -0.18703481171888114,
        0.030841381835986965,
        0.032883011666982945,
        -0.010597401784997278,
    ],
    [
        0.160102397974125,
        0.6038292697974729,
        0.7243085284385744,
        0.13842814590110342,
        -0.24229488706619015,
        -0.03224486958502952,
        0.07757149384006515,
        -0.006241490213011705,
        -0.012580751999015526,
        0.003335725285001549,
    ],
    [
        0.11154074335008017,
        0.4946238903983854,
        0.7511339080215775,
        0.3152503517092432,
        -0.22626469396516913,
        -0.12976686756709563,
        0.09750160558707936,
        0.02752286553001629,
        -0.031582039318031156,
        0.0005538422009938016,
        0.004777257511010651,
        -0.00107730108499558,
    ],
    [
        0.07785205408506236,
        0.39653931948230575,
        0.7291320908465551,
        0.4697822874053586,
        -0.14390600392910627,
        -0.22403618499416572,
        0.07130921926705004,
        0.0806126091510659,
        -0.03802993693503463,
        -0.01657454163101562,
        0.012550998556013784,
        0.00042957797300470274,
        -0.0018016407039998328,
        0.0003537138000010399,
    ],
    [
        0.05441584224308161,
        0.3128715909144659,
        0.6756307362980128,
        0.5853546836548691,
        -0.015829105256023893,
        -0.2840155429624281,
        0.00047248457399797254,
        0.128747426620186,
        -0.01736930100202211,
        -0.04408825393106472,
        0.013981027917015516,
        0.008746094047015655,
        -0.00487035299301066,
        -0.0003917403729959771,
        0.0006754494059985568,
        -0.00011747678400228192,
    ],
]


SIDE = 256
CH = 8
BASES = 8
HALO = 48
BF = jnp.bfloat16
F32 = jnp.float32
WIDE = SIDE + 128
TALL = SIDE + HALO


def rounded(table):
    return np.asarray(table, np.float32).astype(ml_dtypes.bfloat16)


def composite_tables():
    full = np.zeros((BASES, SIDE, SIDE + HALO))
    for degree in range(1, 9):
        taps = np.array(daubechies_taps[degree - 1])
        taps = taps * math.sqrt(2.0) / np.sum(taps)
        length = 2 * degree
        low = np.zeros(16)
        high = np.zeros(16)
        low[:length] = taps
        high[:length] = [(-1.0) ** j * taps[length - 1 - j] for j in range(length)]
        low = rounded(low).astype(np.float64)
        high = rounded(high).astype(np.float64)
        level_low = np.zeros((144, SIDE + HALO))
        level_high = np.zeros((128, SIDE + HALO))
        for k in range(144):
            level_low[k, 2 * k : 2 * k + 16] = low[: min(16, SIDE + HALO - 2 * k)]
        for k in range(128):
            level_high[k, 2 * k : 2 * k + 16] = high
        second = np.zeros((128, 144))
        for m in range(64):
            second[m, 2 * m : 2 * m + 16] = low
            second[64 + m, 2 * m : 2 * m + 16] = high
        full[degree - 1, :128] = second @ level_low
        full[degree - 1, 128:] = level_high
    return rounded(full).astype(np.float32)


@functools.lru_cache(maxsize=1)
def tables():
    full = composite_tables()
    wide = np.concatenate([full, np.zeros((BASES, SIDE, 128 - HALO), np.float32)], axis=2)
    out = {"rows": full, "columns": wide}
    grid = np.arange(SIDE)[:, None] * np.arange(SIDE)[None, :] % SIDE
    angle = grid * (2.0 * math.pi / SIDE)
    cosine = rounded(np.cos(angle) / math.sqrt(SIDE)).astype(np.float64)
    sine = rounded(np.sin(angle) / math.sqrt(SIDE)).astype(np.float64)
    out["fourier"] = np.stack(
        [np.stack([cosine, sine], axis=1), np.stack([-sine, cosine], axis=1)]
    )
    out["back"] = np.stack([cosine, -sine], axis=1)
    out["excess"] = cosine @ cosine + sine @ sine - np.eye(SIDE)
    return {name: rounded(table) for name, table in out.items()}


NEAR = ((1, 0), (3, 0), (0, 1), (0, 3), (1, 1), (1, 3), (3, 1), (3, 3))
FAR = ((2, 0), (0, 2), (2, 1), (2, 3), (1, 2), (3, 2), (2, 2))
THROUGH = (
    ((1, 0), (3, 0)),
    ((0, 1), (0, 3)),
    ((1, 1), (3, 1)),
    ((1, 3), (3, 3)),
    ((1, 1), (1, 3)),
    ((3, 1), (3, 3)),
    ((1, 1), (3, 3)),
)


def choose(j, values):
    out = jnp.int32(values[0])
    for i, value in enumerate(values):
        out = jnp.where(j == i, jnp.int32(value), out)
    return out


def dot(a, b):
    return jnp.dot(a, b, preferred_element_type=F32)


def exchange_kernel(
    n_fy,
    n_fx,
    dest_ref,
    chan_ref,
    count_ref,
    excess,
    planes,
    sky_hbm,
    extended,
    sky,
    model,
    sending,
    arrived,
    relay,
    share_ref,
    shares,
    kron,
    columns,
    beside,
    corner,
    load_sem,
    tile_send,
    tile_recv,
    relay_send,
    relay_recv,
    share_send,
    share_recv,
    halo_send,
    halo_recv,
    columns_send,
    columns_recv,
):
    fy = lax.axis_index("fy")
    fx = lax.axis_index("fx")
    n_z = 4
    n_x = n_fx // n_z
    my_x, my_z = fx // n_z, fx % n_z

    def at(dx, dz):
        return (my_x + dx) % n_x * n_z + (my_z + dz) % n_z

    def peer(k):
        return at(k // n_z, k % n_z)

    load_sky = pltpu.make_async_copy(sky_hbm, sky, load_sem.at[0])
    load_sky.start()

    barrier = pltpu.get_barrier_semaphore()

    def greet(k, carry):
        pl.semaphore_signal(
            barrier, inc=1, device_id={"fx": peer(k)}, device_id_type=pl.DeviceIdType.MESH
        )
        return carry

    lax.fori_loop(1, n_fx, greet, 0)
    up, down = (fy + n_fy - 1) % n_fy, (fy + 1) % n_fy
    prev, nxt = (fx + n_fx - 1) % n_fx, (fx + 1) % n_fx
    for where in ({"fy": up}, {"fy": down}, {"fy": up, "fx": prev}, {"fy": down, "fx": nxt}):
        pl.semaphore_signal(barrier, inc=1, device_id=where, device_id_type=pl.DeviceIdType.MESH)
    pl.semaphore_wait(barrier, n_fx - 1 + 4)

    def share_copy(to, source):
        return pltpu.make_async_remote_copy(
            src_ref=share_ref.at[to],
            dst_ref=shares.at[source],
            send_sem=share_send.at[to],
            recv_sem=share_recv.at[source],
            device_id={"fx": to},
            device_id_type=pl.DeviceIdType.MESH,
        )

    def near(j):
        return choose(j, [o[0] for o in NEAR]), choose(j, [o[1] for o in NEAR])

    def far(j):
        return choose(j, [o[0] for o in FAR]), choose(j, [o[1] for o in FAR])

    def through(j, r):
        return (
            choose(j, [o[r][0] for o in THROUGH]),
            choose(j, [o[r][1] for o in THROUGH]),
        )

    def near_copy(j):
        return pltpu.make_async_remote_copy(
            src_ref=sending.at[len(FAR) + j],
            dst_ref=arrived.at[fx],
            send_sem=tile_send.at[len(FAR) + j, 0],
            recv_sem=tile_recv.at[fx, 0],
            device_id={"fx": at(*near(j))},
            device_id_type=pl.DeviceIdType.MESH,
        )

    def far_copy(j, r):
        return pltpu.make_async_remote_copy(
            src_ref=sending.at[j, r],
            dst_ref=relay.at[j, r],
            send_sem=tile_send.at[j, r],
            recv_sem=relay_recv.at[j, r],
            device_id={"fx": at(*through(j, r))},
            device_id_type=pl.DeviceIdType.MESH,
        )

    def relay_copy(j, r):
        end, mid = far(j), through(j, r)
        source = at(4 - mid[0], 4 - mid[1])
        return pltpu.make_async_remote_copy(
            src_ref=relay.at[j, r],
            dst_ref=arrived.at[source, r],
            send_sem=relay_send.at[j, r],
            recv_sem=tile_recv.at[source, r],
            device_id={"fx": at(end[0] + 4 - mid[0], end[1] + 4 - mid[1])},
            device_id_type=pl.DeviceIdType.MESH,
        )

    def near_arrival(j):
        dx, dz = near(j)
        source = at(4 - dx, 4 - dz)
        return pltpu.make_async_remote_copy(
            src_ref=arrived.at[source],
            dst_ref=arrived.at[source],
            send_sem=tile_send.at[0, 0],
            recv_sem=tile_recv.at[source, 0],
            device_id={"fx": source},
            device_id_type=pl.DeviceIdType.MESH,
        )

    def far_arrival(j, r):
        dx, dz = far(j)
        source = at(4 - dx, 4 - dz)
        return pltpu.make_async_remote_copy(
            src_ref=arrived.at[source, r],
            dst_ref=arrived.at[source, r],
            send_sem=tile_send.at[0, 0],
            recv_sem=tile_recv.at[source, r],
            device_id={"fx": source},
            device_id_type=pl.DeviceIdType.MESH,
        )

    tiles = planes.shape[0]
    row = lax.broadcasted_iota(jnp.int32, (8, 128), 0)
    lane = lax.broadcasted_iota(jnp.int32, (8, 128), 1)

    def slots_for(to):
        found = jnp.int32(0)
        picked = [(jnp.int32(0), jnp.int32(0), jnp.int32(0))] * 2
        for i in range(tiles):
            match = dest_ref[i] == to
            for r in range(2):
                here = match & (found == r)
                new = (jnp.int32(i), count_ref[i], chan_ref[i])
                picked[r] = tuple(jnp.where(here, a, b) for a, b in zip(new, picked[r]))
            found = found + jnp.where(match, 1, 0)
        return [(tile, count.astype(F32) * (1.0 / 64.0), chan) for tile, count, chan in picked]

    def share_rows(slots):
        total = jnp.zeros((8, 128), F32)
        for r, (_, weight, chan) in enumerate(slots):
            total = total + jnp.where((row == r) & (lane == chan), weight, 0.0)
        return total

    def prepare(to, place):
        slots = slots_for(to)
        share_ref[to] = share_rows(slots)
        share_copy(to, fx).start()
        for r in range(2):
            sending[place, r] = planes[slots[r][0]]

    def send_far(j, carry):
        prepare(at(*far(j)), j)
        far_copy(j, 0).start()
        far_copy(j, 1).start()
        return carry

    lax.fori_loop(0, len(FAR), send_far, 0)

    def send_near(j, carry):
        prepare(at(*near(j)), len(FAR) + j)
        near_copy(j).start()
        return carry

    lax.fori_loop(0, len(NEAR), send_near, 0)
    own = slots_for(fx)
    shares[fx] = share_rows(own)
    for r in range(2):
        arrived[fx, r] = planes[own[r][0]]

    load_sky.wait()

    def there_and_back(c, carry):
        pixels = sky[c].astype(BF)
        once = pixels.astype(F32) + dot(excess[...], pixels)
        model[c] = once + dot(once.astype(BF), excess[...])
        return carry

    lax.fori_loop(0, CH, there_and_back, 0)

    def pass_on(j, carry):
        for r in range(2):
            far_copy(j, r).wait_recv()
            relay_copy(j, r).start()
        return carry

    lax.fori_loop(0, len(FAR), pass_on, 0)

    def wait_share(k, carry):
        share_copy(peer(k), peer(k)).wait_recv()
        return carry

    lax.fori_loop(1, n_fx, wait_share, 0)
    slots = n_fx * 2
    wide = slots * 16
    all_shares = shares[...].reshape(n_fx * 8, 128)
    members = jnp.where(all_shares > 0, 1.0, 0.0).astype(BF)
    spread = (
        lax.broadcasted_iota(jnp.int32, (CH * 16, 128), 0) // 16
        == lax.broadcasted_iota(jnp.int32, (CH * 16, 128), 1)
    )
    spread = jnp.where(spread, 1.0, 0.0).astype(BF)
    by_source = lax.dot_general(
        spread, members, (((1,), (1,)), ((), ())), preferred_element_type=F32
    ).astype(BF)
    weights = lax.dot_general(
        spread, all_shares.astype(BF), (((1,), (1,)), ((), ())), preferred_element_type=F32
    )
    totals = jnp.sum(weights, axis=1, keepdims=True)
    src_row = lax.broadcasted_iota(jnp.int32, (n_fx * 8, wide), 0)
    dst_col = lax.broadcasted_iota(jnp.int32, (n_fx * 8, wide), 1)
    widen = (src_row // 8 == dst_col // 32) & (src_row % 8 == dst_col // 16 % 2)
    widened = dot(by_source, jnp.where(widen, 1.0, 0.0).astype(BF))
    diagonal = (
        lax.broadcasted_iota(jnp.int32, (CH * 16, wide), 0) % 16
        == lax.broadcasted_iota(jnp.int32, (CH * 16, wide), 1) % 16
    )
    kron[...] = jnp.where(diagonal, widened, 0.0).astype(BF)
    scale = 1.0 / (1.0 + totals)

    def wait_near(j, carry):
        near_arrival(j).wait_recv()
        return carry

    def wait_far(j, carry):
        for r in range(2):
            far_arrival(j, r).wait_recv()
        return carry

    lax.fori_loop(0, len(NEAR), wait_near, 0)
    lax.fori_loop(0, len(FAR), wait_far, 0)

    def combine(g):
        rows = pl.ds(pl.multiple_of(g * 16, 16), 16)
        gathered = dot(kron[...], arrived[:, :, rows, :].reshape(wide, SIDE))
        pixels = sky[:, rows, :].reshape(CH * 16, SIDE)
        there = model[:, rows, :].reshape(CH * 16, SIDE)
        new = pixels - (totals * there - gathered) * scale
        new = new.reshape(CH // 2, 2, 16, SIDE)
        extended[:, rows, :SIDE] = new.reshape(CH, 16, SIDE).astype(BF)
        low = lax.broadcasted_iota(jnp.int32, (CH // 2, 16, 128), 2) < 64
        second = pltpu.roll(new[:, 1, :, :128].reshape(CH // 2 * 16, 128), 64, 1)
        pair = jnp.where(low, new[:, 0, :, :128], second.reshape(CH // 2, 16, 128))
        columns[:, rows, :] = pair.astype(BF)

    chunks = 4
    deep = SIDE // chunks

    def columns_copy(q):
        rows = pl.ds(pl.multiple_of(q * deep, deep), deep)
        return pltpu.make_async_remote_copy(
            src_ref=columns.at[:, rows, :],
            dst_ref=beside.at[:, rows, :],
            send_sem=columns_send.at[q],
            recv_sem=columns_recv.at[q],
            device_id={"fx": prev},
            device_id_type=pl.DeviceIdType.MESH,
        )

    def halo_copy(i):
        source = (extended.at[:, :HALO, :SIDE], columns.at[:, :HALO, :])[i]
        target = (extended.at[:, SIDE:, :SIDE], corner)[i]
        where = ({"fy": up}, {"fy": up, "fx": prev})[i]
        return pltpu.make_async_remote_copy(
            src_ref=source,
            dst_ref=target,
            send_sem=halo_send.at[i],
            recv_sem=halo_recv.at[i],
            device_id=where,
            device_id_type=pl.DeviceIdType.MESH,
        )

    def make_chunk(q, carry):
        for i in range(deep // 16):
            combine(q * (deep // 16) + i)
        columns_copy(q).start()

        @pl.when(q == 0)
        def _():
            for i in range(2):
                halo_copy(i).start()

        return carry

    lax.fori_loop(0, chunks, make_chunk, 0)

    def place(source, begin, end):
        for p in range(CH // 2):
            first = source[p]
            extended[2 * p, begin:end, SIDE:] = first
            extended[2 * p + 1, begin:end, SIDE:] = pltpu.roll(first.astype(F32), 64, 1).astype(BF)

    halo_copy(1).wait_recv()
    place(corner, SIDE, TALL)
    for q in range(chunks):
        columns_copy(q).wait_recv()
        place(beside.at[:, q * deep : (q + 1) * deep, :], q * deep, (q + 1) * deep)
    halo_copy(0).wait_recv()

    def finish_shares(k, carry):
        share_copy(peer(k), fx).wait_send()
        return carry

    def finish_near(j, carry):
        near_copy(j).wait_send()
        return carry

    def finish_far(j, carry):
        for r in range(2):
            far_copy(j, r).wait_send()
            relay_copy(j, r).wait_send()
        return carry

    lax.fori_loop(1, n_fx, finish_shares, 0)
    lax.fori_loop(0, len(NEAR), finish_near, 0)
    lax.fori_loop(0, len(FAR), finish_far, 0)
    for i in range(2):
        halo_copy(i).wait_send()
    for q in range(chunks):
        columns_copy(q).wait_send()


def passed(value, axes, to):
    sizes = [lax.axis_size(a) for a in axes]
    pairs = []
    for i in np.ndindex(*sizes):
        j = [(a + b) % n for a, b, n in zip(i, to, sizes)]
        pairs.append((int(np.ravel_multi_index(i, sizes)), int(np.ravel_multi_index(j, sizes))))
    return lax.ppermute(value, axes if len(axes) > 1 else axes[0], pairs)


def per_device(n_fy, n_fx, sky_image, vis_tiles, tile_dest, tile_chan, tile_count, thresholds):
    made = {name: jnp.asarray(table) for name, table in tables().items()}
    smem = pl.BlockSpec(memory_space=pltpu.SMEM)
    vmem = pl.BlockSpec(memory_space=pltpu.VMEM)
    anywhere = pl.BlockSpec(memory_space=pl.ANY)
    dma = pltpu.SemaphoreType.DMA
    tiles = vis_tiles.shape[0]
    half = jnp.einsum(
        "ipuv,pvqx->iuqx", vis_tiles, made["fourier"], preferred_element_type=F32
    ).astype(BF)
    planes = jnp.einsum("yqu,iuqx->iyx", made["back"], half, preferred_element_type=F32)
    weight = tile_count.astype(F32) / 64.0
    planes = (planes * weight[:, None, None]).astype(BF)
    extended = pl.pallas_call(
        functools.partial(exchange_kernel, n_fy, n_fx),
        out_shape=jax.ShapeDtypeStruct((CH, TALL, WIDE), BF),
        in_specs=[smem] * 3 + [vmem] * 2 + [anywhere],
        out_specs=vmem,
        scratch_shapes=[
            pltpu.VMEM((CH, SIDE, SIDE), F32),
            pltpu.VMEM((CH, SIDE, SIDE), F32),
            pltpu.VMEM((n_fx, 2, SIDE, SIDE), BF),
            pltpu.VMEM((n_fx, 2, SIDE, SIDE), BF),
            pltpu.VMEM((len(FAR), 2, SIDE, SIDE), BF),
            pltpu.VMEM((n_fx, 8, 128), F32),
            pltpu.VMEM((n_fx, 8, 128), F32),
            pltpu.VMEM((CH * 16, n_fx * 32), BF),
            pltpu.VMEM((CH // 2, SIDE, 128), BF),
            pltpu.VMEM((CH // 2, SIDE, 128), BF),
            pltpu.VMEM((CH // 2, HALO, 128), BF),
            dma((1,)),
            dma((n_fx, 2)),
            dma((n_fx, 2)),
            dma((len(FAR), 2)),
            dma((len(FAR), 2)),
            dma((n_fx,)),
            dma((n_fx,)),
            dma((2,)),
            dma((2,)),
            dma((4,)),
            dma((4,)),
        ],
        compiler_params=pltpu.CompilerParams(
            collective_id=0, has_side_effects=True, vmem_limit_bytes=58 * 1024 * 1024
        ),
    )(
        tile_dest.reshape(tiles),
        tile_chan,
        tile_count,
        made["excess"],
        planes,
        sky_image,
    )
    rows, columns = made["rows"], made["columns"]
    row_sec = jnp.einsum("bkn,cnx->bckx", rows, extended, preferred_element_type=F32).astype(BF)
    coefficient = jnp.einsum("bcyx,bkx->bcyk", row_sec, columns, preferred_element_type=F32)
    limits = thresholds.astype(F32)
    shrunk = (coefficient - jnp.clip(coefficient, -limits, limits)).astype(BF)
    col_sec = jnp.einsum("bcyk,bkx->bcyx", shrunk, columns, preferred_element_type=F32).astype(BF)
    cells = jnp.einsum("bkn,bckx->cnx", rows, col_sec, preferred_element_type=F32)
    spill = cells.astype(BF)
    from_left = passed(spill[:, :SIDE, SIDE:], ("fx",), (1,)).astype(F32)
    from_above = passed(spill[:, SIDE:, :SIDE], ("fy",), (1,)).astype(F32)
    from_corner = passed(spill[:, SIDE:, SIDE:], ("fy", "fx"), (1, 1)).astype(F32)
    left = jnp.pad(from_left, ((0, 0), (0, 0), (0, 128)))
    above = jnp.pad(from_above, ((0, 0), (0, SIDE - HALO), (0, 0)))
    corner = jnp.pad(from_corner, ((0, 0), (0, SIDE - HALO), (0, 128)))
    summed = cells[:, :SIDE, :SIDE] + left + above + corner
    return jnp.maximum(summed * (1.0 / BASES), 0.0)


def solution(mesh):
    in_specs = (
        P(None, "fy", "fx"),
        P(("fy", "fx"), None, None, None),
        P(("fy", "fx"), None),
        P(("fy", "fx")),
        P(("fy", "fx")),
        P(None, None, "fy", "fx"),
    )
    out_specs = P(None, "fy", "fx")
    return jax.shard_map(
        functools.partial(per_device, mesh.shape["fy"], mesh.shape["fx"]),
        mesh=mesh,
        in_specs=in_specs,
        out_specs=out_specs,
        check_vma=False,
    )
```

```python
import functools
import math

import jax
import jax.numpy as jnp
import ml_dtypes
import numpy as np
from jax import lax
from jax.experimental import pallas as pl
from jax.experimental.pallas import tpu as pltpu
from jax.sharding import PartitionSpec as P

daubechies_taps = [
    [0.7071067811865476, 0.7071067811865476],
    [0.48296291314469025, 0.836516303737469, 0.22414386804185735, -0.12940952255092145],
    [
        0.3326705529509569,
        0.8068915093133388,
        0.4598775021193313,
        -0.13501102001039084,
        -0.08544127388224149,
        0.035226291882100656,
    ],
    [
        0.23037781330885523,
        0.7148465705525415,
        0.6308807679295904,
        -0.02798376941698385,
        -0.18703481171888114,
        0.030841381835986965,
        0.032883011666982945,
        -0.010597401784997278,
    ],
    [
        0.160102397974125,
        0.6038292697974729,
        0.7243085284385744,
        0.13842814590110342,
        -0.24229488706619015,
        -0.03224486958502952,
        0.07757149384006515,
        -0.006241490213011705,
        -0.012580751999015526,
        0.003335725285001549,
    ],
    [
        0.11154074335008017,
        0.4946238903983854,
        0.7511339080215775,
        0.3152503517092432,
        -0.22626469396516913,
        -0.12976686756709563,
        0.09750160558707936,
        0.02752286553001629,
        -0.031582039318031156,
        0.0005538422009938016,
        0.004777257511010651,
        -0.00107730108499558,
    ],
    [
        0.07785205408506236,
        0.39653931948230575,
        0.7291320908465551,
        0.4697822874053586,
        -0.14390600392910627,
        -0.22403618499416572,
        0.07130921926705004,
        0.0806126091510659,
        -0.03802993693503463,
        -0.01657454163101562,
        0.012550998556013784,
        0.00042957797300470274,
        -0.0018016407039998328,
        0.0003537138000010399,
    ],
    [
        0.05441584224308161,
        0.3128715909144659,
        0.6756307362980128,
        0.5853546836548691,
        -0.015829105256023893,
        -0.2840155429624281,
        0.00047248457399797254,
        0.128747426620186,
        -0.01736930100202211,
        -0.04408825393106472,
        0.013981027917015516,
        0.008746094047015655,
        -0.00487035299301066,
        -0.0003917403729959771,
        0.0006754494059985568,
        -0.00011747678400228192,
    ],
]


SIDE = 256
CH = 8
BASES = 8
HALO = 48
BF = jnp.bfloat16
F32 = jnp.float32
WIDE = SIDE + 128
TALL = SIDE + HALO


def rounded(table):
    return np.asarray(table, np.float32).astype(ml_dtypes.bfloat16)


def composite_tables():
    full = np.zeros((BASES, SIDE, SIDE + HALO))
    for degree in range(1, 9):
        taps = np.array(daubechies_taps[degree - 1])
        taps = taps * math.sqrt(2.0) / np.sum(taps)
        length = 2 * degree
        low = np.zeros(16)
        high = np.zeros(16)
        low[:length] = taps
        high[:length] = [(-1.0) ** j * taps[length - 1 - j] for j in range(length)]
        low = rounded(low).astype(np.float64)
        high = rounded(high).astype(np.float64)
        level_low = np.zeros((144, SIDE + HALO))
        level_high = np.zeros((128, SIDE + HALO))
        for k in range(144):
            level_low[k, 2 * k : 2 * k + 16] = low[: min(16, SIDE + HALO - 2 * k)]
        for k in range(128):
            level_high[k, 2 * k : 2 * k + 16] = high
        second = np.zeros((128, 144))
        for m in range(64):
            second[m, 2 * m : 2 * m + 16] = low
            second[64 + m, 2 * m : 2 * m + 16] = high
        full[degree - 1, :128] = second @ level_low
        full[degree - 1, 128:] = level_high
    return rounded(full).astype(np.float32)


@functools.lru_cache(maxsize=1)
def tables():
    full = composite_tables()
    wide = np.concatenate([full, np.zeros((BASES, SIDE, 128 - HALO), np.float32)], axis=2)
    out = {"rows": full, "columns": wide}
    grid = np.arange(SIDE)[:, None] * np.arange(SIDE)[None, :] % SIDE
    angle = grid * (2.0 * math.pi / SIDE)
    cosine = rounded(np.cos(angle) / math.sqrt(SIDE)).astype(np.float64)
    sine = rounded(np.sin(angle) / math.sqrt(SIDE)).astype(np.float64)
    out["fourier"] = np.block([[cosine, sine], [-sine, cosine]])
    out["back"] = np.concatenate([cosine, -sine], axis=1)
    out["excess"] = cosine @ cosine + sine @ sine - np.eye(SIDE)
    return {name: rounded(table) for name, table in out.items()}


NEAR = ((1, 0), (0, 1), (3, 0), (0, 3), (1, 1), (3, 3), (1, 3), (3, 1))
FAR = ((2, 0), (0, 2), (2, 1), (2, 3), (1, 2), (3, 2), (2, 2))
THROUGH = ((3, 0), (0, 3), (3, 1), (3, 3), (1, 3), (3, 3), (3, 3))


def choose(j, values):
    out = jnp.int32(values[0])
    for i, value in enumerate(values):
        out = jnp.where(j == i, jnp.int32(value), out)
    return out


def dot(a, b):
    return jnp.dot(a, b, preferred_element_type=F32)


def exchange_kernel(
    n_fy,
    n_fx,
    dest_ref,
    chan_ref,
    count_ref,
    fourier,
    back,
    excess,
    sky_hbm,
    vis_hbm,
    extended,
    vis,
    sky,
    model,
    sending,
    arrived,
    relay,
    half,
    share_ref,
    shares,
    kron,
    columns,
    beside,
    corner,
    load_sem,
    tile_send,
    tile_recv,
    relay_send,
    relay_recv,
    share_send,
    share_recv,
    halo_send,
    halo_recv,
    columns_send,
    columns_recv,
):
    fy = lax.axis_index("fy")
    fx = lax.axis_index("fx")
    n_z = 4
    n_x = n_fx // n_z
    my_x, my_z = fx // n_z, fx % n_z

    def at(dx, dz):
        return (my_x + dx) % n_x * n_z + (my_z + dz) % n_z

    def peer(k):
        return at(k // n_z, k % n_z)

    load_vis = pltpu.make_async_copy(vis_hbm, vis, load_sem.at[0])
    load_sky = pltpu.make_async_copy(sky_hbm, sky, load_sem.at[1])
    load_vis.start()
    load_sky.start()

    barrier = pltpu.get_barrier_semaphore()

    def greet(k, carry):
        pl.semaphore_signal(
            barrier, inc=1, device_id={"fx": peer(k)}, device_id_type=pl.DeviceIdType.MESH
        )
        return carry

    lax.fori_loop(1, n_fx, greet, 0)
    up, down = (fy + n_fy - 1) % n_fy, (fy + 1) % n_fy
    prev, nxt = (fx + n_fx - 1) % n_fx, (fx + 1) % n_fx
    for where in ({"fy": up}, {"fy": down}, {"fy": up, "fx": prev}, {"fy": down, "fx": nxt}):
        pl.semaphore_signal(barrier, inc=1, device_id=where, device_id_type=pl.DeviceIdType.MESH)
    pl.semaphore_wait(barrier, n_fx - 1 + 4)

    def share_copy(to, source):
        return pltpu.make_async_remote_copy(
            src_ref=share_ref.at[to],
            dst_ref=shares.at[source],
            send_sem=share_send.at[to],
            recv_sem=share_recv.at[source],
            device_id={"fx": to},
            device_id_type=pl.DeviceIdType.MESH,
        )

    def near(j):
        return choose(j, [o[0] for o in NEAR]), choose(j, [o[1] for o in NEAR])

    def far(j):
        return choose(j, [o[0] for o in FAR]), choose(j, [o[1] for o in FAR])

    def through(j):
        return choose(j, [o[0] for o in THROUGH]), choose(j, [o[1] for o in THROUGH])

    def near_copy(j):
        return pltpu.make_async_remote_copy(
            src_ref=sending.at[len(FAR) + j],
            dst_ref=arrived.at[fx],
            send_sem=tile_send.at[len(FAR) + j, 0],
            recv_sem=tile_recv.at[fx, 0],
            device_id={"fx": at(*near(j))},
            device_id_type=pl.DeviceIdType.MESH,
        )

    def far_copy(j, r):
        return pltpu.make_async_remote_copy(
            src_ref=sending.at[j, r],
            dst_ref=arrived.at[fx, 0] if r == 0 else relay.at[j],
            send_sem=tile_send.at[j, r],
            recv_sem=tile_recv.at[fx, 0] if r == 0 else relay_recv.at[j],
            device_id={"fx": at(*far(j)) if r == 0 else at(*through(j))},
            device_id_type=pl.DeviceIdType.MESH,
        )

    def relay_copy(j):
        end, mid = far(j), through(j)
        source = at(4 - mid[0], 4 - mid[1])
        return pltpu.make_async_remote_copy(
            src_ref=relay.at[j],
            dst_ref=arrived.at[source, 1],
            send_sem=relay_send.at[j],
            recv_sem=tile_recv.at[source, 1],
            device_id={"fx": at(end[0] + 4 - mid[0], end[1] + 4 - mid[1])},
            device_id_type=pl.DeviceIdType.MESH,
        )

    def near_arrival(j):
        dx, dz = near(j)
        source = at(4 - dx, 4 - dz)
        return pltpu.make_async_remote_copy(
            src_ref=arrived.at[source],
            dst_ref=arrived.at[source],
            send_sem=tile_send.at[0, 0],
            recv_sem=tile_recv.at[source, 0],
            device_id={"fx": source},
            device_id_type=pl.DeviceIdType.MESH,
        )

    def far_arrival(j, r):
        dx, dz = far(j)
        source = at(4 - dx, 4 - dz)
        return pltpu.make_async_remote_copy(
            src_ref=arrived.at[source, r],
            dst_ref=arrived.at[source, r],
            send_sem=tile_send.at[0, 0],
            recv_sem=tile_recv.at[source, r],
            device_id={"fx": source},
            device_id_type=pl.DeviceIdType.MESH,
        )

    tiles = vis_hbm.shape[0]
    row = lax.broadcasted_iota(jnp.int32, (8, 128), 0)
    lane = lax.broadcasted_iota(jnp.int32, (8, 128), 1)

    def slots_for(to):
        found = jnp.int32(0)
        picked = [(jnp.int32(0), jnp.int32(0), jnp.int32(0))] * 2
        for i in range(tiles):
            match = dest_ref[i] == to
            for r in range(2):
                here = match & (found == r)
                new = (jnp.int32(i), count_ref[i], chan_ref[i])
                picked[r] = tuple(jnp.where(here, a, b) for a, b in zip(new, picked[r]))
            found = found + jnp.where(match, 1, 0)
        return [(tile, count.astype(F32) * (1.0 / 64.0), chan) for tile, count, chan in picked]

    def share_rows(slots):
        total = jnp.zeros((8, 128), F32)
        for r, (_, weight, chan) in enumerate(slots):
            total = total + jnp.where((row == r) & (lane == chan), weight, 0.0)
        return total

    load_vis.wait()

    def planes(slots):
        for i, (t, _, _) in enumerate(slots):
            spectrum = jnp.concatenate([vis[t, 0], vis[t, 1]], axis=1)
            for part in range(2):
                half[i, part * SIDE : (part + 1) * SIDE] = dot(
                    spectrum, fourier[:, part * SIDE : (part + 1) * SIDE]
                ).astype(BF)
        return [(dot(back[...], half[i]) * slots[i][1]).astype(BF) for i in range(2)]

    def prepare(to, place):
        slots = slots_for(to)
        share_ref[to] = share_rows(slots)
        share_copy(to, fx).start()
        sending[place, 0], sending[place, 1] = planes(slots)

    def send_far(j, carry):
        prepare(at(*far(j)), j)
        far_copy(j, 1).start()
        far_copy(j, 0).start()
        return carry

    lax.fori_loop(0, len(FAR), send_far, 0)

    def send_near(j, carry):
        prepare(at(*near(j)), len(FAR) + j)
        near_copy(j).start()

        @pl.when(j >= 1)
        def _():
            far_copy(j - 1, 1).wait_recv()
            relay_copy(j - 1).start()

        return carry

    lax.fori_loop(0, len(NEAR), send_near, 0)
    own = slots_for(fx)
    shares[fx] = share_rows(own)
    arrived[fx, 0], arrived[fx, 1] = planes(own)

    load_sky.wait()

    def there_and_back(c, carry):
        pixels = sky[c].astype(BF)
        once = pixels.astype(F32) + dot(excess[...], pixels)
        model[c] = once + dot(once.astype(BF), excess[...])
        return carry

    lax.fori_loop(0, CH, there_and_back, 0)

    def wait_share(k, carry):
        share_copy(peer(k), peer(k)).wait_recv()
        return carry

    lax.fori_loop(1, n_fx, wait_share, 0)
    slots = n_fx * 2
    wide = slots * 16
    all_shares = shares[...].reshape(n_fx * 8, 128)
    members = jnp.where(all_shares > 0, 1.0, 0.0).astype(BF)
    spread = (
        lax.broadcasted_iota(jnp.int32, (CH * 16, 128), 0) // 16
        == lax.broadcasted_iota(jnp.int32, (CH * 16, 128), 1)
    )
    spread = jnp.where(spread, 1.0, 0.0).astype(BF)
    by_source = lax.dot_general(
        spread, members, (((1,), (1,)), ((), ())), preferred_element_type=F32
    ).astype(BF)
    weights = lax.dot_general(
        spread, all_shares.astype(BF), (((1,), (1,)), ((), ())), preferred_element_type=F32
    )
    totals = jnp.sum(weights, axis=1, keepdims=True)
    src_row = lax.broadcasted_iota(jnp.int32, (n_fx * 8, wide), 0)
    dst_col = lax.broadcasted_iota(jnp.int32, (n_fx * 8, wide), 1)
    widen = (src_row // 8 == dst_col // 32) & (src_row % 8 == dst_col // 16 % 2)
    widened = dot(by_source, jnp.where(widen, 1.0, 0.0).astype(BF))
    diagonal = (
        lax.broadcasted_iota(jnp.int32, (CH * 16, wide), 0) % 16
        == lax.broadcasted_iota(jnp.int32, (CH * 16, wide), 1) % 16
    )
    kron[...] = jnp.where(diagonal, widened, 0.0).astype(BF)
    scale = 1.0 / (1.0 + totals)

    def wait_near(j, carry):
        near_arrival(j).wait_recv()
        return carry

    def wait_far(j, carry):
        for r in range(2):
            far_arrival(j, r).wait_recv()
        return carry

    lax.fori_loop(0, len(NEAR), wait_near, 0)
    lax.fori_loop(0, len(FAR), wait_far, 0)

    def combine(g):
        rows = pl.ds(pl.multiple_of(g * 16, 16), 16)
        gathered = dot(kron[...], arrived[:, :, rows, :].reshape(wide, SIDE))
        pixels = sky[:, rows, :].reshape(CH * 16, SIDE)
        there = model[:, rows, :].reshape(CH * 16, SIDE)
        new = pixels - (totals * there - gathered) * scale
        new = new.reshape(CH // 2, 2, 16, SIDE)
        extended[:, rows, :SIDE] = new.reshape(CH, 16, SIDE).astype(BF)
        low = lax.broadcasted_iota(jnp.int32, (CH // 2, 16, 128), 2) < 64
        second = pltpu.roll(new[:, 1, :, :128].reshape(CH // 2 * 16, 128), 64, 1)
        pair = jnp.where(low, new[:, 0, :, :128], second.reshape(CH // 2, 16, 128))
        columns[:, rows, :] = pair.astype(BF)

    chunks = 4
    deep = SIDE // chunks

    def columns_copy(q):
        rows = pl.ds(pl.multiple_of(q * deep, deep), deep)
        return pltpu.make_async_remote_copy(
            src_ref=columns.at[:, rows, :],
            dst_ref=beside.at[:, rows, :],
            send_sem=columns_send.at[q],
            recv_sem=columns_recv.at[q],
            device_id={"fx": prev},
            device_id_type=pl.DeviceIdType.MESH,
        )

    def halo_copy(i):
        source = (extended.at[:, :HALO, :SIDE], columns.at[:, :HALO, :])[i]
        target = (extended.at[:, SIDE:, :SIDE], corner)[i]
        where = ({"fy": up}, {"fy": up, "fx": prev})[i]
        return pltpu.make_async_remote_copy(
            src_ref=source,
            dst_ref=target,
            send_sem=halo_send.at[i],
            recv_sem=halo_recv.at[i],
            device_id=where,
            device_id_type=pl.DeviceIdType.MESH,
        )

    def make_chunk(q, carry):
        for i in range(deep // 16):
            combine(q * (deep // 16) + i)
        columns_copy(q).start()

        @pl.when(q == 0)
        def _():
            for i in range(2):
                halo_copy(i).start()

        return carry

    lax.fori_loop(0, chunks, make_chunk, 0)

    def place(source, begin, end):
        for p in range(CH // 2):
            first = source[p]
            extended[2 * p, begin:end, SIDE:] = first
            extended[2 * p + 1, begin:end, SIDE:] = pltpu.roll(first.astype(F32), 64, 1).astype(BF)

    halo_copy(1).wait_recv()
    place(corner, SIDE, TALL)
    for q in range(chunks):
        columns_copy(q).wait_recv()
        place(beside.at[:, q * deep : (q + 1) * deep, :], q * deep, (q + 1) * deep)
    halo_copy(0).wait_recv()

    def finish_shares(k, carry):
        share_copy(peer(k), fx).wait_send()
        return carry

    def finish_near(j, carry):
        near_copy(j).wait_send()
        return carry

    def finish_far(j, carry):
        for r in range(2):
            far_copy(j, r).wait_send()
        relay_copy(j).wait_send()
        return carry

    lax.fori_loop(1, n_fx, finish_shares, 0)
    lax.fori_loop(0, len(NEAR), finish_near, 0)
    lax.fori_loop(0, len(FAR), finish_far, 0)
    for i in range(2):
        halo_copy(i).wait_send()
    for q in range(chunks):
        columns_copy(q).wait_send()


def passed(value, axes, to):
    sizes = [lax.axis_size(a) for a in axes]
    pairs = []
    for i in np.ndindex(*sizes):
        j = [(a + b) % n for a, b, n in zip(i, to, sizes)]
        pairs.append((int(np.ravel_multi_index(i, sizes)), int(np.ravel_multi_index(j, sizes))))
    return lax.ppermute(value, axes if len(axes) > 1 else axes[0], pairs)


def per_device(n_fy, n_fx, sky_image, vis_tiles, tile_dest, tile_chan, tile_count, thresholds):
    made = {name: jnp.asarray(table) for name, table in tables().items()}
    smem = pl.BlockSpec(memory_space=pltpu.SMEM)
    vmem = pl.BlockSpec(memory_space=pltpu.VMEM)
    anywhere = pl.BlockSpec(memory_space=pl.ANY)
    dma = pltpu.SemaphoreType.DMA
    tiles = vis_tiles.shape[0]
    extended = pl.pallas_call(
        functools.partial(exchange_kernel, n_fy, n_fx),
        out_shape=jax.ShapeDtypeStruct((CH, TALL, WIDE), BF),
        in_specs=[smem] * 3 + [vmem] * 3 + [anywhere] * 2,
        out_specs=vmem,
        scratch_shapes=[
            pltpu.VMEM((tiles, 2, SIDE, SIDE), BF),
            pltpu.VMEM((CH, SIDE, SIDE), F32),
            pltpu.VMEM((CH, SIDE, SIDE), F32),
            pltpu.VMEM((n_fx, 2, SIDE, SIDE), BF),
            pltpu.VMEM((n_fx, 2, SIDE, SIDE), BF),
            pltpu.VMEM((len(FAR), SIDE, SIDE), BF),
            pltpu.VMEM((2, 2 * SIDE, SIDE), BF),
            pltpu.VMEM((n_fx, 8, 128), F32),
            pltpu.VMEM((n_fx, 8, 128), F32),
            pltpu.VMEM((CH * 16, n_fx * 32), BF),
            pltpu.VMEM((CH // 2, SIDE, 128), BF),
            pltpu.VMEM((CH // 2, SIDE, 128), BF),
            pltpu.VMEM((CH // 2, HALO, 128), BF),
            dma((2,)),
            dma((n_fx, 2)),
            dma((n_fx, 2)),
            dma((len(FAR),)),
            dma((len(FAR),)),
            dma((n_fx,)),
            dma((n_fx,)),
            dma((2,)),
            dma((2,)),
            dma((4,)),
            dma((4,)),
        ],
        compiler_params=pltpu.CompilerParams(
            collective_id=0, has_side_effects=True, vmem_limit_bytes=58 * 1024 * 1024
        ),
    )(
        tile_dest.reshape(tiles),
        tile_chan,
        tile_count,
        made["fourier"],
        made["back"],
        made["excess"],
        sky_image,
        vis_tiles,
    )
    rows, columns = made["rows"], made["columns"]
    row_sec = jnp.einsum("bkn,cnx->bckx", rows, extended, preferred_element_type=F32).astype(BF)
    coefficient = jnp.einsum("bcyx,bkx->bcyk", row_sec, columns, preferred_element_type=F32)
    limits = thresholds.astype(F32)
    shrunk = (coefficient - jnp.clip(coefficient, -limits, limits)).astype(BF)
    col_sec = jnp.einsum("bcyk,bkx->bcyx", shrunk, columns, preferred_element_type=F32).astype(BF)
    cells = jnp.einsum("bkn,bckx->cnx", rows, col_sec, preferred_element_type=F32)
    spill = cells.astype(BF)
    from_left = passed(spill[:, :SIDE, SIDE:TALL], ("fx",), (1,)).astype(F32)
    from_above = passed(spill[:, SIDE:, :SIDE], ("fy",), (1,)).astype(F32)
    from_corner = passed(spill[:, SIDE:, SIDE:TALL], ("fy", "fx"), (1, 1)).astype(F32)
    left = jnp.pad(from_left, ((0, 0), (0, 0), (0, SIDE - HALO)))
    above = jnp.pad(from_above, ((0, 0), (0, SIDE - HALO), (0, 0)))
    corner = jnp.pad(from_corner, ((0, 0), (0, SIDE - HALO), (0, SIDE - HALO)))
    summed = cells[:, :SIDE, :SIDE] + left + above + corner
    return jnp.maximum(summed * (1.0 / BASES), 0.0)


def solution(mesh):
    in_specs = (
        P(None, "fy", "fx"),
        P(("fy", "fx"), None, None, None),
        P(("fy", "fx"), None),
        P(("fy", "fx")),
        P(("fy", "fx")),
        P(None, None, "fy", "fx"),
    )
    out_specs = P(None, "fy", "fx")
    return jax.shard_map(
        functools.partial(per_device, mesh.shape["fy"], mesh.shape["fx"]),
        mesh=mesh,
        in_specs=in_specs,
        out_specs=out_specs,
        check_vma=False,
    )
```

```python
import functools
import math

import jax
import jax.numpy as jnp
import ml_dtypes
import numpy as np
from jax import lax
from jax.experimental import pallas as pl
from jax.experimental.pallas import tpu as pltpu
from jax.sharding import PartitionSpec as P

daubechies_taps = [
    [0.7071067811865476, 0.7071067811865476],
    [0.48296291314469025, 0.836516303737469, 0.22414386804185735, -0.12940952255092145],
    [
        0.3326705529509569,
        0.8068915093133388,
        0.4598775021193313,
        -0.13501102001039084,
        -0.08544127388224149,
        0.035226291882100656,
    ],
    [
        0.23037781330885523,
        0.7148465705525415,
        0.6308807679295904,
        -0.02798376941698385,
        -0.18703481171888114,
        0.030841381835986965,
        0.032883011666982945,
        -0.010597401784997278,
    ],
    [
        0.160102397974125,
        0.6038292697974729,
        0.7243085284385744,
        0.13842814590110342,
        -0.24229488706619015,
        -0.03224486958502952,
        0.07757149384006515,
        -0.006241490213011705,
        -0.012580751999015526,
        0.003335725285001549,
    ],
    [
        0.11154074335008017,
        0.4946238903983854,
        0.7511339080215775,
        0.3152503517092432,
        -0.22626469396516913,
        -0.12976686756709563,
        0.09750160558707936,
        0.02752286553001629,
        -0.031582039318031156,
        0.0005538422009938016,
        0.004777257511010651,
        -0.00107730108499558,
    ],
    [
        0.07785205408506236,
        0.39653931948230575,
        0.7291320908465551,
        0.4697822874053586,
        -0.14390600392910627,
        -0.22403618499416572,
        0.07130921926705004,
        0.0806126091510659,
        -0.03802993693503463,
        -0.01657454163101562,
        0.012550998556013784,
        0.00042957797300470274,
        -0.0018016407039998328,
        0.0003537138000010399,
    ],
    [
        0.05441584224308161,
        0.3128715909144659,
        0.6756307362980128,
        0.5853546836548691,
        -0.015829105256023893,
        -0.2840155429624281,
        0.00047248457399797254,
        0.128747426620186,
        -0.01736930100202211,
        -0.04408825393106472,
        0.013981027917015516,
        0.008746094047015655,
        -0.00487035299301066,
        -0.0003917403729959771,
        0.0006754494059985568,
        -0.00011747678400228192,
    ],
]


SIDE = 256
CH = 8
BASES = 8
HALO = 48
BF = jnp.bfloat16
F32 = jnp.float32
WIDE = SIDE + 128
TALL = SIDE + HALO


def rounded(table):
    return np.asarray(table, np.float32).astype(ml_dtypes.bfloat16)


def composite_tables():
    full = np.zeros((BASES, SIDE, SIDE + HALO))
    for degree in range(1, 9):
        taps = np.array(daubechies_taps[degree - 1])
        taps = taps * math.sqrt(2.0) / np.sum(taps)
        length = 2 * degree
        low = np.zeros(16)
        high = np.zeros(16)
        low[:length] = taps
        high[:length] = [(-1.0) ** j * taps[length - 1 - j] for j in range(length)]
        low = rounded(low).astype(np.float64)
        high = rounded(high).astype(np.float64)
        level_low = np.zeros((144, SIDE + HALO))
        level_high = np.zeros((128, SIDE + HALO))
        for k in range(144):
            level_low[k, 2 * k : 2 * k + 16] = low[: min(16, SIDE + HALO - 2 * k)]
        for k in range(128):
            level_high[k, 2 * k : 2 * k + 16] = high
        second = np.zeros((128, 144))
        for m in range(64):
            second[m, 2 * m : 2 * m + 16] = low
            second[64 + m, 2 * m : 2 * m + 16] = high
        full[degree - 1, :128] = second @ level_low
        full[degree - 1, 128:] = level_high
    return rounded(full).astype(np.float32)


@functools.lru_cache(maxsize=1)
def tables():
    full = composite_tables()
    wide = np.concatenate([full, np.zeros((BASES, SIDE, 128 - HALO), np.float32)], axis=2)
    out = {"rows": full, "columns": wide}
    grid = np.arange(SIDE)[:, None] * np.arange(SIDE)[None, :] % SIDE
    angle = grid * (2.0 * math.pi / SIDE)
    cosine = rounded(np.cos(angle) / math.sqrt(SIDE)).astype(np.float64)
    sine = rounded(np.sin(angle) / math.sqrt(SIDE)).astype(np.float64)
    out["fourier"] = np.block([[cosine, sine], [-sine, cosine]])
    out["back"] = np.concatenate([cosine, -sine], axis=1)
    out["excess"] = cosine @ cosine + sine @ sine - np.eye(SIDE)
    return {name: rounded(table) for name, table in out.items()}


NEAR = ((1, 0), (0, 1), (3, 0), (0, 3), (1, 1), (3, 3), (1, 3), (3, 1))
FAR = ((2, 0), (0, 2), (2, 1), (2, 3), (1, 2), (3, 2), (2, 2))
THROUGH = ((1, 0), (0, 1), (1, 1), (1, 3), (1, 1), (3, 1), (1, 1))


def choose(j, values):
    out = jnp.int32(values[0])
    for i, value in enumerate(values):
        out = jnp.where(j == i, jnp.int32(value), out)
    return out


def dot(a, b):
    return jnp.dot(a, b, preferred_element_type=F32)


def exchange_kernel(
    n_fy,
    n_fx,
    dest_ref,
    chan_ref,
    count_ref,
    fourier,
    back,
    excess,
    sky_hbm,
    vis_hbm,
    extended,
    vis,
    sky,
    model,
    sending,
    arrived,
    relay,
    half,
    share_ref,
    shares,
    kron,
    columns,
    beside,
    corner,
    load_sem,
    tile_send,
    tile_recv,
    relay_send,
    relay_recv,
    share_send,
    share_recv,
    halo_send,
    halo_recv,
    columns_send,
    columns_recv,
):
    fy = lax.axis_index("fy")
    fx = lax.axis_index("fx")
    n_z = 4
    n_x = n_fx // n_z
    my_x, my_z = fx // n_z, fx % n_z

    def at(dx, dz):
        return (my_x + dx) % n_x * n_z + (my_z + dz) % n_z

    def peer(k):
        return at(k // n_z, k % n_z)

    load_vis = pltpu.make_async_copy(vis_hbm, vis, load_sem.at[0])
    load_sky = pltpu.make_async_copy(sky_hbm, sky, load_sem.at[1])
    load_vis.start()
    load_sky.start()

    barrier = pltpu.get_barrier_semaphore()

    def greet(k, carry):
        pl.semaphore_signal(
            barrier, inc=1, device_id={"fx": peer(k)}, device_id_type=pl.DeviceIdType.MESH
        )
        return carry

    lax.fori_loop(1, n_fx, greet, 0)
    up, down = (fy + n_fy - 1) % n_fy, (fy + 1) % n_fy
    prev, nxt = (fx + n_fx - 1) % n_fx, (fx + 1) % n_fx
    for where in ({"fy": up}, {"fy": down}, {"fy": up, "fx": prev}, {"fy": down, "fx": nxt}):
        pl.semaphore_signal(barrier, inc=1, device_id=where, device_id_type=pl.DeviceIdType.MESH)
    pl.semaphore_wait(barrier, n_fx - 1 + 4)

    def share_copy(to, source):
        return pltpu.make_async_remote_copy(
            src_ref=share_ref.at[to],
            dst_ref=shares.at[source],
            send_sem=share_send.at[to],
            recv_sem=share_recv.at[source],
            device_id={"fx": to},
            device_id_type=pl.DeviceIdType.MESH,
        )

    def near(j):
        return choose(j, [o[0] for o in NEAR]), choose(j, [o[1] for o in NEAR])

    def far(j):
        return choose(j, [o[0] for o in FAR]), choose(j, [o[1] for o in FAR])

    def through(j):
        return choose(j, [o[0] for o in THROUGH]), choose(j, [o[1] for o in THROUGH])

    def near_copy(j):
        return pltpu.make_async_remote_copy(
            src_ref=sending.at[len(FAR) + j],
            dst_ref=arrived.at[fx],
            send_sem=tile_send.at[len(FAR) + j, 0],
            recv_sem=tile_recv.at[fx, 0],
            device_id={"fx": at(*near(j))},
            device_id_type=pl.DeviceIdType.MESH,
        )

    def far_copy(j, r):
        return pltpu.make_async_remote_copy(
            src_ref=sending.at[j, r],
            dst_ref=arrived.at[fx, 0] if r == 0 else relay.at[j],
            send_sem=tile_send.at[j, r],
            recv_sem=tile_recv.at[fx, 0] if r == 0 else relay_recv.at[j],
            device_id={"fx": at(*far(j)) if r == 0 else at(*through(j))},
            device_id_type=pl.DeviceIdType.MESH,
        )

    def relay_copy(j):
        end, mid = far(j), through(j)
        source = at(4 - mid[0], 4 - mid[1])
        return pltpu.make_async_remote_copy(
            src_ref=relay.at[j],
            dst_ref=arrived.at[source, 1],
            send_sem=relay_send.at[j],
            recv_sem=tile_recv.at[source, 1],
            device_id={"fx": at(end[0] + 4 - mid[0], end[1] + 4 - mid[1])},
            device_id_type=pl.DeviceIdType.MESH,
        )

    def near_arrival(j):
        dx, dz = near(j)
        source = at(4 - dx, 4 - dz)
        return pltpu.make_async_remote_copy(
            src_ref=arrived.at[source],
            dst_ref=arrived.at[source],
            send_sem=tile_send.at[0, 0],
            recv_sem=tile_recv.at[source, 0],
            device_id={"fx": source},
            device_id_type=pl.DeviceIdType.MESH,
        )

    def far_arrival(j, r):
        dx, dz = far(j)
        source = at(4 - dx, 4 - dz)
        return pltpu.make_async_remote_copy(
            src_ref=arrived.at[source, r],
            dst_ref=arrived.at[source, r],
            send_sem=tile_send.at[0, 0],
            recv_sem=tile_recv.at[source, r],
            device_id={"fx": source},
            device_id_type=pl.DeviceIdType.MESH,
        )

    tiles = vis_hbm.shape[0]
    row = lax.broadcasted_iota(jnp.int32, (8, 128), 0)
    lane = lax.broadcasted_iota(jnp.int32, (8, 128), 1)

    def slots_for(to):
        found = jnp.int32(0)
        picked = [(jnp.int32(0), jnp.int32(0), jnp.int32(0))] * 2
        for i in range(tiles):
            match = dest_ref[i] == to
            for r in range(2):
                here = match & (found == r)
                new = (jnp.int32(i), count_ref[i], chan_ref[i])
                picked[r] = tuple(jnp.where(here, a, b) for a, b in zip(new, picked[r]))
            found = found + jnp.where(match, 1, 0)
        return [(tile, count.astype(F32) * (1.0 / 64.0), chan) for tile, count, chan in picked]

    def share_rows(slots):
        total = jnp.zeros((8, 128), F32)
        for r, (_, weight, chan) in enumerate(slots):
            total = total + jnp.where((row == r) & (lane == chan), weight, 0.0)
        return total

    load_vis.wait()

    def planes(slots):
        for i, (t, _, _) in enumerate(slots):
            spectrum = jnp.concatenate([vis[t, 0], vis[t, 1]], axis=1)
            for part in range(2):
                half[i, part * SIDE : (part + 1) * SIDE] = dot(
                    spectrum, fourier[:, part * SIDE : (part + 1) * SIDE]
                ).astype(BF)
        return [(dot(back[...], half[i]) * slots[i][1]).astype(BF) for i in range(2)]

    def prepare(to, place):
        slots = slots_for(to)
        share_ref[to] = share_rows(slots)
        share_copy(to, fx).start()
        sending[place, 0], sending[place, 1] = planes(slots)

    def send_far(j, carry):
        prepare(at(*far(j)), j)
        far_copy(j, 1).start()
        far_copy(j, 0).start()
        return carry

    lax.fori_loop(0, len(FAR), send_far, 0)

    def send_near(j, carry):
        prepare(at(*near(j)), len(FAR) + j)
        near_copy(j).start()

        @pl.when(j >= 1)
        def _():
            far_copy(j - 1, 1).wait_recv()
            relay_copy(j - 1).start()

        return carry

    lax.fori_loop(0, len(NEAR), send_near, 0)
    own = slots_for(fx)
    shares[fx] = share_rows(own)
    arrived[fx, 0], arrived[fx, 1] = planes(own)

    load_sky.wait()

    def there_and_back(c, carry):
        pixels = sky[c].astype(BF)
        once = pixels.astype(F32) + dot(excess[...], pixels)
        model[c] = once + dot(once.astype(BF), excess[...])
        return carry

    lax.fori_loop(0, CH, there_and_back, 0)

    def wait_share(k, carry):
        share_copy(peer(k), peer(k)).wait_recv()
        return carry

    lax.fori_loop(1, n_fx, wait_share, 0)
    slots = n_fx * 2
    wide = slots * 16
    all_shares = shares[...].reshape(n_fx * 8, 128)
    members = jnp.where(all_shares > 0, 1.0, 0.0).astype(BF)
    spread = (
        lax.broadcasted_iota(jnp.int32, (CH * 16, 128), 0) // 16
        == lax.broadcasted_iota(jnp.int32, (CH * 16, 128), 1)
    )
    spread = jnp.where(spread, 1.0, 0.0).astype(BF)
    by_source = lax.dot_general(
        spread, members, (((1,), (1,)), ((), ())), preferred_element_type=F32
    ).astype(BF)
    weights = lax.dot_general(
        spread, all_shares.astype(BF), (((1,), (1,)), ((), ())), preferred_element_type=F32
    )
    totals = jnp.sum(weights, axis=1, keepdims=True)
    src_row = lax.broadcasted_iota(jnp.int32, (n_fx * 8, wide), 0)
    dst_col = lax.broadcasted_iota(jnp.int32, (n_fx * 8, wide), 1)
    widen = (src_row // 8 == dst_col // 32) & (src_row % 8 == dst_col // 16 % 2)
    widened = dot(by_source, jnp.where(widen, 1.0, 0.0).astype(BF))
    diagonal = (
        lax.broadcasted_iota(jnp.int32, (CH * 16, wide), 0) % 16
        == lax.broadcasted_iota(jnp.int32, (CH * 16, wide), 1) % 16
    )
    kron[...] = jnp.where(diagonal, widened, 0.0).astype(BF)
    scale = 1.0 / (1.0 + totals)

    def wait_near(j, carry):
        near_arrival(j).wait_recv()
        return carry

    def wait_far(j, carry):
        for r in range(2):
            far_arrival(j, r).wait_recv()
        return carry

    lax.fori_loop(0, len(NEAR), wait_near, 0)
    lax.fori_loop(0, len(FAR), wait_far, 0)

    def combine(g):
        rows = pl.ds(pl.multiple_of(g * 16, 16), 16)
        gathered = dot(kron[...], arrived[:, :, rows, :].reshape(wide, SIDE))
        pixels = sky[:, rows, :].reshape(CH * 16, SIDE)
        there = model[:, rows, :].reshape(CH * 16, SIDE)
        new = pixels - (totals * there - gathered) * scale
        new = new.reshape(CH // 2, 2, 16, SIDE)
        extended[:, rows, :SIDE] = new.reshape(CH, 16, SIDE).astype(BF)
        low = lax.broadcasted_iota(jnp.int32, (CH // 2, 16, 128), 2) < 64
        second = pltpu.roll(new[:, 1, :, :128].reshape(CH // 2 * 16, 128), 64, 1)
        pair = jnp.where(low, new[:, 0, :, :128], second.reshape(CH // 2, 16, 128))
        columns[:, rows, :] = pair.astype(BF)

    chunks = 4
    deep = SIDE // chunks

    def columns_copy(q):
        rows = pl.ds(pl.multiple_of(q * deep, deep), deep)
        return pltpu.make_async_remote_copy(
            src_ref=columns.at[:, rows, :],
            dst_ref=beside.at[:, rows, :],
            send_sem=columns_send.at[q],
            recv_sem=columns_recv.at[q],
            device_id={"fx": prev},
            device_id_type=pl.DeviceIdType.MESH,
        )

    def halo_copy(i):
        source = (extended.at[:, :HALO, :SIDE], columns.at[:, :HALO, :])[i]
        target = (extended.at[:, SIDE:, :SIDE], corner)[i]
        where = ({"fy": up}, {"fy": up, "fx": prev})[i]
        return pltpu.make_async_remote_copy(
            src_ref=source,
            dst_ref=target,
            send_sem=halo_send.at[i],
            recv_sem=halo_recv.at[i],
            device_id=where,
            device_id_type=pl.DeviceIdType.MESH,
        )

    def make_chunk(q, carry):
        for i in range(deep // 16):
            combine(q * (deep // 16) + i)
        columns_copy(q).start()

        @pl.when(q == 0)
        def _():
            for i in range(2):
                halo_copy(i).start()

        return carry

    lax.fori_loop(0, chunks, make_chunk, 0)

    def place(source, begin, end):
        for p in range(CH // 2):
            first = source[p]
            extended[2 * p, begin:end, SIDE:] = first
            extended[2 * p + 1, begin:end, SIDE:] = pltpu.roll(first.astype(F32), 64, 1).astype(BF)

    halo_copy(1).wait_recv()
    place(corner, SIDE, TALL)
    for q in range(chunks):
        columns_copy(q).wait_recv()
        place(beside.at[:, q * deep : (q + 1) * deep, :], q * deep, (q + 1) * deep)
    halo_copy(0).wait_recv()

    def finish_shares(k, carry):
        share_copy(peer(k), fx).wait_send()
        return carry

    def finish_near(j, carry):
        near_copy(j).wait_send()
        return carry

    def finish_far(j, carry):
        for r in range(2):
            far_copy(j, r).wait_send()
        relay_copy(j).wait_send()
        return carry

    lax.fori_loop(1, n_fx, finish_shares, 0)
    lax.fori_loop(0, len(NEAR), finish_near, 0)
    lax.fori_loop(0, len(FAR), finish_far, 0)
    for i in range(2):
        halo_copy(i).wait_send()
    for q in range(chunks):
        columns_copy(q).wait_send()


def passed(value, axes, to):
    sizes = [lax.axis_size(a) for a in axes]
    pairs = []
    for i in np.ndindex(*sizes):
        j = [(a + b) % n for a, b, n in zip(i, to, sizes)]
        pairs.append((int(np.ravel_multi_index(i, sizes)), int(np.ravel_multi_index(j, sizes))))
    return lax.ppermute(value, axes if len(axes) > 1 else axes[0], pairs)


def per_device(n_fy, n_fx, sky_image, vis_tiles, tile_dest, tile_chan, tile_count, thresholds):
    made = {name: jnp.asarray(table) for name, table in tables().items()}
    smem = pl.BlockSpec(memory_space=pltpu.SMEM)
    vmem = pl.BlockSpec(memory_space=pltpu.VMEM)
    anywhere = pl.BlockSpec(memory_space=pl.ANY)
    dma = pltpu.SemaphoreType.DMA
    tiles = vis_tiles.shape[0]
    extended = pl.pallas_call(
        functools.partial(exchange_kernel, n_fy, n_fx),
        out_shape=jax.ShapeDtypeStruct((CH, TALL, WIDE), BF),
        in_specs=[smem] * 3 + [vmem] * 3 + [anywhere] * 2,
        out_specs=vmem,
        scratch_shapes=[
            pltpu.VMEM((tiles, 2, SIDE, SIDE), BF),
            pltpu.VMEM((CH, SIDE, SIDE), F32),
            pltpu.VMEM((CH, SIDE, SIDE), F32),
            pltpu.VMEM((n_fx, 2, SIDE, SIDE), BF),
            pltpu.VMEM((n_fx, 2, SIDE, SIDE), BF),
            pltpu.VMEM((len(FAR), SIDE, SIDE), BF),
            pltpu.VMEM((2, 2 * SIDE, SIDE), BF),
            pltpu.VMEM((n_fx, 8, 128), F32),
            pltpu.VMEM((n_fx, 8, 128), F32),
            pltpu.VMEM((CH * 16, n_fx * 32), BF),
            pltpu.VMEM((CH // 2, SIDE, 128), BF),
            pltpu.VMEM((CH // 2, SIDE, 128), BF),
            pltpu.VMEM((CH // 2, HALO, 128), BF),
            dma((2,)),
            dma((n_fx, 2)),
            dma((n_fx, 2)),
            dma((len(FAR),)),
            dma((len(FAR),)),
            dma((n_fx,)),
            dma((n_fx,)),
            dma((2,)),
            dma((2,)),
            dma((4,)),
            dma((4,)),
        ],
        compiler_params=pltpu.CompilerParams(
            collective_id=0, has_side_effects=True, vmem_limit_bytes=58 * 1024 * 1024
        ),
    )(
        tile_dest.reshape(tiles),
        tile_chan,
        tile_count,
        made["fourier"],
        made["back"],
        made["excess"],
        sky_image,
        vis_tiles,
    )
    rows, columns = made["rows"], made["columns"]
    row_sec = jnp.einsum("bkn,cnx->bckx", rows, extended, preferred_element_type=F32).astype(BF)
    coefficient = jnp.einsum("bcyx,bkx->bcyk", row_sec, columns, preferred_element_type=F32)
    limits = thresholds.astype(F32)
    shrunk = (coefficient - jnp.clip(coefficient, -limits, limits)).astype(BF)
    near_rows, far_rows = rows[:, :, :SIDE], rows[:, :, SIDE:]
    near_columns, far_columns = columns[:, :, :SIDE], columns[:, :, SIDE:]
    side = jnp.einsum("bcyk,bkx->bcyx", shrunk, far_columns, preferred_element_type=F32).astype(BF)
    right = jnp.einsum("bkn,bckx->cnx", rows, side, preferred_element_type=F32).astype(BF)
    from_left = passed(right[:, :SIDE], ("fx",), (1,)).astype(F32)
    from_corner = passed(right[:, SIDE:], ("fy", "fx"), (1, 1)).astype(F32)
    low = jnp.einsum("bkn,bckx->bcnx", far_rows, shrunk, preferred_element_type=F32).astype(BF)
    bottom = jnp.einsum("bcnk,bkx->cnx", low, near_columns, preferred_element_type=F32).astype(BF)
    from_above = passed(bottom, ("fy",), (1,)).astype(F32)
    col_sec = jnp.einsum(
        "bcyk,bkx->bcyx", shrunk, near_columns, preferred_element_type=F32
    ).astype(BF)
    cells = jnp.einsum("bkn,bckx->cnx", near_rows, col_sec, preferred_element_type=F32)
    left = jnp.pad(from_left, ((0, 0), (0, 0), (0, 128)))
    above = jnp.pad(from_above, ((0, 0), (0, SIDE - HALO), (0, 0)))
    corner = jnp.pad(from_corner, ((0, 0), (0, SIDE - HALO), (0, 128)))
    summed = cells + left + above + corner
    return jnp.maximum(summed * (1.0 / BASES), 0.0)


def solution(mesh):
    in_specs = (
        P(None, "fy", "fx"),
        P(("fy", "fx"), None, None, None),
        P(("fy", "fx"), None),
        P(("fy", "fx")),
        P(("fy", "fx")),
        P(None, None, "fy", "fx"),
    )
    out_specs = P(None, "fy", "fx")
    return jax.shard_map(
        functools.partial(per_device, mesh.shape["fy"], mesh.shape["fx"]),
        mesh=mesh,
        in_specs=in_specs,
        out_specs=out_specs,
        check_vma=False,
    )
```

```python
import functools
import math

import jax
import jax.numpy as jnp
import ml_dtypes
import numpy as np
from jax import lax
from jax.experimental import pallas as pl
from jax.experimental.layout import Layout, with_layout_constraint
from jax.experimental.pallas import tpu as pltpu
from jax.sharding import PartitionSpec as P

daubechies_taps = [
    [0.7071067811865476, 0.7071067811865476],
    [0.48296291314469025, 0.836516303737469, 0.22414386804185735, -0.12940952255092145],
    [
        0.3326705529509569,
        0.8068915093133388,
        0.4598775021193313,
        -0.13501102001039084,
        -0.08544127388224149,
        0.035226291882100656,
    ],
    [
        0.23037781330885523,
        0.7148465705525415,
        0.6308807679295904,
        -0.02798376941698385,
        -0.18703481171888114,
        0.030841381835986965,
        0.032883011666982945,
        -0.010597401784997278,
    ],
    [
        0.160102397974125,
        0.6038292697974729,
        0.7243085284385744,
        0.13842814590110342,
        -0.24229488706619015,
        -0.03224486958502952,
        0.07757149384006515,
        -0.006241490213011705,
        -0.012580751999015526,
        0.003335725285001549,
    ],
    [
        0.11154074335008017,
        0.4946238903983854,
        0.7511339080215775,
        0.3152503517092432,
        -0.22626469396516913,
        -0.12976686756709563,
        0.09750160558707936,
        0.02752286553001629,
        -0.031582039318031156,
        0.0005538422009938016,
        0.004777257511010651,
        -0.00107730108499558,
    ],
    [
        0.07785205408506236,
        0.39653931948230575,
        0.7291320908465551,
        0.4697822874053586,
        -0.14390600392910627,
        -0.22403618499416572,
        0.07130921926705004,
        0.0806126091510659,
        -0.03802993693503463,
        -0.01657454163101562,
        0.012550998556013784,
        0.00042957797300470274,
        -0.0018016407039998328,
        0.0003537138000010399,
    ],
    [
        0.05441584224308161,
        0.3128715909144659,
        0.6756307362980128,
        0.5853546836548691,
        -0.015829105256023893,
        -0.2840155429624281,
        0.00047248457399797254,
        0.128747426620186,
        -0.01736930100202211,
        -0.04408825393106472,
        0.013981027917015516,
        0.008746094047015655,
        -0.00487035299301066,
        -0.0003917403729959771,
        0.0006754494059985568,
        -0.00011747678400228192,
    ],
]


SIDE = 256
CH = 8
BASES = 8
HALO = 48
BF = jnp.bfloat16
F32 = jnp.float32
WIDE = SIDE + 128
TALL = SIDE + HALO


def rounded(table):
    return np.asarray(table, np.float32).astype(ml_dtypes.bfloat16)


def composite_tables():
    full = np.zeros((BASES, SIDE, SIDE + HALO))
    for degree in range(1, 9):
        taps = np.array(daubechies_taps[degree - 1])
        taps = taps * math.sqrt(2.0) / np.sum(taps)
        length = 2 * degree
        low = np.zeros(16)
        high = np.zeros(16)
        low[:length] = taps
        high[:length] = [(-1.0) ** j * taps[length - 1 - j] for j in range(length)]
        low = rounded(low).astype(np.float64)
        high = rounded(high).astype(np.float64)
        level_low = np.zeros((144, SIDE + HALO))
        level_high = np.zeros((128, SIDE + HALO))
        for k in range(144):
            level_low[k, 2 * k : 2 * k + 16] = low[: min(16, SIDE + HALO - 2 * k)]
        for k in range(128):
            level_high[k, 2 * k : 2 * k + 16] = high
        second = np.zeros((128, 144))
        for m in range(64):
            second[m, 2 * m : 2 * m + 16] = low
            second[64 + m, 2 * m : 2 * m + 16] = high
        full[degree - 1, :128] = second @ level_low
        full[degree - 1, 128:] = level_high
    return rounded(full).astype(np.float32)


@functools.lru_cache(maxsize=1)
def tables():
    full = composite_tables()
    wide = np.concatenate([full, np.zeros((BASES, SIDE, 128 - HALO), np.float32)], axis=2)
    out = {"rows": full, "columns": wide}
    grid = np.arange(SIDE)[:, None] * np.arange(SIDE)[None, :] % SIDE
    angle = grid * (2.0 * math.pi / SIDE)
    cosine = rounded(np.cos(angle) / math.sqrt(SIDE)).astype(np.float64)
    sine = rounded(np.sin(angle) / math.sqrt(SIDE)).astype(np.float64)
    out["fourier"] = np.block([[cosine, sine], [-sine, cosine]])
    out["back"] = np.concatenate([cosine, -sine], axis=1)
    out["excess"] = cosine @ cosine + sine @ sine - np.eye(SIDE)
    return {name: rounded(table) for name, table in out.items()}


NEAR = ((1, 0), (0, 1), (3, 0), (0, 3), (1, 1), (3, 3), (1, 3), (3, 1))
FAR = ((2, 0), (0, 2), (2, 1), (2, 3), (1, 2), (3, 2), (2, 2))
THROUGH = (
    ((1, 0), (3, 0)),
    ((0, 1), (0, 3)),
    ((1, 1), (3, 1)),
    ((1, 3), (3, 3)),
    ((1, 1), (1, 3)),
    ((3, 1), (3, 3)),
    ((1, 1), (3, 3)),
)


def choose(j, values):
    out = jnp.int32(values[0])
    for i, value in enumerate(values):
        out = jnp.where(j == i, jnp.int32(value), out)
    return out


def dot(a, b):
    return jnp.dot(a, b, preferred_element_type=F32)


def exchange_kernel(
    n_fy,
    n_fx,
    dest_ref,
    chan_ref,
    count_ref,
    fourier,
    back,
    excess,
    sky_hbm,
    vis_hbm,
    extended,
    vis,
    sky,
    model,
    sending,
    arrived,
    relay,
    half,
    share_ref,
    shares,
    kron,
    columns,
    beside,
    corner,
    load_sem,
    tile_send,
    tile_recv,
    relay_send,
    relay_recv,
    share_send,
    share_recv,
    halo_send,
    halo_recv,
    columns_send,
    columns_recv,
):
    fy = lax.axis_index("fy")
    fx = lax.axis_index("fx")
    n_z = 4
    n_x = n_fx // n_z
    my_x, my_z = fx // n_z, fx % n_z

    def at(dx, dz):
        return (my_x + dx) % n_x * n_z + (my_z + dz) % n_z

    def peer(k):
        return at(k // n_z, k % n_z)

    load_vis = pltpu.make_async_copy(vis_hbm, vis, load_sem.at[0])
    load_sky = pltpu.make_async_copy(sky_hbm, sky, load_sem.at[1])
    load_vis.start()
    load_sky.start()

    barrier = pltpu.get_barrier_semaphore()

    def greet(k, carry):
        pl.semaphore_signal(
            barrier, inc=1, device_id={"fx": peer(k)}, device_id_type=pl.DeviceIdType.MESH
        )
        return carry

    lax.fori_loop(1, n_fx, greet, 0)
    up, down = (fy + n_fy - 1) % n_fy, (fy + 1) % n_fy
    prev, nxt = (fx + n_fx - 1) % n_fx, (fx + 1) % n_fx
    for where in ({"fy": up}, {"fy": down}, {"fy": up, "fx": prev}, {"fy": down, "fx": nxt}):
        pl.semaphore_signal(barrier, inc=1, device_id=where, device_id_type=pl.DeviceIdType.MESH)
    pl.semaphore_wait(barrier, n_fx - 1 + 4)

    def share_copy(to, source):
        return pltpu.make_async_remote_copy(
            src_ref=share_ref.at[to],
            dst_ref=shares.at[source],
            send_sem=share_send.at[to],
            recv_sem=share_recv.at[source],
            device_id={"fx": to},
            device_id_type=pl.DeviceIdType.MESH,
        )

    def near(j):
        return choose(j, [o[0] for o in NEAR]), choose(j, [o[1] for o in NEAR])

    def far(j):
        return choose(j, [o[0] for o in FAR]), choose(j, [o[1] for o in FAR])

    def through(j, r):
        return (
            choose(j, [o[r][0] for o in THROUGH]),
            choose(j, [o[r][1] for o in THROUGH]),
        )

    def near_copy(j, r):
        return pltpu.make_async_remote_copy(
            src_ref=sending.at[len(FAR) + j, r],
            dst_ref=arrived.at[fx, r],
            send_sem=tile_send.at[len(FAR) + j, r],
            recv_sem=tile_recv.at[fx, r],
            device_id={"fx": at(*near(j))},
            device_id_type=pl.DeviceIdType.MESH,
        )

    def far_copy(j, r):
        return pltpu.make_async_remote_copy(
            src_ref=sending.at[j, r],
            dst_ref=relay.at[j, r],
            send_sem=tile_send.at[j, r],
            recv_sem=relay_recv.at[j, r],
            device_id={"fx": at(*through(j, r))},
            device_id_type=pl.DeviceIdType.MESH,
        )

    def relay_copy(j, r):
        end, mid = far(j), through(j, r)
        source = at(4 - mid[0], 4 - mid[1])
        return pltpu.make_async_remote_copy(
            src_ref=relay.at[j, r],
            dst_ref=arrived.at[source, r],
            send_sem=relay_send.at[j, r],
            recv_sem=tile_recv.at[source, r],
            device_id={"fx": at(end[0] + 4 - mid[0], end[1] + 4 - mid[1])},
            device_id_type=pl.DeviceIdType.MESH,
        )

    def arrival(source, r):
        return pltpu.make_async_remote_copy(
            src_ref=arrived.at[source, r],
            dst_ref=arrived.at[source, r],
            send_sem=tile_send.at[0, 0],
            recv_sem=tile_recv.at[source, r],
            device_id={"fx": source},
            device_id_type=pl.DeviceIdType.MESH,
        )

    tiles = vis_hbm.shape[0]
    row = lax.broadcasted_iota(jnp.int32, (8, 128), 0)
    lane = lax.broadcasted_iota(jnp.int32, (8, 128), 1)

    def slots_for(to):
        found = jnp.int32(0)
        picked = [(jnp.int32(0), jnp.int32(0), jnp.int32(0))] * 2
        for i in range(tiles):
            match = dest_ref[i] == to
            for r in range(2):
                here = match & (found == r)
                new = (jnp.int32(i), count_ref[i], chan_ref[i])
                picked[r] = tuple(jnp.where(here, a, b) for a, b in zip(new, picked[r]))
            found = found + jnp.where(match, 1, 0)
        return [(tile, count.astype(F32) * (1.0 / 64.0), chan) for tile, count, chan in picked]

    def share_rows(slots):
        total = jnp.zeros((8, 128), F32)
        for r, (_, weight, chan) in enumerate(slots):
            total = total + jnp.where((row == r) & (lane == chan), weight, 0.0)
        return total

    load_vis.wait()

    def planes(slots):
        for i, (t, _, _) in enumerate(slots):
            spectrum = jnp.concatenate([vis[t, 0], vis[t, 1]], axis=1)
            for part in range(2):
                half[i, part * SIDE : (part + 1) * SIDE] = dot(
                    spectrum, fourier[:, part * SIDE : (part + 1) * SIDE]
                ).astype(BF)
        return [(dot(back[...], half[i]) * slots[i][1]).astype(BF) for i in range(2)]

    def prepare(to, place):
        slots = slots_for(to)
        share_ref[to] = share_rows(slots)
        share_copy(to, fx).start()
        sending[place, 0], sending[place, 1] = planes(slots)

    def send_far(j, carry):
        prepare(at(*far(j)), j)
        far_copy(j, 0).start()
        far_copy(j, 1).start()
        return carry

    lax.fori_loop(0, len(FAR), send_far, 0)

    def send_near(j, carry):
        prepare(at(*near(j)), len(FAR) + j)
        near_copy(j, 0).start()
        near_copy(j, 1).start()

        @pl.when(j >= 1)
        def _():
            for r in range(2):
                far_copy(j - 1, r).wait_recv()
                relay_copy(j - 1, r).start()

        return carry

    lax.fori_loop(0, len(NEAR), send_near, 0)
    own = slots_for(fx)
    shares[fx] = share_rows(own)
    arrived[fx, 0], arrived[fx, 1] = planes(own)

    load_sky.wait()

    def there_and_back(c, carry):
        pixels = sky[c].astype(BF)
        once = pixels.astype(F32) + dot(excess[...], pixels)
        model[c] = once + dot(once.astype(BF), excess[...])
        return carry

    lax.fori_loop(0, CH, there_and_back, 0)

    def wait_share(k, carry):
        share_copy(peer(k), peer(k)).wait_recv()
        return carry

    lax.fori_loop(1, n_fx, wait_share, 0)
    slots = n_fx * 2
    wide = slots * 16
    all_shares = shares[...].reshape(n_fx * 8, 128)
    members = jnp.where(all_shares > 0, 1.0, 0.0).astype(BF)
    spread = (
        lax.broadcasted_iota(jnp.int32, (CH * 16, 128), 0) // 16
        == lax.broadcasted_iota(jnp.int32, (CH * 16, 128), 1)
    )
    spread = jnp.where(spread, 1.0, 0.0).astype(BF)
    by_source = lax.dot_general(
        spread, members, (((1,), (1,)), ((), ())), preferred_element_type=F32
    ).astype(BF)
    weights = lax.dot_general(
        spread, all_shares.astype(BF), (((1,), (1,)), ((), ())), preferred_element_type=F32
    )
    totals = jnp.sum(weights, axis=1, keepdims=True)
    src_row = lax.broadcasted_iota(jnp.int32, (n_fx * 8, wide), 0)
    dst_col = lax.broadcasted_iota(jnp.int32, (n_fx * 8, wide), 1)
    widen = (src_row // 8 == dst_col // 32) & (src_row % 8 == dst_col // 16 % 2)
    widened = dot(by_source, jnp.where(widen, 1.0, 0.0).astype(BF))
    diagonal = (
        lax.broadcasted_iota(jnp.int32, (CH * 16, wide), 0) % 16
        == lax.broadcasted_iota(jnp.int32, (CH * 16, wide), 1) % 16
    )
    kron[...] = jnp.where(diagonal, widened, 0.0).astype(BF)
    scale = 1.0 / (1.0 + totals)

    def wait_tiles(k, carry):
        for r in range(2):
            arrival(peer(k), r).wait_recv()
        return carry

    lax.fori_loop(1, n_fx, wait_tiles, 0)

    def combine(g):
        rows = pl.ds(pl.multiple_of(g * 16, 16), 16)
        gathered = dot(kron[...], arrived[:, :, rows, :].reshape(wide, SIDE))
        pixels = sky[:, rows, :].reshape(CH * 16, SIDE)
        there = model[:, rows, :].reshape(CH * 16, SIDE)
        new = pixels - (totals * there - gathered) * scale
        new = new.reshape(CH // 2, 2, 16, SIDE)
        extended[:, rows, :SIDE] = new.reshape(CH, 16, SIDE).astype(BF)
        low = lax.broadcasted_iota(jnp.int32, (CH // 2, 16, 128), 2) < 64
        second = pltpu.roll(new[:, 1, :, :128].reshape(CH // 2 * 16, 128), 64, 1)
        pair = jnp.where(low, new[:, 0, :, :128], second.reshape(CH // 2, 16, 128))
        columns[:, rows, :] = pair.astype(BF)

    chunks = 4
    deep = SIDE // chunks

    def columns_copy(q):
        rows = pl.ds(pl.multiple_of(q * deep, deep), deep)
        return pltpu.make_async_remote_copy(
            src_ref=columns.at[:, rows, :],
            dst_ref=beside.at[:, rows, :],
            send_sem=columns_send.at[q],
            recv_sem=columns_recv.at[q],
            device_id={"fx": prev},
            device_id_type=pl.DeviceIdType.MESH,
        )

    def halo_copy(i):
        source = (extended.at[:, :HALO, :SIDE], columns.at[:, :HALO, :])[i]
        target = (extended.at[:, SIDE:, :SIDE], corner)[i]
        where = ({"fy": up}, {"fy": up, "fx": prev})[i]
        return pltpu.make_async_remote_copy(
            src_ref=source,
            dst_ref=target,
            send_sem=halo_send.at[i],
            recv_sem=halo_recv.at[i],
            device_id=where,
            device_id_type=pl.DeviceIdType.MESH,
        )

    def make_chunk(q, carry):
        for i in range(deep // 16):
            combine(q * (deep // 16) + i)
        columns_copy(q).start()

        @pl.when(q == 0)
        def _():
            for i in range(2):
                halo_copy(i).start()

        return carry

    lax.fori_loop(0, chunks, make_chunk, 0)

    def place(source, begin, end):
        for p in range(CH // 2):
            first = source[p]
            extended[2 * p, begin:end, SIDE:] = first
            extended[2 * p + 1, begin:end, SIDE:] = pltpu.roll(first.astype(F32), 64, 1).astype(BF)

    halo_copy(1).wait_recv()
    place(corner, SIDE, TALL)
    for q in range(chunks):
        columns_copy(q).wait_recv()
        place(beside.at[:, q * deep : (q + 1) * deep, :], q * deep, (q + 1) * deep)
    halo_copy(0).wait_recv()

    def finish_shares(k, carry):
        share_copy(peer(k), fx).wait_send()
        return carry

    def finish_near(j, carry):
        for r in range(2):
            near_copy(j, r).wait_send()
        return carry

    def finish_far(j, carry):
        for r in range(2):
            far_copy(j, r).wait_send()
            relay_copy(j, r).wait_send()
        return carry

    lax.fori_loop(1, n_fx, finish_shares, 0)
    lax.fori_loop(0, len(NEAR), finish_near, 0)
    lax.fori_loop(0, len(FAR), finish_far, 0)
    for i in range(2):
        halo_copy(i).wait_send()
    for q in range(chunks):
        columns_copy(q).wait_send()


def passed(value, axes, to):
    sizes = [lax.axis_size(a) for a in axes]
    pairs = []
    for i in np.ndindex(*sizes):
        j = [(a + b) % n for a, b, n in zip(i, to, sizes)]
        pairs.append((int(np.ravel_multi_index(i, sizes)), int(np.ravel_multi_index(j, sizes))))
    return lax.ppermute(value, axes if len(axes) > 1 else axes[0], pairs)


def per_device(n_fy, n_fx, sky_image, vis_tiles, tile_dest, tile_chan, tile_count, thresholds):
    made = {name: jnp.asarray(table) for name, table in tables().items()}
    smem = pl.BlockSpec(memory_space=pltpu.SMEM)
    vmem = pl.BlockSpec(memory_space=pltpu.VMEM)
    anywhere = pl.BlockSpec(memory_space=pl.ANY)
    dma = pltpu.SemaphoreType.DMA
    tiles = vis_tiles.shape[0]
    extended = pl.pallas_call(
        functools.partial(exchange_kernel, n_fy, n_fx),
        out_shape=jax.ShapeDtypeStruct((CH, TALL, WIDE), BF),
        in_specs=[smem] * 3 + [vmem] * 3 + [anywhere] * 2,
        out_specs=vmem,
        scratch_shapes=[
            pltpu.VMEM((tiles, 2, SIDE, SIDE), BF),
            pltpu.VMEM((CH, SIDE, SIDE), F32),
            pltpu.VMEM((CH, SIDE, SIDE), F32),
            pltpu.VMEM((n_fx, 2, SIDE, SIDE), BF),
            pltpu.VMEM((n_fx, 2, SIDE, SIDE), BF),
            pltpu.VMEM((len(FAR), 2, SIDE, SIDE), BF),
            pltpu.VMEM((2, 2 * SIDE, SIDE), BF),
            pltpu.VMEM((n_fx, 8, 128), F32),
            pltpu.VMEM((n_fx, 8, 128), F32),
            pltpu.VMEM((CH * 16, n_fx * 32), BF),
            pltpu.VMEM((CH // 2, SIDE, 128), BF),
            pltpu.VMEM((CH // 2, SIDE, 128), BF),
            pltpu.VMEM((CH // 2, HALO, 128), BF),
            dma((2,)),
            dma((n_fx, 2)),
            dma((n_fx, 2)),
            dma((len(FAR), 2)),
            dma((len(FAR), 2)),
            dma((n_fx,)),
            dma((n_fx,)),
            dma((2,)),
            dma((2,)),
            dma((4,)),
            dma((4,)),
        ],
        compiler_params=pltpu.CompilerParams(
            collective_id=0, has_side_effects=True, vmem_limit_bytes=58 * 1024 * 1024
        ),
    )(
        tile_dest.reshape(tiles),
        tile_chan,
        tile_count,
        made["fourier"],
        made["back"],
        made["excess"],
        sky_image,
        vis_tiles,
    )
    rows, columns = made["rows"], made["columns"]
    col_sec = jnp.einsum("cyx,bkx->bcyk", extended, columns, preferred_element_type=F32).astype(BF)
    coefficient = jnp.einsum("bjy,bcyk->bcjk", rows, col_sec, preferred_element_type=F32)
    coefficient = with_layout_constraint(coefficient, Layout(major_to_minor=(0, 1, 2, 3)))
    limits = thresholds.astype(F32)
    shrunk = (coefficient - jnp.clip(coefficient, -limits, limits)).astype(BF)
    row_sec = jnp.einsum("bjy,bcjk->bcyk", rows, shrunk, preferred_element_type=F32).astype(BF)
    cells = jnp.einsum("bcyk,bkx->cyx", row_sec, columns, preferred_element_type=F32)
    spill = cells.astype(BF)
    from_left = passed(spill[:, :SIDE, SIDE:TALL], ("fx",), (1,)).astype(F32)
    from_above = passed(spill[:, SIDE:, :SIDE], ("fy",), (1,)).astype(F32)
    from_corner = passed(spill[:, SIDE:, SIDE:TALL], ("fy", "fx"), (1, 1)).astype(F32)
    left = jnp.pad(from_left, ((0, 0), (0, 0), (0, SIDE - HALO)))
    above = jnp.pad(from_above, ((0, 0), (0, SIDE - HALO), (0, 0)))
    corner = jnp.pad(from_corner, ((0, 0), (0, SIDE - HALO), (0, SIDE - HALO)))
    summed = cells[:, :SIDE, :SIDE] + left + above + corner
    return jnp.maximum(summed * (1.0 / BASES), 0.0)


def solution(mesh):
    in_specs = (
        P(None, "fy", "fx"),
        P(("fy", "fx"), None, None, None),
        P(("fy", "fx"), None),
        P(("fy", "fx")),
        P(("fy", "fx")),
        P(None, None, "fy", "fx"),
    )
    out_specs = P(None, "fy", "fx")
    return jax.shard_map(
        functools.partial(per_device, mesh.shape["fy"], mesh.shape["fx"]),
        mesh=mesh,
        in_specs=in_specs,
        out_specs=out_specs,
        check_vma=False,
    )
```

```python
import functools
import math

import jax
import jax.numpy as jnp
import ml_dtypes
import numpy as np
from jax import lax
from jax.experimental import pallas as pl
from jax.experimental.pallas import tpu as pltpu
from jax.sharding import PartitionSpec as P

daubechies_taps = [
    [0.7071067811865476, 0.7071067811865476],
    [0.48296291314469025, 0.836516303737469, 0.22414386804185735, -0.12940952255092145],
    [
        0.3326705529509569,
        0.8068915093133388,
        0.4598775021193313,
        -0.13501102001039084,
        -0.08544127388224149,
        0.035226291882100656,
    ],
    [
        0.23037781330885523,
        0.7148465705525415,
        0.6308807679295904,
        -0.02798376941698385,
        -0.18703481171888114,
        0.030841381835986965,
        0.032883011666982945,
        -0.010597401784997278,
    ],
    [
        0.160102397974125,
        0.6038292697974729,
        0.7243085284385744,
        0.13842814590110342,
        -0.24229488706619015,
        -0.03224486958502952,
        0.07757149384006515,
        -0.006241490213011705,
        -0.012580751999015526,
        0.003335725285001549,
    ],
    [
        0.11154074335008017,
        0.4946238903983854,
        0.7511339080215775,
        0.3152503517092432,
        -0.22626469396516913,
        -0.12976686756709563,
        0.09750160558707936,
        0.02752286553001629,
        -0.031582039318031156,
        0.0005538422009938016,
        0.004777257511010651,
        -0.00107730108499558,
    ],
    [
        0.07785205408506236,
        0.39653931948230575,
        0.7291320908465551,
        0.4697822874053586,
        -0.14390600392910627,
        -0.22403618499416572,
        0.07130921926705004,
        0.0806126091510659,
        -0.03802993693503463,
        -0.01657454163101562,
        0.012550998556013784,
        0.00042957797300470274,
        -0.0018016407039998328,
        0.0003537138000010399,
    ],
    [
        0.05441584224308161,
        0.3128715909144659,
        0.6756307362980128,
        0.5853546836548691,
        -0.015829105256023893,
        -0.2840155429624281,
        0.00047248457399797254,
        0.128747426620186,
        -0.01736930100202211,
        -0.04408825393106472,
        0.013981027917015516,
        0.008746094047015655,
        -0.00487035299301066,
        -0.0003917403729959771,
        0.0006754494059985568,
        -0.00011747678400228192,
    ],
]


SIDE = 256
CH = 8
BASES = 8
HALO = 48
BF = jnp.bfloat16
F32 = jnp.float32
WIDE = SIDE + 128
TALL = SIDE + HALO


def rounded(table):
    return np.asarray(table, np.float32).astype(ml_dtypes.bfloat16)


def composite_tables():
    full = np.zeros((BASES, SIDE, SIDE + HALO))
    for degree in range(1, 9):
        taps = np.array(daubechies_taps[degree - 1])
        taps = taps * math.sqrt(2.0) / np.sum(taps)
        length = 2 * degree
        low = np.zeros(16)
        high = np.zeros(16)
        low[:length] = taps
        high[:length] = [(-1.0) ** j * taps[length - 1 - j] for j in range(length)]
        low = rounded(low).astype(np.float64)
        high = rounded(high).astype(np.float64)
        level_low = np.zeros((144, SIDE + HALO))
        level_high = np.zeros((128, SIDE + HALO))
        for k in range(144):
            level_low[k, 2 * k : 2 * k + 16] = low[: min(16, SIDE + HALO - 2 * k)]
        for k in range(128):
            level_high[k, 2 * k : 2 * k + 16] = high
        second = np.zeros((128, 144))
        for m in range(64):
            second[m, 2 * m : 2 * m + 16] = low
            second[64 + m, 2 * m : 2 * m + 16] = high
        full[degree - 1, :128] = second @ level_low
        full[degree - 1, 128:] = level_high
    return rounded(full).astype(np.float32)


@functools.lru_cache(maxsize=1)
def tables():
    full = composite_tables()
    wide = np.concatenate([full, np.zeros((BASES, SIDE, 128 - HALO), np.float32)], axis=2)
    out = {"rows": full, "columns": wide}
    grid = np.arange(SIDE)[:, None] * np.arange(SIDE)[None, :] % SIDE
    angle = grid * (2.0 * math.pi / SIDE)
    cosine = rounded(np.cos(angle) / math.sqrt(SIDE)).astype(np.float64)
    sine = rounded(np.sin(angle) / math.sqrt(SIDE)).astype(np.float64)
    out["fourier"] = np.block([[cosine, sine], [-sine, cosine]])
    out["back"] = np.concatenate([cosine, -sine], axis=1)
    out["excess"] = cosine @ cosine + sine @ sine - np.eye(SIDE)
    return {name: rounded(table) for name, table in out.items()}


PLACES = (
    (2, 2),
    (2, 1),
    (1, 2),
    (2, 3),
    (3, 2),
    (1, 1),
    (3, 3),
    (1, 3),
    (3, 1),
    (2, 0),
    (0, 2),
    (1, 0),
    (0, 1),
    (3, 0),
    (0, 3),
)


def path(place, r):
    ups = {0: (), 1: (1,), 2: (1, 1) if r == 0 else (3, 3), 3: (3,)}
    along_x = [(d, 0) for d in ups[place[0]]]
    along_z = [(0, d) for d in ups[place[1]]]
    return along_x + along_z if r == 0 else along_z + along_x


PATHS = [[path(place, r) for place in PLACES] for r in range(2)]
HOPS = [sum(len(p) > h for p in PATHS[0]) for h in range(5)]
BASE = [0] + [2 * sum(HOPS[1:h]) for h in range(1, 5)]
LAG = 3


def choose(j, values):
    out = jnp.int32(values[0])
    for i, value in enumerate(values):
        out = jnp.where(j == i, jnp.int32(value), out)
    return out


def dot(a, b):
    return jnp.dot(a, b, preferred_element_type=F32)


def exchange_kernel(
    n_fy,
    n_fx,
    dest_ref,
    chan_ref,
    count_ref,
    fourier,
    back,
    excess,
    sky_hbm,
    vis_hbm,
    extended,
    vis,
    sky,
    model,
    sending,
    arrived,
    relay,
    half,
    share_ref,
    shares,
    kron,
    columns,
    beside,
    corner,
    load_sem,
    tile_send,
    tile_recv,
    relay_send,
    relay_recv,
    share_send,
    share_recv,
    halo_send,
    halo_recv,
    columns_send,
    columns_recv,
):
    fy = lax.axis_index("fy")
    fx = lax.axis_index("fx")
    n_z = 4
    n_x = n_fx // n_z
    my_x, my_z = fx // n_z, fx % n_z

    def at(dx, dz):
        return (my_x + dx) % n_x * n_z + (my_z + dz) % n_z

    def peer(k):
        return at(k // n_z, k % n_z)

    load_vis = pltpu.make_async_copy(vis_hbm, vis, load_sem.at[0])
    load_sky = pltpu.make_async_copy(sky_hbm, sky, load_sem.at[1])
    load_vis.start()
    load_sky.start()

    barrier = pltpu.get_barrier_semaphore()

    def greet(k, carry):
        pl.semaphore_signal(
            barrier, inc=1, device_id={"fx": peer(k)}, device_id_type=pl.DeviceIdType.MESH
        )
        return carry

    lax.fori_loop(1, n_fx, greet, 0)
    up, down = (fy + n_fy - 1) % n_fy, (fy + 1) % n_fy
    prev, nxt = (fx + n_fx - 1) % n_fx, (fx + 1) % n_fx
    for where in ({"fy": up}, {"fy": down}, {"fy": up, "fx": prev}, {"fy": down, "fx": nxt}):
        pl.semaphore_signal(barrier, inc=1, device_id=where, device_id_type=pl.DeviceIdType.MESH)
    pl.semaphore_wait(barrier, n_fx - 1 + 4)

    def share_copy(to, source):
        return pltpu.make_async_remote_copy(
            src_ref=share_ref.at[to],
            dst_ref=shares.at[source],
            send_sem=share_send.at[to],
            recv_sem=share_recv.at[source],
            device_id={"fx": to},
            device_id_type=pl.DeviceIdType.MESH,
        )

    def hop_copy(h, i, r, last):
        paths = PATHS[r][: HOPS[h]]
        so_far = [[sum(step[a] for step in p[:h]) % 4 for p in paths] for a in range(2)]
        source = at(4 - choose(i, so_far[0]), 4 - choose(i, so_far[1]))
        to = at(choose(i, [p[h][0] for p in paths]), choose(i, [p[h][1] for p in paths]))
        own = i * 2 + r
        return pltpu.make_async_remote_copy(
            src_ref=sending.at[i, r] if h == 0 else relay.at[BASE[h] + own],
            dst_ref=arrived.at[source, r] if last else relay.at[BASE[h + 1] + own],
            send_sem=tile_send.at[own] if h == 0 else relay_send.at[BASE[h] + own],
            recv_sem=tile_recv.at[source, r] if last else relay_recv.at[BASE[h + 1] + own],
            device_id={"fx": to},
            device_id_type=pl.DeviceIdType.MESH,
        )

    def hop_start(h, i):
        for r in range(2):
            if h > 0:
                slot = BASE[h] + i * 2 + r
                pltpu.make_async_remote_copy(
                    src_ref=relay.at[slot],
                    dst_ref=relay.at[slot],
                    send_sem=relay_send.at[slot],
                    recv_sem=relay_recv.at[slot],
                    device_id={"fx": at(1, 0)},
                    device_id_type=pl.DeviceIdType.MESH,
                ).wait_recv()
            if HOPS[h + 1] == 0:
                hop_copy(h, i, r, True).start()
            else:

                @pl.when(i >= HOPS[h + 1])
                def _():
                    hop_copy(h, i, r, True).start()

                @pl.when(i < HOPS[h + 1])
                def _():
                    hop_copy(h, i, r, False).start()

    def arrival(source, r):
        return pltpu.make_async_remote_copy(
            src_ref=arrived.at[source, r],
            dst_ref=arrived.at[source, r],
            send_sem=tile_send.at[0],
            recv_sem=tile_recv.at[source, r],
            device_id={"fx": source},
            device_id_type=pl.DeviceIdType.MESH,
        )

    tiles = vis_hbm.shape[0]
    row = lax.broadcasted_iota(jnp.int32, (8, 128), 0)
    lane = lax.broadcasted_iota(jnp.int32, (8, 128), 1)

    def slots_for(to):
        found = jnp.int32(0)
        picked = [(jnp.int32(0), jnp.int32(0), jnp.int32(0))] * 2
        for i in range(tiles):
            match = dest_ref[i] == to
            for r in range(2):
                here = match & (found == r)
                new = (jnp.int32(i), count_ref[i], chan_ref[i])
                picked[r] = tuple(jnp.where(here, a, b) for a, b in zip(new, picked[r]))
            found = found + jnp.where(match, 1, 0)
        return [(tile, count.astype(F32) * (1.0 / 64.0), chan) for tile, count, chan in picked]

    def share_rows(slots):
        total = jnp.zeros((8, 128), F32)
        for r, (_, weight, chan) in enumerate(slots):
            total = total + jnp.where((row == r) & (lane == chan), weight, 0.0)
        return total

    load_vis.wait()

    def planes(slots):
        for i, (t, _, _) in enumerate(slots):
            spectrum = jnp.concatenate([vis[t, 0], vis[t, 1]], axis=1)
            for part in range(2):
                half[i, part * SIDE : (part + 1) * SIDE] = dot(
                    spectrum, fourier[:, part * SIDE : (part + 1) * SIDE]
                ).astype(BF)
        return [(dot(back[...], half[i]) * slots[i][1]).astype(BF) for i in range(2)]

    def prepare(to, place):
        slots = slots_for(to)
        share_ref[to] = share_rows(slots)
        share_copy(to, fx).start()
        sending[place, 0], sending[place, 1] = planes(slots)

    def send_tiles(i, carry):
        prepare(at(choose(i, [p[0] for p in PLACES]), choose(i, [p[1] for p in PLACES])), i)
        hop_start(0, i)
        for h in range(1, 4):
            before = i - h * LAG

            @pl.when((before >= 0) & (before < HOPS[h]))
            def _():
                hop_start(h, before)

        return carry

    assert all(HOPS[h] + h * LAG <= len(PLACES) for h in range(4))
    lax.fori_loop(0, len(PLACES), send_tiles, 0)
    own = slots_for(fx)
    shares[fx] = share_rows(own)
    arrived[fx, 0], arrived[fx, 1] = planes(own)

    load_sky.wait()

    def there_and_back(c, carry):
        pixels = sky[c].astype(BF)
        once = pixels.astype(F32) + dot(excess[...], pixels)
        model[c] = once + dot(once.astype(BF), excess[...])
        return carry

    lax.fori_loop(0, CH, there_and_back, 0)

    def wait_share(k, carry):
        share_copy(peer(k), peer(k)).wait_recv()
        return carry

    lax.fori_loop(1, n_fx, wait_share, 0)
    slots = n_fx * 2
    wide = slots * 16
    all_shares = shares[...].reshape(n_fx * 8, 128)
    members = jnp.where(all_shares > 0, 1.0, 0.0).astype(BF)
    spread = (
        lax.broadcasted_iota(jnp.int32, (CH * 16, 128), 0) // 16
        == lax.broadcasted_iota(jnp.int32, (CH * 16, 128), 1)
    )
    spread = jnp.where(spread, 1.0, 0.0).astype(BF)
    by_source = lax.dot_general(
        spread, members, (((1,), (1,)), ((), ())), preferred_element_type=F32
    ).astype(BF)
    weights = lax.dot_general(
        spread, all_shares.astype(BF), (((1,), (1,)), ((), ())), preferred_element_type=F32
    )
    totals = jnp.sum(weights, axis=1, keepdims=True)
    src_row = lax.broadcasted_iota(jnp.int32, (n_fx * 8, wide), 0)
    dst_col = lax.broadcasted_iota(jnp.int32, (n_fx * 8, wide), 1)
    widen = (src_row // 8 == dst_col // 32) & (src_row % 8 == dst_col // 16 % 2)
    widened = dot(by_source, jnp.where(widen, 1.0, 0.0).astype(BF))
    diagonal = (
        lax.broadcasted_iota(jnp.int32, (CH * 16, wide), 0) % 16
        == lax.broadcasted_iota(jnp.int32, (CH * 16, wide), 1) % 16
    )
    kron[...] = jnp.where(diagonal, widened, 0.0).astype(BF)
    scale = 1.0 / (1.0 + totals)

    def wait_tiles(k, carry):
        for r in range(2):
            arrival(peer(k), r).wait_recv()
        return carry

    lax.fori_loop(1, n_fx, wait_tiles, 0)

    def combine(g):
        rows = pl.ds(pl.multiple_of(g * 16, 16), 16)
        gathered = dot(kron[...], arrived[:, :, rows, :].reshape(wide, SIDE))
        pixels = sky[:, rows, :].reshape(CH * 16, SIDE)
        there = model[:, rows, :].reshape(CH * 16, SIDE)
        new = pixels - (totals * there - gathered) * scale
        new = new.reshape(CH // 2, 2, 16, SIDE)
        extended[:, rows, :SIDE] = new.reshape(CH, 16, SIDE).astype(BF)
        low = lax.broadcasted_iota(jnp.int32, (CH // 2, 16, 128), 2) < 64
        second = pltpu.roll(new[:, 1, :, :128].reshape(CH // 2 * 16, 128), 64, 1)
        pair = jnp.where(low, new[:, 0, :, :128], second.reshape(CH // 2, 16, 128))
        columns[:, rows, :] = pair.astype(BF)

    chunks = 4
    deep = SIDE // chunks

    def columns_copy(q):
        rows = pl.ds(pl.multiple_of(q * deep, deep), deep)
        return pltpu.make_async_remote_copy(
            src_ref=columns.at[:, rows, :],
            dst_ref=beside.at[:, rows, :],
            send_sem=columns_send.at[q],
            recv_sem=columns_recv.at[q],
            device_id={"fx": prev},
            device_id_type=pl.DeviceIdType.MESH,
        )

    def halo_copy(i):
        source = (extended.at[:, :HALO, :SIDE], columns.at[:, :HALO, :])[i]
        target = (extended.at[:, SIDE:, :SIDE], corner)[i]
        where = ({"fy": up}, {"fy": up, "fx": prev})[i]
        return pltpu.make_async_remote_copy(
            src_ref=source,
            dst_ref=target,
            send_sem=halo_send.at[i],
            recv_sem=halo_recv.at[i],
            device_id=where,
            device_id_type=pl.DeviceIdType.MESH,
        )

    def make_chunk(q, carry):
        for i in range(deep // 16):
            combine(q * (deep // 16) + i)
        columns_copy(q).start()

        @pl.when(q == 0)
        def _():
            for i in range(2):
                halo_copy(i).start()

        return carry

    lax.fori_loop(0, chunks, make_chunk, 0)

    def place(source, begin, end):
        for p in range(CH // 2):
            first = source[p]
            extended[2 * p, begin:end, SIDE:] = first
            extended[2 * p + 1, begin:end, SIDE:] = pltpu.roll(first.astype(F32), 64, 1).astype(BF)

    halo_copy(1).wait_recv()
    place(corner, SIDE, TALL)
    for q in range(chunks):
        columns_copy(q).wait_recv()
        place(beside.at[:, q * deep : (q + 1) * deep, :], q * deep, (q + 1) * deep)
    halo_copy(0).wait_recv()

    def finish_shares(k, carry):
        share_copy(peer(k), fx).wait_send()
        return carry

    def finish_hops(h, i, carry):
        for r in range(2):
            hop_copy(h, i, r, True).wait_send()
        return carry

    lax.fori_loop(1, n_fx, finish_shares, 0)
    for h in range(4):
        lax.fori_loop(0, HOPS[h], functools.partial(finish_hops, h), 0)
    for i in range(2):
        halo_copy(i).wait_send()
    for q in range(chunks):
        columns_copy(q).wait_send()


def passed(value, axes, to):
    sizes = [lax.axis_size(a) for a in axes]
    pairs = []
    for i in np.ndindex(*sizes):
        j = [(a + b) % n for a, b, n in zip(i, to, sizes)]
        pairs.append((int(np.ravel_multi_index(i, sizes)), int(np.ravel_multi_index(j, sizes))))
    return lax.ppermute(value, axes if len(axes) > 1 else axes[0], pairs)


def per_device(n_fy, n_fx, sky_image, vis_tiles, tile_dest, tile_chan, tile_count, thresholds):
    made = {name: jnp.asarray(table) for name, table in tables().items()}
    smem = pl.BlockSpec(memory_space=pltpu.SMEM)
    vmem = pl.BlockSpec(memory_space=pltpu.VMEM)
    anywhere = pl.BlockSpec(memory_space=pl.ANY)
    dma = pltpu.SemaphoreType.DMA
    tiles = vis_tiles.shape[0]
    extended = pl.pallas_call(
        functools.partial(exchange_kernel, n_fy, n_fx),
        out_shape=jax.ShapeDtypeStruct((CH, TALL, WIDE), BF),
        in_specs=[smem] * 3 + [vmem] * 3 + [anywhere] * 2,
        out_specs=vmem,
        scratch_shapes=[
            pltpu.VMEM((tiles, 2, SIDE, SIDE), BF),
            pltpu.VMEM((CH, SIDE, SIDE), F32),
            pltpu.VMEM((CH, SIDE, SIDE), F32),
            pltpu.VMEM((n_fx, 2, SIDE, SIDE), BF),
            pltpu.VMEM((n_fx, 2, SIDE, SIDE), BF),
            pltpu.VMEM((BASE[4], SIDE, SIDE), BF),
            pltpu.VMEM((2, 2 * SIDE, SIDE), BF),
            pltpu.VMEM((n_fx, 8, 128), F32),
            pltpu.VMEM((n_fx, 8, 128), F32),
            pltpu.VMEM((CH * 16, n_fx * 32), BF),
            pltpu.VMEM((CH // 2, SIDE, 128), BF),
            pltpu.VMEM((CH // 2, SIDE, 128), BF),
            pltpu.VMEM((CH // 2, HALO, 128), BF),
            dma((2,)),
            dma((2 * len(PLACES),)),
            dma((n_fx, 2)),
            dma((BASE[4],)),
            dma((BASE[4],)),
            dma((n_fx,)),
            dma((n_fx,)),
            dma((2,)),
            dma((2,)),
            dma((4,)),
            dma((4,)),
        ],
        compiler_params=pltpu.CompilerParams(
            collective_id=0, has_side_effects=True, vmem_limit_bytes=58 * 1024 * 1024
        ),
    )(
        tile_dest.reshape(tiles),
        tile_chan,
        tile_count,
        made["fourier"],
        made["back"],
        made["excess"],
        sky_image,
        vis_tiles,
    )
    rows, columns = made["rows"], made["columns"]
    row_sec = jnp.einsum("bkn,cnx->bckx", rows, extended, preferred_element_type=F32).astype(BF)
    coefficient = jnp.einsum("bcyx,bkx->bcyk", row_sec, columns, preferred_element_type=F32)
    limits = thresholds.astype(F32)
    shrunk = (coefficient - jnp.clip(coefficient, -limits, limits)).astype(BF)
    row_sec = jnp.einsum("bjy,bcjk->bcyk", rows, shrunk, preferred_element_type=F32).astype(BF)
    cells = jnp.einsum("bcyk,bkx->cyx", row_sec, columns, preferred_element_type=F32)
    spill = cells.astype(BF)
    from_left = passed(spill[:, :SIDE, SIDE:TALL], ("fx",), (1,)).astype(F32)
    from_above = passed(spill[:, SIDE:, :SIDE], ("fy",), (1,)).astype(F32)
    from_corner = passed(spill[:, SIDE:, SIDE:TALL], ("fy", "fx"), (1, 1)).astype(F32)
    left = jnp.pad(from_left, ((0, 0), (0, 0), (0, SIDE - HALO)))
    above = jnp.pad(from_above, ((0, 0), (0, SIDE - HALO), (0, 0)))
    corner = jnp.pad(from_corner, ((0, 0), (0, SIDE - HALO), (0, SIDE - HALO)))
    summed = cells[:, :SIDE, :SIDE] + left + above + corner
    return jnp.maximum(summed * (1.0 / BASES), 0.0)


def solution(mesh):
    in_specs = (
        P(None, "fy", "fx"),
        P(("fy", "fx"), None, None, None),
        P(("fy", "fx"), None),
        P(("fy", "fx")),
        P(("fy", "fx")),
        P(None, None, "fy", "fx"),
    )
    out_specs = P(None, "fy", "fx")
    return jax.shard_map(
        functools.partial(per_device, mesh.shape["fy"], mesh.shape["fx"]),
        mesh=mesh,
        in_specs=in_specs,
        out_specs=out_specs,
        check_vma=False,
    )
```

```python
import functools
import math

import jax
import jax.numpy as jnp
import ml_dtypes
import numpy as np
from jax import lax
from jax.experimental import pallas as pl
from jax.experimental.pallas import tpu as pltpu
from jax.sharding import PartitionSpec as P

daubechies_taps = [
    [0.7071067811865476, 0.7071067811865476],
    [0.48296291314469025, 0.836516303737469, 0.22414386804185735, -0.12940952255092145],
    [
        0.3326705529509569,
        0.8068915093133388,
        0.4598775021193313,
        -0.13501102001039084,
        -0.08544127388224149,
        0.035226291882100656,
    ],
    [
        0.23037781330885523,
        0.7148465705525415,
        0.6308807679295904,
        -0.02798376941698385,
        -0.18703481171888114,
        0.030841381835986965,
        0.032883011666982945,
        -0.010597401784997278,
    ],
    [
        0.160102397974125,
        0.6038292697974729,
        0.7243085284385744,
        0.13842814590110342,
        -0.24229488706619015,
        -0.03224486958502952,
        0.07757149384006515,
        -0.006241490213011705,
        -0.012580751999015526,
        0.003335725285001549,
    ],
    [
        0.11154074335008017,
        0.4946238903983854,
        0.7511339080215775,
        0.3152503517092432,
        -0.22626469396516913,
        -0.12976686756709563,
        0.09750160558707936,
        0.02752286553001629,
        -0.031582039318031156,
        0.0005538422009938016,
        0.004777257511010651,
        -0.00107730108499558,
    ],
    [
        0.07785205408506236,
        0.39653931948230575,
        0.7291320908465551,
        0.4697822874053586,
        -0.14390600392910627,
        -0.22403618499416572,
        0.07130921926705004,
        0.0806126091510659,
        -0.03802993693503463,
        -0.01657454163101562,
        0.012550998556013784,
        0.00042957797300470274,
        -0.0018016407039998328,
        0.0003537138000010399,
    ],
    [
        0.05441584224308161,
        0.3128715909144659,
        0.6756307362980128,
        0.5853546836548691,
        -0.015829105256023893,
        -0.2840155429624281,
        0.00047248457399797254,
        0.128747426620186,
        -0.01736930100202211,
        -0.04408825393106472,
        0.013981027917015516,
        0.008746094047015655,
        -0.00487035299301066,
        -0.0003917403729959771,
        0.0006754494059985568,
        -0.00011747678400228192,
    ],
]


SIDE = 256
CH = 8
BASES = 8
HALO = 48
BF = jnp.bfloat16
F32 = jnp.float32
WIDE = SIDE + 128
TALL = SIDE + HALO


def rounded(table):
    return np.asarray(table, np.float32).astype(ml_dtypes.bfloat16)


def composite_tables():
    full = np.zeros((BASES, SIDE, SIDE + HALO))
    for degree in range(1, 9):
        taps = np.array(daubechies_taps[degree - 1])
        taps = taps * math.sqrt(2.0) / np.sum(taps)
        length = 2 * degree
        low = np.zeros(16)
        high = np.zeros(16)
        low[:length] = taps
        high[:length] = [(-1.0) ** j * taps[length - 1 - j] for j in range(length)]
        low = rounded(low).astype(np.float64)
        high = rounded(high).astype(np.float64)
        level_low = np.zeros((144, SIDE + HALO))
        level_high = np.zeros((128, SIDE + HALO))
        for k in range(144):
            level_low[k, 2 * k : 2 * k + 16] = low[: min(16, SIDE + HALO - 2 * k)]
        for k in range(128):
            level_high[k, 2 * k : 2 * k + 16] = high
        second = np.zeros((128, 144))
        for m in range(64):
            second[m, 2 * m : 2 * m + 16] = low
            second[64 + m, 2 * m : 2 * m + 16] = high
        full[degree - 1, :128] = second @ level_low
        full[degree - 1, 128:] = level_high
    return rounded(full).astype(np.float32)


@functools.lru_cache(maxsize=1)
def tables():
    full = composite_tables()
    wide = np.concatenate([full, np.zeros((BASES, SIDE, 128 - HALO), np.float32)], axis=2)
    spread = wide.copy()
    spread[:, :, TALL + 16 : TALL + 16 + HALO] = full[:, :, SIDE:]
    out = {"rows": full, "columns": wide, "spread": spread}
    grid = np.arange(SIDE)[:, None] * np.arange(SIDE)[None, :] % SIDE
    angle = grid * (2.0 * math.pi / SIDE)
    cosine = rounded(np.cos(angle) / math.sqrt(SIDE)).astype(np.float64)
    sine = rounded(np.sin(angle) / math.sqrt(SIDE)).astype(np.float64)
    out["fourier"] = np.block([[cosine, sine], [-sine, cosine]])
    out["back"] = np.concatenate([cosine, -sine], axis=1)
    out["excess"] = cosine @ cosine + sine @ sine - np.eye(SIDE)
    return {name: rounded(table) for name, table in out.items()}


PLACES = (
    (2, 2),
    (2, 1),
    (1, 2),
    (2, 3),
    (3, 2),
    (1, 1),
    (3, 3),
    (1, 3),
    (3, 1),
    (2, 0),
    (0, 2),
    (1, 0),
    (0, 1),
    (3, 0),
    (0, 3),
)


def path(place, r):
    ups = {0: (), 1: (1,), 2: (1, 1) if r == 0 else (3, 3), 3: (3,)}
    along_x = [(d, 0) for d in ups[place[0]]]
    along_z = [(0, d) for d in ups[place[1]]]
    return along_x + along_z if r == 0 else along_z + along_x


PATHS = [[path(place, r) for place in PLACES] for r in range(2)]
HOPS = [sum(len(p) > h for p in PATHS[0]) for h in range(5)]
BASE = [0] + [2 * sum(HOPS[1:h]) for h in range(1, 5)]
LAG = 3


def choose(j, values):
    out = jnp.int32(values[0])
    for i, value in enumerate(values):
        out = jnp.where(j == i, jnp.int32(value), out)
    return out


def dot(a, b):
    return jnp.dot(a, b, preferred_element_type=F32)


def exchange_kernel(
    n_fy,
    n_fx,
    dest_ref,
    chan_ref,
    count_ref,
    fourier,
    back,
    excess,
    sky_hbm,
    vis_hbm,
    extended,
    vis,
    sky,
    model,
    partial,
    sending,
    arrived,
    relay,
    half,
    share_ref,
    shares,
    kron,
    columns,
    beside,
    corner,
    load_sem,
    tile_send,
    tile_recv,
    relay_send,
    relay_recv,
    share_send,
    share_recv,
    halo_send,
    halo_recv,
    columns_send,
    columns_recv,
):
    fy = lax.axis_index("fy")
    fx = lax.axis_index("fx")
    n_z = 4
    n_x = n_fx // n_z
    my_x, my_z = fx // n_z, fx % n_z

    def at(dx, dz):
        return (my_x + dx) % n_x * n_z + (my_z + dz) % n_z

    def peer(k):
        return at(k // n_z, k % n_z)

    load_vis = pltpu.make_async_copy(vis_hbm, vis, load_sem.at[0])
    load_sky = pltpu.make_async_copy(sky_hbm, sky, load_sem.at[1])
    load_vis.start()
    load_sky.start()

    barrier = pltpu.get_barrier_semaphore()

    def greet(k, carry):
        pl.semaphore_signal(
            barrier, inc=1, device_id={"fx": peer(k)}, device_id_type=pl.DeviceIdType.MESH
        )
        return carry

    lax.fori_loop(1, n_fx, greet, 0)
    up, down = (fy + n_fy - 1) % n_fy, (fy + 1) % n_fy
    prev, nxt = (fx + n_fx - 1) % n_fx, (fx + 1) % n_fx
    for where in ({"fy": up}, {"fy": down}, {"fy": up, "fx": prev}, {"fy": down, "fx": nxt}):
        pl.semaphore_signal(barrier, inc=1, device_id=where, device_id_type=pl.DeviceIdType.MESH)

    def place_of(i):
        return at(choose(i, [p[0] for p in PLACES]), choose(i, [p[1] for p in PLACES]))

    def share_copy(i):
        return pltpu.make_async_remote_copy(
            src_ref=share_ref.at[1 + i],
            dst_ref=shares.at[1 + i],
            send_sem=share_send.at[1 + i],
            recv_sem=share_recv.at[1 + i],
            device_id={"fx": place_of(i)},
            device_id_type=pl.DeviceIdType.MESH,
        )

    def hop_copy(h, i, r, last):
        paths = PATHS[r][: HOPS[h]]
        to = at(choose(i, [p[h][0] for p in paths]), choose(i, [p[h][1] for p in paths]))
        own = i * 2 + r
        return pltpu.make_async_remote_copy(
            src_ref=sending.at[i, r] if h == 0 else relay.at[BASE[h] + own],
            dst_ref=arrived.at[1 + i, r] if last else relay.at[BASE[h + 1] + own],
            send_sem=tile_send.at[own] if h == 0 else relay_send.at[BASE[h] + own],
            recv_sem=tile_recv.at[1 + i, r] if last else relay_recv.at[BASE[h + 1] + own],
            device_id={"fx": to},
            device_id_type=pl.DeviceIdType.MESH,
        )

    def hop_start(h, i):
        for r in range(2):
            if h > 0:
                slot = BASE[h] + i * 2 + r
                pltpu.make_async_remote_copy(
                    src_ref=relay.at[slot],
                    dst_ref=relay.at[slot],
                    send_sem=relay_send.at[slot],
                    recv_sem=relay_recv.at[slot],
                    device_id={"fx": at(1, 0)},
                    device_id_type=pl.DeviceIdType.MESH,
                ).wait_recv()
            if HOPS[h + 1] == 0:
                hop_copy(h, i, r, True).start()
            else:

                @pl.when(i >= HOPS[h + 1])
                def _():
                    hop_copy(h, i, r, True).start()

                @pl.when(i < HOPS[h + 1])
                def _():
                    hop_copy(h, i, r, False).start()

    def arrival(i, r):
        return pltpu.make_async_remote_copy(
            src_ref=arrived.at[1 + i, r],
            dst_ref=arrived.at[1 + i, r],
            send_sem=tile_send.at[0],
            recv_sem=tile_recv.at[1 + i, r],
            device_id={"fx": at(1, 0)},
            device_id_type=pl.DeviceIdType.MESH,
        )

    tiles = vis_hbm.shape[0]
    row = lax.broadcasted_iota(jnp.int32, (8, 128), 0)
    lane = lax.broadcasted_iota(jnp.int32, (8, 128), 1)

    def slots_for(to):
        found = jnp.int32(0)
        picked = [(jnp.int32(0), jnp.int32(0), jnp.int32(0))] * 2
        for i in range(tiles):
            match = dest_ref[i] == to
            for r in range(2):
                here = match & (found == r)
                new = (jnp.int32(i), count_ref[i], chan_ref[i])
                picked[r] = tuple(jnp.where(here, a, b) for a, b in zip(new, picked[r]))
            found = found + jnp.where(match, 1, 0)
        return [(tile, count.astype(F32) * (1.0 / 64.0), chan) for tile, count, chan in picked]

    def share_rows(slots):
        total = jnp.zeros((8, 128), F32)
        for r, (_, weight, chan) in enumerate(slots):
            total = total + jnp.where((row == r) & (lane == chan), weight, 0.0)
        return total

    load_vis.wait()

    def planes(slots):
        for i, (t, _, _) in enumerate(slots):
            spectrum = jnp.concatenate([vis[t, 0], vis[t, 1]], axis=1)
            for part in range(2):
                half[i, part * SIDE : (part + 1) * SIDE] = dot(
                    spectrum, fourier[:, part * SIDE : (part + 1) * SIDE]
                ).astype(BF)
        return [(dot(back[...], half[i]) * slots[i][1]).astype(BF) for i in range(2)]

    def prepare(i):
        slots = slots_for(place_of(i))
        share_ref[1 + i] = share_rows(slots)
        sending[i, 0], sending[i, 1] = planes(slots)

    prepare(jnp.int32(0))
    pl.semaphore_wait(barrier, n_fx - 1 + 4)

    def send_tiles(i, carry):
        share_copy(i).start()
        hop_start(0, i)
        for h in range(1, 4):
            before = i - h * LAG

            @pl.when((before >= 0) & (before < HOPS[h]))
            def _():
                hop_start(h, before)

        @pl.when(i < len(PLACES) - 1)
        def _():
            prepare(i + 1)

        return carry

    assert all(HOPS[h] + h * LAG <= len(PLACES) for h in range(4))
    lax.fori_loop(0, len(PLACES), send_tiles, 0)
    own = slots_for(fx)
    shares[0] = share_rows(own)
    arrived[0, 0], arrived[0, 1] = planes(own)

    load_sky.wait()

    def there_and_back(c, carry):
        pixels = sky[c].astype(BF)
        once = pixels.astype(F32) + dot(excess[...], pixels)
        model[c] = once + dot(once.astype(BF), excess[...])
        return carry

    lax.fori_loop(0, CH, there_and_back, 0)

    def wait_share(i, carry):
        share_copy(i).wait_recv()
        return carry

    lax.fori_loop(0, len(PLACES), wait_share, 0)
    slots = n_fx * 2
    wide = slots * 16
    all_shares = shares[...].reshape(n_fx * 8, 128)
    members = jnp.where(all_shares > 0, 1.0, 0.0).astype(BF)
    spread = (
        lax.broadcasted_iota(jnp.int32, (CH * 16, 128), 0) // 16
        == lax.broadcasted_iota(jnp.int32, (CH * 16, 128), 1)
    )
    spread = jnp.where(spread, 1.0, 0.0).astype(BF)
    by_source = lax.dot_general(
        spread, members, (((1,), (1,)), ((), ())), preferred_element_type=F32
    ).astype(BF)
    weights = lax.dot_general(
        spread, all_shares.astype(BF), (((1,), (1,)), ((), ())), preferred_element_type=F32
    )
    totals = jnp.sum(weights, axis=1, keepdims=True)
    src_row = lax.broadcasted_iota(jnp.int32, (n_fx * 8, wide), 0)
    dst_col = lax.broadcasted_iota(jnp.int32, (n_fx * 8, wide), 1)
    widen = (src_row // 8 == dst_col // 32) & (src_row % 8 == dst_col // 16 % 2)
    widened = dot(by_source, jnp.where(widen, 1.0, 0.0).astype(BF))
    diagonal = (
        lax.broadcasted_iota(jnp.int32, (CH * 16, wide), 0) % 16
        == lax.broadcasted_iota(jnp.int32, (CH * 16, wide), 1) % 16
    )
    kron[...] = jnp.where(diagonal, widened, 0.0).astype(BF)
    scale = 1.0 / (1.0 + totals)

    def group_rows(g):
        return pl.ds(pl.multiple_of(g * 16, 16), 16)

    def begin(g, carry):
        pixels = sky[:, group_rows(g), :].reshape(CH * 16, SIDE)
        there = model[:, group_rows(g), :].reshape(CH * 16, SIDE)
        partial[g] = pixels - (totals * scale) * there
        return carry

    lax.fori_loop(0, SIDE // 16, begin, 0)

    def wait_tiles(i, carry):
        for r in range(2):
            arrival(i, r).wait_recv()
        return carry

    def with_sources(g, first, last):
        held = arrived[first:last, :, group_rows(g), :].reshape((last - first) * 32, SIDE)
        return partial[g] + scale * dot(kron[:, first * 32 : last * 32], held)

    for first, last in ((0, 8), (8, 12)):
        lax.fori_loop(max(first - 1, 0), last - 1, wait_tiles, 0)

        def add_sources(q, carry):
            for i in range(4):
                partial[q * 4 + i] = with_sources(q * 4 + i, first, last)
            return carry

        lax.fori_loop(0, SIDE // 64, add_sources, 0)
    lax.fori_loop(11, len(PLACES), wait_tiles, 0)

    def combine(g):
        rows = group_rows(g)
        new = with_sources(g, 12, 16).reshape(CH // 2, 2, 16, SIDE)
        extended[:, rows, :SIDE] = new.reshape(CH, 16, SIDE).astype(BF)
        low = lax.broadcasted_iota(jnp.int32, (CH // 2, 16, 128), 2) < 64
        second = pltpu.roll(new[:, 1, :, :128].reshape(CH // 2 * 16, 128), 64, 1)
        pair = jnp.where(low, new[:, 0, :, :128], second.reshape(CH // 2, 16, 128))
        columns[:, rows, :] = pair.astype(BF)

    chunks = 4
    deep = SIDE // chunks

    def columns_copy(q):
        rows = pl.ds(pl.multiple_of(q * deep, deep), deep)
        return pltpu.make_async_remote_copy(
            src_ref=columns.at[:, rows, :],
            dst_ref=beside.at[:, rows, :],
            send_sem=columns_send.at[q],
            recv_sem=columns_recv.at[q],
            device_id={"fx": prev},
            device_id_type=pl.DeviceIdType.MESH,
        )

    def halo_copy(i):
        source = (extended.at[:, :HALO, :SIDE], columns.at[:, :HALO, :])[i]
        target = (extended.at[:, SIDE:, :SIDE], corner)[i]
        where = ({"fy": up}, {"fy": up, "fx": prev})[i]
        return pltpu.make_async_remote_copy(
            src_ref=source,
            dst_ref=target,
            send_sem=halo_send.at[i],
            recv_sem=halo_recv.at[i],
            device_id=where,
            device_id_type=pl.DeviceIdType.MESH,
        )

    def make_chunk(q, carry):
        for i in range(deep // 16):
            combine(q * (deep // 16) + i)
        columns_copy(q).start()

        @pl.when(q == 0)
        def _():
            for i in range(2):
                halo_copy(i).start()

        return carry

    lax.fori_loop(0, chunks, make_chunk, 0)

    def place(source, begin, end):
        for p in range(CH // 2):
            first = source[p]
            extended[2 * p, begin:end, SIDE:] = first
            extended[2 * p + 1, begin:end, SIDE:] = pltpu.roll(first.astype(F32), 64, 1).astype(BF)

    halo_copy(1).wait_recv()
    place(corner, SIDE, TALL)
    for q in range(chunks):
        columns_copy(q).wait_recv()
        place(beside.at[:, q * deep : (q + 1) * deep, :], q * deep, (q + 1) * deep)
    halo_copy(0).wait_recv()

    def finish_shares(i, carry):
        share_copy(i).wait_send()
        return carry

    def finish_hops(h, i, carry):
        for r in range(2):
            hop_copy(h, i, r, True).wait_send()
        return carry

    lax.fori_loop(0, len(PLACES), finish_shares, 0)
    for h in range(4):
        lax.fori_loop(0, HOPS[h], functools.partial(finish_hops, h), 0)
    for i in range(2):
        halo_copy(i).wait_send()
    for q in range(chunks):
        columns_copy(q).wait_send()


def passed(value, axes, to):
    sizes = [lax.axis_size(a) for a in axes]
    pairs = []
    for i in np.ndindex(*sizes):
        j = [(a + b) % n for a, b, n in zip(i, to, sizes)]
        pairs.append((int(np.ravel_multi_index(i, sizes)), int(np.ravel_multi_index(j, sizes))))
    return lax.ppermute(value, axes if len(axes) > 1 else axes[0], pairs)


def first_half(shape):
    return lax.broadcasted_iota(jnp.int32, shape, len(shape) - 1) < 64


def pack_kernel(cells, right, corner, below, side, bottom, sem):
    load_side = pltpu.make_async_copy(cells.at[:, :, SIDE:], side, sem.at[0])
    load_bottom = pltpu.make_async_copy(cells.at[:, SIDE:, :SIDE], bottom, sem.at[1])
    load_side.start()
    load_bottom.start()
    load_side.wait()
    for p in range(CH // 2):
        both = jnp.where(first_half((TALL, 128)), side[2 * p], side[2 * p + 1]).astype(BF)
        right[p] = both[:SIDE]
        corner[p] = both[SIDE:]
    load_bottom.wait()
    below[...] = bottom[...].astype(BF)


def add_kernel(cells, left, above, corner, out):
    for h in range(2):

        def columns(pairs):
            pairs = pairs.astype(F32)
            if h == 1:
                pairs = pltpu.roll(pairs, 64, 1)
            return jnp.where(first_half(pairs.shape), pairs, 0.0)

        def finished(total):
            return jnp.maximum(total * (1.0 / BASES), 0.0)

        from_left = columns(left[0])
        from_above = above[h].astype(F32)
        first = from_left[:HALO] + from_above[:, :128] + columns(corner[0])
        out[h, :HALO, :128] = finished(cells[h, :HALO, :128] + first)
        out[h, :HALO, 128:] = finished(cells[h, :HALO, 128:] + from_above[:, 128:])
        out[h, HALO:, :128] = finished(cells[h, HALO:, :128] + from_left[HALO:])
        out[h, HALO:, 128:] = finished(cells[h, HALO:, 128:])


def per_device(n_fy, n_fx, sky_image, vis_tiles, tile_dest, tile_chan, tile_count, thresholds):
    made = {name: jnp.asarray(table) for name, table in tables().items()}
    smem = pl.BlockSpec(memory_space=pltpu.SMEM)
    vmem = pl.BlockSpec(memory_space=pltpu.VMEM)
    anywhere = pl.BlockSpec(memory_space=pl.ANY)
    dma = pltpu.SemaphoreType.DMA
    tiles = vis_tiles.shape[0]
    extended = pl.pallas_call(
        functools.partial(exchange_kernel, n_fy, n_fx),
        out_shape=pltpu.VMEM((CH, TALL, WIDE), BF),
        in_specs=[smem] * 3 + [vmem] * 3 + [anywhere] * 2,
        scratch_shapes=[
            pltpu.VMEM((tiles, 2, SIDE, SIDE), BF),
            pltpu.VMEM((CH, SIDE, SIDE), F32),
            pltpu.VMEM((CH, SIDE, SIDE), F32),
            pltpu.VMEM((SIDE // 16, CH * 16, SIDE), F32),
            pltpu.VMEM((n_fx, 2, SIDE, SIDE), BF),
            pltpu.VMEM((n_fx, 2, SIDE, SIDE), BF),
            pltpu.VMEM((BASE[4], SIDE, SIDE), BF),
            pltpu.VMEM((2, 2 * SIDE, SIDE), BF),
            pltpu.VMEM((n_fx, 8, 128), F32),
            pltpu.VMEM((n_fx, 8, 128), F32),
            pltpu.VMEM((CH * 16, n_fx * 32), BF),
            pltpu.VMEM((CH // 2, SIDE, 128), BF),
            pltpu.VMEM((CH // 2, SIDE, 128), BF),
            pltpu.VMEM((CH // 2, HALO, 128), BF),
            dma((2,)),
            dma((2 * len(PLACES),)),
            dma((n_fx, 2)),
            dma((BASE[4],)),
            dma((BASE[4],)),
            dma((n_fx,)),
            dma((n_fx,)),
            dma((2,)),
            dma((2,)),
            dma((4,)),
            dma((4,)),
        ],
        compiler_params=pltpu.CompilerParams(
            collective_id=0, has_side_effects=True, vmem_limit_bytes=58 * 1024 * 1024
        ),
    )(
        tile_dest.reshape(tiles),
        tile_chan,
        tile_count,
        made["fourier"],
        made["back"],
        made["excess"],
        sky_image,
        vis_tiles,
    )
    rows, columns = made["rows"], made["columns"]
    row_sec = jnp.einsum("bkn,cnx->bckx", rows, extended, preferred_element_type=F32).astype(BF)
    coefficient = jnp.einsum("bcyx,bkx->bcyk", row_sec, columns, preferred_element_type=F32)
    limits = thresholds.astype(F32)
    shrunk = (coefficient - jnp.clip(coefficient, -limits, limits)).astype(BF)
    row_sec = jnp.einsum("bjy,bcjk->bcyk", rows, shrunk, preferred_element_type=F32).astype(BF)
    cells = jnp.einsum("bcyk,bkx->cyx", row_sec, made["spread"], preferred_element_type=F32)
    right, corner, below = pl.pallas_call(
        pack_kernel,
        out_shape=(
            jax.ShapeDtypeStruct((CH // 2, SIDE, 128), BF),
            jax.ShapeDtypeStruct((CH // 2, HALO, 128), BF),
            jax.ShapeDtypeStruct((CH, HALO, SIDE), BF),
        ),
        in_specs=[anywhere],
        out_specs=[vmem] * 3,
        scratch_shapes=[
            pltpu.VMEM((CH, TALL, 128), F32),
            pltpu.VMEM((CH, HALO, SIDE), F32),
            dma((2,)),
        ],
        compiler_params=pltpu.CompilerParams(vmem_limit_bytes=16 * 1024 * 1024),
    )(cells)
    left = passed(right, ("fx",), (1,))
    above = passed(below, ("fy",), (1,))
    corner = passed(corner, ("fy", "fx"), (1, 1))
    return pl.pallas_call(
        add_kernel,
        out_shape=jax.ShapeDtypeStruct((CH, SIDE, SIDE), F32),
        grid=(CH // 2,),
        in_specs=[
            pl.BlockSpec((2, SIDE, SIDE), lambda p: (p, 0, 0)),
            pl.BlockSpec((1, SIDE, 128), lambda p: (p, 0, 0)),
            pl.BlockSpec((2, HALO, SIDE), lambda p: (p, 0, 0)),
            pl.BlockSpec((1, HALO, 128), lambda p: (p, 0, 0)),
        ],
        out_specs=pl.BlockSpec((2, SIDE, SIDE), lambda p: (p, 0, 0)),
        compiler_params=pltpu.CompilerParams(vmem_limit_bytes=16 * 1024 * 1024),
    )(cells, left, above, corner)


def solution(mesh):
    in_specs = (
        P(None, "fy", "fx"),
        P(("fy", "fx"), None, None, None),
        P(("fy", "fx"), None),
        P(("fy", "fx")),
        P(("fy", "fx")),
        P(None, None, "fy", "fx"),
    )
    out_specs = P(None, "fy", "fx")
    return jax.shard_map(
        functools.partial(per_device, mesh.shape["fy"], mesh.shape["fx"]),
        mesh=mesh,
        in_specs=in_specs,
        out_specs=out_specs,
        check_vma=False,
    )
```

```python
import functools
import math

import jax
import jax.numpy as jnp
import ml_dtypes
import numpy as np
from jax import lax
from jax.experimental import pallas as pl
from jax.experimental.pallas import tpu as pltpu
from jax.sharding import PartitionSpec as P

daubechies_taps = [
    [0.7071067811865476, 0.7071067811865476],
    [0.48296291314469025, 0.836516303737469, 0.22414386804185735, -0.12940952255092145],
    [
        0.3326705529509569,
        0.8068915093133388,
        0.4598775021193313,
        -0.13501102001039084,
        -0.08544127388224149,
        0.035226291882100656,
    ],
    [
        0.23037781330885523,
        0.7148465705525415,
        0.6308807679295904,
        -0.02798376941698385,
        -0.18703481171888114,
        0.030841381835986965,
        0.032883011666982945,
        -0.010597401784997278,
    ],
    [
        0.160102397974125,
        0.6038292697974729,
        0.7243085284385744,
        0.13842814590110342,
        -0.24229488706619015,
        -0.03224486958502952,
        0.07757149384006515,
        -0.006241490213011705,
        -0.012580751999015526,
        0.003335725285001549,
    ],
    [
        0.11154074335008017,
        0.4946238903983854,
        0.7511339080215775,
        0.3152503517092432,
        -0.22626469396516913,
        -0.12976686756709563,
        0.09750160558707936,
        0.02752286553001629,
        -0.031582039318031156,
        0.0005538422009938016,
        0.004777257511010651,
        -0.00107730108499558,
    ],
    [
        0.07785205408506236,
        0.39653931948230575,
        0.7291320908465551,
        0.4697822874053586,
        -0.14390600392910627,
        -0.22403618499416572,
        0.07130921926705004,
        0.0806126091510659,
        -0.03802993693503463,
        -0.01657454163101562,
        0.012550998556013784,
        0.00042957797300470274,
        -0.0018016407039998328,
        0.0003537138000010399,
    ],
    [
        0.05441584224308161,
        0.3128715909144659,
        0.6756307362980128,
        0.5853546836548691,
        -0.015829105256023893,
        -0.2840155429624281,
        0.00047248457399797254,
        0.128747426620186,
        -0.01736930100202211,
        -0.04408825393106472,
        0.013981027917015516,
        0.008746094047015655,
        -0.00487035299301066,
        -0.0003917403729959771,
        0.0006754494059985568,
        -0.00011747678400228192,
    ],
]


SIDE = 256
CH = 8
BASES = 8
HALO = 48
BF = jnp.bfloat16
F32 = jnp.float32
WIDE = SIDE + 128
TALL = SIDE + HALO


def rounded(table):
    return np.asarray(table, np.float32).astype(ml_dtypes.bfloat16)


def composite_tables():
    full = np.zeros((BASES, SIDE, SIDE + HALO))
    for degree in range(1, 9):
        taps = np.array(daubechies_taps[degree - 1])
        taps = taps * math.sqrt(2.0) / np.sum(taps)
        length = 2 * degree
        low = np.zeros(16)
        high = np.zeros(16)
        low[:length] = taps
        high[:length] = [(-1.0) ** j * taps[length - 1 - j] for j in range(length)]
        low = rounded(low).astype(np.float64)
        high = rounded(high).astype(np.float64)
        level_low = np.zeros((144, SIDE + HALO))
        level_high = np.zeros((128, SIDE + HALO))
        for k in range(144):
            level_low[k, 2 * k : 2 * k + 16] = low[: min(16, SIDE + HALO - 2 * k)]
        for k in range(128):
            level_high[k, 2 * k : 2 * k + 16] = high
        second = np.zeros((128, 144))
        for m in range(64):
            second[m, 2 * m : 2 * m + 16] = low
            second[64 + m, 2 * m : 2 * m + 16] = high
        full[degree - 1, :128] = second @ level_low
        full[degree - 1, 128:] = level_high
    return rounded(full).astype(np.float32)


@functools.lru_cache(maxsize=1)
def tables():
    full = composite_tables()
    wide = np.concatenate([full, np.zeros((BASES, SIDE, 128 - HALO), np.float32)], axis=2)
    spread = wide.copy()
    spread[:, :, TALL + 16 : TALL + 16 + HALO] = full[:, :, SIDE:]
    out = {"rows": full, "columns": wide, "spread": spread}
    grid = np.arange(SIDE)[:, None] * np.arange(SIDE)[None, :] % SIDE
    angle = grid * (2.0 * math.pi / SIDE)
    cosine = rounded(np.cos(angle) / math.sqrt(SIDE)).astype(np.float64)
    sine = rounded(np.sin(angle) / math.sqrt(SIDE)).astype(np.float64)
    out["fourier"] = np.block([[cosine, sine], [-sine, cosine]])
    out["back"] = np.concatenate([cosine, -sine], axis=1)
    out["excess"] = cosine @ cosine + sine @ sine - np.eye(SIDE)
    return {name: rounded(table) for name, table in out.items()}


PLACES = (
    (2, 2),
    (1, 2),
    (3, 3),
    (3, 2),
    (3, 1),
    (2, 1),
    (2, 3),
    (1, 1),
    (0, 3),
    (1, 3),
    (0, 2),
    (0, 1),
    (1, 0),
    (2, 0),
    (3, 0),
)
STEP_X, STEP_Z = (1, 3, 0, 0), (0, 0, 1, 3)
PATHS = (
    (
        (3, 0, 0, 3),
        (2, 0, 2),
        (1, 3),
        (1, 3, 3),
        (2, 1),
        (2, 1, 1),
        (1, 1, 3),
        (0, 2),
        (3,),
        (0, 3),
        (3, 3),
        (2,),
        (0,),
        (0, 0),
        (1,),
    ),
    (
        (1, 2, 2, 1),
        (0, 2, 2),
        (3, 1),
        (3, 3, 1),
        (1, 2),
        (0, 2, 0),
        (0, 0, 3),
        (0, 2),
        (3,),
        (3, 0),
        (2, 2),
        (2,),
        (0,),
        (1, 1),
        (1,),
    ),
)
FORWARDS = (
    (),
    (),
    ((0, 0, 1), (0, 1, 1)),
    ((1, 0, 1), (1, 1, 1)),
    ((2, 0, 1), (2, 1, 1)),
    ((0, 0, 2), (0, 1, 2)),
    ((3, 0, 1), (3, 1, 1), (1, 0, 2), (1, 1, 2)),
    ((4, 1, 1), (4, 0, 1), (5, 1, 1)),
    ((3, 0, 2),),
    ((0, 0, 3), (5, 0, 1)),
    ((3, 1, 2), (6, 0, 1), (0, 1, 3), (6, 1, 1)),
    (),
    ((7, 0, 1),),
    ((5, 0, 2), (7, 1, 1)),
    ((9, 0, 1),),
    ((6, 0, 2), (9, 1, 1), (5, 1, 2), (6, 1, 2), (10, 1, 1), (10, 0, 1), (13, 1, 1), (13, 0, 1)),
)
COMING = (2, 8, 1, 3, 4, 0, 12, 11, 9, 6, 14, 5, 7, 10, 13)

IN_ORDER = [hop for step in FORWARDS for hop in step]
FIRST = [sum(len(step) for step in FORWARDS[:i]) for i in range(len(FORWARDS) + 1)]
RANK = [COMING.index(i) for i in range(len(PLACES))]


def coded(place, r, hop):
    steps = PATHS[r][place]
    if hop + 1 == len(steps):
        return steps[hop] + 4 + 8 * (2 * (1 + RANK[place]) + r)
    return steps[hop] + 8 * IN_ORDER.index((place, r, hop + 1))


START = [[coded(place, r, 0) for place in range(len(PLACES))] for r in range(2)]
ONWARD = [coded(*hop) for hop in IN_ORDER]
assert len(IN_ORDER) == sum(len(p) - 1 for r in range(2) for p in PATHS[r])
assert len(IN_ORDER) - FIRST[-2] >= CH


def choose(j, values):
    out = jnp.int32(values[0])
    for i, value in enumerate(values):
        out = jnp.where(j == i, jnp.int32(value), out)
    return out


def dot(a, b):
    return jnp.dot(a, b, preferred_element_type=F32)


def exchange_kernel(
    n_fy,
    n_fx,
    dest_ref,
    chan_ref,
    count_ref,
    fourier,
    back,
    excess,
    sky_hbm,
    vis_hbm,
    extended,
    vis,
    sky,
    model,
    partial,
    sending,
    arrived,
    relay,
    half,
    share_ref,
    shares,
    kron,
    columns,
    beside,
    corner,
    load_sem,
    tile_send,
    tile_recv,
    relay_send,
    relay_recv,
    share_send,
    share_recv,
    halo_send,
    halo_recv,
    columns_send,
    columns_recv,
):
    fy = lax.axis_index("fy")
    fx = lax.axis_index("fx")
    n_z = 4
    n_x = n_fx // n_z
    my_x, my_z = fx // n_z, fx % n_z

    def at(dx, dz):
        return (my_x + dx) % n_x * n_z + (my_z + dz) % n_z

    def peer(k):
        return at(k // n_z, k % n_z)

    load_vis = pltpu.make_async_copy(vis_hbm, vis, load_sem.at[0])
    load_sky = pltpu.make_async_copy(sky_hbm, sky, load_sem.at[1])
    load_vis.start()
    load_sky.start()

    barrier = pltpu.get_barrier_semaphore()

    def greet(k, carry):
        pl.semaphore_signal(
            barrier, inc=1, device_id={"fx": peer(k)}, device_id_type=pl.DeviceIdType.MESH
        )
        return carry

    lax.fori_loop(1, n_fx, greet, 0)
    up, down = (fy + n_fy - 1) % n_fy, (fy + 1) % n_fy
    prev, nxt = (fx + n_fx - 1) % n_fx, (fx + 1) % n_fx
    for where in ({"fy": up}, {"fy": down}, {"fy": up, "fx": prev}, {"fy": down, "fx": nxt}):
        pl.semaphore_signal(barrier, inc=1, device_id=where, device_id_type=pl.DeviceIdType.MESH)

    def place_of(i):
        return at(choose(i, [p[0] for p in PLACES]), choose(i, [p[1] for p in PLACES]))

    def share_copy(i):
        rank = 1 + choose(i, RANK)
        return pltpu.make_async_remote_copy(
            src_ref=share_ref.at[rank],
            dst_ref=shares.at[rank],
            send_sem=share_send.at[rank],
            recv_sem=share_recv.at[rank],
            device_id={"fx": place_of(i)},
            device_id_type=pl.DeviceIdType.MESH,
        )

    def hop_copy(source, send_sem, code, last):
        step, to = code % 4, code // 8
        return pltpu.make_async_remote_copy(
            src_ref=source,
            dst_ref=arrived.at[to] if last else relay.at[to],
            send_sem=send_sem,
            recv_sem=tile_recv.at[to] if last else relay_recv.at[to],
            device_id={"fx": at(choose(step, STEP_X), choose(step, STEP_Z))},
            device_id_type=pl.DeviceIdType.MESH,
        )

    def hop_start(source, send_sem, code):
        @pl.when(code // 4 % 2 == 1)
        def _():
            hop_copy(source, send_sem, code, True).start()

        @pl.when(code // 4 % 2 == 0)
        def _():
            hop_copy(source, send_sem, code, False).start()

    def landed(buffer, sem):
        return pltpu.make_async_remote_copy(
            src_ref=buffer,
            dst_ref=buffer,
            send_sem=tile_send.at[0],
            recv_sem=sem,
            device_id={"fx": at(1, 0)},
            device_id_type=pl.DeviceIdType.MESH,
        )

    def forward(f, carry):
        landed(relay.at[f], relay_recv.at[f]).wait_recv()
        hop_start(relay.at[f], relay_send.at[f], choose(f, ONWARD))
        return carry

    tiles = vis_hbm.shape[0]
    row = lax.broadcasted_iota(jnp.int32, (8, 128), 0)
    lane = lax.broadcasted_iota(jnp.int32, (8, 128), 1)

    def slots_for(to):
        found = jnp.int32(0)
        picked = [(jnp.int32(0), jnp.int32(0), jnp.int32(0))] * 2
        for i in range(tiles):
            match = dest_ref[i] == to
            for r in range(2):
                here = match & (found == r)
                new = (jnp.int32(i), count_ref[i], chan_ref[i])
                picked[r] = tuple(jnp.where(here, a, b) for a, b in zip(new, picked[r]))
            found = found + jnp.where(match, 1, 0)
        return [(tile, count.astype(F32) * (1.0 / 64.0), chan) for tile, count, chan in picked]

    def share_rows(slots):
        total = jnp.zeros((8, 128), F32)
        for r, (_, weight, chan) in enumerate(slots):
            total = total + jnp.where((row == r) & (lane == chan), weight, 0.0)
        return total

    load_vis.wait()

    def planes(slots):
        for i, (t, _, _) in enumerate(slots):
            spectrum = jnp.concatenate([vis[t, 0], vis[t, 1]], axis=1)
            for part in range(2):
                half[i, part * SIDE : (part + 1) * SIDE] = dot(
                    spectrum, fourier[:, part * SIDE : (part + 1) * SIDE]
                ).astype(BF)
        return [(dot(back[...], half[i]) * slots[i][1]).astype(BF) for i in range(2)]

    def prepare(i):
        slots = slots_for(place_of(i))
        share_ref[1 + choose(i, RANK)] = share_rows(slots)
        sending[i, 0], sending[i, 1] = planes(slots)

    prepare(jnp.int32(0))
    pl.semaphore_wait(barrier, n_fx - 1 + 4)

    def send_tiles(i, carry):
        share_copy(i).start()
        for r in range(2):
            hop_start(sending.at[i, r], tile_send.at[2 * i + r], choose(i, START[r]))
        lax.fori_loop(choose(i, FIRST), choose(i + 1, FIRST), forward, 0)

        @pl.when(i < len(PLACES) - 1)
        def _():
            prepare(i + 1)

        return carry

    lax.fori_loop(0, len(PLACES), send_tiles, 0)

    load_sky.wait()

    def there_and_back(c, carry):
        pixels = sky[c].astype(BF)
        once = pixels.astype(F32) + dot(excess[...], pixels)
        model[c] = once + dot(once.astype(BF), excess[...])
        return carry

    def forward_and_work(j, carry):
        forward(FIRST[-2] + j, 0)

        @pl.when(j == 0)
        def _():
            own = slots_for(fx)
            shares[0] = share_rows(own)
            arrived[0], arrived[1] = planes(own)

        @pl.when(j < CH)
        def _():
            there_and_back(j, 0)

        return carry

    lax.fori_loop(0, len(IN_ORDER) - FIRST[-2], forward_and_work, 0)

    def wait_share(i, carry):
        share_copy(i).wait_recv()
        return carry

    lax.fori_loop(0, len(PLACES), wait_share, 0)
    slots = n_fx * 2
    wide = slots * 16
    all_shares = shares[...].reshape(n_fx * 8, 128)
    members = jnp.where(all_shares > 0, 1.0, 0.0).astype(BF)
    spread = (
        lax.broadcasted_iota(jnp.int32, (CH * 16, 128), 0) // 16
        == lax.broadcasted_iota(jnp.int32, (CH * 16, 128), 1)
    )
    spread = jnp.where(spread, 1.0, 0.0).astype(BF)
    by_source = lax.dot_general(
        spread, members, (((1,), (1,)), ((), ())), preferred_element_type=F32
    ).astype(BF)
    weights = lax.dot_general(
        spread, all_shares.astype(BF), (((1,), (1,)), ((), ())), preferred_element_type=F32
    )
    totals = jnp.sum(weights, axis=1, keepdims=True)
    src_row = lax.broadcasted_iota(jnp.int32, (n_fx * 8, wide), 0)
    dst_col = lax.broadcasted_iota(jnp.int32, (n_fx * 8, wide), 1)
    widen = (src_row // 8 == dst_col // 32) & (src_row % 8 == dst_col // 16 % 2)
    widened = dot(by_source, jnp.where(widen, 1.0, 0.0).astype(BF))
    diagonal = (
        lax.broadcasted_iota(jnp.int32, (CH * 16, wide), 0) % 16
        == lax.broadcasted_iota(jnp.int32, (CH * 16, wide), 1) % 16
    )
    kron[...] = jnp.where(diagonal, widened, 0.0).astype(BF)
    scale = 1.0 / (1.0 + totals)

    def group_rows(g):
        return pl.ds(pl.multiple_of(g * 16, 16), 16)

    def without_tiles(g):
        pixels = sky[:, group_rows(g), :].reshape(CH * 16, SIDE)
        there = model[:, group_rows(g), :].reshape(CH * 16, SIDE)
        return pixels - (totals * scale) * there

    def wait_tiles(i, carry):
        landed(arrived.at[2 + i], tile_recv.at[2 + i]).wait_recv()
        return carry

    def with_sources(g, first, last):
        held = arrived[2 * first : 2 * last, group_rows(g), :].reshape((last - first) * 32, SIDE)
        before = without_tiles(g) if first == 0 else partial[g]
        return before + scale * dot(kron[:, first * 32 : last * 32], held)

    for first, last in ((0, 8), (8, 12)):
        lax.fori_loop(max(2 * first - 2, 0), 2 * last - 2, wait_tiles, 0)

        def add_sources(q, carry):
            for i in range(4):
                partial[q * 4 + i] = with_sources(q * 4 + i, first, last)
            return carry

        lax.fori_loop(0, SIDE // 64, add_sources, 0)
    lax.fori_loop(22, 2 * len(PLACES), wait_tiles, 0)

    def combine(g):
        rows = group_rows(g)
        new = with_sources(g, 12, 16).reshape(CH // 2, 2, 16, SIDE)
        extended[:, rows, :SIDE] = new.reshape(CH, 16, SIDE).astype(BF)
        low = lax.broadcasted_iota(jnp.int32, (CH // 2, 16, 128), 2) < 64
        second = pltpu.roll(new[:, 1, :, :128].reshape(CH // 2 * 16, 128), 64, 1)
        pair = jnp.where(low, new[:, 0, :, :128], second.reshape(CH // 2, 16, 128))
        columns[:, rows, :] = pair.astype(BF)

    chunks = 4
    deep = SIDE // chunks

    def columns_copy(q):
        rows = pl.ds(pl.multiple_of(q * deep, deep), deep)
        return pltpu.make_async_remote_copy(
            src_ref=columns.at[:, rows, :],
            dst_ref=beside.at[:, rows, :],
            send_sem=columns_send.at[q],
            recv_sem=columns_recv.at[q],
            device_id={"fx": prev},
            device_id_type=pl.DeviceIdType.MESH,
        )

    def halo_copy(i):
        source = (extended.at[:, :HALO, :SIDE], columns.at[:, :HALO, :])[i]
        target = (extended.at[:, SIDE:, :SIDE], corner)[i]
        where = ({"fy": up}, {"fy": up, "fx": prev})[i]
        return pltpu.make_async_remote_copy(
            src_ref=source,
            dst_ref=target,
            send_sem=halo_send.at[i],
            recv_sem=halo_recv.at[i],
            device_id=where,
            device_id_type=pl.DeviceIdType.MESH,
        )

    def make_chunk(q, carry):
        for i in range(deep // 16):
            combine(q * (deep // 16) + i)
        columns_copy(q).start()

        @pl.when(q == 0)
        def _():
            for i in range(2):
                halo_copy(i).start()

        return carry

    lax.fori_loop(0, chunks, make_chunk, 0)

    def place(source, begin, end):
        for p in range(CH // 2):
            first = source[p]
            extended[2 * p, begin:end, SIDE:] = first
            extended[2 * p + 1, begin:end, SIDE:] = pltpu.roll(first.astype(F32), 64, 1).astype(BF)

    halo_copy(1).wait_recv()
    place(corner, SIDE, TALL)
    for q in range(chunks):
        columns_copy(q).wait_recv()
        place(beside.at[:, q * deep : (q + 1) * deep, :], q * deep, (q + 1) * deep)
    halo_copy(0).wait_recv()

    def finish_shares(i, carry):
        share_copy(i).wait_send()
        return carry

    def finish_sent(i, carry):
        for r in range(2):
            hop_copy(sending.at[i, r], tile_send.at[2 * i + r], jnp.int32(0), False).wait_send()
        return carry

    def finish_forwards(f, carry):
        hop_copy(relay.at[f], relay_send.at[f], jnp.int32(0), False).wait_send()
        return carry

    lax.fori_loop(0, len(PLACES), finish_shares, 0)
    lax.fori_loop(0, len(PLACES), finish_sent, 0)
    lax.fori_loop(0, len(IN_ORDER), finish_forwards, 0)
    for i in range(2):
        halo_copy(i).wait_send()
    for q in range(chunks):
        columns_copy(q).wait_send()


def passed(value, axes, to):
    sizes = [lax.axis_size(a) for a in axes]
    pairs = []
    for i in np.ndindex(*sizes):
        j = [(a + b) % n for a, b, n in zip(i, to, sizes)]
        pairs.append((int(np.ravel_multi_index(i, sizes)), int(np.ravel_multi_index(j, sizes))))
    return lax.ppermute(value, axes if len(axes) > 1 else axes[0], pairs)


def first_half(shape):
    return lax.broadcasted_iota(jnp.int32, shape, len(shape) - 1) < 64


def pack_kernel(cells, right, corner, below, side, bottom, sem):
    load_side = pltpu.make_async_copy(cells.at[:, :, SIDE:], side, sem.at[0])
    load_bottom = pltpu.make_async_copy(cells.at[:, SIDE:, :SIDE], bottom, sem.at[1])
    load_side.start()
    load_bottom.start()
    load_side.wait()
    for p in range(CH // 2):
        both = jnp.where(first_half((TALL, 128)), side[2 * p], side[2 * p + 1]).astype(BF)
        right[p] = both[:SIDE]
        corner[p] = both[SIDE:]
    load_bottom.wait()
    below[...] = bottom[...].astype(BF)


def add_kernel(cells, left, above, corner, out):
    for h in range(2):

        def columns(pairs):
            pairs = pairs.astype(F32)
            if h == 1:
                pairs = pltpu.roll(pairs, 64, 1)
            return jnp.where(first_half(pairs.shape), pairs, 0.0)

        def finished(total):
            return jnp.maximum(total * (1.0 / BASES), 0.0)

        from_left = columns(left[0])
        from_above = above[h].astype(F32)
        first = from_left[:HALO] + from_above[:, :128] + columns(corner[0])
        out[h, :HALO, :128] = finished(cells[h, :HALO, :128] + first)
        out[h, :HALO, 128:] = finished(cells[h, :HALO, 128:] + from_above[:, 128:])
        out[h, HALO:, :128] = finished(cells[h, HALO:, :128] + from_left[HALO:])
        out[h, HALO:, 128:] = finished(cells[h, HALO:, 128:])


def per_device(n_fy, n_fx, sky_image, vis_tiles, tile_dest, tile_chan, tile_count, thresholds):
    made = {name: jnp.asarray(table) for name, table in tables().items()}
    smem = pl.BlockSpec(memory_space=pltpu.SMEM)
    vmem = pl.BlockSpec(memory_space=pltpu.VMEM)
    anywhere = pl.BlockSpec(memory_space=pl.ANY)
    dma = pltpu.SemaphoreType.DMA
    tiles = vis_tiles.shape[0]
    extended = pl.pallas_call(
        functools.partial(exchange_kernel, n_fy, n_fx),
        out_shape=pltpu.VMEM((CH, TALL, WIDE), BF),
        in_specs=[smem] * 3 + [vmem] * 3 + [anywhere] * 2,
        scratch_shapes=[
            pltpu.VMEM((tiles, 2, SIDE, SIDE), BF),
            pltpu.VMEM((CH, SIDE, SIDE), F32),
            pltpu.VMEM((CH, SIDE, SIDE), F32),
            pltpu.VMEM((SIDE // 16, CH * 16, SIDE), F32),
            pltpu.VMEM((n_fx, 2, SIDE, SIDE), BF),
            pltpu.VMEM((2 * n_fx, SIDE, SIDE), BF),
            pltpu.VMEM((len(IN_ORDER), SIDE, SIDE), BF),
            pltpu.VMEM((2, 2 * SIDE, SIDE), BF),
            pltpu.VMEM((n_fx, 8, 128), F32),
            pltpu.VMEM((n_fx, 8, 128), F32),
            pltpu.VMEM((CH * 16, n_fx * 32), BF),
            pltpu.VMEM((CH // 2, SIDE, 128), BF),
            pltpu.VMEM((CH // 2, SIDE, 128), BF),
            pltpu.VMEM((CH // 2, HALO, 128), BF),
            dma((2,)),
            dma((2 * len(PLACES),)),
            dma((2 * n_fx,)),
            dma((len(IN_ORDER),)),
            dma((len(IN_ORDER),)),
            dma((n_fx,)),
            dma((n_fx,)),
            dma((2,)),
            dma((2,)),
            dma((4,)),
            dma((4,)),
        ],
        compiler_params=pltpu.CompilerParams(
            collective_id=0, has_side_effects=True, vmem_limit_bytes=58 * 1024 * 1024
        ),
    )(
        tile_dest.reshape(tiles),
        tile_chan,
        tile_count,
        made["fourier"],
        made["back"],
        made["excess"],
        sky_image,
        vis_tiles,
    )
    rows, columns = made["rows"], made["columns"]
    row_sec = jnp.einsum("bkn,cnx->bckx", rows, extended, preferred_element_type=F32).astype(BF)
    coefficient = jnp.einsum("bcyx,bkx->bcyk", row_sec, columns, preferred_element_type=F32)
    limits = thresholds.astype(F32)
    shrunk = (coefficient - jnp.clip(coefficient, -limits, limits)).astype(BF)
    row_sec = jnp.einsum("bjy,bcjk->bcyk", rows, shrunk, preferred_element_type=F32).astype(BF)
    cells = jnp.einsum("bcyk,bkx->cyx", row_sec, made["spread"], preferred_element_type=F32)
    right, corner, below = pl.pallas_call(
        pack_kernel,
        out_shape=(
            jax.ShapeDtypeStruct((CH // 2, SIDE, 128), BF),
            jax.ShapeDtypeStruct((CH // 2, HALO, 128), BF),
            jax.ShapeDtypeStruct((CH, HALO, SIDE), BF),
        ),
        in_specs=[pl.BlockSpec(memory_space=pltpu.HBM)],
        out_specs=[vmem] * 3,
        scratch_shapes=[
            pltpu.VMEM((CH, TALL, 128), F32),
            pltpu.VMEM((CH, HALO, SIDE), F32),
            dma((2,)),
        ],
        compiler_params=pltpu.CompilerParams(vmem_limit_bytes=16 * 1024 * 1024),
    )(cells)
    left = passed(right, ("fx",), (1,))
    above = passed(below, ("fy",), (1,))
    corner = passed(corner, ("fy", "fx"), (1, 1))
    return pl.pallas_call(
        add_kernel,
        out_shape=jax.ShapeDtypeStruct((CH, SIDE, SIDE), F32),
        grid=(CH // 2,),
        in_specs=[
            pl.BlockSpec((2, SIDE, SIDE), lambda p: (p, 0, 0)),
            pl.BlockSpec((1, SIDE, 128), lambda p: (p, 0, 0)),
            pl.BlockSpec((2, HALO, SIDE), lambda p: (p, 0, 0)),
            pl.BlockSpec((1, HALO, 128), lambda p: (p, 0, 0)),
        ],
        out_specs=pl.BlockSpec((2, SIDE, SIDE), lambda p: (p, 0, 0)),
        compiler_params=pltpu.CompilerParams(vmem_limit_bytes=16 * 1024 * 1024),
    )(cells, left, above, corner)


def solution(mesh):
    in_specs = (
        P(None, "fy", "fx"),
        P(("fy", "fx"), None, None, None),
        P(("fy", "fx"), None),
        P(("fy", "fx")),
        P(("fy", "fx")),
        P(None, None, "fy", "fx"),
    )
    out_specs = P(None, "fy", "fx")
    return jax.shard_map(
        functools.partial(per_device, mesh.shape["fy"], mesh.shape["fx"]),
        mesh=mesh,
        in_specs=in_specs,
        out_specs=out_specs,
        check_vma=False,
    )
```

```python
import functools
import math

import jax
import jax.numpy as jnp
import ml_dtypes
import numpy as np
from jax import lax
from jax.experimental import pallas as pl
from jax.experimental.pallas import tpu as pltpu
from jax.sharding import PartitionSpec as P

daubechies_taps = [
    [0.7071067811865476, 0.7071067811865476],
    [0.48296291314469025, 0.836516303737469, 0.22414386804185735, -0.12940952255092145],
    [
        0.3326705529509569,
        0.8068915093133388,
        0.4598775021193313,
        -0.13501102001039084,
        -0.08544127388224149,
        0.035226291882100656,
    ],
    [
        0.23037781330885523,
        0.7148465705525415,
        0.6308807679295904,
        -0.02798376941698385,
        -0.18703481171888114,
        0.030841381835986965,
        0.032883011666982945,
        -0.010597401784997278,
    ],
    [
        0.160102397974125,
        0.6038292697974729,
        0.7243085284385744,
        0.13842814590110342,
        -0.24229488706619015,
        -0.03224486958502952,
        0.07757149384006515,
        -0.006241490213011705,
        -0.012580751999015526,
        0.003335725285001549,
    ],
    [
        0.11154074335008017,
        0.4946238903983854,
        0.7511339080215775,
        0.3152503517092432,
        -0.22626469396516913,
        -0.12976686756709563,
        0.09750160558707936,
        0.02752286553001629,
        -0.031582039318031156,
        0.0005538422009938016,
        0.004777257511010651,
        -0.00107730108499558,
    ],
    [
        0.07785205408506236,
        0.39653931948230575,
        0.7291320908465551,
        0.4697822874053586,
        -0.14390600392910627,
        -0.22403618499416572,
        0.07130921926705004,
        0.0806126091510659,
        -0.03802993693503463,
        -0.01657454163101562,
        0.012550998556013784,
        0.00042957797300470274,
        -0.0018016407039998328,
        0.0003537138000010399,
    ],
    [
        0.05441584224308161,
        0.3128715909144659,
        0.6756307362980128,
        0.5853546836548691,
        -0.015829105256023893,
        -0.2840155429624281,
        0.00047248457399797254,
        0.128747426620186,
        -0.01736930100202211,
        -0.04408825393106472,
        0.013981027917015516,
        0.008746094047015655,
        -0.00487035299301066,
        -0.0003917403729959771,
        0.0006754494059985568,
        -0.00011747678400228192,
    ],
]


SIDE = 256
CH = 8
BASES = 8
HALO = 48
BF = jnp.bfloat16
F32 = jnp.float32
WIDE = SIDE + 128
TALL = SIDE + HALO
PART = SIDE // 2
PART_TALL = PART + HALO


def rounded(table):
    return np.asarray(table, np.float32).astype(ml_dtypes.bfloat16)


def composite_tables():
    full = np.zeros((BASES, SIDE, SIDE + HALO))
    for degree in range(1, 9):
        taps = np.array(daubechies_taps[degree - 1])
        taps = taps * math.sqrt(2.0) / np.sum(taps)
        length = 2 * degree
        low = np.zeros(16)
        high = np.zeros(16)
        low[:length] = taps
        high[:length] = [(-1.0) ** j * taps[length - 1 - j] for j in range(length)]
        low = rounded(low).astype(np.float64)
        high = rounded(high).astype(np.float64)
        level_low = np.zeros((144, SIDE + HALO))
        level_high = np.zeros((128, SIDE + HALO))
        for k in range(144):
            level_low[k, 2 * k : 2 * k + 16] = low[: min(16, SIDE + HALO - 2 * k)]
        for k in range(128):
            level_high[k, 2 * k : 2 * k + 16] = high
        second = np.zeros((128, 144))
        for m in range(64):
            second[m, 2 * m : 2 * m + 16] = low
            second[64 + m, 2 * m : 2 * m + 16] = high
        full[degree - 1, :128] = second @ level_low
        full[degree - 1, 128:] = level_high
    return rounded(full).astype(np.float32)


def half_blocks(g):
    return ((32 * g, 32), (64 + 32 * g, 32), (128 + 64 * g, 64))


def half_rows(g):
    return np.concatenate([np.arange(first, first + rows) for first, rows in half_blocks(g)])


@functools.lru_cache(maxsize=1)
def tables():
    full = composite_tables()
    wide = np.concatenate([full, np.zeros((BASES, SIDE, 128 - HALO), np.float32)], axis=2)
    spread = wide.copy()
    spread[:, :, TALL + 16 : TALL + 16 + HALO] = full[:, :, SIDE:]
    halves = [full[:, half_rows(g), g * PART : g * PART + PART_TALL] for g in range(2)]
    assert np.array_equal(halves[0], halves[1])
    assert np.count_nonzero(halves[0]) * 2 == np.count_nonzero(full)
    out = {"rows": halves[0], "columns": wide, "spread": spread}
    grid = np.arange(SIDE)[:, None] * np.arange(SIDE)[None, :] % SIDE
    angle = grid * (2.0 * math.pi / SIDE)
    cosine = rounded(np.cos(angle) / math.sqrt(SIDE)).astype(np.float64)
    sine = rounded(np.sin(angle) / math.sqrt(SIDE)).astype(np.float64)
    out["fourier"] = np.block([[cosine, sine], [-sine, cosine]])
    out["back"] = np.concatenate([cosine, -sine], axis=1)
    out["excess"] = cosine @ cosine + sine @ sine - np.eye(SIDE)
    return {name: rounded(table) for name, table in out.items()}


PLACES = (
    (2, 2),
    (1, 2),
    (3, 3),
    (3, 2),
    (3, 1),
    (2, 1),
    (2, 3),
    (1, 1),
    (0, 3),
    (1, 3),
    (0, 2),
    (0, 1),
    (1, 0),
    (2, 0),
    (3, 0),
)
STEP_X, STEP_Z = (1, 3, 0, 0), (0, 0, 1, 3)
PATHS = (
    (
        (3, 0, 0, 3),
        (2, 0, 2),
        (1, 3),
        (1, 3, 3),
        (2, 1),
        (2, 1, 1),
        (1, 1, 3),
        (0, 2),
        (3,),
        (0, 3),
        (3, 3),
        (2,),
        (0,),
        (0, 0),
        (1,),
    ),
    (
        (1, 2, 2, 1),
        (0, 2, 2),
        (3, 1),
        (3, 3, 1),
        (1, 2),
        (0, 2, 0),
        (0, 0, 3),
        (0, 2),
        (3,),
        (3, 0),
        (2, 2),
        (2,),
        (0,),
        (1, 1),
        (1,),
    ),
)
FORWARDS = (
    (),
    (),
    ((0, 0, 1), (0, 1, 1)),
    ((1, 0, 1), (1, 1, 1)),
    ((2, 0, 1), (2, 1, 1)),
    ((0, 0, 2), (0, 1, 2)),
    ((3, 0, 1), (3, 1, 1), (1, 0, 2), (1, 1, 2)),
    ((4, 1, 1), (4, 0, 1), (5, 1, 1)),
    ((3, 0, 2),),
    ((0, 0, 3), (5, 0, 1)),
    ((3, 1, 2), (6, 0, 1), (0, 1, 3), (6, 1, 1)),
    (),
    ((7, 0, 1),),
    ((5, 0, 2), (7, 1, 1)),
    ((9, 0, 1),),
    ((6, 0, 2), (9, 1, 1), (5, 1, 2), (6, 1, 2), (10, 1, 1), (10, 0, 1), (13, 1, 1), (13, 0, 1)),
)
COMING = (2, 8, 1, 3, 4, 0, 12, 11, 9, 6, 14, 5, 7, 10, 13)

IN_ORDER = [hop for step in FORWARDS for hop in step]
FIRST = [sum(len(step) for step in FORWARDS[:i]) for i in range(len(FORWARDS) + 1)]
RANK = [COMING.index(i) for i in range(len(PLACES))]


def coded(place, r, hop):
    steps = PATHS[r][place]
    if hop + 1 == len(steps):
        return steps[hop] + 4 + 8 * (2 * (1 + RANK[place]) + r)
    return steps[hop] + 8 * IN_ORDER.index((place, r, hop + 1))


START = [[coded(place, r, 0) for place in range(len(PLACES))] for r in range(2)]
ONWARD = [coded(*hop) for hop in IN_ORDER]
assert len(IN_ORDER) == sum(len(p) - 1 for r in range(2) for p in PATHS[r])
assert len(IN_ORDER) - FIRST[-2] >= CH


def choose(j, values):
    out = jnp.int32(values[0])
    for i, value in enumerate(values):
        out = jnp.where(j == i, jnp.int32(value), out)
    return out


def dot(a, b):
    return jnp.dot(a, b, preferred_element_type=F32)


def exchange_kernel(
    n_fy,
    n_fx,
    dest_ref,
    chan_ref,
    count_ref,
    fourier,
    back,
    excess,
    sky_hbm,
    vis_hbm,
    thr_hbm,
    upper,
    lower,
    thr_upper,
    thr_lower,
    vis,
    sky,
    model,
    partial,
    sending,
    arrived,
    relay,
    half,
    share_ref,
    shares,
    kron,
    columns,
    beside,
    corner,
    load_sem,
    tile_send,
    tile_recv,
    relay_send,
    relay_recv,
    share_send,
    share_recv,
    halo_send,
    halo_recv,
    columns_send,
    columns_recv,
    thr_sem,
):
    fy = lax.axis_index("fy")
    fx = lax.axis_index("fx")
    n_z = 4
    n_x = n_fx // n_z
    my_x, my_z = fx // n_z, fx % n_z

    def at(dx, dz):
        return (my_x + dx) % n_x * n_z + (my_z + dz) % n_z

    def peer(k):
        return at(k // n_z, k % n_z)

    load_vis = pltpu.make_async_copy(vis_hbm, vis, load_sem.at[0])
    load_sky = pltpu.make_async_copy(sky_hbm, sky, load_sem.at[1])
    load_vis.start()
    load_sky.start()

    barrier = pltpu.get_barrier_semaphore()

    def greet(k, carry):
        pl.semaphore_signal(
            barrier, inc=1, device_id={"fx": peer(k)}, device_id_type=pl.DeviceIdType.MESH
        )
        return carry

    lax.fori_loop(1, n_fx, greet, 0)
    up, down = (fy + n_fy - 1) % n_fy, (fy + 1) % n_fy
    prev, nxt = (fx + n_fx - 1) % n_fx, (fx + 1) % n_fx
    for where in ({"fy": up}, {"fy": down}, {"fy": up, "fx": prev}, {"fy": down, "fx": nxt}):
        pl.semaphore_signal(barrier, inc=1, device_id=where, device_id_type=pl.DeviceIdType.MESH)

    def place_of(i):
        return at(choose(i, [p[0] for p in PLACES]), choose(i, [p[1] for p in PLACES]))

    def share_copy(i):
        rank = 1 + choose(i, RANK)
        return pltpu.make_async_remote_copy(
            src_ref=share_ref.at[rank],
            dst_ref=shares.at[rank],
            send_sem=share_send.at[rank],
            recv_sem=share_recv.at[rank],
            device_id={"fx": place_of(i)},
            device_id_type=pl.DeviceIdType.MESH,
        )

    def hop_copy(source, send_sem, code, last):
        step, to = code % 4, code // 8
        return pltpu.make_async_remote_copy(
            src_ref=source,
            dst_ref=arrived.at[to] if last else relay.at[to],
            send_sem=send_sem,
            recv_sem=tile_recv.at[to] if last else relay_recv.at[to],
            device_id={"fx": at(choose(step, STEP_X), choose(step, STEP_Z))},
            device_id_type=pl.DeviceIdType.MESH,
        )

    def hop_start(source, send_sem, code):
        @pl.when(code // 4 % 2 == 1)
        def _():
            hop_copy(source, send_sem, code, True).start()

        @pl.when(code // 4 % 2 == 0)
        def _():
            hop_copy(source, send_sem, code, False).start()

    def landed(buffer, sem):
        return pltpu.make_async_remote_copy(
            src_ref=buffer,
            dst_ref=buffer,
            send_sem=tile_send.at[0],
            recv_sem=sem,
            device_id={"fx": at(1, 0)},
            device_id_type=pl.DeviceIdType.MESH,
        )

    def forward(f, carry):
        landed(relay.at[f], relay_recv.at[f]).wait_recv()
        hop_start(relay.at[f], relay_send.at[f], choose(f, ONWARD))
        return carry

    tiles = vis_hbm.shape[0]
    row = lax.broadcasted_iota(jnp.int32, (8, 128), 0)
    lane = lax.broadcasted_iota(jnp.int32, (8, 128), 1)

    def slots_for(to):
        found = jnp.int32(0)
        picked = [(jnp.int32(0), jnp.int32(0), jnp.int32(0))] * 2
        for i in range(tiles):
            match = dest_ref[i] == to
            for r in range(2):
                here = match & (found == r)
                new = (jnp.int32(i), count_ref[i], chan_ref[i])
                picked[r] = tuple(jnp.where(here, a, b) for a, b in zip(new, picked[r]))
            found = found + jnp.where(match, 1, 0)
        return [(tile, count.astype(F32) * (1.0 / 64.0), chan) for tile, count, chan in picked]

    def share_rows(slots):
        total = jnp.zeros((8, 128), F32)
        for r, (_, weight, chan) in enumerate(slots):
            total = total + jnp.where((row == r) & (lane == chan), weight, 0.0)
        return total

    load_vis.wait()
    thr_copies = []
    for g, target in enumerate((thr_upper, thr_lower)):
        begin = 0
        for i, (first, rows) in enumerate(half_blocks(g)):
            thr_copies.append(
                pltpu.make_async_copy(
                    thr_hbm.at[:, :, first : first + rows, :],
                    target.at[:, :, begin : begin + rows, :],
                    thr_sem.at[3 * g + i],
                )
            )
            begin += rows
    for copy in thr_copies:
        copy.start()

    def planes(slots):
        for i, (t, _, _) in enumerate(slots):
            spectrum = jnp.concatenate([vis[t, 0], vis[t, 1]], axis=1)
            for part in range(2):
                half[i, part * SIDE : (part + 1) * SIDE] = dot(
                    spectrum, fourier[:, part * SIDE : (part + 1) * SIDE]
                ).astype(BF)
        return [(dot(back[...], half[i]) * slots[i][1]).astype(BF) for i in range(2)]

    def prepare(i):
        slots = slots_for(place_of(i))
        share_ref[1 + choose(i, RANK)] = share_rows(slots)
        sending[i, 0], sending[i, 1] = planes(slots)

    prepare(jnp.int32(0))
    pl.semaphore_wait(barrier, n_fx - 1 + 4)

    def send_tiles(i, carry):
        share_copy(i).start()
        for r in range(2):
            hop_start(sending.at[i, r], tile_send.at[2 * i + r], choose(i, START[r]))
        lax.fori_loop(choose(i, FIRST), choose(i + 1, FIRST), forward, 0)

        @pl.when(i < len(PLACES) - 1)
        def _():
            prepare(i + 1)

        return carry

    lax.fori_loop(0, len(PLACES), send_tiles, 0)

    load_sky.wait()

    def there_and_back(c, carry):
        pixels = sky[c].astype(BF)
        once = pixels.astype(F32) + dot(excess[...], pixels)
        model[c] = once + dot(once.astype(BF), excess[...])
        return carry

    def forward_and_work(j, carry):
        forward(FIRST[-2] + j, 0)

        @pl.when(j == 0)
        def _():
            own = slots_for(fx)
            shares[0] = share_rows(own)
            arrived[0], arrived[1] = planes(own)

        @pl.when(j < CH)
        def _():
            there_and_back(j, 0)

        return carry

    lax.fori_loop(0, len(IN_ORDER) - FIRST[-2], forward_and_work, 0)

    def wait_share(i, carry):
        share_copy(i).wait_recv()
        return carry

    lax.fori_loop(0, len(PLACES), wait_share, 0)
    slots = n_fx * 2
    wide = slots * 16
    all_shares = shares[...].reshape(n_fx * 8, 128)
    members = jnp.where(all_shares > 0, 1.0, 0.0).astype(BF)
    spread = (
        lax.broadcasted_iota(jnp.int32, (CH * 16, 128), 0) // 16
        == lax.broadcasted_iota(jnp.int32, (CH * 16, 128), 1)
    )
    spread = jnp.where(spread, 1.0, 0.0).astype(BF)
    by_source = lax.dot_general(
        spread, members, (((1,), (1,)), ((), ())), preferred_element_type=F32
    ).astype(BF)
    weights = lax.dot_general(
        spread, all_shares.astype(BF), (((1,), (1,)), ((), ())), preferred_element_type=F32
    )
    totals = jnp.sum(weights, axis=1, keepdims=True)
    src_row = lax.broadcasted_iota(jnp.int32, (n_fx * 8, wide), 0)
    dst_col = lax.broadcasted_iota(jnp.int32, (n_fx * 8, wide), 1)
    widen = (src_row // 8 == dst_col // 32) & (src_row % 8 == dst_col // 16 % 2)
    widened = dot(by_source, jnp.where(widen, 1.0, 0.0).astype(BF))
    diagonal = (
        lax.broadcasted_iota(jnp.int32, (CH * 16, wide), 0) % 16
        == lax.broadcasted_iota(jnp.int32, (CH * 16, wide), 1) % 16
    )
    kron[...] = jnp.where(diagonal, widened, 0.0).astype(BF)
    scale = 1.0 / (1.0 + totals)

    def group_rows(g):
        return pl.ds(pl.multiple_of(g * 16, 16), 16)

    def without_tiles(g):
        pixels = sky[:, group_rows(g), :].reshape(CH * 16, SIDE)
        there = model[:, group_rows(g), :].reshape(CH * 16, SIDE)
        return pixels - (totals * scale) * there

    def wait_tiles(i, carry):
        landed(arrived.at[2 + i], tile_recv.at[2 + i]).wait_recv()
        return carry

    def with_sources(g, first, last):
        held = arrived[2 * first : 2 * last, group_rows(g), :].reshape((last - first) * 32, SIDE)
        before = without_tiles(g) if first == 0 else partial[g]
        return before + scale * dot(kron[:, first * 32 : last * 32], held)

    for first, last in ((0, 8), (8, 12)):
        lax.fori_loop(max(2 * first - 2, 0), 2 * last - 2, wait_tiles, 0)

        def add_sources(q, carry):
            for i in range(4):
                partial[q * 4 + i] = with_sources(q * 4 + i, first, last)
            return carry

        lax.fori_loop(0, SIDE // 64, add_sources, 0)
    lax.fori_loop(22, 2 * len(PLACES), wait_tiles, 0)

    def combine(g):
        rows = group_rows(g)
        new = with_sources(g, 12, 16).reshape(CH // 2, 2, 16, SIDE)
        made = new.reshape(CH, 16, SIDE).astype(BF)

        @pl.when(g < PART_TALL // 16)
        def _():
            upper[:, rows, :SIDE] = made

        @pl.when(g >= PART // 16)
        def _():
            lower[:, group_rows(g - PART // 16), :SIDE] = made

        low = lax.broadcasted_iota(jnp.int32, (CH // 2, 16, 128), 2) < 64
        second = pltpu.roll(new[:, 1, :, :128].reshape(CH // 2 * 16, 128), 64, 1)
        pair = jnp.where(low, new[:, 0, :, :128], second.reshape(CH // 2, 16, 128))
        columns[:, rows, :] = pair.astype(BF)

    chunks = 4
    deep = SIDE // chunks

    def columns_copy(q):
        rows = pl.ds(pl.multiple_of(q * deep, deep), deep)
        return pltpu.make_async_remote_copy(
            src_ref=columns.at[:, rows, :],
            dst_ref=beside.at[:, rows, :],
            send_sem=columns_send.at[q],
            recv_sem=columns_recv.at[q],
            device_id={"fx": prev},
            device_id_type=pl.DeviceIdType.MESH,
        )

    def halo_copy(i):
        source = (upper.at[:, :HALO, :SIDE], columns.at[:, :HALO, :])[i]
        target = (lower.at[:, PART:, :SIDE], corner)[i]
        where = ({"fy": up}, {"fy": up, "fx": prev})[i]
        return pltpu.make_async_remote_copy(
            src_ref=source,
            dst_ref=target,
            send_sem=halo_send.at[i],
            recv_sem=halo_recv.at[i],
            device_id=where,
            device_id_type=pl.DeviceIdType.MESH,
        )

    def make_chunk(q, carry):
        for i in range(deep // 16):
            combine(q * (deep // 16) + i)
        columns_copy(q).start()

        @pl.when(q == 0)
        def _():
            for i in range(2):
                halo_copy(i).start()

        return carry

    lax.fori_loop(0, chunks, make_chunk, 0)

    def place(source, begin, end):
        for p in range(CH // 2):
            first = source[p]
            second = pltpu.roll(first.astype(F32), 64, 1).astype(BF)
            for target, low, high in ((upper, 0, PART_TALL), (lower, PART, TALL)):
                a, e = max(begin, low), min(end, high)
                if a < e:
                    target[2 * p, a - low : e - low, SIDE:] = first[a - begin : e - begin]
                    target[2 * p + 1, a - low : e - low, SIDE:] = second[a - begin : e - begin]

    halo_copy(1).wait_recv()
    place(corner, SIDE, TALL)
    for q in range(chunks):
        columns_copy(q).wait_recv()
        place(beside.at[:, q * deep : (q + 1) * deep, :], q * deep, (q + 1) * deep)
    halo_copy(0).wait_recv()

    def finish_shares(i, carry):
        share_copy(i).wait_send()
        return carry

    def finish_sent(i, carry):
        for r in range(2):
            hop_copy(sending.at[i, r], tile_send.at[2 * i + r], jnp.int32(0), False).wait_send()
        return carry

    def finish_forwards(f, carry):
        hop_copy(relay.at[f], relay_send.at[f], jnp.int32(0), False).wait_send()
        return carry

    lax.fori_loop(0, len(PLACES), finish_shares, 0)
    lax.fori_loop(0, len(PLACES), finish_sent, 0)
    lax.fori_loop(0, len(IN_ORDER), finish_forwards, 0)
    for i in range(2):
        halo_copy(i).wait_send()
    for q in range(chunks):
        columns_copy(q).wait_send()
    for copy in thr_copies:
        copy.wait()


def passed(value, axes, to):
    sizes = [lax.axis_size(a) for a in axes]
    pairs = []
    for i in np.ndindex(*sizes):
        j = [(a + b) % n for a, b, n in zip(i, to, sizes)]
        pairs.append((int(np.ravel_multi_index(i, sizes)), int(np.ravel_multi_index(j, sizes))))
    return lax.ppermute(value, axes if len(axes) > 1 else axes[0], pairs)


def first_half(shape):
    return lax.broadcasted_iota(jnp.int32, shape, len(shape) - 1) < 64


def pack_kernel(upper, lower, right, corner, below, side_up, side_low, bottom, sem):
    loads = [
        pltpu.make_async_copy(upper.at[:, :, SIDE:], side_up, sem.at[0]),
        pltpu.make_async_copy(lower.at[:, :, SIDE:], side_low, sem.at[1]),
        pltpu.make_async_copy(lower.at[:, PART:, :SIDE], bottom, sem.at[2]),
    ]
    for load in loads:
        load.start()
    for load in loads:
        load.wait()

    def pair(side, p, begin, end):
        first, second = side[2 * p, begin:end], side[2 * p + 1, begin:end]
        return jnp.where(first_half(first.shape), first, second)

    for p in range(CH // 2):
        right[p, :PART] = pair(side_up, p, 0, PART).astype(BF)
        shared = pair(side_up, p, PART, PART_TALL) + pair(side_low, p, 0, HALO)
        right[p, PART:PART_TALL] = shared.astype(BF)
        right[p, PART_TALL:] = pair(side_low, p, HALO, PART).astype(BF)
        corner[p] = pair(side_low, p, PART, PART_TALL).astype(BF)
    below[...] = bottom[...].astype(BF)


def add_kernel(upper, lower, left, above, corner, out):
    for h in range(2):

        def columns(pairs):
            pairs = pairs.astype(F32)
            if h == 1:
                pairs = pltpu.roll(pairs, 64, 1)
            return jnp.where(first_half(pairs.shape), pairs, 0.0)

        def finished(total):
            return jnp.maximum(total * (1.0 / BASES), 0.0)

        from_left = columns(left[0])
        from_above = above[h].astype(F32)
        first = from_left[:HALO] + from_above[:, :128] + columns(corner[0])
        out[h, :HALO, :128] = finished(upper[h, :HALO, :128] + first)
        out[h, :HALO, 128:] = finished(upper[h, :HALO, 128:] + from_above[:, 128:])
        for lanes in (slice(0, 128), slice(128, SIDE)):

            def more(begin, end):
                return from_left[begin:end] if lanes.start == 0 else 0.0

            out[h, HALO:PART, lanes] = finished(upper[h, HALO:PART, lanes] + more(HALO, PART))
            shared = upper[h, PART:PART_TALL, lanes] + lower[h, :HALO, lanes]
            out[h, PART:PART_TALL, lanes] = finished(shared + more(PART, PART_TALL))
            out[h, PART_TALL:, lanes] = finished(
                lower[h, HALO:PART, lanes] + more(PART_TALL, SIDE)
            )


def per_device(n_fy, n_fx, sky_image, vis_tiles, tile_dest, tile_chan, tile_count, thresholds):
    made = {name: jnp.asarray(table) for name, table in tables().items()}
    smem = pl.BlockSpec(memory_space=pltpu.SMEM)
    vmem = pl.BlockSpec(memory_space=pltpu.VMEM)
    anywhere = pl.BlockSpec(memory_space=pl.ANY)
    dma = pltpu.SemaphoreType.DMA
    tiles = vis_tiles.shape[0]
    upper, lower, thr_upper, thr_lower = pl.pallas_call(
        functools.partial(exchange_kernel, n_fy, n_fx),
        out_shape=(
            pltpu.VMEM((CH, PART_TALL, WIDE), BF),
            pltpu.VMEM((CH, PART_TALL, WIDE), BF),
            pltpu.HBM((BASES, CH, PART, SIDE), BF),
            pltpu.HBM((BASES, CH, PART, SIDE), BF),
        ),
        in_specs=[smem] * 3 + [vmem] * 3 + [anywhere] * 3,
        scratch_shapes=[
            pltpu.VMEM((tiles, 2, SIDE, SIDE), BF),
            pltpu.VMEM((CH, SIDE, SIDE), F32),
            pltpu.VMEM((CH, SIDE, SIDE), F32),
            pltpu.VMEM((SIDE // 16, CH * 16, SIDE), F32),
            pltpu.VMEM((n_fx, 2, SIDE, SIDE), BF),
            pltpu.VMEM((2 * n_fx, SIDE, SIDE), BF),
            pltpu.VMEM((len(IN_ORDER), SIDE, SIDE), BF),
            pltpu.VMEM((2, 2 * SIDE, SIDE), BF),
            pltpu.VMEM((n_fx, 8, 128), F32),
            pltpu.VMEM((n_fx, 8, 128), F32),
            pltpu.VMEM((CH * 16, n_fx * 32), BF),
            pltpu.VMEM((CH // 2, SIDE, 128), BF),
            pltpu.VMEM((CH // 2, SIDE, 128), BF),
            pltpu.VMEM((CH // 2, HALO, 128), BF),
            dma((2,)),
            dma((2 * len(PLACES),)),
            dma((2 * n_fx,)),
            dma((len(IN_ORDER),)),
            dma((len(IN_ORDER),)),
            dma((n_fx,)),
            dma((n_fx,)),
            dma((2,)),
            dma((2,)),
            dma((4,)),
            dma((4,)),
            dma((6,)),
        ],
        compiler_params=pltpu.CompilerParams(
            collective_id=0, has_side_effects=True, vmem_limit_bytes=58 * 1024 * 1024
        ),
    )(
        tile_dest.reshape(tiles),
        tile_chan,
        tile_count,
        made["fourier"],
        made["back"],
        made["excess"],
        sky_image,
        vis_tiles,
        thresholds,
    )
    rows, columns, spread = made["rows"], made["columns"], made["spread"]
    cells = []
    for near, limits in ((upper, thr_upper), (lower, thr_lower)):
        row_sec = jnp.einsum("bjy,cyx->bcjx", rows, near, preferred_element_type=F32).astype(BF)
        coefficient = jnp.einsum("bcjx,bkx->bcjk", row_sec, columns, preferred_element_type=F32)
        limits = limits.astype(F32)
        shrunk = (coefficient - jnp.clip(coefficient, -limits, limits)).astype(BF)
        col_sec = jnp.einsum("bcjk,bkx->bcjx", shrunk, spread, preferred_element_type=F32)
        cells.append(
            jnp.einsum("bjy,bcjx->cyx", rows, col_sec.astype(BF), preferred_element_type=F32)
        )
    right, corner, below = pl.pallas_call(
        pack_kernel,
        out_shape=(
            jax.ShapeDtypeStruct((CH // 2, SIDE, 128), BF),
            jax.ShapeDtypeStruct((CH // 2, HALO, 128), BF),
            jax.ShapeDtypeStruct((CH, HALO, SIDE), BF),
        ),
        in_specs=[pl.BlockSpec(memory_space=pltpu.HBM)] * 2,
        out_specs=[vmem] * 3,
        scratch_shapes=[
            pltpu.VMEM((CH, PART_TALL, 128), F32),
            pltpu.VMEM((CH, PART_TALL, 128), F32),
            pltpu.VMEM((CH, HALO, SIDE), F32),
            dma((3,)),
        ],
        compiler_params=pltpu.CompilerParams(vmem_limit_bytes=58 * 1024 * 1024),
    )(*cells)
    left = passed(right, ("fx",), (1,))
    above = passed(below, ("fy",), (1,))
    corner = passed(corner, ("fy", "fx"), (1, 1))
    return pl.pallas_call(
        add_kernel,
        out_shape=jax.ShapeDtypeStruct((CH, SIDE, SIDE), F32),
        grid=(CH // 2,),
        in_specs=[
            pl.BlockSpec((2, PART_TALL, SIDE), lambda p: (p, 0, 0)),
            pl.BlockSpec((2, PART_TALL, SIDE), lambda p: (p, 0, 0)),
            pl.BlockSpec((1, SIDE, 128), lambda p: (p, 0, 0)),
            pl.BlockSpec((2, HALO, SIDE), lambda p: (p, 0, 0)),
            pl.BlockSpec((1, HALO, 128), lambda p: (p, 0, 0)),
        ],
        out_specs=pl.BlockSpec((2, SIDE, SIDE), lambda p: (p, 0, 0)),
        compiler_params=pltpu.CompilerParams(vmem_limit_bytes=16 * 1024 * 1024),
    )(*cells, left, above, corner)


def solution(mesh):
    in_specs = (
        P(None, "fy", "fx"),
        P(("fy", "fx"), None, None, None),
        P(("fy", "fx"), None),
        P(("fy", "fx")),
        P(("fy", "fx")),
        P(None, None, "fy", "fx"),
    )
    out_specs = P(None, "fy", "fx")
    return jax.shard_map(
        functools.partial(per_device, mesh.shape["fy"], mesh.shape["fx"]),
        mesh=mesh,
        in_specs=in_specs,
        out_specs=out_specs,
        check_vma=False,
    )
```

```python
import functools
import math

import jax
import jax.numpy as jnp
import ml_dtypes
import numpy as np
from jax import lax
from jax.experimental import pallas as pl
from jax.experimental.pallas import tpu as pltpu
from jax.sharding import PartitionSpec as P

daubechies_taps = [
    [0.7071067811865476, 0.7071067811865476],
    [0.48296291314469025, 0.836516303737469, 0.22414386804185735, -0.12940952255092145],
    [
        0.3326705529509569,
        0.8068915093133388,
        0.4598775021193313,
        -0.13501102001039084,
        -0.08544127388224149,
        0.035226291882100656,
    ],
    [
        0.23037781330885523,
        0.7148465705525415,
        0.6308807679295904,
        -0.02798376941698385,
        -0.18703481171888114,
        0.030841381835986965,
        0.032883011666982945,
        -0.010597401784997278,
    ],
    [
        0.160102397974125,
        0.6038292697974729,
        0.7243085284385744,
        0.13842814590110342,
        -0.24229488706619015,
        -0.03224486958502952,
        0.07757149384006515,
        -0.006241490213011705,
        -0.012580751999015526,
        0.003335725285001549,
    ],
    [
        0.11154074335008017,
        0.4946238903983854,
        0.7511339080215775,
        0.3152503517092432,
        -0.22626469396516913,
        -0.12976686756709563,
        0.09750160558707936,
        0.02752286553001629,
        -0.031582039318031156,
        0.0005538422009938016,
        0.004777257511010651,
        -0.00107730108499558,
    ],
    [
        0.07785205408506236,
        0.39653931948230575,
        0.7291320908465551,
        0.4697822874053586,
        -0.14390600392910627,
        -0.22403618499416572,
        0.07130921926705004,
        0.0806126091510659,
        -0.03802993693503463,
        -0.01657454163101562,
        0.012550998556013784,
        0.00042957797300470274,
        -0.0018016407039998328,
        0.0003537138000010399,
    ],
    [
        0.05441584224308161,
        0.3128715909144659,
        0.6756307362980128,
        0.5853546836548691,
        -0.015829105256023893,
        -0.2840155429624281,
        0.00047248457399797254,
        0.128747426620186,
        -0.01736930100202211,
        -0.04408825393106472,
        0.013981027917015516,
        0.008746094047015655,
        -0.00487035299301066,
        -0.0003917403729959771,
        0.0006754494059985568,
        -0.00011747678400228192,
    ],
]


SIDE = 256
CH = 8
BASES = 8
HALO = 48
BF = jnp.bfloat16
F32 = jnp.float32
WIDE = SIDE + 128
TALL = SIDE + HALO
REACH = 42
PACKS = 3


def rounded(table):
    return np.asarray(table, np.float32).astype(ml_dtypes.bfloat16)


def composite_tables():
    full = np.zeros((BASES, SIDE, SIDE + HALO))
    for degree in range(1, 9):
        taps = np.array(daubechies_taps[degree - 1])
        taps = taps * math.sqrt(2.0) / np.sum(taps)
        length = 2 * degree
        low = np.zeros(16)
        high = np.zeros(16)
        low[:length] = taps
        high[:length] = [(-1.0) ** j * taps[length - 1 - j] for j in range(length)]
        low = rounded(low).astype(np.float64)
        high = rounded(high).astype(np.float64)
        level_low = np.zeros((144, SIDE + HALO))
        level_high = np.zeros((128, SIDE + HALO))
        for k in range(144):
            level_low[k, 2 * k : 2 * k + 16] = low[: min(16, SIDE + HALO - 2 * k)]
        for k in range(128):
            level_high[k, 2 * k : 2 * k + 16] = high
        second = np.zeros((128, 144))
        for m in range(64):
            second[m, 2 * m : 2 * m + 16] = low
            second[64 + m, 2 * m : 2 * m + 16] = high
        full[degree - 1, :128] = second @ level_low
        full[degree - 1, 128:] = level_high
    return rounded(full).astype(np.float32)


@functools.lru_cache(maxsize=1)
def tables():
    full = composite_tables()
    wide = np.concatenate([full, np.zeros((BASES, SIDE, 128 - HALO), np.float32)], axis=2)
    assert not np.any(full[:, :, SIDE + REACH :])
    spread = wide.copy()
    for m in range(1, 3):
        at = SIDE + m * REACH
        spread[:, :, at : at + REACH] = full[:, :, SIDE : SIDE + REACH]
    out = {"rows": full, "columns": wide, "spread": spread}
    grid = np.arange(SIDE)[:, None] * np.arange(SIDE)[None, :] % SIDE
    angle = grid * (2.0 * math.pi / SIDE)
    cosine = rounded(np.cos(angle) / math.sqrt(SIDE)).astype(np.float64)
    sine = rounded(np.sin(angle) / math.sqrt(SIDE)).astype(np.float64)
    out["fourier"] = np.block([[cosine, sine], [-sine, cosine]])
    out["back"] = np.concatenate([cosine, -sine], axis=1)
    out["excess"] = cosine @ cosine + sine @ sine - np.eye(SIDE)
    return {name: rounded(table) for name, table in out.items()}


PLACES = (
    (2, 2),
    (1, 2),
    (3, 3),
    (3, 2),
    (3, 1),
    (2, 1),
    (2, 3),
    (1, 1),
    (0, 3),
    (1, 3),
    (0, 2),
    (0, 1),
    (1, 0),
    (2, 0),
    (3, 0),
)
STEP_X, STEP_Z = (1, 3, 0, 0), (0, 0, 1, 3)
PATHS = (
    (
        (3, 0, 0, 3),
        (2, 0, 2),
        (1, 3),
        (1, 3, 3),
        (2, 1),
        (2, 1, 1),
        (1, 1, 3),
        (0, 2),
        (3,),
        (0, 3),
        (3, 3),
        (2,),
        (0,),
        (0, 0),
        (1,),
    ),
    (
        (1, 2, 2, 1),
        (0, 2, 2),
        (3, 1),
        (3, 3, 1),
        (1, 2),
        (0, 2, 0),
        (0, 0, 3),
        (0, 2),
        (3,),
        (3, 0),
        (2, 2),
        (2,),
        (0,),
        (1, 1),
        (1,),
    ),
)
FORWARDS = (
    (),
    (),
    ((0, 0, 1), (0, 1, 1)),
    ((1, 0, 1), (1, 1, 1)),
    ((2, 0, 1), (2, 1, 1)),
    ((0, 0, 2), (0, 1, 2)),
    ((3, 0, 1), (3, 1, 1), (1, 0, 2), (1, 1, 2)),
    ((4, 1, 1), (4, 0, 1), (5, 1, 1)),
    ((3, 0, 2),),
    ((0, 0, 3), (5, 0, 1)),
    ((3, 1, 2), (6, 0, 1), (0, 1, 3), (6, 1, 1)),
    (),
    ((7, 0, 1),),
    ((5, 0, 2), (7, 1, 1)),
    ((9, 0, 1),),
    ((6, 0, 2), (9, 1, 1), (5, 1, 2), (6, 1, 2), (10, 1, 1), (10, 0, 1), (13, 1, 1), (13, 0, 1)),
)
COMING = (2, 8, 1, 3, 4, 0, 12, 11, 9, 6, 14, 5, 7, 10, 13)

IN_ORDER = [hop for step in FORWARDS for hop in step]
FIRST = [sum(len(step) for step in FORWARDS[:i]) for i in range(len(FORWARDS) + 1)]
RANK = [COMING.index(i) for i in range(len(PLACES))]


def coded(place, r, hop):
    steps = PATHS[r][place]
    if hop + 1 == len(steps):
        return steps[hop] + 4 + 8 * (2 * (1 + RANK[place]) + r)
    return steps[hop] + 8 * IN_ORDER.index((place, r, hop + 1))


START = [[coded(place, r, 0) for place in range(len(PLACES))] for r in range(2)]
ONWARD = [coded(*hop) for hop in IN_ORDER]
assert len(IN_ORDER) == sum(len(p) - 1 for r in range(2) for p in PATHS[r])
assert len(IN_ORDER) - FIRST[-2] > CH // 2


def choose(j, values):
    out = jnp.int32(values[0])
    for i, value in enumerate(values):
        out = jnp.where(j == i, jnp.int32(value), out)
    return out


def three_beside(first, second, third):
    lane = lax.broadcasted_iota(jnp.int32, first.shape, len(first.shape) - 1)
    return jnp.where(lane < REACH, first, jnp.where(lane < 2 * REACH, second, third))


def turned(values, m):
    return pltpu.roll(values, 128 - m * REACH, 1) if m else values


def dot(a, b):
    return jnp.dot(a, b, preferred_element_type=F32)


def exchange_kernel(
    n_fy,
    n_fx,
    dest_ref,
    chan_ref,
    count_ref,
    fourier_hbm,
    back_hbm,
    excess_hbm,
    sky_hbm,
    vis_hbm,
    extended,
    fourier,
    back,
    excess,
    vis,
    sky,
    model,
    partial,
    sending,
    arrived,
    relay,
    half,
    share_ref,
    shares,
    kron,
    columns,
    beside,
    corner,
    load_sem,
    tile_send,
    tile_recv,
    relay_send,
    relay_recv,
    share_send,
    share_recv,
    halo_send,
    halo_recv,
    columns_send,
    columns_recv,
):
    fy = lax.axis_index("fy")
    fx = lax.axis_index("fx")
    n_z = 4
    n_x = n_fx // n_z
    my_x, my_z = fx // n_z, fx % n_z

    def at(dx, dz):
        return (my_x + dx) % n_x * n_z + (my_z + dz) % n_z

    def peer(k):
        return at(k // n_z, k % n_z)

    load_vis = pltpu.make_async_copy(vis_hbm, vis, load_sem.at[0])
    load_sky = pltpu.make_async_copy(sky_hbm, sky, load_sem.at[1])
    load_vis.start()
    load_fourier = pltpu.make_async_copy(fourier_hbm, fourier, load_sem.at[2])
    load_back = pltpu.make_async_copy(back_hbm, back, load_sem.at[3])
    load_excess = pltpu.make_async_copy(excess_hbm, excess, load_sem.at[4])
    load_fourier.start()
    load_back.start()
    load_excess.start()
    load_sky.start()

    barrier = pltpu.get_barrier_semaphore()

    def greet(k, carry):
        pl.semaphore_signal(
            barrier, inc=1, device_id={"fx": peer(k)}, device_id_type=pl.DeviceIdType.MESH
        )
        return carry

    lax.fori_loop(1, n_fx, greet, 0)
    up, down = (fy + n_fy - 1) % n_fy, (fy + 1) % n_fy
    prev, nxt = (fx + n_fx - 1) % n_fx, (fx + 1) % n_fx
    for where in ({"fy": up}, {"fy": down}, {"fy": up, "fx": prev}, {"fy": down, "fx": nxt}):
        pl.semaphore_signal(barrier, inc=1, device_id=where, device_id_type=pl.DeviceIdType.MESH)

    def place_of(i):
        return at(choose(i, [p[0] for p in PLACES]), choose(i, [p[1] for p in PLACES]))

    def share_copy(i):
        rank = 1 + choose(i, RANK)
        return pltpu.make_async_remote_copy(
            src_ref=share_ref.at[rank],
            dst_ref=shares.at[rank],
            send_sem=share_send.at[rank],
            recv_sem=share_recv.at[rank],
            device_id={"fx": place_of(i)},
            device_id_type=pl.DeviceIdType.MESH,
        )

    def hop_copy(source, send_sem, code, last):
        step, to = code % 4, code // 8
        return pltpu.make_async_remote_copy(
            src_ref=source,
            dst_ref=arrived.at[to] if last else relay.at[to],
            send_sem=send_sem,
            recv_sem=tile_recv.at[to] if last else relay_recv.at[to],
            device_id={"fx": at(choose(step, STEP_X), choose(step, STEP_Z))},
            device_id_type=pl.DeviceIdType.MESH,
        )

    def hop_start(source, send_sem, code):
        @pl.when(code // 4 % 2 == 1)
        def _():
            hop_copy(source, send_sem, code, True).start()

        @pl.when(code // 4 % 2 == 0)
        def _():
            hop_copy(source, send_sem, code, False).start()

    def landed(buffer, sem):
        return pltpu.make_async_remote_copy(
            src_ref=buffer,
            dst_ref=buffer,
            send_sem=tile_send.at[0],
            recv_sem=sem,
            device_id={"fx": at(1, 0)},
            device_id_type=pl.DeviceIdType.MESH,
        )

    def forward(f, carry):
        landed(relay.at[f], relay_recv.at[f]).wait_recv()
        hop_start(relay.at[f], relay_send.at[f], choose(f, ONWARD))
        return carry

    tiles = vis_hbm.shape[0]
    row = lax.broadcasted_iota(jnp.int32, (8, 128), 0)
    lane = lax.broadcasted_iota(jnp.int32, (8, 128), 1)

    def slots_for(to):
        found = jnp.int32(0)
        picked = [(jnp.int32(0), jnp.int32(0), jnp.int32(0))] * 2
        for i in range(tiles):
            match = dest_ref[i] == to
            for r in range(2):
                here = match & (found == r)
                new = (jnp.int32(i), count_ref[i], chan_ref[i])
                picked[r] = tuple(jnp.where(here, a, b) for a, b in zip(new, picked[r]))
            found = found + jnp.where(match, 1, 0)
        return [(tile, count.astype(F32) * (1.0 / 64.0), chan) for tile, count, chan in picked]

    def share_rows(slots):
        total = jnp.zeros((8, 128), F32)
        for r, (_, weight, chan) in enumerate(slots):
            total = total + jnp.where((row == r) & (lane == chan), weight, 0.0)
        return total

    load_fourier.wait()
    load_back.wait()
    load_vis.wait()

    def planes(slots):
        for i, (t, _, _) in enumerate(slots):
            spectrum = jnp.concatenate([vis[t, 0], vis[t, 1]], axis=1)
            for part in range(2):
                half[i, part * SIDE : (part + 1) * SIDE] = dot(
                    spectrum, fourier[:, part * SIDE : (part + 1) * SIDE]
                ).astype(BF)
        return [(dot(back[...], half[i]) * slots[i][1]).astype(BF) for i in range(2)]

    def prepare(i):
        slots = slots_for(place_of(i))
        share_ref[1 + choose(i, RANK)] = share_rows(slots)
        sending[i, 0], sending[i, 1] = planes(slots)

    prepare(jnp.int32(0))
    pl.semaphore_wait(barrier, n_fx - 1 + 4)

    def send_tiles(i, carry):
        share_copy(i).start()
        for r in range(2):
            hop_start(sending.at[i, r], tile_send.at[2 * i + r], choose(i, START[r]))
        lax.fori_loop(choose(i, FIRST), choose(i + 1, FIRST), forward, 0)

        @pl.when(i < len(PLACES) - 1)
        def _():
            prepare(i + 1)

        return carry

    lax.fori_loop(0, len(PLACES), send_tiles, 0)

    load_sky.wait()
    load_excess.wait()

    def there_and_back(c):
        pixels = jnp.concatenate([sky[c].astype(BF), sky[c + 1].astype(BF)], axis=1)
        once = pixels.astype(F32) + dot(excess[...], pixels)
        once = jnp.concatenate([once[:, :SIDE], once[:, SIDE:]], axis=0)
        both = once + dot(once.astype(BF), excess[...])
        model[c] = both[:SIDE]
        model[c + 1] = both[SIDE:]

    def forward_and_work(j, carry):
        forward(FIRST[-2] + j, 0)

        @pl.when(j == 0)
        def _():
            own = slots_for(fx)
            shares[0] = share_rows(own)
            arrived[0], arrived[1] = planes(own)

        @pl.when((j >= 1) & (j <= CH // 2))
        def _():
            there_and_back(2 * (j - 1))

        return carry

    lax.fori_loop(0, len(IN_ORDER) - FIRST[-2], forward_and_work, 0)

    def wait_share(i, carry):
        share_copy(i).wait_recv()
        return carry

    lax.fori_loop(0, len(PLACES), wait_share, 0)
    slots = n_fx * 2
    wide = slots * 16
    all_shares = shares[...].reshape(n_fx * 8, 128)
    members = jnp.where(all_shares > 0, 1.0, 0.0).astype(BF)
    spread = (
        lax.broadcasted_iota(jnp.int32, (CH * 16, 128), 0) // 16
        == lax.broadcasted_iota(jnp.int32, (CH * 16, 128), 1)
    )
    spread = jnp.where(spread, 1.0, 0.0).astype(BF)
    by_source = lax.dot_general(
        spread, members, (((1,), (1,)), ((), ())), preferred_element_type=F32
    ).astype(BF)
    weights = lax.dot_general(
        spread, all_shares.astype(BF), (((1,), (1,)), ((), ())), preferred_element_type=F32
    )
    totals = jnp.sum(weights, axis=1, keepdims=True)
    src_row = lax.broadcasted_iota(jnp.int32, (n_fx * 8, wide), 0)
    dst_col = lax.broadcasted_iota(jnp.int32, (n_fx * 8, wide), 1)
    widen = (src_row // 8 == dst_col // 32) & (src_row % 8 == dst_col // 16 % 2)
    widened = dot(by_source, jnp.where(widen, 1.0, 0.0).astype(BF))
    diagonal = (
        lax.broadcasted_iota(jnp.int32, (CH * 16, wide), 0) % 16
        == lax.broadcasted_iota(jnp.int32, (CH * 16, wide), 1) % 16
    )
    kron[...] = jnp.where(diagonal, widened, 0.0).astype(BF)
    scale = 1.0 / (1.0 + totals)

    def group_rows(g):
        return pl.ds(pl.multiple_of(g * 16, 16), 16)

    def without_tiles(g):
        pixels = sky[:, group_rows(g), :].reshape(CH * 16, SIDE)
        there = model[:, group_rows(g), :].reshape(CH * 16, SIDE)
        return pixels - (totals * scale) * there

    def wait_tiles(i, carry):
        landed(arrived.at[2 + i], tile_recv.at[2 + i]).wait_recv()
        return carry

    def with_sources(g, first, last):
        held = arrived[2 * first : 2 * last, group_rows(g), :].reshape((last - first) * 32, SIDE)
        before = without_tiles(g) if first == 0 else partial[g]
        return before + scale * dot(kron[:, first * 32 : last * 32], held)

    for first, last in ((0, 8), (8, 12)):
        lax.fori_loop(max(2 * first - 2, 0), 2 * last - 2, wait_tiles, 0)

        def add_sources(q, carry):
            for i in range(4):
                partial[q * 4 + i] = with_sources(q * 4 + i, first, last)
            return carry

        lax.fori_loop(0, SIDE // 64, add_sources, 0)
    lax.fori_loop(22, 2 * len(PLACES), wait_tiles, 0)

    def combine(g):
        rows = group_rows(g)
        new = with_sources(g, 12, 16).reshape(CH, 16, SIDE)
        extended[:, rows, :SIDE] = new.astype(BF)
        for k in range(PACKS):
            parts = [new[min(3 * k + m, CH - 1), :, :128] for m in range(3)]
            parts = [pltpu.roll(part, m * REACH, 1) if m else part for m, part in enumerate(parts)]
            columns[k, rows, :] = three_beside(*parts).astype(BF)

    chunks = 4
    deep = SIDE // chunks

    def columns_copy(q):
        rows = pl.ds(pl.multiple_of(q * deep, deep), deep)
        return pltpu.make_async_remote_copy(
            src_ref=columns.at[:, rows, :],
            dst_ref=beside.at[:, rows, :],
            send_sem=columns_send.at[q],
            recv_sem=columns_recv.at[q],
            device_id={"fx": prev},
            device_id_type=pl.DeviceIdType.MESH,
        )

    def halo_copy(i):
        source = (extended.at[:, :HALO, :SIDE], columns.at[:, :HALO, :])[i]
        target = (extended.at[:, SIDE:, :SIDE], corner)[i]
        where = ({"fy": up}, {"fy": up, "fx": prev})[i]
        return pltpu.make_async_remote_copy(
            src_ref=source,
            dst_ref=target,
            send_sem=halo_send.at[i],
            recv_sem=halo_recv.at[i],
            device_id=where,
            device_id_type=pl.DeviceIdType.MESH,
        )

    def make_chunk(q, carry):
        for i in range(deep // 16):
            combine(q * (deep // 16) + i)
        columns_copy(q).start()

        @pl.when(q == 0)
        def _():
            for i in range(2):
                halo_copy(i).start()

        return carry

    lax.fori_loop(0, chunks, make_chunk, 0)

    def place(source, begin, end):
        for c in range(CH):
            values = turned(source[c // 3].astype(F32), c % 3)
            extended[c, begin:end, SIDE:] = values.astype(BF)

    halo_copy(1).wait_recv()
    place(corner, SIDE, TALL)
    for q in range(chunks):
        columns_copy(q).wait_recv()
        place(beside.at[:, q * deep : (q + 1) * deep, :], q * deep, (q + 1) * deep)
    halo_copy(0).wait_recv()

    def finish_shares(i, carry):
        share_copy(i).wait_send()
        return carry

    def finish_sent(i, carry):
        for r in range(2):
            hop_copy(sending.at[i, r], tile_send.at[2 * i + r], jnp.int32(0), False).wait_send()
        return carry

    def finish_forwards(f, carry):
        hop_copy(relay.at[f], relay_send.at[f], jnp.int32(0), False).wait_send()
        return carry

    lax.fori_loop(0, len(PLACES), finish_shares, 0)
    lax.fori_loop(0, len(PLACES), finish_sent, 0)
    lax.fori_loop(0, len(IN_ORDER), finish_forwards, 0)
    for i in range(2):
        halo_copy(i).wait_send()
    for q in range(chunks):
        columns_copy(q).wait_send()


def passed(value, axes, to):
    sizes = [lax.axis_size(a) for a in axes]
    pairs = []
    for i in np.ndindex(*sizes):
        j = [(a + b) % n for a, b, n in zip(i, to, sizes)]
        pairs.append((int(np.ravel_multi_index(i, sizes)), int(np.ravel_multi_index(j, sizes))))
    return lax.ppermute(value, axes if len(axes) > 1 else axes[0], pairs)


def pack_kernel(cells, right, corner, below, side, bottom, sem):
    load_side = pltpu.make_async_copy(cells.at[:, :, SIDE:], side, sem.at[0])
    load_bottom = pltpu.make_async_copy(cells.at[:, SIDE:, :SIDE], bottom, sem.at[1])
    load_side.start()
    load_bottom.start()
    load_side.wait()
    for k in range(PACKS):
        packed = three_beside(*[side[min(3 * k + m, CH - 1)] for m in range(3)]).astype(BF)
        right[k] = packed[:SIDE]
        corner[k] = packed[SIDE:]
    load_bottom.wait()
    below[...] = bottom[...].astype(BF)


def add_kernel(cells, left, above, corner, out):
    for h in range(2):

        channel = 2 * pl.program_id(0) + h

        def columns(packed):
            values = packed[channel // 3].astype(F32)
            for m in range(1, 3):
                values = jnp.where(channel % 3 == m, turned(packed[channel // 3].astype(F32), m), values)
            lane = lax.broadcasted_iota(jnp.int32, values.shape, 1)
            return jnp.where(lane < REACH, values, 0.0)

        def finished(total):
            return jnp.maximum(total * (1.0 / BASES), 0.0)

        from_left = columns(left)
        from_above = above[h].astype(F32)
        first = from_left[:HALO] + from_above[:, :128] + columns(corner)
        out[h, :HALO, :128] = finished(cells[h, :HALO, :128] + first)
        out[h, :HALO, 128:] = finished(cells[h, :HALO, 128:] + from_above[:, 128:])
        out[h, HALO:, :128] = finished(cells[h, HALO:, :128] + from_left[HALO:])
        out[h, HALO:, 128:] = finished(cells[h, HALO:, 128:])


def per_device(n_fy, n_fx, sky_image, vis_tiles, tile_dest, tile_chan, tile_count, thresholds):
    made = {name: jnp.asarray(table) for name, table in tables().items()}
    smem = pl.BlockSpec(memory_space=pltpu.SMEM)
    vmem = pl.BlockSpec(memory_space=pltpu.VMEM)
    anywhere = pl.BlockSpec(memory_space=pl.ANY)
    dma = pltpu.SemaphoreType.DMA
    tiles = vis_tiles.shape[0]
    extended = pl.pallas_call(
        functools.partial(exchange_kernel, n_fy, n_fx),
        out_shape=pltpu.VMEM((CH, TALL, WIDE), BF),
        in_specs=[smem] * 3 + [anywhere] * 5,
        scratch_shapes=[
            pltpu.VMEM((2 * SIDE, 2 * SIDE), BF),
            pltpu.VMEM((SIDE, 2 * SIDE), BF),
            pltpu.VMEM((SIDE, SIDE), BF),
            pltpu.VMEM((tiles, 2, SIDE, SIDE), BF),
            pltpu.VMEM((CH, SIDE, SIDE), F32),
            pltpu.VMEM((CH, SIDE, SIDE), F32),
            pltpu.VMEM((SIDE // 16, CH * 16, SIDE), F32),
            pltpu.VMEM((n_fx, 2, SIDE, SIDE), BF),
            pltpu.VMEM((2 * n_fx, SIDE, SIDE), BF),
            pltpu.VMEM((len(IN_ORDER), SIDE, SIDE), BF),
            pltpu.VMEM((2, 2 * SIDE, SIDE), BF),
            pltpu.VMEM((n_fx, 8, 128), F32),
            pltpu.VMEM((n_fx, 8, 128), F32),
            pltpu.VMEM((CH * 16, n_fx * 32), BF),
            pltpu.VMEM((PACKS, SIDE, 128), BF),
            pltpu.VMEM((PACKS, SIDE, 128), BF),
            pltpu.VMEM((PACKS, HALO, 128), BF),
            dma((5,)),
            dma((2 * len(PLACES),)),
            dma((2 * n_fx,)),
            dma((len(IN_ORDER),)),
            dma((len(IN_ORDER),)),
            dma((n_fx,)),
            dma((n_fx,)),
            dma((2,)),
            dma((2,)),
            dma((4,)),
            dma((4,)),
        ],
        compiler_params=pltpu.CompilerParams(
            collective_id=0, has_side_effects=True, vmem_limit_bytes=58 * 1024 * 1024
        ),
    )(
        tile_dest.reshape(tiles),
        tile_chan,
        tile_count,
        made["fourier"],
        made["back"],
        made["excess"],
        sky_image,
        vis_tiles,
    )
    rows, columns = made["rows"], made["columns"]
    row_sec = jnp.einsum("bkn,cnx->bckx", rows, extended, preferred_element_type=F32).astype(BF)
    coefficient = jnp.einsum("bcyx,bkx->bcyk", row_sec, columns, preferred_element_type=F32)
    limits = thresholds.astype(F32)
    shrunk = (coefficient - jnp.clip(coefficient, -limits, limits)).astype(BF)
    row_sec = jnp.einsum("bjy,bcjk->bcyk", rows, shrunk, preferred_element_type=F32).astype(BF)
    cells = jnp.einsum("bcyk,bkx->cyx", row_sec, made["spread"], preferred_element_type=F32)
    right, corner, below = pl.pallas_call(
        pack_kernel,
        out_shape=(
            jax.ShapeDtypeStruct((PACKS, SIDE, 128), BF),
            jax.ShapeDtypeStruct((PACKS, HALO, 128), BF),
            jax.ShapeDtypeStruct((CH, HALO, SIDE), BF),
        ),
        in_specs=[anywhere],
        out_specs=[vmem] * 3,
        scratch_shapes=[
            pltpu.VMEM((CH, TALL, 128), F32),
            pltpu.VMEM((CH, HALO, SIDE), F32),
            dma((2,)),
        ],
        compiler_params=pltpu.CompilerParams(vmem_limit_bytes=16 * 1024 * 1024),
    )(cells)
    left = passed(right, ("fx",), (1,))
    above = passed(below, ("fy",), (1,))
    corner = passed(corner, ("fy", "fx"), (1, 1))
    return pl.pallas_call(
        add_kernel,
        out_shape=jax.ShapeDtypeStruct((CH, SIDE, SIDE), F32),
        grid=(CH // 2,),
        in_specs=[
            pl.BlockSpec((2, SIDE, SIDE), lambda p: (p, 0, 0)),
            pl.BlockSpec((PACKS, SIDE, 128), lambda p: (0, 0, 0)),
            pl.BlockSpec((2, HALO, SIDE), lambda p: (p, 0, 0)),
            pl.BlockSpec((PACKS, HALO, 128), lambda p: (0, 0, 0)),
        ],
        out_specs=pl.BlockSpec((2, SIDE, SIDE), lambda p: (p, 0, 0)),
        compiler_params=pltpu.CompilerParams(vmem_limit_bytes=16 * 1024 * 1024),
    )(cells, left, above, corner)


def solution(mesh):
    in_specs = (
        P(None, "fy", "fx"),
        P(("fy", "fx"), None, None, None),
        P(("fy", "fx"), None),
        P(("fy", "fx")),
        P(("fy", "fx")),
        P(None, None, "fy", "fx"),
    )
    out_specs = P(None, "fy", "fx")
    return jax.shard_map(
        functools.partial(per_device, mesh.shape["fy"], mesh.shape["fx"]),
        mesh=mesh,
        in_specs=in_specs,
        out_specs=out_specs,
        check_vma=False,
    )
```

```python
import functools
import math

import jax
import jax.numpy as jnp
import ml_dtypes
import numpy as np
from jax import lax
from jax.experimental import pallas as pl
from jax.experimental.pallas import tpu as pltpu
from jax.sharding import PartitionSpec as P

daubechies_taps = [
    [0.7071067811865476, 0.7071067811865476],
    [0.48296291314469025, 0.836516303737469, 0.22414386804185735, -0.12940952255092145],
    [
        0.3326705529509569,
        0.8068915093133388,
        0.4598775021193313,
        -0.13501102001039084,
        -0.08544127388224149,
        0.035226291882100656,
    ],
    [
        0.23037781330885523,
        0.7148465705525415,
        0.6308807679295904,
        -0.02798376941698385,
        -0.18703481171888114,
        0.030841381835986965,
        0.032883011666982945,
        -0.010597401784997278,
    ],
    [
        0.160102397974125,
        0.6038292697974729,
        0.7243085284385744,
        0.13842814590110342,
        -0.24229488706619015,
        -0.03224486958502952,
        0.07757149384006515,
        -0.006241490213011705,
        -0.012580751999015526,
        0.003335725285001549,
    ],
    [
        0.11154074335008017,
        0.4946238903983854,
        0.7511339080215775,
        0.3152503517092432,
        -0.22626469396516913,
        -0.12976686756709563,
        0.09750160558707936,
        0.02752286553001629,
        -0.031582039318031156,
        0.0005538422009938016,
        0.004777257511010651,
        -0.00107730108499558,
    ],
    [
        0.07785205408506236,
        0.39653931948230575,
        0.7291320908465551,
        0.4697822874053586,
        -0.14390600392910627,
        -0.22403618499416572,
        0.07130921926705004,
        0.0806126091510659,
        -0.03802993693503463,
        -0.01657454163101562,
        0.012550998556013784,
        0.00042957797300470274,
        -0.0018016407039998328,
        0.0003537138000010399,
    ],
    [
        0.05441584224308161,
        0.3128715909144659,
        0.6756307362980128,
        0.5853546836548691,
        -0.015829105256023893,
        -0.2840155429624281,
        0.00047248457399797254,
        0.128747426620186,
        -0.01736930100202211,
        -0.04408825393106472,
        0.013981027917015516,
        0.008746094047015655,
        -0.00487035299301066,
        -0.0003917403729959771,
        0.0006754494059985568,
        -0.00011747678400228192,
    ],
]


SIDE = 256
CH = 8
BASES = 8
HALO = 48
BF = jnp.bfloat16
F32 = jnp.float32
WIDE = SIDE + 128
TALL = SIDE + HALO
REACH = 42
PACKS = 3


def rounded(table):
    return np.asarray(table, np.float32).astype(ml_dtypes.bfloat16)


def composite_tables():
    full = np.zeros((BASES, SIDE, SIDE + HALO))
    for degree in range(1, 9):
        taps = np.array(daubechies_taps[degree - 1])
        taps = taps * math.sqrt(2.0) / np.sum(taps)
        length = 2 * degree
        low = np.zeros(16)
        high = np.zeros(16)
        low[:length] = taps
        high[:length] = [(-1.0) ** j * taps[length - 1 - j] for j in range(length)]
        low = rounded(low).astype(np.float64)
        high = rounded(high).astype(np.float64)
        level_low = np.zeros((144, SIDE + HALO))
        level_high = np.zeros((128, SIDE + HALO))
        for k in range(144):
            level_low[k, 2 * k : 2 * k + 16] = low[: min(16, SIDE + HALO - 2 * k)]
        for k in range(128):
            level_high[k, 2 * k : 2 * k + 16] = high
        second = np.zeros((128, 144))
        for m in range(64):
            second[m, 2 * m : 2 * m + 16] = low
            second[64 + m, 2 * m : 2 * m + 16] = high
        full[degree - 1, :128] = second @ level_low
        full[degree - 1, 128:] = level_high
    return rounded(full).astype(np.float32)


@functools.lru_cache(maxsize=1)
def tables():
    full = composite_tables()
    wide = np.concatenate([full, np.zeros((BASES, SIDE, 128 - HALO), np.float32)], axis=2)
    assert not np.any(full[:, :, SIDE + REACH :])
    spread = wide.copy()
    for m in range(1, 3):
        at = SIDE + m * REACH
        spread[:, :, at : at + REACH] = full[:, :, SIDE : SIDE + REACH]
    out = {"rows": full, "columns": wide, "spread": spread}
    grid = np.arange(SIDE)[:, None] * np.arange(SIDE)[None, :] % SIDE
    angle = grid * (2.0 * math.pi / SIDE)
    cosine = rounded(np.cos(angle) / math.sqrt(SIDE)).astype(np.float64)
    sine = rounded(np.sin(angle) / math.sqrt(SIDE)).astype(np.float64)
    out["fourier"] = np.block([[cosine, sine], [-sine, cosine]])
    out["back"] = np.concatenate([cosine, -sine], axis=1)
    out["excess"] = cosine @ cosine + sine @ sine - np.eye(SIDE)
    return {name: rounded(table) for name, table in out.items()}


PLACES = (
    (2, 2),
    (1, 2),
    (3, 3),
    (3, 2),
    (3, 1),
    (2, 1),
    (2, 3),
    (1, 1),
    (0, 3),
    (1, 3),
    (0, 2),
    (0, 1),
    (1, 0),
    (2, 0),
    (3, 0),
)
STEP_X, STEP_Z = (1, 3, 0, 0), (0, 0, 1, 3)
PATHS = (
    (
        (3, 0, 0, 3),
        (2, 0, 2),
        (1, 3),
        (1, 3, 3),
        (2, 1),
        (2, 1, 1),
        (1, 1, 3),
        (0, 2),
        (3,),
        (0, 3),
        (3, 3),
        (2,),
        (0,),
        (0, 0),
        (1,),
    ),
    (
        (1, 2, 2, 1),
        (0, 2, 2),
        (3, 1),
        (3, 3, 1),
        (1, 2),
        (0, 2, 0),
        (0, 0, 3),
        (0, 2),
        (3,),
        (3, 0),
        (2, 2),
        (2,),
        (0,),
        (1, 1),
        (1,),
    ),
)
FORWARDS = (
    (),
    (),
    ((0, 0, 1), (0, 1, 1)),
    ((1, 0, 1), (1, 1, 1)),
    ((2, 0, 1), (2, 1, 1)),
    ((0, 0, 2), (0, 1, 2)),
    ((3, 0, 1), (3, 1, 1), (1, 0, 2), (1, 1, 2)),
    ((4, 1, 1), (4, 0, 1), (5, 1, 1)),
    ((3, 0, 2),),
    ((0, 0, 3), (5, 0, 1)),
    ((3, 1, 2), (6, 0, 1), (0, 1, 3), (6, 1, 1)),
    (),
    ((7, 0, 1),),
    ((5, 0, 2), (7, 1, 1)),
    ((9, 0, 1),),
    ((6, 0, 2), (9, 1, 1), (5, 1, 2), (6, 1, 2), (10, 1, 1), (10, 0, 1), (13, 1, 1), (13, 0, 1)),
)
COMING = (2, 8, 1, 3, 4, 0, 12, 11, 9, 6, 14, 5, 7, 10, 13)

IN_ORDER = [hop for step in FORWARDS for hop in step]
FIRST = [sum(len(step) for step in FORWARDS[:i]) for i in range(len(FORWARDS) + 1)]
RANK = [COMING.index(i) for i in range(len(PLACES))]


def coded(place, r, hop):
    steps = PATHS[r][place]
    if hop + 1 == len(steps):
        return steps[hop] + 4 + 8 * (2 * (1 + RANK[place]) + r)
    return steps[hop] + 8 * IN_ORDER.index((place, r, hop + 1))


START = [[coded(place, r, 0) for place in range(len(PLACES))] for r in range(2)]
ONWARD = [coded(*hop) for hop in IN_ORDER]
assert len(IN_ORDER) == sum(len(p) - 1 for r in range(2) for p in PATHS[r])
assert len(IN_ORDER) - FIRST[-2] > CH // 2


def choose(j, values):
    out = jnp.int32(values[0])
    for i, value in enumerate(values):
        out = jnp.where(j == i, jnp.int32(value), out)
    return out


def three_beside(first, second, third):
    lane = lax.broadcasted_iota(jnp.int32, first.shape, len(first.shape) - 1)
    return jnp.where(lane < REACH, first, jnp.where(lane < 2 * REACH, second, third))


def turned(values, m):
    return pltpu.roll(values, 128 - m * REACH, 1) if m else values


def dot(a, b):
    return jnp.dot(a, b, preferred_element_type=F32)


def exchange_kernel(
    n_fy,
    n_fx,
    dest_ref,
    chan_ref,
    count_ref,
    fourier_hbm,
    back_hbm,
    excess_hbm,
    sky_hbm,
    vis_hbm,
    extended,
    fourier,
    back,
    excess,
    vis,
    sky,
    model,
    partial,
    sending,
    arrived,
    relay,
    half,
    share_ref,
    shares,
    kron,
    columns,
    beside,
    corner,
    load_sem,
    tile_send,
    tile_recv,
    relay_send,
    relay_recv,
    share_send,
    share_recv,
    halo_send,
    halo_recv,
    columns_send,
    columns_recv,
):
    fy = lax.axis_index("fy")
    fx = lax.axis_index("fx")
    n_z = 4
    n_x = n_fx // n_z
    my_x, my_z = fx // n_z, fx % n_z

    def at(dx, dz):
        return (my_x + dx) % n_x * n_z + (my_z + dz) % n_z

    def peer(k):
        return at(k // n_z, k % n_z)

    load_vis = pltpu.make_async_copy(vis_hbm, vis, load_sem.at[0])
    load_sky = pltpu.make_async_copy(sky_hbm, sky, load_sem.at[1])
    load_vis.start()
    load_fourier = pltpu.make_async_copy(fourier_hbm, fourier, load_sem.at[2])
    load_back = pltpu.make_async_copy(back_hbm, back, load_sem.at[3])
    load_excess = pltpu.make_async_copy(excess_hbm, excess, load_sem.at[4])
    load_fourier.start()
    load_back.start()
    load_excess.start()
    load_sky.start()

    barrier = pltpu.get_barrier_semaphore()

    def greet(k, carry):
        pl.semaphore_signal(
            barrier, inc=1, device_id={"fx": peer(k)}, device_id_type=pl.DeviceIdType.MESH
        )
        return carry

    lax.fori_loop(1, n_fx, greet, 0)
    up, down = (fy + n_fy - 1) % n_fy, (fy + 1) % n_fy
    prev, nxt = (fx + n_fx - 1) % n_fx, (fx + 1) % n_fx
    for where in ({"fy": up}, {"fy": down}, {"fy": up, "fx": prev}, {"fy": down, "fx": nxt}):
        pl.semaphore_signal(barrier, inc=1, device_id=where, device_id_type=pl.DeviceIdType.MESH)

    def place_of(i):
        return at(choose(i, [p[0] for p in PLACES]), choose(i, [p[1] for p in PLACES]))

    def share_copy(i):
        rank = 1 + choose(i, RANK)
        return pltpu.make_async_remote_copy(
            src_ref=share_ref.at[rank],
            dst_ref=shares.at[rank],
            send_sem=share_send.at[rank],
            recv_sem=share_recv.at[rank],
            device_id={"fx": place_of(i)},
            device_id_type=pl.DeviceIdType.MESH,
        )

    def hop_copy(source, send_sem, code, last):
        step, to = code % 4, code // 8
        return pltpu.make_async_remote_copy(
            src_ref=source,
            dst_ref=arrived.at[to] if last else relay.at[to],
            send_sem=send_sem,
            recv_sem=tile_recv.at[to] if last else relay_recv.at[to],
            device_id={"fx": at(choose(step, STEP_X), choose(step, STEP_Z))},
            device_id_type=pl.DeviceIdType.MESH,
        )

    def hop_start(source, send_sem, code):
        @pl.when(code // 4 % 2 == 1)
        def _():
            hop_copy(source, send_sem, code, True).start()

        @pl.when(code // 4 % 2 == 0)
        def _():
            hop_copy(source, send_sem, code, False).start()

    def landed(buffer, sem):
        return pltpu.make_async_remote_copy(
            src_ref=buffer,
            dst_ref=buffer,
            send_sem=tile_send.at[0],
            recv_sem=sem,
            device_id={"fx": at(1, 0)},
            device_id_type=pl.DeviceIdType.MESH,
        )

    def forward(f, carry):
        landed(relay.at[f], relay_recv.at[f]).wait_recv()
        hop_start(relay.at[f], relay_send.at[f], choose(f, ONWARD))
        return carry

    tiles = vis_hbm.shape[0]
    row = lax.broadcasted_iota(jnp.int32, (8, 128), 0)
    lane = lax.broadcasted_iota(jnp.int32, (8, 128), 1)

    def slots_for(to):
        found = jnp.int32(0)
        picked = [(jnp.int32(0), jnp.int32(0), jnp.int32(0))] * 2
        for i in range(tiles):
            match = dest_ref[i] == to
            for r in range(2):
                here = match & (found == r)
                new = (jnp.int32(i), count_ref[i], chan_ref[i])
                picked[r] = tuple(jnp.where(here, a, b) for a, b in zip(new, picked[r]))
            found = found + jnp.where(match, 1, 0)
        return [(tile, count.astype(F32) * (1.0 / 64.0), chan) for tile, count, chan in picked]

    def share_rows(slots):
        total = jnp.zeros((8, 128), F32)
        for r, (_, weight, chan) in enumerate(slots):
            total = total + jnp.where((row == r) & (lane == chan), weight, 0.0)
        return total

    load_fourier.wait()
    load_back.wait()
    load_vis.wait()

    def planes(slots):
        for i, (t, _, _) in enumerate(slots):
            spectrum = jnp.concatenate([vis[t, 0], vis[t, 1]], axis=1)
            for part in range(2):
                half[i, part * SIDE : (part + 1) * SIDE] = dot(
                    spectrum, fourier[:, part * SIDE : (part + 1) * SIDE]
                ).astype(BF)
        return [(dot(back[...], half[i]) * slots[i][1]).astype(BF) for i in range(2)]

    def prepare(i):
        slots = slots_for(place_of(i))
        share_ref[1 + choose(i, RANK)] = share_rows(slots)
        sending[i, 0], sending[i, 1] = planes(slots)

    prepare(jnp.int32(0))
    pl.semaphore_wait(barrier, n_fx - 1 + 4)

    def send_tiles(i, carry):
        share_copy(i).start()
        for r in range(2):
            hop_start(sending.at[i, r], tile_send.at[2 * i + r], choose(i, START[r]))
        lax.fori_loop(choose(i, FIRST), choose(i + 1, FIRST), forward, 0)

        @pl.when(i < len(PLACES) - 1)
        def _():
            prepare(i + 1)

        return carry

    lax.fori_loop(0, len(PLACES), send_tiles, 0)

    load_sky.wait()
    load_excess.wait()

    def there_and_back(c):
        pixels = jnp.concatenate([sky[c].astype(BF), sky[c + 1].astype(BF)], axis=1)
        once = pixels.astype(F32) + dot(excess[...], pixels)
        once = jnp.concatenate([once[:, :SIDE], once[:, SIDE:]], axis=0)
        both = once + dot(once.astype(BF), excess[...])
        model[c] = both[:SIDE]
        model[c + 1] = both[SIDE:]

    def forward_and_work(j, carry):
        forward(FIRST[-2] + j, 0)

        @pl.when(j == 0)
        def _():
            own = slots_for(fx)
            shares[0] = share_rows(own)
            arrived[0], arrived[1] = planes(own)

        @pl.when((j >= 1) & (j <= CH // 2))
        def _():
            there_and_back(2 * (j - 1))

        return carry

    lax.fori_loop(0, len(IN_ORDER) - FIRST[-2], forward_and_work, 0)

    def wait_share(i, carry):
        share_copy(i).wait_recv()
        return carry

    lax.fori_loop(0, len(PLACES), wait_share, 0)
    slots = n_fx * 2
    wide = slots * 16
    all_shares = shares[...].reshape(n_fx * 8, 128)
    members = jnp.where(all_shares > 0, 1.0, 0.0).astype(BF)
    spread = (
        lax.broadcasted_iota(jnp.int32, (CH * 16, 128), 0) // 16
        == lax.broadcasted_iota(jnp.int32, (CH * 16, 128), 1)
    )
    spread = jnp.where(spread, 1.0, 0.0).astype(BF)
    by_source = lax.dot_general(
        spread, members, (((1,), (1,)), ((), ())), preferred_element_type=F32
    ).astype(BF)
    weights = lax.dot_general(
        spread, all_shares.astype(BF), (((1,), (1,)), ((), ())), preferred_element_type=F32
    )
    totals = jnp.sum(weights, axis=1, keepdims=True)
    src_row = lax.broadcasted_iota(jnp.int32, (n_fx * 8, wide), 0)
    dst_col = lax.broadcasted_iota(jnp.int32, (n_fx * 8, wide), 1)
    widen = (src_row // 8 == dst_col // 32) & (src_row % 8 == dst_col // 16 % 2)
    widened = dot(by_source, jnp.where(widen, 1.0, 0.0).astype(BF))
    diagonal = (
        lax.broadcasted_iota(jnp.int32, (CH * 16, wide), 0) % 16
        == lax.broadcasted_iota(jnp.int32, (CH * 16, wide), 1) % 16
    )
    kron[...] = jnp.where(diagonal, widened, 0.0).astype(BF)
    scale = 1.0 / (1.0 + totals)

    def group_rows(g):
        return pl.ds(pl.multiple_of(g * 16, 16), 16)

    def without_tiles(g):
        pixels = sky[:, group_rows(g), :].reshape(CH * 16, SIDE)
        there = model[:, group_rows(g), :].reshape(CH * 16, SIDE)
        return pixels - (totals * scale) * there

    def wait_tiles(i, carry):
        landed(arrived.at[2 + i], tile_recv.at[2 + i]).wait_recv()
        return carry

    def with_sources(g, first, last):
        held = arrived[2 * first : 2 * last, group_rows(g), :].reshape((last - first) * 32, SIDE)
        before = without_tiles(g) if first == 0 else partial[g]
        return before + scale * dot(kron[:, first * 32 : last * 32], held)

    for first, last in ((0, 8), (8, 12)):
        lax.fori_loop(max(2 * first - 2, 0), 2 * last - 2, wait_tiles, 0)

        def add_sources(q, carry):
            for i in range(4):
                partial[q * 4 + i] = with_sources(q * 4 + i, first, last)
            return carry

        lax.fori_loop(0, SIDE // 64, add_sources, 0)
    lax.fori_loop(22, 2 * len(PLACES), wait_tiles, 0)

    def combine(g):
        rows = group_rows(g)
        new = with_sources(g, 12, 16).reshape(CH, 16, SIDE)
        extended[:, rows, :SIDE] = new.astype(BF)
        for k in range(PACKS):
            parts = [new[min(3 * k + m, CH - 1), :, :128] for m in range(3)]
            parts = [pltpu.roll(part, m * REACH, 1) if m else part for m, part in enumerate(parts)]
            columns[k, rows, :] = three_beside(*parts).astype(BF)

    chunks = 4
    deep = SIDE // chunks

    def columns_copy(q):
        rows = pl.ds(pl.multiple_of(q * deep, deep), deep)
        return pltpu.make_async_remote_copy(
            src_ref=columns.at[:, rows, :],
            dst_ref=beside.at[:, rows, :],
            send_sem=columns_send.at[q],
            recv_sem=columns_recv.at[q],
            device_id={"fx": prev},
            device_id_type=pl.DeviceIdType.MESH,
        )

    def halo_copy(i):
        source = (extended.at[:, :HALO, :SIDE], columns.at[:, :HALO, :])[i]
        target = (extended.at[:, SIDE:, :SIDE], corner)[i]
        where = ({"fy": up}, {"fy": up, "fx": prev})[i]
        return pltpu.make_async_remote_copy(
            src_ref=source,
            dst_ref=target,
            send_sem=halo_send.at[i],
            recv_sem=halo_recv.at[i],
            device_id=where,
            device_id_type=pl.DeviceIdType.MESH,
        )

    def make_chunk(q, carry):
        for i in range(deep // 16):
            combine(q * (deep // 16) + i)
        columns_copy(q).start()

        @pl.when(q == 0)
        def _():
            for i in range(2):
                halo_copy(i).start()

        return carry

    lax.fori_loop(0, chunks, make_chunk, 0)

    def place(source, begin, end):
        for c in range(CH):
            values = turned(source[c // 3].astype(F32), c % 3)
            extended[c, begin:end, SIDE:] = values.astype(BF)

    halo_copy(1).wait_recv()
    place(corner, SIDE, TALL)
    for q in range(chunks):
        columns_copy(q).wait_recv()
        place(beside.at[:, q * deep : (q + 1) * deep, :], q * deep, (q + 1) * deep)
    halo_copy(0).wait_recv()

    def finish_shares(i, carry):
        share_copy(i).wait_send()
        return carry

    def finish_sent(i, carry):
        for r in range(2):
            hop_copy(sending.at[i, r], tile_send.at[2 * i + r], jnp.int32(0), False).wait_send()
        return carry

    def finish_forwards(f, carry):
        hop_copy(relay.at[f], relay_send.at[f], jnp.int32(0), False).wait_send()
        return carry

    lax.fori_loop(0, len(PLACES), finish_shares, 0)
    lax.fori_loop(0, len(PLACES), finish_sent, 0)
    lax.fori_loop(0, len(IN_ORDER), finish_forwards, 0)
    for i in range(2):
        halo_copy(i).wait_send()
    for q in range(chunks):
        columns_copy(q).wait_send()


def spill_kernel(
    n_fy,
    n_fx,
    cells,
    left,
    above,
    corner,
    side,
    bottom,
    to_right,
    to_below,
    to_corner,
    load_sem,
    send_sem,
    recv_sem,
):
    load_side = pltpu.make_async_copy(cells.at[:, :, SIDE:], side, load_sem.at[0])
    load_bottom = pltpu.make_async_copy(cells.at[:, SIDE:, :SIDE], bottom, load_sem.at[1])
    load_side.start()
    load_bottom.start()
    fy = lax.axis_index("fy")
    fx = lax.axis_index("fx")
    up, down = (fy + n_fy - 1) % n_fy, (fy + 1) % n_fy
    prev, nxt = (fx + n_fx - 1) % n_fx, (fx + 1) % n_fx
    barrier = pltpu.get_barrier_semaphore()
    for where in (
        {"fy": up},
        {"fy": down},
        {"fx": prev},
        {"fx": nxt},
        {"fy": up, "fx": prev},
        {"fy": down, "fx": nxt},
    ):
        pl.semaphore_signal(barrier, inc=1, device_id=where, device_id_type=pl.DeviceIdType.MESH)
    load_side.wait()
    for k in range(PACKS):
        packed = three_beside(*[side[min(3 * k + m, CH - 1)] for m in range(3)]).astype(BF)
        to_right[k] = packed[:SIDE]
        to_corner[k] = packed[SIDE:]
    load_bottom.wait()
    to_below[...] = bottom[...].astype(BF)
    pl.semaphore_wait(barrier, 6)

    def spill_copy(i):
        return pltpu.make_async_remote_copy(
            src_ref=(to_right, to_below, to_corner)[i],
            dst_ref=(left, above, corner)[i],
            send_sem=send_sem.at[i],
            recv_sem=recv_sem.at[i],
            device_id=({"fx": nxt}, {"fy": down}, {"fy": down, "fx": nxt})[i],
            device_id_type=pl.DeviceIdType.MESH,
        )

    for i in range(3):
        spill_copy(i).start()
    for i in range(3):
        spill_copy(i).wait()


def add_kernel(cells, left, above, corner, out):
    for h in range(2):

        channel = 2 * pl.program_id(0) + h

        def columns(packed):
            values = packed[channel // 3].astype(F32)
            for m in range(1, 3):
                values = jnp.where(channel % 3 == m, turned(packed[channel // 3].astype(F32), m), values)
            lane = lax.broadcasted_iota(jnp.int32, values.shape, 1)
            return jnp.where(lane < REACH, values, 0.0)

        def finished(total):
            return jnp.maximum(total * (1.0 / BASES), 0.0)

        from_left = columns(left)
        from_above = above[h].astype(F32)
        first = from_left[:HALO] + from_above[:, :128] + columns(corner)
        out[h, :HALO, :128] = finished(cells[h, :HALO, :128] + first)
        out[h, :HALO, 128:] = finished(cells[h, :HALO, 128:] + from_above[:, 128:])
        out[h, HALO:, :128] = finished(cells[h, HALO:, :128] + from_left[HALO:])
        out[h, HALO:, 128:] = finished(cells[h, HALO:, 128:])


def per_device(n_fy, n_fx, sky_image, vis_tiles, tile_dest, tile_chan, tile_count, thresholds):
    made = {name: jnp.asarray(table) for name, table in tables().items()}
    smem = pl.BlockSpec(memory_space=pltpu.SMEM)
    vmem = pl.BlockSpec(memory_space=pltpu.VMEM)
    anywhere = pl.BlockSpec(memory_space=pl.ANY)
    dma = pltpu.SemaphoreType.DMA
    tiles = vis_tiles.shape[0]
    extended = pl.pallas_call(
        functools.partial(exchange_kernel, n_fy, n_fx),
        out_shape=pltpu.VMEM((CH, TALL, WIDE), BF),
        in_specs=[smem] * 3 + [anywhere] * 5,
        scratch_shapes=[
            pltpu.VMEM((2 * SIDE, 2 * SIDE), BF),
            pltpu.VMEM((SIDE, 2 * SIDE), BF),
            pltpu.VMEM((SIDE, SIDE), BF),
            pltpu.VMEM((tiles, 2, SIDE, SIDE), BF),
            pltpu.VMEM((CH, SIDE, SIDE), F32),
            pltpu.VMEM((CH, SIDE, SIDE), F32),
            pltpu.VMEM((SIDE // 16, CH * 16, SIDE), F32),
            pltpu.VMEM((n_fx, 2, SIDE, SIDE), BF),
            pltpu.VMEM((2 * n_fx, SIDE, SIDE), BF),
            pltpu.VMEM((len(IN_ORDER), SIDE, SIDE), BF),
            pltpu.VMEM((2, 2 * SIDE, SIDE), BF),
            pltpu.VMEM((n_fx, 8, 128), F32),
            pltpu.VMEM((n_fx, 8, 128), F32),
            pltpu.VMEM((CH * 16, n_fx * 32), BF),
            pltpu.VMEM((PACKS, SIDE, 128), BF),
            pltpu.VMEM((PACKS, SIDE, 128), BF),
            pltpu.VMEM((PACKS, HALO, 128), BF),
            dma((5,)),
            dma((2 * len(PLACES),)),
            dma((2 * n_fx,)),
            dma((len(IN_ORDER),)),
            dma((len(IN_ORDER),)),
            dma((n_fx,)),
            dma((n_fx,)),
            dma((2,)),
            dma((2,)),
            dma((4,)),
            dma((4,)),
        ],
        compiler_params=pltpu.CompilerParams(
            collective_id=0, has_side_effects=True, vmem_limit_bytes=58 * 1024 * 1024
        ),
    )(
        tile_dest.reshape(tiles),
        tile_chan,
        tile_count,
        made["fourier"],
        made["back"],
        made["excess"],
        sky_image,
        vis_tiles,
    )
    rows, columns = made["rows"], made["columns"]
    row_sec = jnp.einsum("bkn,cnx->bckx", rows, extended, preferred_element_type=F32).astype(BF)
    coefficient = jnp.einsum("bcyx,bkx->bcyk", row_sec, columns, preferred_element_type=F32)
    limits = thresholds.astype(F32)
    shrunk = (coefficient - jnp.clip(coefficient, -limits, limits)).astype(BF)
    row_sec = jnp.einsum("bjy,bcjk->bcyk", rows, shrunk, preferred_element_type=F32).astype(BF)
    cells = jnp.einsum("bcyk,bkx->cyx", row_sec, made["spread"], preferred_element_type=F32)
    left, above, corner = pl.pallas_call(
        functools.partial(spill_kernel, n_fy, n_fx),
        out_shape=(
            jax.ShapeDtypeStruct((PACKS, SIDE, 128), BF),
            jax.ShapeDtypeStruct((CH, HALO, SIDE), BF),
            jax.ShapeDtypeStruct((PACKS, HALO, 128), BF),
        ),
        in_specs=[anywhere],
        out_specs=[vmem] * 3,
        scratch_shapes=[
            pltpu.VMEM((CH, TALL, 128), F32),
            pltpu.VMEM((CH, HALO, SIDE), F32),
            pltpu.VMEM((PACKS, SIDE, 128), BF),
            pltpu.VMEM((CH, HALO, SIDE), BF),
            pltpu.VMEM((PACKS, HALO, 128), BF),
            dma((2,)),
            dma((3,)),
            dma((3,)),
        ],
        compiler_params=pltpu.CompilerParams(
            collective_id=1, has_side_effects=True, vmem_limit_bytes=58 * 1024 * 1024
        ),
    )(cells)
    return pl.pallas_call(
        add_kernel,
        out_shape=jax.ShapeDtypeStruct((CH, SIDE, SIDE), F32),
        grid=(CH // 2,),
        in_specs=[
            pl.BlockSpec((2, SIDE, SIDE), lambda p: (p, 0, 0)),
            pl.BlockSpec((PACKS, SIDE, 128), lambda p: (0, 0, 0)),
            pl.BlockSpec((2, HALO, SIDE), lambda p: (p, 0, 0)),
            pl.BlockSpec((PACKS, HALO, 128), lambda p: (0, 0, 0)),
        ],
        out_specs=pl.BlockSpec((2, SIDE, SIDE), lambda p: (p, 0, 0)),
        compiler_params=pltpu.CompilerParams(vmem_limit_bytes=16 * 1024 * 1024),
    )(cells, left, above, corner)


def solution(mesh):
    in_specs = (
        P(None, "fy", "fx"),
        P(("fy", "fx"), None, None, None),
        P(("fy", "fx"), None),
        P(("fy", "fx")),
        P(("fy", "fx")),
        P(None, None, "fy", "fx"),
    )
    out_specs = P(None, "fy", "fx")
    return jax.shard_map(
        functools.partial(per_device, mesh.shape["fy"], mesh.shape["fx"]),
        mesh=mesh,
        in_specs=in_specs,
        out_specs=out_specs,
        check_vma=False,
    )
```

```python
import functools
import math

import jax
import jax.numpy as jnp
import ml_dtypes
import numpy as np
from jax import lax
from jax.experimental import pallas as pl
from jax.experimental.pallas import tpu as pltpu
from jax.sharding import PartitionSpec as P

daubechies_taps = [
    [0.7071067811865476, 0.7071067811865476],
    [0.48296291314469025, 0.836516303737469, 0.22414386804185735, -0.12940952255092145],
    [
        0.3326705529509569,
        0.8068915093133388,
        0.4598775021193313,
        -0.13501102001039084,
        -0.08544127388224149,
        0.035226291882100656,
    ],
    [
        0.23037781330885523,
        0.7148465705525415,
        0.6308807679295904,
        -0.02798376941698385,
        -0.18703481171888114,
        0.030841381835986965,
        0.032883011666982945,
        -0.010597401784997278,
    ],
    [
        0.160102397974125,
        0.6038292697974729,
        0.7243085284385744,
        0.13842814590110342,
        -0.24229488706619015,
        -0.03224486958502952,
        0.07757149384006515,
        -0.006241490213011705,
        -0.012580751999015526,
        0.003335725285001549,
    ],
    [
        0.11154074335008017,
        0.4946238903983854,
        0.7511339080215775,
        0.3152503517092432,
        -0.22626469396516913,
        -0.12976686756709563,
        0.09750160558707936,
        0.02752286553001629,
        -0.031582039318031156,
        0.0005538422009938016,
        0.004777257511010651,
        -0.00107730108499558,
    ],
    [
        0.07785205408506236,
        0.39653931948230575,
        0.7291320908465551,
        0.4697822874053586,
        -0.14390600392910627,
        -0.22403618499416572,
        0.07130921926705004,
        0.0806126091510659,
        -0.03802993693503463,
        -0.01657454163101562,
        0.012550998556013784,
        0.00042957797300470274,
        -0.0018016407039998328,
        0.0003537138000010399,
    ],
    [
        0.05441584224308161,
        0.3128715909144659,
        0.6756307362980128,
        0.5853546836548691,
        -0.015829105256023893,
        -0.2840155429624281,
        0.00047248457399797254,
        0.128747426620186,
        -0.01736930100202211,
        -0.04408825393106472,
        0.013981027917015516,
        0.008746094047015655,
        -0.00487035299301066,
        -0.0003917403729959771,
        0.0006754494059985568,
        -0.00011747678400228192,
    ],
]


SIDE = 256
CH = 8
BASES = 8
HALO = 48
BF = jnp.bfloat16
F32 = jnp.float32
WIDE = SIDE + 128
TALL = SIDE + HALO
REACH = 42
PACKS = 3


def rounded(table):
    return np.asarray(table, np.float32).astype(ml_dtypes.bfloat16)


def composite_tables():
    full = np.zeros((BASES, SIDE, SIDE + HALO))
    for degree in range(1, 9):
        taps = np.array(daubechies_taps[degree - 1])
        taps = taps * math.sqrt(2.0) / np.sum(taps)
        length = 2 * degree
        low = np.zeros(16)
        high = np.zeros(16)
        low[:length] = taps
        high[:length] = [(-1.0) ** j * taps[length - 1 - j] for j in range(length)]
        low = rounded(low).astype(np.float64)
        high = rounded(high).astype(np.float64)
        level_low = np.zeros((144, SIDE + HALO))
        level_high = np.zeros((128, SIDE + HALO))
        for k in range(144):
            level_low[k, 2 * k : 2 * k + 16] = low[: min(16, SIDE + HALO - 2 * k)]
        for k in range(128):
            level_high[k, 2 * k : 2 * k + 16] = high
        second = np.zeros((128, 144))
        for m in range(64):
            second[m, 2 * m : 2 * m + 16] = low
            second[64 + m, 2 * m : 2 * m + 16] = high
        full[degree - 1, :128] = second @ level_low
        full[degree - 1, 128:] = level_high
    return rounded(full).astype(np.float32)


@functools.lru_cache(maxsize=1)
def tables():
    full = composite_tables()
    wide = np.concatenate([full, np.zeros((BASES, SIDE, 128 - HALO), np.float32)], axis=2)
    assert not np.any(full[:, :, SIDE + REACH :])
    spread = wide.copy()
    for m in range(1, 3):
        at = SIDE + m * REACH
        spread[:, :, at : at + REACH] = full[:, :, SIDE : SIDE + REACH]
    out = {"rows": full, "columns": wide, "spread": spread}
    grid = np.arange(SIDE)[:, None] * np.arange(SIDE)[None, :] % SIDE
    angle = grid * (2.0 * math.pi / SIDE)
    cosine = rounded(np.cos(angle) / math.sqrt(SIDE)).astype(np.float64)
    sine = rounded(np.sin(angle) / math.sqrt(SIDE)).astype(np.float64)
    out["fourier"] = np.block([[cosine, sine], [-sine, cosine]])
    out["back"] = np.concatenate([cosine, -sine], axis=1)
    out["excess"] = cosine @ cosine + sine @ sine - np.eye(SIDE)
    return {name: rounded(table) for name, table in out.items()}


PLACES = (
    (2, 2),
    (1, 2),
    (3, 3),
    (3, 2),
    (3, 1),
    (2, 1),
    (2, 3),
    (1, 1),
    (0, 3),
    (1, 3),
    (0, 2),
    (0, 1),
    (1, 0),
    (2, 0),
    (3, 0),
)
STEP_X, STEP_Z = (1, 3, 0, 0), (0, 0, 1, 3)
PATHS = (
    (
        (3, 0, 0, 3),
        (2, 0, 2),
        (1, 3),
        (1, 3, 3),
        (2, 1),
        (2, 1, 1),
        (1, 1, 3),
        (0, 2),
        (3,),
        (0, 3),
        (3, 3),
        (2,),
        (0,),
        (0, 0),
        (1,),
    ),
    (
        (1, 2, 2, 1),
        (0, 2, 2),
        (3, 1),
        (3, 3, 1),
        (1, 2),
        (0, 2, 0),
        (0, 0, 3),
        (0, 2),
        (3,),
        (3, 0),
        (2, 2),
        (2,),
        (0,),
        (1, 1),
        (1,),
    ),
)
FORWARDS = (
    (),
    (),
    ((0, 0, 1), (0, 1, 1)),
    ((1, 0, 1), (1, 1, 1)),
    ((2, 0, 1), (2, 1, 1)),
    ((0, 0, 2), (0, 1, 2)),
    ((3, 0, 1), (3, 1, 1), (1, 0, 2), (1, 1, 2)),
    ((4, 1, 1), (4, 0, 1), (5, 1, 1)),
    ((3, 0, 2),),
    ((0, 0, 3), (5, 0, 1)),
    ((3, 1, 2), (6, 0, 1), (0, 1, 3), (6, 1, 1)),
    (),
    ((7, 0, 1),),
    ((5, 0, 2), (7, 1, 1)),
    ((9, 0, 1),),
    ((6, 0, 2), (9, 1, 1), (5, 1, 2), (6, 1, 2), (10, 1, 1), (10, 0, 1), (13, 1, 1), (13, 0, 1)),
)
COMING = (2, 8, 1, 3, 4, 0, 12, 11, 9, 6, 14, 5, 7, 10, 13)

IN_ORDER = [hop for step in FORWARDS for hop in step]
FIRST = [sum(len(step) for step in FORWARDS[:i]) for i in range(len(FORWARDS) + 1)]
RANK = [COMING.index(i) for i in range(len(PLACES))]


def coded(place, r, hop):
    steps = PATHS[r][place]
    if hop + 1 == len(steps):
        return steps[hop] + 4 + 8 * (2 * (1 + RANK[place]) + r)
    return steps[hop] + 8 * IN_ORDER.index((place, r, hop + 1))


START = [[coded(place, r, 0) for place in range(len(PLACES))] for r in range(2)]
ONWARD = [coded(*hop) for hop in IN_ORDER]
assert len(IN_ORDER) == sum(len(p) - 1 for r in range(2) for p in PATHS[r])
assert len(IN_ORDER) - 2 - FIRST[-2] > CH // 2
assert all(RANK[place] >= 7 for place, _, _ in IN_ORDER[-2:])


def choose(j, values):
    out = jnp.int32(values[0])
    for i, value in enumerate(values):
        out = jnp.where(j == i, jnp.int32(value), out)
    return out


def three_beside(first, second, third):
    lane = lax.broadcasted_iota(jnp.int32, first.shape, len(first.shape) - 1)
    return jnp.where(lane < REACH, first, jnp.where(lane < 2 * REACH, second, third))


def turned(values, m):
    return pltpu.roll(values, 128 - m * REACH, 1) if m else values


def dot(a, b):
    return jnp.dot(a, b, preferred_element_type=F32)


def exchange_kernel(
    n_fy,
    n_fx,
    dest_ref,
    chan_ref,
    count_ref,
    fourier_hbm,
    back_hbm,
    excess_hbm,
    sky_hbm,
    vis_hbm,
    extended,
    fourier,
    back,
    excess,
    vis,
    sky,
    model,
    partial,
    sending,
    arrived,
    relay,
    half,
    share_ref,
    shares,
    kron,
    columns,
    beside,
    corner,
    load_sem,
    tile_send,
    tile_recv,
    relay_send,
    relay_recv,
    share_send,
    share_recv,
    halo_send,
    halo_recv,
    columns_send,
    columns_recv,
):
    fy = lax.axis_index("fy")
    fx = lax.axis_index("fx")
    n_z = 4
    n_x = n_fx // n_z
    my_x, my_z = fx // n_z, fx % n_z

    def at(dx, dz):
        return (my_x + dx) % n_x * n_z + (my_z + dz) % n_z

    def peer(k):
        return at(k // n_z, k % n_z)

    load_vis = pltpu.make_async_copy(vis_hbm, vis, load_sem.at[0])
    load_sky = pltpu.make_async_copy(sky_hbm, sky, load_sem.at[1])
    load_vis.start()
    load_fourier = pltpu.make_async_copy(fourier_hbm, fourier, load_sem.at[2])
    load_back = pltpu.make_async_copy(back_hbm, back, load_sem.at[3])
    load_excess = pltpu.make_async_copy(excess_hbm, excess, load_sem.at[4])
    load_fourier.start()
    load_back.start()
    load_excess.start()
    load_sky.start()

    barrier = pltpu.get_barrier_semaphore()

    def greet(k, carry):
        pl.semaphore_signal(
            barrier, inc=1, device_id={"fx": peer(k)}, device_id_type=pl.DeviceIdType.MESH
        )
        return carry

    lax.fori_loop(1, n_fx, greet, 0)
    up, down = (fy + n_fy - 1) % n_fy, (fy + 1) % n_fy
    prev, nxt = (fx + n_fx - 1) % n_fx, (fx + 1) % n_fx
    for where in ({"fy": up}, {"fy": down}, {"fy": up, "fx": prev}, {"fy": down, "fx": nxt}):
        pl.semaphore_signal(barrier, inc=1, device_id=where, device_id_type=pl.DeviceIdType.MESH)

    def place_of(i):
        return at(choose(i, [p[0] for p in PLACES]), choose(i, [p[1] for p in PLACES]))

    def share_copy(i):
        rank = 1 + choose(i, RANK)
        return pltpu.make_async_remote_copy(
            src_ref=share_ref.at[rank],
            dst_ref=shares.at[rank],
            send_sem=share_send.at[rank],
            recv_sem=share_recv.at[rank],
            device_id={"fx": place_of(i)},
            device_id_type=pl.DeviceIdType.MESH,
        )

    def hop_copy(source, send_sem, code, last):
        step, to = code % 4, code // 8
        return pltpu.make_async_remote_copy(
            src_ref=source,
            dst_ref=arrived.at[to] if last else relay.at[to],
            send_sem=send_sem,
            recv_sem=tile_recv.at[to] if last else relay_recv.at[to],
            device_id={"fx": at(choose(step, STEP_X), choose(step, STEP_Z))},
            device_id_type=pl.DeviceIdType.MESH,
        )

    def hop_start(source, send_sem, code):
        @pl.when(code // 4 % 2 == 1)
        def _():
            hop_copy(source, send_sem, code, True).start()

        @pl.when(code // 4 % 2 == 0)
        def _():
            hop_copy(source, send_sem, code, False).start()

    def landed(buffer, sem):
        return pltpu.make_async_remote_copy(
            src_ref=buffer,
            dst_ref=buffer,
            send_sem=tile_send.at[0],
            recv_sem=sem,
            device_id={"fx": at(1, 0)},
            device_id_type=pl.DeviceIdType.MESH,
        )

    def forward(f, carry):
        landed(relay.at[f], relay_recv.at[f]).wait_recv()
        hop_start(relay.at[f], relay_send.at[f], choose(f, ONWARD))
        return carry

    tiles = vis_hbm.shape[0]
    row = lax.broadcasted_iota(jnp.int32, (8, 128), 0)
    lane = lax.broadcasted_iota(jnp.int32, (8, 128), 1)

    def slots_for(to):
        found = jnp.int32(0)
        picked = [(jnp.int32(0), jnp.int32(0), jnp.int32(0))] * 2
        for i in range(tiles):
            match = dest_ref[i] == to
            for r in range(2):
                here = match & (found == r)
                new = (jnp.int32(i), count_ref[i], chan_ref[i])
                picked[r] = tuple(jnp.where(here, a, b) for a, b in zip(new, picked[r]))
            found = found + jnp.where(match, 1, 0)
        return [(tile, count.astype(F32) * (1.0 / 64.0), chan) for tile, count, chan in picked]

    def share_rows(slots):
        total = jnp.zeros((8, 128), F32)
        for r, (_, weight, chan) in enumerate(slots):
            total = total + jnp.where((row == r) & (lane == chan), weight, 0.0)
        return total

    load_fourier.wait()
    load_back.wait()
    load_vis.wait()

    def planes(slots):
        for i, (t, _, _) in enumerate(slots):
            spectrum = jnp.concatenate([vis[t, 0], vis[t, 1]], axis=1)
            for part in range(2):
                half[i, part * SIDE : (part + 1) * SIDE] = dot(
                    spectrum, fourier[:, part * SIDE : (part + 1) * SIDE]
                ).astype(BF)
        return [(dot(back[...], half[i]) * slots[i][1]).astype(BF) for i in range(2)]

    def prepare(i):
        slots = slots_for(place_of(i))
        share_ref[1 + choose(i, RANK)] = share_rows(slots)
        sending[i, 0], sending[i, 1] = planes(slots)

    prepare(jnp.int32(0))
    pl.semaphore_wait(barrier, n_fx - 1 + 4)

    def send_tiles(i, carry):
        share_copy(i).start()
        for r in range(2):
            hop_start(sending.at[i, r], tile_send.at[2 * i + r], choose(i, START[r]))
        lax.fori_loop(choose(i, FIRST), choose(i + 1, FIRST), forward, 0)

        @pl.when(i < len(PLACES) - 1)
        def _():
            prepare(i + 1)

        return carry

    lax.fori_loop(0, len(PLACES), send_tiles, 0)

    load_sky.wait()
    load_excess.wait()

    def there_and_back(c):
        pixels = jnp.concatenate([sky[c].astype(BF), sky[c + 1].astype(BF)], axis=1)
        once = pixels.astype(F32) + dot(excess[...], pixels)
        once = jnp.concatenate([once[:, :SIDE], once[:, SIDE:]], axis=0)
        both = once + dot(once.astype(BF), excess[...])
        model[c] = both[:SIDE]
        model[c + 1] = both[SIDE:]

    def forward_and_work(j, carry):
        forward(FIRST[-2] + j, 0)

        @pl.when(j == 0)
        def _():
            own = slots_for(fx)
            shares[0] = share_rows(own)
            arrived[0], arrived[1] = planes(own)

        @pl.when((j >= 1) & (j <= CH // 2))
        def _():
            there_and_back(2 * (j - 1))

        return carry

    lax.fori_loop(0, len(IN_ORDER) - 2 - FIRST[-2], forward_and_work, 0)

    def wait_share(i, carry):
        share_copy(i).wait_recv()
        return carry

    lax.fori_loop(0, len(PLACES), wait_share, 0)
    slots = n_fx * 2
    wide = slots * 16
    all_shares = shares[...].reshape(n_fx * 8, 128)
    members = jnp.where(all_shares > 0, 1.0, 0.0).astype(BF)
    spread = (
        lax.broadcasted_iota(jnp.int32, (CH * 16, 128), 0) // 16
        == lax.broadcasted_iota(jnp.int32, (CH * 16, 128), 1)
    )
    spread = jnp.where(spread, 1.0, 0.0).astype(BF)
    by_source = lax.dot_general(
        spread, members, (((1,), (1,)), ((), ())), preferred_element_type=F32
    ).astype(BF)
    weights = lax.dot_general(
        spread, all_shares.astype(BF), (((1,), (1,)), ((), ())), preferred_element_type=F32
    )
    totals = jnp.sum(weights, axis=1, keepdims=True)
    src_row = lax.broadcasted_iota(jnp.int32, (n_fx * 8, wide), 0)
    dst_col = lax.broadcasted_iota(jnp.int32, (n_fx * 8, wide), 1)
    widen = (src_row // 8 == dst_col // 32) & (src_row % 8 == dst_col // 16 % 2)
    widened = dot(by_source, jnp.where(widen, 1.0, 0.0).astype(BF))
    diagonal = (
        lax.broadcasted_iota(jnp.int32, (CH * 16, wide), 0) % 16
        == lax.broadcasted_iota(jnp.int32, (CH * 16, wide), 1) % 16
    )
    kron[...] = jnp.where(diagonal, widened, 0.0).astype(BF)
    scale = 1.0 / (1.0 + totals)

    def group_rows(g):
        return pl.ds(pl.multiple_of(g * 16, 16), 16)

    def without_tiles(g):
        pixels = sky[:, group_rows(g), :].reshape(CH * 16, SIDE)
        there = model[:, group_rows(g), :].reshape(CH * 16, SIDE)
        return pixels - (totals * scale) * there

    def wait_tiles(i, carry):
        landed(arrived.at[2 + i], tile_recv.at[2 + i]).wait_recv()
        return carry

    def with_sources(g, first, last):
        held = arrived[2 * first : 2 * last, group_rows(g), :].reshape((last - first) * 32, SIDE)
        before = without_tiles(g) if first == 0 else partial[g]
        return before + scale * dot(kron[:, first * 32 : last * 32], held)

    for first, last in ((0, 8), (8, 12)):
        lax.fori_loop(max(2 * first - 2, 0), 2 * last - 2, wait_tiles, 0)

        def add_sources(q, carry):
            for i in range(4):
                partial[q * 4 + i] = with_sources(q * 4 + i, first, last)
            return carry

        if first == 0:
            for k in range(2):
                forward(jnp.int32(len(IN_ORDER) - 2 + k), 0)
                lax.fori_loop(2 * k, 2 * k + 2, add_sources, 0)
        else:
            lax.fori_loop(0, SIDE // 64, add_sources, 0)
    lax.fori_loop(22, 2 * len(PLACES), wait_tiles, 0)

    def combine(g):
        rows = group_rows(g)
        new = with_sources(g, 12, 16).reshape(CH, 16, SIDE)
        extended[:, rows, :SIDE] = new.astype(BF)
        for k in range(PACKS):
            parts = [new[min(3 * k + m, CH - 1), :, :128] for m in range(3)]
            parts = [pltpu.roll(part, m * REACH, 1) if m else part for m, part in enumerate(parts)]
            columns[k, rows, :] = three_beside(*parts).astype(BF)

    chunks = 4
    deep = SIDE // chunks

    def columns_copy(q):
        rows = pl.ds(pl.multiple_of(q * deep, deep), deep)
        return pltpu.make_async_remote_copy(
            src_ref=columns.at[:, rows, :],
            dst_ref=beside.at[:, rows, :],
            send_sem=columns_send.at[q],
            recv_sem=columns_recv.at[q],
            device_id={"fx": prev},
            device_id_type=pl.DeviceIdType.MESH,
        )

    def halo_copy(i):
        source = (extended.at[:, :HALO, :SIDE], columns.at[:, :HALO, :])[i]
        target = (extended.at[:, SIDE:, :SIDE], corner)[i]
        where = ({"fy": up}, {"fy": up, "fx": prev})[i]
        return pltpu.make_async_remote_copy(
            src_ref=source,
            dst_ref=target,
            send_sem=halo_send.at[i],
            recv_sem=halo_recv.at[i],
            device_id=where,
            device_id_type=pl.DeviceIdType.MESH,
        )

    def make_chunk(q, carry):
        for i in range(deep // 16):
            combine(q * (deep // 16) + i)
        columns_copy(q).start()

        @pl.when(q == 0)
        def _():
            for i in range(2):
                halo_copy(i).start()

        return carry

    lax.fori_loop(0, chunks, make_chunk, 0)

    def place(source, begin, end):
        for c in range(CH):
            values = turned(source[c // 3].astype(F32), c % 3)
            extended[c, begin:end, SIDE:] = values.astype(BF)

    halo_copy(1).wait_recv()
    place(corner, SIDE, TALL)
    for q in range(chunks):
        columns_copy(q).wait_recv()
        place(beside.at[:, q * deep : (q + 1) * deep, :], q * deep, (q + 1) * deep)
    halo_copy(0).wait_recv()

    def finish_shares(i, carry):
        share_copy(i).wait_send()
        return carry

    def finish_sent(i, carry):
        for r in range(2):
            hop_copy(sending.at[i, r], tile_send.at[2 * i + r], jnp.int32(0), False).wait_send()
        return carry

    def finish_forwards(f, carry):
        hop_copy(relay.at[f], relay_send.at[f], jnp.int32(0), False).wait_send()
        return carry

    lax.fori_loop(0, len(PLACES), finish_shares, 0)
    lax.fori_loop(0, len(PLACES), finish_sent, 0)
    lax.fori_loop(0, len(IN_ORDER), finish_forwards, 0)
    for i in range(2):
        halo_copy(i).wait_send()
    for q in range(chunks):
        columns_copy(q).wait_send()


def spill_kernel(
    n_fy,
    n_fx,
    cells,
    left,
    above,
    corner,
    side,
    bottom,
    to_right,
    to_below,
    to_corner,
    load_sem,
    send_sem,
    recv_sem,
):
    load_side = pltpu.make_async_copy(cells.at[:, :, SIDE:], side, load_sem.at[0])
    load_bottom = pltpu.make_async_copy(cells.at[:, SIDE:, :SIDE], bottom, load_sem.at[1])
    load_side.start()
    load_bottom.start()
    fy = lax.axis_index("fy")
    fx = lax.axis_index("fx")
    up, down = (fy + n_fy - 1) % n_fy, (fy + 1) % n_fy
    prev, nxt = (fx + n_fx - 1) % n_fx, (fx + 1) % n_fx
    barrier = pltpu.get_barrier_semaphore()
    for where in (
        {"fy": up},
        {"fy": down},
        {"fx": prev},
        {"fx": nxt},
        {"fy": up, "fx": prev},
        {"fy": down, "fx": nxt},
    ):
        pl.semaphore_signal(barrier, inc=1, device_id=where, device_id_type=pl.DeviceIdType.MESH)
    load_side.wait()
    for k in range(PACKS):
        packed = three_beside(*[side[min(3 * k + m, CH - 1)] for m in range(3)]).astype(BF)
        to_right[k] = packed[:SIDE]
        to_corner[k] = packed[SIDE:]
    load_bottom.wait()
    to_below[...] = bottom[...].astype(BF)
    pl.semaphore_wait(barrier, 6)

    def spill_copy(i):
        return pltpu.make_async_remote_copy(
            src_ref=(to_right, to_below, to_corner)[i],
            dst_ref=(left, above, corner)[i],
            send_sem=send_sem.at[i],
            recv_sem=recv_sem.at[i],
            device_id=({"fx": nxt}, {"fy": down}, {"fy": down, "fx": nxt})[i],
            device_id_type=pl.DeviceIdType.MESH,
        )

    for i in range(3):
        spill_copy(i).start()
    for i in range(3):
        spill_copy(i).wait()


def add_kernel(cells, left, above, corner, out):
    for h in range(2):

        channel = 2 * pl.program_id(0) + h

        def columns(packed):
            values = packed[channel // 3].astype(F32)
            for m in range(1, 3):
                values = jnp.where(channel % 3 == m, turned(packed[channel // 3].astype(F32), m), values)
            lane = lax.broadcasted_iota(jnp.int32, values.shape, 1)
            return jnp.where(lane < REACH, values, 0.0)

        def finished(total):
            return jnp.maximum(total * (1.0 / BASES), 0.0)

        from_left = columns(left)
        from_above = above[h].astype(F32)
        first = from_left[:HALO] + from_above[:, :128] + columns(corner)
        out[h, :HALO, :128] = finished(cells[h, :HALO, :128] + first)
        out[h, :HALO, 128:] = finished(cells[h, :HALO, 128:] + from_above[:, 128:])
        out[h, HALO:, :128] = finished(cells[h, HALO:, :128] + from_left[HALO:])
        out[h, HALO:, 128:] = finished(cells[h, HALO:, 128:])


def per_device(n_fy, n_fx, sky_image, vis_tiles, tile_dest, tile_chan, tile_count, thresholds):
    made = {name: jnp.asarray(table) for name, table in tables().items()}
    smem = pl.BlockSpec(memory_space=pltpu.SMEM)
    vmem = pl.BlockSpec(memory_space=pltpu.VMEM)
    anywhere = pl.BlockSpec(memory_space=pl.ANY)
    dma = pltpu.SemaphoreType.DMA
    tiles = vis_tiles.shape[0]
    extended = pl.pallas_call(
        functools.partial(exchange_kernel, n_fy, n_fx),
        out_shape=pltpu.VMEM((CH, TALL, WIDE), BF),
        in_specs=[smem] * 3 + [anywhere] * 5,
        scratch_shapes=[
            pltpu.VMEM((2 * SIDE, 2 * SIDE), BF),
            pltpu.VMEM((SIDE, 2 * SIDE), BF),
            pltpu.VMEM((SIDE, SIDE), BF),
            pltpu.VMEM((tiles, 2, SIDE, SIDE), BF),
            pltpu.VMEM((CH, SIDE, SIDE), F32),
            pltpu.VMEM((CH, SIDE, SIDE), F32),
            pltpu.VMEM((SIDE // 16, CH * 16, SIDE), F32),
            pltpu.VMEM((n_fx, 2, SIDE, SIDE), BF),
            pltpu.VMEM((2 * n_fx, SIDE, SIDE), BF),
            pltpu.VMEM((len(IN_ORDER), SIDE, SIDE), BF),
            pltpu.VMEM((2, 2 * SIDE, SIDE), BF),
            pltpu.VMEM((n_fx, 8, 128), F32),
            pltpu.VMEM((n_fx, 8, 128), F32),
            pltpu.VMEM((CH * 16, n_fx * 32), BF),
            pltpu.VMEM((PACKS, SIDE, 128), BF),
            pltpu.VMEM((PACKS, SIDE, 128), BF),
            pltpu.VMEM((PACKS, HALO, 128), BF),
            dma((5,)),
            dma((2 * len(PLACES),)),
            dma((2 * n_fx,)),
            dma((len(IN_ORDER),)),
            dma((len(IN_ORDER),)),
            dma((n_fx,)),
            dma((n_fx,)),
            dma((2,)),
            dma((2,)),
            dma((4,)),
            dma((4,)),
        ],
        compiler_params=pltpu.CompilerParams(
            collective_id=0, has_side_effects=True, vmem_limit_bytes=58 * 1024 * 1024
        ),
    )(
        tile_dest.reshape(tiles),
        tile_chan,
        tile_count,
        made["fourier"],
        made["back"],
        made["excess"],
        sky_image,
        vis_tiles,
    )
    rows, columns = made["rows"], made["columns"]
    row_sec = jnp.einsum("bkn,cnx->bckx", rows, extended, preferred_element_type=F32).astype(BF)
    coefficient = jnp.einsum("bcyx,bkx->bcyk", row_sec, columns, preferred_element_type=F32)
    limits = thresholds.astype(F32)
    shrunk = (coefficient - jnp.clip(coefficient, -limits, limits)).astype(BF)
    row_sec = jnp.einsum("bjy,bcjk->bcyk", rows, shrunk, preferred_element_type=F32).astype(BF)
    cells = jnp.einsum("bcyk,bkx->cyx", row_sec, made["spread"], preferred_element_type=F32)
    left, above, corner = pl.pallas_call(
        functools.partial(spill_kernel, n_fy, n_fx),
        out_shape=(
            pltpu.VMEM((PACKS, SIDE, 128), BF),
            pltpu.VMEM((CH, HALO, SIDE), BF),
            pltpu.VMEM((PACKS, HALO, 128), BF),
        ),
        in_specs=[anywhere],
        scratch_shapes=[
            pltpu.VMEM((CH, TALL, 128), F32),
            pltpu.VMEM((CH, HALO, SIDE), F32),
            pltpu.VMEM((PACKS, SIDE, 128), BF),
            pltpu.VMEM((CH, HALO, SIDE), BF),
            pltpu.VMEM((PACKS, HALO, 128), BF),
            dma((2,)),
            dma((3,)),
            dma((3,)),
        ],
        compiler_params=pltpu.CompilerParams(
            collective_id=1, has_side_effects=True, vmem_limit_bytes=58 * 1024 * 1024
        ),
    )(cells)
    return pl.pallas_call(
        add_kernel,
        out_shape=jax.ShapeDtypeStruct((CH, SIDE, SIDE), F32),
        grid=(CH // 2,),
        in_specs=[
            pl.BlockSpec((2, SIDE, SIDE), lambda p: (p, 0, 0)),
            pl.BlockSpec((PACKS, SIDE, 128), lambda p: (0, 0, 0)),
            pl.BlockSpec((2, HALO, SIDE), lambda p: (p, 0, 0)),
            pl.BlockSpec((PACKS, HALO, 128), lambda p: (0, 0, 0)),
        ],
        out_specs=pl.BlockSpec((2, SIDE, SIDE), lambda p: (p, 0, 0)),
        compiler_params=pltpu.CompilerParams(vmem_limit_bytes=16 * 1024 * 1024),
    )(cells, left, above, corner)


def solution(mesh):
    in_specs = (
        P(None, "fy", "fx"),
        P(("fy", "fx"), None, None, None),
        P(("fy", "fx"), None),
        P(("fy", "fx")),
        P(("fy", "fx")),
        P(None, None, "fy", "fx"),
    )
    out_specs = P(None, "fy", "fx")
    return jax.shard_map(
        functools.partial(per_device, mesh.shape["fy"], mesh.shape["fx"]),
        mesh=mesh,
        in_specs=in_specs,
        out_specs=out_specs,
        check_vma=False,
    )
```

```python
import functools
import math

import jax
import jax.numpy as jnp
import ml_dtypes
import numpy as np
from jax import lax
from jax.experimental import pallas as pl
from jax.experimental.pallas import tpu as pltpu
from jax.sharding import PartitionSpec as P

daubechies_taps = [
    [0.7071067811865476, 0.7071067811865476],
    [0.48296291314469025, 0.836516303737469, 0.22414386804185735, -0.12940952255092145],
    [
        0.3326705529509569,
        0.8068915093133388,
        0.4598775021193313,
        -0.13501102001039084,
        -0.08544127388224149,
        0.035226291882100656,
    ],
    [
        0.23037781330885523,
        0.7148465705525415,
        0.6308807679295904,
        -0.02798376941698385,
        -0.18703481171888114,
        0.030841381835986965,
        0.032883011666982945,
        -0.010597401784997278,
    ],
    [
        0.160102397974125,
        0.6038292697974729,
        0.7243085284385744,
        0.13842814590110342,
        -0.24229488706619015,
        -0.03224486958502952,
        0.07757149384006515,
        -0.006241490213011705,
        -0.012580751999015526,
        0.003335725285001549,
    ],
    [
        0.11154074335008017,
        0.4946238903983854,
        0.7511339080215775,
        0.3152503517092432,
        -0.22626469396516913,
        -0.12976686756709563,
        0.09750160558707936,
        0.02752286553001629,
        -0.031582039318031156,
        0.0005538422009938016,
        0.004777257511010651,
        -0.00107730108499558,
    ],
    [
        0.07785205408506236,
        0.39653931948230575,
        0.7291320908465551,
        0.4697822874053586,
        -0.14390600392910627,
        -0.22403618499416572,
        0.07130921926705004,
        0.0806126091510659,
        -0.03802993693503463,
        -0.01657454163101562,
        0.012550998556013784,
        0.00042957797300470274,
        -0.0018016407039998328,
        0.0003537138000010399,
    ],
    [
        0.05441584224308161,
        0.3128715909144659,
        0.6756307362980128,
        0.5853546836548691,
        -0.015829105256023893,
        -0.2840155429624281,
        0.00047248457399797254,
        0.128747426620186,
        -0.01736930100202211,
        -0.04408825393106472,
        0.013981027917015516,
        0.008746094047015655,
        -0.00487035299301066,
        -0.0003917403729959771,
        0.0006754494059985568,
        -0.00011747678400228192,
    ],
]


SIDE = 256
CH = 8
BASES = 8
HALO = 48
BF = jnp.bfloat16
F32 = jnp.float32
WIDE = SIDE + 128
TALL = SIDE + HALO
REACH = 42
PACKS = 3


def rounded(table):
    return np.asarray(table, np.float32).astype(ml_dtypes.bfloat16)


def composite_tables():
    full = np.zeros((BASES, SIDE, SIDE + HALO))
    for degree in range(1, 9):
        taps = np.array(daubechies_taps[degree - 1])
        taps = taps * math.sqrt(2.0) / np.sum(taps)
        length = 2 * degree
        low = np.zeros(16)
        high = np.zeros(16)
        low[:length] = taps
        high[:length] = [(-1.0) ** j * taps[length - 1 - j] for j in range(length)]
        low = rounded(low).astype(np.float64)
        high = rounded(high).astype(np.float64)
        level_low = np.zeros((144, SIDE + HALO))
        level_high = np.zeros((128, SIDE + HALO))
        for k in range(144):
            level_low[k, 2 * k : 2 * k + 16] = low[: min(16, SIDE + HALO - 2 * k)]
        for k in range(128):
            level_high[k, 2 * k : 2 * k + 16] = high
        second = np.zeros((128, 144))
        for m in range(64):
            second[m, 2 * m : 2 * m + 16] = low
            second[64 + m, 2 * m : 2 * m + 16] = high
        full[degree - 1, :128] = second @ level_low
        full[degree - 1, 128:] = level_high
    return rounded(full).astype(np.float32)


@functools.lru_cache(maxsize=1)
def tables():
    full = composite_tables()
    wide = np.concatenate([full, np.zeros((BASES, SIDE, 128 - HALO), np.float32)], axis=2)
    assert not np.any(full[:, :, SIDE + REACH :])
    spread = wide.copy()
    for m in range(1, 3):
        at = SIDE + m * REACH
        spread[:, :, at : at + REACH] = full[:, :, SIDE : SIDE + REACH]
    out = {"rows": full, "columns": wide, "spread": spread}
    grid = np.arange(SIDE)[:, None] * np.arange(SIDE)[None, :] % SIDE
    angle = grid * (2.0 * math.pi / SIDE)
    cosine = rounded(np.cos(angle) / math.sqrt(SIDE)).astype(np.float64)
    sine = rounded(np.sin(angle) / math.sqrt(SIDE)).astype(np.float64)
    out["fourier"] = np.block([[cosine, sine], [-sine, cosine]])
    out["back"] = np.concatenate([cosine, -sine], axis=1)
    out["excess"] = cosine @ cosine + sine @ sine - np.eye(SIDE)
    return {name: rounded(table) for name, table in out.items()}


PLACES = (
    (2, 2),
    (1, 2),
    (3, 3),
    (3, 2),
    (3, 1),
    (2, 1),
    (2, 3),
    (1, 1),
    (0, 3),
    (1, 3),
    (0, 2),
    (0, 1),
    (1, 0),
    (2, 0),
    (3, 0),
)
STEP_X, STEP_Z = (1, 3, 0, 0), (0, 0, 1, 3)
PATHS = (
    (
        (3, 0, 0, 3),
        (2, 0, 2),
        (1, 3),
        (1, 3, 3),
        (2, 1),
        (2, 1, 1),
        (1, 1, 3),
        (0, 2),
        (3,),
        (0, 3),
        (3, 3),
        (2,),
        (0,),
        (0, 0),
        (1,),
    ),
    (
        (1, 2, 2, 1),
        (0, 2, 2),
        (3, 1),
        (3, 3, 1),
        (1, 2),
        (0, 2, 0),
        (0, 0, 3),
        (0, 2),
        (3,),
        (3, 0),
        (2, 2),
        (2,),
        (0,),
        (1, 1),
        (1,),
    ),
)
FORWARDS = (
    (),
    (),
    ((0, 0, 1), (0, 1, 1)),
    ((1, 0, 1), (1, 1, 1)),
    ((2, 0, 1), (2, 1, 1)),
    ((0, 0, 2), (0, 1, 2)),
    ((3, 0, 1), (3, 1, 1), (1, 0, 2), (1, 1, 2)),
    ((4, 1, 1), (4, 0, 1), (5, 1, 1)),
    ((3, 0, 2),),
    ((0, 0, 3), (5, 0, 1)),
    ((3, 1, 2), (6, 0, 1), (0, 1, 3), (6, 1, 1)),
    (),
    ((7, 0, 1),),
    ((5, 0, 2), (7, 1, 1)),
    ((9, 0, 1),),
    ((6, 0, 2), (9, 1, 1), (5, 1, 2), (6, 1, 2), (10, 1, 1), (10, 0, 1), (13, 1, 1), (13, 0, 1)),
)
COMING = (2, 8, 1, 3, 4, 0, 12, 11, 9, 6, 14, 5, 7, 10, 13)

IN_ORDER = [hop for step in FORWARDS for hop in step]
FIRST = [sum(len(step) for step in FORWARDS[:i]) for i in range(len(FORWARDS) + 1)]
RANK = [COMING.index(i) for i in range(len(PLACES))]


def coded(place, r, hop):
    steps = PATHS[r][place]
    if hop + 1 == len(steps):
        return steps[hop] + 4 + 8 * (2 * (1 + RANK[place]) + r)
    return steps[hop] + 8 * IN_ORDER.index((place, r, hop + 1))


START = [[coded(place, r, 0) for place in range(len(PLACES))] for r in range(2)]
ONWARD = [coded(*hop) for hop in IN_ORDER]
assert len(IN_ORDER) == sum(len(p) - 1 for r in range(2) for p in PATHS[r])
assert len(IN_ORDER) - 2 - FIRST[-2] > CH // 2
assert all(RANK[place] >= 7 for place, _, _ in IN_ORDER[-2:])


def choose(j, values):
    out = jnp.int32(values[0])
    for i, value in enumerate(values):
        out = jnp.where(j == i, jnp.int32(value), out)
    return out


def three_beside(first, second, third):
    lane = lax.broadcasted_iota(jnp.int32, first.shape, len(first.shape) - 1)
    return jnp.where(lane < REACH, first, jnp.where(lane < 2 * REACH, second, third))


def turned(values, m):
    return pltpu.roll(values, 128 - m * REACH, 1) if m else values


def dot(a, b):
    return jnp.dot(a, b, preferred_element_type=F32)


def exchange_kernel(
    n_fy,
    n_fx,
    dest_ref,
    chan_ref,
    count_ref,
    fourier_hbm,
    back_hbm,
    excess_hbm,
    sky_hbm,
    vis_hbm,
    extended,
    fourier,
    back,
    excess,
    vis,
    sky,
    model,
    partial,
    sending,
    arrived,
    relay,
    half,
    share_ref,
    shares,
    kron,
    columns,
    beside,
    corner,
    load_sem,
    tile_send,
    tile_recv,
    relay_send,
    relay_recv,
    share_send,
    share_recv,
    halo_send,
    halo_recv,
    columns_send,
    columns_recv,
):
    fy = lax.axis_index("fy")
    fx = lax.axis_index("fx")
    n_z = 4
    n_x = n_fx // n_z
    my_x, my_z = fx // n_z, fx % n_z

    def at(dx, dz):
        return (my_x + dx) % n_x * n_z + (my_z + dz) % n_z

    def peer(k):
        return at(k // n_z, k % n_z)

    load_vis = pltpu.make_async_copy(vis_hbm, vis, load_sem.at[0])
    load_sky = pltpu.make_async_copy(sky_hbm, sky, load_sem.at[1])
    load_vis.start()
    load_fourier = pltpu.make_async_copy(fourier_hbm, fourier, load_sem.at[2])
    load_back = pltpu.make_async_copy(back_hbm, back, load_sem.at[3])
    load_excess = pltpu.make_async_copy(excess_hbm, excess, load_sem.at[4])
    load_fourier.start()
    load_back.start()
    load_excess.start()
    load_sky.start()

    barrier = pltpu.get_barrier_semaphore()

    def greet(k, carry):
        pl.semaphore_signal(
            barrier, inc=1, device_id={"fx": peer(k)}, device_id_type=pl.DeviceIdType.MESH
        )
        return carry

    lax.fori_loop(1, n_fx, greet, 0)
    up, down = (fy + n_fy - 1) % n_fy, (fy + 1) % n_fy
    prev, nxt = (fx + n_fx - 1) % n_fx, (fx + 1) % n_fx
    for where in ({"fy": up}, {"fy": down}, {"fy": up, "fx": prev}, {"fy": down, "fx": nxt}):
        pl.semaphore_signal(barrier, inc=1, device_id=where, device_id_type=pl.DeviceIdType.MESH)

    def place_of(i):
        return at(choose(i, [p[0] for p in PLACES]), choose(i, [p[1] for p in PLACES]))

    def share_copy(i):
        rank = 1 + choose(i, RANK)
        return pltpu.make_async_remote_copy(
            src_ref=share_ref.at[rank],
            dst_ref=shares.at[rank],
            send_sem=share_send.at[rank],
            recv_sem=share_recv.at[rank],
            device_id={"fx": place_of(i)},
            device_id_type=pl.DeviceIdType.MESH,
        )

    def hop_copy(source, send_sem, code, last):
        step, to = code % 4, code // 8
        return pltpu.make_async_remote_copy(
            src_ref=source,
            dst_ref=arrived.at[to] if last else relay.at[to],
            send_sem=send_sem,
            recv_sem=tile_recv.at[to] if last else relay_recv.at[to],
            device_id={"fx": at(choose(step, STEP_X), choose(step, STEP_Z))},
            device_id_type=pl.DeviceIdType.MESH,
        )

    def hop_start(source, send_sem, code):
        @pl.when(code // 4 % 2 == 1)
        def _():
            hop_copy(source, send_sem, code, True).start()

        @pl.when(code // 4 % 2 == 0)
        def _():
            hop_copy(source, send_sem, code, False).start()

    def landed(buffer, sem):
        return pltpu.make_async_remote_copy(
            src_ref=buffer,
            dst_ref=buffer,
            send_sem=tile_send.at[0],
            recv_sem=sem,
            device_id={"fx": at(1, 0)},
            device_id_type=pl.DeviceIdType.MESH,
        )

    def forward(f, carry):
        landed(relay.at[f], relay_recv.at[f]).wait_recv()
        hop_start(relay.at[f], relay_send.at[f], choose(f, ONWARD))
        return carry

    tiles = vis_hbm.shape[0]
    row = lax.broadcasted_iota(jnp.int32, (8, 128), 0)
    lane = lax.broadcasted_iota(jnp.int32, (8, 128), 1)

    def slots_for(to):
        found = jnp.int32(0)
        picked = [(jnp.int32(0), jnp.int32(0), jnp.int32(0))] * 2
        for i in range(tiles):
            match = dest_ref[i] == to
            for r in range(2):
                here = match & (found == r)
                new = (jnp.int32(i), count_ref[i], chan_ref[i])
                picked[r] = tuple(jnp.where(here, a, b) for a, b in zip(new, picked[r]))
            found = found + jnp.where(match, 1, 0)
        return [(tile, count.astype(F32) * (1.0 / 64.0), chan) for tile, count, chan in picked]

    def share_rows(slots):
        total = jnp.zeros((8, 128), F32)
        for r, (_, weight, chan) in enumerate(slots):
            total = total + jnp.where((row == r) & (lane == chan), weight, 0.0)
        return total

    load_fourier.wait()
    load_back.wait()
    load_vis.wait()

    def planes(slots):
        for i, (t, _, _) in enumerate(slots):
            spectrum = jnp.concatenate([vis[t, 0], vis[t, 1]], axis=1)
            for part in range(2):
                half[i, part * SIDE : (part + 1) * SIDE] = dot(
                    spectrum, fourier[:, part * SIDE : (part + 1) * SIDE]
                ).astype(BF)
        return [(dot(back[...], half[i]) * slots[i][1]).astype(BF) for i in range(2)]

    def prepare(i):
        slots = slots_for(place_of(i))
        share_ref[1 + choose(i, RANK)] = share_rows(slots)
        sending[i, 0], sending[i, 1] = planes(slots)

    prepare(jnp.int32(0))
    pl.semaphore_wait(barrier, n_fx - 1 + 4)

    def send_tiles(i, carry):
        share_copy(i).start()
        for r in range(2):
            hop_start(sending.at[i, r], tile_send.at[2 * i + r], choose(i, START[r]))
        lax.fori_loop(choose(i, FIRST), choose(i + 1, FIRST), forward, 0)

        @pl.when(i < len(PLACES) - 1)
        def _():
            prepare(i + 1)

        return carry

    lax.fori_loop(0, len(PLACES), send_tiles, 0)

    load_sky.wait()
    load_excess.wait()

    def there_and_back(c):
        pixels = jnp.concatenate([sky[c].astype(BF), sky[c + 1].astype(BF)], axis=1)
        once = pixels.astype(F32) + dot(excess[...], pixels)
        once = jnp.concatenate([once[:, :SIDE], once[:, SIDE:]], axis=0)
        both = once + dot(once.astype(BF), excess[...])
        model[c] = both[:SIDE]
        model[c + 1] = both[SIDE:]

    def forward_and_work(j, carry):
        forward(FIRST[-2] + j, 0)

        @pl.when(j == 0)
        def _():
            own = slots_for(fx)
            shares[0] = share_rows(own)
            arrived[0], arrived[1] = planes(own)

        @pl.when((j >= 1) & (j <= CH // 2))
        def _():
            there_and_back(2 * (j - 1))

        return carry

    lax.fori_loop(0, len(IN_ORDER) - 2 - FIRST[-2], forward_and_work, 0)

    def wait_share(i, carry):
        share_copy(i).wait_recv()
        return carry

    lax.fori_loop(0, len(PLACES), wait_share, 0)
    slots = n_fx * 2
    wide = slots * 16
    all_shares = shares[...].reshape(n_fx * 8, 128)
    members = jnp.where(all_shares > 0, 1.0, 0.0).astype(BF)
    spread = (
        lax.broadcasted_iota(jnp.int32, (CH * 16, 128), 0) // 16
        == lax.broadcasted_iota(jnp.int32, (CH * 16, 128), 1)
    )
    spread = jnp.where(spread, 1.0, 0.0).astype(BF)
    by_source = lax.dot_general(
        spread, members, (((1,), (1,)), ((), ())), preferred_element_type=F32
    ).astype(BF)
    weights = lax.dot_general(
        spread, all_shares.astype(BF), (((1,), (1,)), ((), ())), preferred_element_type=F32
    )
    totals = jnp.sum(weights, axis=1, keepdims=True)
    src_row = lax.broadcasted_iota(jnp.int32, (n_fx * 8, wide), 0)
    dst_col = lax.broadcasted_iota(jnp.int32, (n_fx * 8, wide), 1)
    widen = (src_row // 8 == dst_col // 32) & (src_row % 8 == dst_col // 16 % 2)
    widened = dot(by_source, jnp.where(widen, 1.0, 0.0).astype(BF))
    diagonal = (
        lax.broadcasted_iota(jnp.int32, (CH * 16, wide), 0) % 16
        == lax.broadcasted_iota(jnp.int32, (CH * 16, wide), 1) % 16
    )
    kron[...] = jnp.where(diagonal, widened, 0.0).astype(BF)
    scale = 1.0 / (1.0 + totals)

    def group_rows(g):
        return pl.ds(pl.multiple_of(g * 16, 16), 16)

    def without_tiles(g):
        pixels = sky[:, group_rows(g), :].reshape(CH * 16, SIDE)
        there = model[:, group_rows(g), :].reshape(CH * 16, SIDE)
        return pixels - (totals * scale) * there

    def wait_tiles(i, carry):
        landed(arrived.at[2 + i], tile_recv.at[2 + i]).wait_recv()
        return carry

    def with_sources(g, first, last):
        held = arrived[2 * first : 2 * last, group_rows(g), :].reshape((last - first) * 32, SIDE)
        before = without_tiles(g) if first == 0 else partial[g]
        return before + scale * dot(kron[:, first * 32 : last * 32], held)

    for first, last in ((0, 8), (8, 12)):
        lax.fori_loop(max(2 * first - 2, 0), 2 * last - 2, wait_tiles, 0)

        def add_sources(q, carry):
            for i in range(4):
                partial[q * 4 + i] = with_sources(q * 4 + i, first, last)
            return carry

        if first == 0:
            for k in range(2):
                forward(jnp.int32(len(IN_ORDER) - 2 + k), 0)
                lax.fori_loop(2 * k, 2 * k + 2, add_sources, 0)
        else:
            lax.fori_loop(0, SIDE // 64, add_sources, 0)
    lax.fori_loop(22, 2 * len(PLACES), wait_tiles, 0)

    def combine(g):
        rows = group_rows(g)
        new = with_sources(g, 12, 16).reshape(CH, 16, SIDE)
        extended[:, rows, :SIDE] = new.astype(BF)
        for k in range(PACKS):
            parts = [new[min(3 * k + m, CH - 1), :, :128] for m in range(3)]
            parts = [pltpu.roll(part, m * REACH, 1) if m else part for m, part in enumerate(parts)]
            columns[k, rows, :] = three_beside(*parts).astype(BF)

    chunks = 8
    deep = SIDE // chunks

    def columns_copy(q):
        rows = pl.ds(pl.multiple_of(q * deep, deep), deep)
        return pltpu.make_async_remote_copy(
            src_ref=columns.at[:, rows, :],
            dst_ref=beside.at[:, rows, :],
            send_sem=columns_send.at[q],
            recv_sem=columns_recv.at[q],
            device_id={"fx": prev},
            device_id_type=pl.DeviceIdType.MESH,
        )

    def halo_copy(i):
        source = (extended.at[:, :HALO, :SIDE], columns.at[:, :HALO, :])[i]
        target = (extended.at[:, SIDE:, :SIDE], corner)[i]
        where = ({"fy": up}, {"fy": up, "fx": prev})[i]
        return pltpu.make_async_remote_copy(
            src_ref=source,
            dst_ref=target,
            send_sem=halo_send.at[i],
            recv_sem=halo_recv.at[i],
            device_id=where,
            device_id_type=pl.DeviceIdType.MESH,
        )

    def make_chunk(q, carry):
        for i in range(deep // 16):
            combine(q * (deep // 16) + i)
        columns_copy(q).start()

        @pl.when(q == (HALO - 1) // deep)
        def _():
            for i in range(2):
                halo_copy(i).start()

        return carry

    lax.fori_loop(0, chunks, make_chunk, 0)

    def place(source, begin, end):
        for c in range(CH):
            values = turned(source[c // 3].astype(F32), c % 3)
            extended[c, begin:end, SIDE:] = values.astype(BF)

    halo_copy(1).wait_recv()
    place(corner, SIDE, TALL)
    for q in range(chunks):
        columns_copy(q).wait_recv()
        place(beside.at[:, q * deep : (q + 1) * deep, :], q * deep, (q + 1) * deep)
    halo_copy(0).wait_recv()

    def finish_shares(i, carry):
        share_copy(i).wait_send()
        return carry

    def finish_sent(i, carry):
        for r in range(2):
            hop_copy(sending.at[i, r], tile_send.at[2 * i + r], jnp.int32(0), False).wait_send()
        return carry

    def finish_forwards(f, carry):
        hop_copy(relay.at[f], relay_send.at[f], jnp.int32(0), False).wait_send()
        return carry

    lax.fori_loop(0, len(PLACES), finish_shares, 0)
    lax.fori_loop(0, len(PLACES), finish_sent, 0)
    lax.fori_loop(0, len(IN_ORDER), finish_forwards, 0)
    for i in range(2):
        halo_copy(i).wait_send()
    for q in range(chunks):
        columns_copy(q).wait_send()


def spill_kernel(
    n_fy,
    n_fx,
    cells,
    left,
    above,
    corner,
    side,
    bottom,
    to_right,
    to_below,
    to_corner,
    load_sem,
    send_sem,
    recv_sem,
):
    threes = [(3 * k, min(3 * k + 3, CH)) for k in range(PACKS)]
    loads = [
        pltpu.make_async_copy(cells.at[a:e, :, SIDE:], side.at[a:e], load_sem.at[k])
        for k, (a, e) in enumerate(threes)
    ]
    load_bottom = pltpu.make_async_copy(cells.at[:, SIDE:, :SIDE], bottom, load_sem.at[PACKS])
    for load in loads:
        load.start()
    load_bottom.start()
    fy = lax.axis_index("fy")
    fx = lax.axis_index("fx")
    up, down = (fy + n_fy - 1) % n_fy, (fy + 1) % n_fy
    prev, nxt = (fx + n_fx - 1) % n_fx, (fx + 1) % n_fx
    barrier = pltpu.get_barrier_semaphore()
    for where in (
        {"fy": up},
        {"fy": down},
        {"fx": prev},
        {"fx": nxt},
        {"fy": up, "fx": prev},
        {"fy": down, "fx": nxt},
    ):
        pl.semaphore_signal(barrier, inc=1, device_id=where, device_id_type=pl.DeviceIdType.MESH)
    pl.semaphore_wait(barrier, 6)

    def spill_copy(source, target, where, sem):
        return pltpu.make_async_remote_copy(
            src_ref=source,
            dst_ref=target,
            send_sem=send_sem.at[sem],
            recv_sem=recv_sem.at[sem],
            device_id=where,
            device_id_type=pl.DeviceIdType.MESH,
        )

    copies = []
    for k in range(PACKS):
        loads[k].wait()
        packed = three_beside(*[side[min(3 * k + m, CH - 1)] for m in range(3)]).astype(BF)
        to_right[k] = packed[:SIDE]
        to_corner[k] = packed[SIDE:]
        copies.append(spill_copy(to_right.at[k], left.at[k], {"fx": nxt}, k))
        copies[-1].start()
    copies.append(spill_copy(to_corner, corner, {"fy": down, "fx": nxt}, PACKS))
    copies[-1].start()
    load_bottom.wait()
    to_below[...] = bottom[...].astype(BF)
    copies.append(spill_copy(to_below, above, {"fy": down}, PACKS + 1))
    copies[-1].start()
    for copy in copies:
        copy.wait()


def add_kernel(cells, left, above, corner, out):
    for h in range(4):

        channel = 4 * pl.program_id(0) + h

        def columns(packed):
            values = packed[channel // 3].astype(F32)
            for m in range(1, 3):
                values = jnp.where(channel % 3 == m, turned(packed[channel // 3].astype(F32), m), values)
            lane = lax.broadcasted_iota(jnp.int32, values.shape, 1)
            return jnp.where(lane < REACH, values, 0.0)

        def finished(total):
            return jnp.maximum(total * (1.0 / BASES), 0.0)

        from_left = columns(left)
        from_above = above[h].astype(F32)
        first = from_left[:HALO] + from_above[:, :128] + columns(corner)
        out[h, :HALO, :128] = finished(cells[h, :HALO, :128] + first)
        out[h, :HALO, 128:] = finished(cells[h, :HALO, 128:] + from_above[:, 128:])
        out[h, HALO:, :128] = finished(cells[h, HALO:, :128] + from_left[HALO:])
        out[h, HALO:, 128:] = finished(cells[h, HALO:, 128:])


def per_device(n_fy, n_fx, sky_image, vis_tiles, tile_dest, tile_chan, tile_count, thresholds):
    made = {name: jnp.asarray(table) for name, table in tables().items()}
    smem = pl.BlockSpec(memory_space=pltpu.SMEM)
    vmem = pl.BlockSpec(memory_space=pltpu.VMEM)
    anywhere = pl.BlockSpec(memory_space=pl.ANY)
    dma = pltpu.SemaphoreType.DMA
    tiles = vis_tiles.shape[0]
    extended = pl.pallas_call(
        functools.partial(exchange_kernel, n_fy, n_fx),
        out_shape=pltpu.VMEM((CH, TALL, WIDE), BF),
        in_specs=[smem] * 3 + [anywhere] * 5,
        scratch_shapes=[
            pltpu.VMEM((2 * SIDE, 2 * SIDE), BF),
            pltpu.VMEM((SIDE, 2 * SIDE), BF),
            pltpu.VMEM((SIDE, SIDE), BF),
            pltpu.VMEM((tiles, 2, SIDE, SIDE), BF),
            pltpu.VMEM((CH, SIDE, SIDE), F32),
            pltpu.VMEM((CH, SIDE, SIDE), F32),
            pltpu.VMEM((SIDE // 16, CH * 16, SIDE), F32),
            pltpu.VMEM((n_fx, 2, SIDE, SIDE), BF),
            pltpu.VMEM((2 * n_fx, SIDE, SIDE), BF),
            pltpu.VMEM((len(IN_ORDER), SIDE, SIDE), BF),
            pltpu.VMEM((2, 2 * SIDE, SIDE), BF),
            pltpu.VMEM((n_fx, 8, 128), F32),
            pltpu.VMEM((n_fx, 8, 128), F32),
            pltpu.VMEM((CH * 16, n_fx * 32), BF),
            pltpu.VMEM((PACKS, SIDE, 128), BF),
            pltpu.VMEM((PACKS, SIDE, 128), BF),
            pltpu.VMEM((PACKS, HALO, 128), BF),
            dma((5,)),
            dma((2 * len(PLACES),)),
            dma((2 * n_fx,)),
            dma((len(IN_ORDER),)),
            dma((len(IN_ORDER),)),
            dma((n_fx,)),
            dma((n_fx,)),
            dma((2,)),
            dma((2,)),
            dma((8,)),
            dma((8,)),
        ],
        compiler_params=pltpu.CompilerParams(
            collective_id=0, has_side_effects=True, vmem_limit_bytes=58 * 1024 * 1024
        ),
    )(
        tile_dest.reshape(tiles),
        tile_chan,
        tile_count,
        made["fourier"],
        made["back"],
        made["excess"],
        sky_image,
        vis_tiles,
    )
    rows, columns = made["rows"], made["columns"]
    row_sec = jnp.einsum("bkn,cnx->bckx", rows, extended, preferred_element_type=F32).astype(BF)
    coefficient = jnp.einsum("bcyx,bkx->bcyk", row_sec, columns, preferred_element_type=F32)
    limits = thresholds.astype(F32)
    shrunk = (coefficient - jnp.clip(coefficient, -limits, limits)).astype(BF)
    row_sec = jnp.einsum("bjy,bcjk->bcyk", rows, shrunk, preferred_element_type=F32).astype(BF)
    cells = jnp.einsum("bcyk,bkx->cyx", row_sec, made["spread"], preferred_element_type=F32)
    left, above, corner = pl.pallas_call(
        functools.partial(spill_kernel, n_fy, n_fx),
        out_shape=(
            pltpu.VMEM((PACKS, SIDE, 128), BF),
            pltpu.VMEM((CH, HALO, SIDE), BF),
            pltpu.VMEM((PACKS, HALO, 128), BF),
        ),
        in_specs=[anywhere],
        scratch_shapes=[
            pltpu.VMEM((CH, TALL, 128), F32),
            pltpu.VMEM((CH, HALO, SIDE), F32),
            pltpu.VMEM((PACKS, SIDE, 128), BF),
            pltpu.VMEM((CH, HALO, SIDE), BF),
            pltpu.VMEM((PACKS, HALO, 128), BF),
            dma((PACKS + 1,)),
            dma((PACKS + 2,)),
            dma((PACKS + 2,)),
        ],
        compiler_params=pltpu.CompilerParams(
            collective_id=1, has_side_effects=True, vmem_limit_bytes=58 * 1024 * 1024
        ),
    )(cells)
    return pl.pallas_call(
        add_kernel,
        out_shape=jax.ShapeDtypeStruct((CH, SIDE, SIDE), F32),
        grid=(CH // 4,),
        in_specs=[
            pl.BlockSpec((4, SIDE, SIDE), lambda p: (p, 0, 0)),
            pl.BlockSpec((PACKS, SIDE, 128), lambda p: (0, 0, 0)),
            pl.BlockSpec((4, HALO, SIDE), lambda p: (p, 0, 0)),
            pl.BlockSpec((PACKS, HALO, 128), lambda p: (0, 0, 0)),
        ],
        out_specs=pl.BlockSpec((4, SIDE, SIDE), lambda p: (p, 0, 0)),
        compiler_params=pltpu.CompilerParams(vmem_limit_bytes=16 * 1024 * 1024),
    )(cells, left, above, corner)


def solution(mesh):
    in_specs = (
        P(None, "fy", "fx"),
        P(("fy", "fx"), None, None, None),
        P(("fy", "fx"), None),
        P(("fy", "fx")),
        P(("fy", "fx")),
        P(None, None, "fy", "fx"),
    )
    out_specs = P(None, "fy", "fx")
    return jax.shard_map(
        functools.partial(per_device, mesh.shape["fy"], mesh.shape["fx"]),
        mesh=mesh,
        in_specs=in_specs,
        out_specs=out_specs,
        check_vma=False,
    )
```

```python
import functools
import math

import jax
import jax.numpy as jnp
import ml_dtypes
import numpy as np
from jax import lax
from jax.experimental import pallas as pl
from jax.experimental.pallas import tpu as pltpu
from jax.sharding import PartitionSpec as P

daubechies_taps = [
    [0.7071067811865476, 0.7071067811865476],
    [0.48296291314469025, 0.836516303737469, 0.22414386804185735, -0.12940952255092145],
    [
        0.3326705529509569,
        0.8068915093133388,
        0.4598775021193313,
        -0.13501102001039084,
        -0.08544127388224149,
        0.035226291882100656,
    ],
    [
        0.23037781330885523,
        0.7148465705525415,
        0.6308807679295904,
        -0.02798376941698385,
        -0.18703481171888114,
        0.030841381835986965,
        0.032883011666982945,
        -0.010597401784997278,
    ],
    [
        0.160102397974125,
        0.6038292697974729,
        0.7243085284385744,
        0.13842814590110342,
        -0.24229488706619015,
        -0.03224486958502952,
        0.07757149384006515,
        -0.006241490213011705,
        -0.012580751999015526,
        0.003335725285001549,
    ],
    [
        0.11154074335008017,
        0.4946238903983854,
        0.7511339080215775,
        0.3152503517092432,
        -0.22626469396516913,
        -0.12976686756709563,
        0.09750160558707936,
        0.02752286553001629,
        -0.031582039318031156,
        0.0005538422009938016,
        0.004777257511010651,
        -0.00107730108499558,
    ],
    [
        0.07785205408506236,
        0.39653931948230575,
        0.7291320908465551,
        0.4697822874053586,
        -0.14390600392910627,
        -0.22403618499416572,
        0.07130921926705004,
        0.0806126091510659,
        -0.03802993693503463,
        -0.01657454163101562,
        0.012550998556013784,
        0.00042957797300470274,
        -0.0018016407039998328,
        0.0003537138000010399,
    ],
    [
        0.05441584224308161,
        0.3128715909144659,
        0.6756307362980128,
        0.5853546836548691,
        -0.015829105256023893,
        -0.2840155429624281,
        0.00047248457399797254,
        0.128747426620186,
        -0.01736930100202211,
        -0.04408825393106472,
        0.013981027917015516,
        0.008746094047015655,
        -0.00487035299301066,
        -0.0003917403729959771,
        0.0006754494059985568,
        -0.00011747678400228192,
    ],
]


SIDE = 256
CH = 8
BASES = 8
HALO = 48
BF = jnp.bfloat16
F32 = jnp.float32
WIDE = SIDE + 128
TALL = SIDE + HALO
REACH = 42
PACKS = 3


def rounded(table):
    return np.asarray(table, np.float32).astype(ml_dtypes.bfloat16)


def composite_tables():
    full = np.zeros((BASES, SIDE, SIDE + HALO))
    for degree in range(1, 9):
        taps = np.array(daubechies_taps[degree - 1])
        taps = taps * math.sqrt(2.0) / np.sum(taps)
        length = 2 * degree
        low = np.zeros(16)
        high = np.zeros(16)
        low[:length] = taps
        high[:length] = [(-1.0) ** j * taps[length - 1 - j] for j in range(length)]
        low = rounded(low).astype(np.float64)
        high = rounded(high).astype(np.float64)
        level_low = np.zeros((144, SIDE + HALO))
        level_high = np.zeros((128, SIDE + HALO))
        for k in range(144):
            level_low[k, 2 * k : 2 * k + 16] = low[: min(16, SIDE + HALO - 2 * k)]
        for k in range(128):
            level_high[k, 2 * k : 2 * k + 16] = high
        second = np.zeros((128, 144))
        for m in range(64):
            second[m, 2 * m : 2 * m + 16] = low
            second[64 + m, 2 * m : 2 * m + 16] = high
        full[degree - 1, :128] = second @ level_low
        full[degree - 1, 128:] = level_high
    return rounded(full).astype(np.float32)


@functools.lru_cache(maxsize=1)
def tables():
    full = composite_tables()
    wide = np.concatenate([full, np.zeros((BASES, SIDE, 128 - HALO), np.float32)], axis=2)
    assert not np.any(full[:, :, SIDE + REACH :])
    spread = wide.copy()
    for m in range(1, 3):
        at = SIDE + m * REACH
        spread[:, :, at : at + REACH] = full[:, :, SIDE : SIDE + REACH]
    out = {"rows": full, "columns": wide, "spread": spread}
    grid = np.arange(SIDE)[:, None] * np.arange(SIDE)[None, :] % SIDE
    angle = grid * (2.0 * math.pi / SIDE)
    cosine = rounded(np.cos(angle) / math.sqrt(SIDE)).astype(np.float64)
    sine = rounded(np.sin(angle) / math.sqrt(SIDE)).astype(np.float64)
    out["fourier"] = np.block([[cosine, sine], [-sine, cosine]])
    out["back"] = np.concatenate([cosine, -sine], axis=1)
    out["excess"] = cosine @ cosine + sine @ sine - np.eye(SIDE)
    return {name: rounded(table) for name, table in out.items()}


PLACES = (
    (2, 2),
    (1, 2),
    (3, 3),
    (3, 2),
    (3, 1),
    (2, 1),
    (2, 3),
    (1, 1),
    (0, 3),
    (1, 3),
    (0, 2),
    (0, 1),
    (1, 0),
    (2, 0),
    (3, 0),
)
STEP_X, STEP_Z = (1, 3, 0, 0), (0, 0, 1, 3)
PATHS = (
    (
        (3, 0, 0, 3),
        (2, 0, 2),
        (1, 3),
        (1, 3, 3),
        (2, 1),
        (2, 1, 1),
        (1, 1, 3),
        (0, 2),
        (3,),
        (0, 3),
        (3, 3),
        (2,),
        (0,),
        (0, 0),
        (1,),
    ),
    (
        (1, 2, 2, 1),
        (0, 2, 2),
        (3, 1),
        (3, 3, 1),
        (1, 2),
        (0, 2, 0),
        (0, 0, 3),
        (0, 2),
        (3,),
        (3, 0),
        (2, 2),
        (2,),
        (0,),
        (1, 1),
        (1,),
    ),
)
FORWARDS = (
    (),
    (),
    ((0, 0, 1), (0, 1, 1)),
    ((1, 0, 1), (1, 1, 1)),
    ((2, 0, 1), (2, 1, 1)),
    ((0, 0, 2), (0, 1, 2)),
    ((3, 0, 1), (3, 1, 1), (1, 0, 2), (1, 1, 2)),
    ((4, 1, 1), (4, 0, 1), (5, 1, 1)),
    ((3, 0, 2),),
    ((0, 0, 3), (5, 0, 1)),
    ((3, 1, 2), (6, 0, 1), (0, 1, 3), (6, 1, 1)),
    (),
    ((7, 0, 1),),
    ((5, 0, 2), (7, 1, 1)),
    ((9, 0, 1),),
    ((6, 0, 2), (9, 1, 1), (5, 1, 2), (6, 1, 2), (10, 1, 1), (10, 0, 1), (13, 1, 1), (13, 0, 1)),
)
COMING = (2, 8, 1, 3, 4, 0, 12, 11, 9, 6, 14, 5, 7, 10, 13)

IN_ORDER = [hop for step in FORWARDS for hop in step]
FIRST = [sum(len(step) for step in FORWARDS[:i]) for i in range(len(FORWARDS) + 1)]
RANK = [COMING.index(i) for i in range(len(PLACES))]


def coded(place, r, hop):
    steps = PATHS[r][place]
    if hop + 1 == len(steps):
        return steps[hop] + 4 + 8 * (2 * (1 + RANK[place]) + r)
    return steps[hop] + 8 * IN_ORDER.index((place, r, hop + 1))


START = [[coded(place, r, 0) for place in range(len(PLACES))] for r in range(2)]
ONWARD = [coded(*hop) for hop in IN_ORDER]
assert len(IN_ORDER) == sum(len(p) - 1 for r in range(2) for p in PATHS[r])
assert len(IN_ORDER) - 2 - FIRST[-2] > CH // 2
assert all(RANK[place] >= 7 for place, _, _ in IN_ORDER[-2:])


def choose(j, values):
    out = jnp.int32(values[0])
    for i, value in enumerate(values):
        out = jnp.where(j == i, jnp.int32(value), out)
    return out


def three_beside(first, second, third):
    lane = lax.broadcasted_iota(jnp.int32, first.shape, len(first.shape) - 1)
    return jnp.where(lane < REACH, first, jnp.where(lane < 2 * REACH, second, third))


def turned(values, m):
    return pltpu.roll(values, 128 - m * REACH, 1) if m else values


def dot(a, b):
    return jnp.dot(a, b, preferred_element_type=F32)


def exchange_kernel(
    n_fy,
    n_fx,
    dest_ref,
    chan_ref,
    count_ref,
    fourier_hbm,
    back_hbm,
    excess_hbm,
    sky_hbm,
    vis_hbm,
    extended,
    fourier,
    back,
    excess,
    vis,
    sky,
    model,
    partial,
    sending,
    arrived,
    relay,
    half,
    share_ref,
    shares,
    kron,
    columns,
    beside,
    corner,
    load_sem,
    tile_send,
    tile_recv,
    relay_send,
    relay_recv,
    share_send,
    share_recv,
    halo_send,
    halo_recv,
    columns_send,
    columns_recv,
):
    fy = lax.axis_index("fy")
    fx = lax.axis_index("fx")
    n_z = 4
    n_x = n_fx // n_z
    my_x, my_z = fx // n_z, fx % n_z

    def at(dx, dz):
        return (my_x + dx) % n_x * n_z + (my_z + dz) % n_z

    def peer(k):
        return at(k // n_z, k % n_z)

    load_vis = pltpu.make_async_copy(vis_hbm, vis, load_sem.at[0])
    load_sky = pltpu.make_async_copy(sky_hbm, sky, load_sem.at[1])
    load_vis.start()
    load_fourier = pltpu.make_async_copy(fourier_hbm, fourier, load_sem.at[2])
    load_back = pltpu.make_async_copy(back_hbm, back, load_sem.at[3])
    load_excess = pltpu.make_async_copy(excess_hbm, excess, load_sem.at[4])
    load_fourier.start()
    load_back.start()
    load_excess.start()
    load_sky.start()

    barrier = pltpu.get_barrier_semaphore()

    def greet(k, carry):
        pl.semaphore_signal(
            barrier, inc=1, device_id={"fx": peer(k)}, device_id_type=pl.DeviceIdType.MESH
        )
        return carry

    lax.fori_loop(1, n_fx, greet, 0)
    up, down = (fy + n_fy - 1) % n_fy, (fy + 1) % n_fy
    prev, nxt = (fx + n_fx - 1) % n_fx, (fx + 1) % n_fx
    for where in ({"fy": up}, {"fy": down}, {"fy": up, "fx": prev}, {"fy": down, "fx": nxt}):
        pl.semaphore_signal(barrier, inc=1, device_id=where, device_id_type=pl.DeviceIdType.MESH)

    def place_of(i):
        return at(choose(i, [p[0] for p in PLACES]), choose(i, [p[1] for p in PLACES]))

    def share_copy(i):
        rank = 1 + choose(i, RANK)
        return pltpu.make_async_remote_copy(
            src_ref=share_ref.at[rank],
            dst_ref=shares.at[rank],
            send_sem=share_send.at[rank],
            recv_sem=share_recv.at[rank],
            device_id={"fx": place_of(i)},
            device_id_type=pl.DeviceIdType.MESH,
        )

    def hop_copy(source, send_sem, code, last):
        step, to = code % 4, code // 8
        return pltpu.make_async_remote_copy(
            src_ref=source,
            dst_ref=arrived.at[to] if last else relay.at[to],
            send_sem=send_sem,
            recv_sem=tile_recv.at[to] if last else relay_recv.at[to],
            device_id={"fx": at(choose(step, STEP_X), choose(step, STEP_Z))},
            device_id_type=pl.DeviceIdType.MESH,
        )

    def hop_start(source, send_sem, code):
        @pl.when(code // 4 % 2 == 1)
        def _():
            hop_copy(source, send_sem, code, True).start()

        @pl.when(code // 4 % 2 == 0)
        def _():
            hop_copy(source, send_sem, code, False).start()

    def landed(buffer, sem):
        return pltpu.make_async_remote_copy(
            src_ref=buffer,
            dst_ref=buffer,
            send_sem=tile_send.at[0],
            recv_sem=sem,
            device_id={"fx": at(1, 0)},
            device_id_type=pl.DeviceIdType.MESH,
        )

    def forward(f, carry):
        landed(relay.at[f], relay_recv.at[f]).wait_recv()
        hop_start(relay.at[f], relay_send.at[f], choose(f, ONWARD))
        return carry

    tiles = vis_hbm.shape[0]
    row = lax.broadcasted_iota(jnp.int32, (8, 128), 0)
    lane = lax.broadcasted_iota(jnp.int32, (8, 128), 1)

    def slots_for(to):
        found = jnp.int32(0)
        picked = [(jnp.int32(0), jnp.int32(0), jnp.int32(0))] * 2
        for i in range(tiles):
            match = dest_ref[i] == to
            for r in range(2):
                here = match & (found == r)
                new = (jnp.int32(i), count_ref[i], chan_ref[i])
                picked[r] = tuple(jnp.where(here, a, b) for a, b in zip(new, picked[r]))
            found = found + jnp.where(match, 1, 0)
        return [(tile, count.astype(F32) * (1.0 / 64.0), chan) for tile, count, chan in picked]

    def share_rows(slots):
        total = jnp.zeros((8, 128), F32)
        for r, (_, weight, chan) in enumerate(slots):
            total = total + jnp.where((row == r) & (lane == chan), weight, 0.0)
        return total

    load_fourier.wait()
    load_back.wait()
    load_vis.wait()

    def planes(slots):
        for i, (t, _, _) in enumerate(slots):
            spectrum = jnp.concatenate([vis[t, 0], vis[t, 1]], axis=1)
            for part in range(2):
                half[i, part * SIDE : (part + 1) * SIDE] = dot(
                    spectrum, fourier[:, part * SIDE : (part + 1) * SIDE]
                ).astype(BF)
        return [(dot(back[...], half[i]) * slots[i][1]).astype(BF) for i in range(2)]

    def prepare(i):
        slots = slots_for(place_of(i))
        share_ref[1 + choose(i, RANK)] = share_rows(slots)
        sending[i, 0], sending[i, 1] = planes(slots)

    prepare(jnp.int32(0))
    pl.semaphore_wait(barrier, n_fx - 1 + 4)

    def send_tiles(i, carry):
        share_copy(i).start()
        for r in range(2):
            hop_start(sending.at[i, r], tile_send.at[2 * i + r], choose(i, START[r]))
        lax.fori_loop(choose(i, FIRST), choose(i + 1, FIRST), forward, 0)

        @pl.when(i < len(PLACES) - 1)
        def _():
            prepare(i + 1)

        return carry

    lax.fori_loop(0, len(PLACES), send_tiles, 0)

    load_sky.wait()
    load_excess.wait()

    def there_and_back(c):
        pixels = jnp.concatenate([sky[c].astype(BF), sky[c + 1].astype(BF)], axis=1)
        once = pixels.astype(F32) + dot(excess[...], pixels)
        once = jnp.concatenate([once[:, :SIDE], once[:, SIDE:]], axis=0)
        both = once + dot(once.astype(BF), excess[...])
        model[c] = both[:SIDE]
        model[c + 1] = both[SIDE:]

    def forward_and_work(j, carry):
        forward(FIRST[-2] + j, 0)

        @pl.when(j == 0)
        def _():
            own = slots_for(fx)
            shares[0] = share_rows(own)
            arrived[0], arrived[1] = planes(own)

        @pl.when((j >= 1) & (j <= CH // 2))
        def _():
            there_and_back(2 * (j - 1))

        return carry

    lax.fori_loop(0, len(IN_ORDER) - 2 - FIRST[-2], forward_and_work, 0)

    def wait_share(i, carry):
        share_copy(i).wait_recv()
        return carry

    lax.fori_loop(0, len(PLACES), wait_share, 0)
    slots = n_fx * 2
    wide = slots * 16
    all_shares = shares[...].reshape(n_fx * 8, 128)
    members = jnp.where(all_shares > 0, 1.0, 0.0).astype(BF)
    spread = (
        lax.broadcasted_iota(jnp.int32, (CH * 16, 128), 0) // 16
        == lax.broadcasted_iota(jnp.int32, (CH * 16, 128), 1)
    )
    spread = jnp.where(spread, 1.0, 0.0).astype(BF)
    by_source = lax.dot_general(
        spread, members, (((1,), (1,)), ((), ())), preferred_element_type=F32
    ).astype(BF)
    weights = lax.dot_general(
        spread, all_shares.astype(BF), (((1,), (1,)), ((), ())), preferred_element_type=F32
    )
    totals = jnp.sum(weights, axis=1, keepdims=True)
    src_row = lax.broadcasted_iota(jnp.int32, (n_fx * 8, wide), 0)
    dst_col = lax.broadcasted_iota(jnp.int32, (n_fx * 8, wide), 1)
    widen = (src_row // 8 == dst_col // 32) & (src_row % 8 == dst_col // 16 % 2)
    widened = dot(by_source, jnp.where(widen, 1.0, 0.0).astype(BF))
    diagonal = (
        lax.broadcasted_iota(jnp.int32, (CH * 16, wide), 0) % 16
        == lax.broadcasted_iota(jnp.int32, (CH * 16, wide), 1) % 16
    )
    kron[...] = jnp.where(diagonal, widened, 0.0).astype(BF)
    scale = 1.0 / (1.0 + totals)

    def group_rows(g):
        return pl.ds(pl.multiple_of(g * 16, 16), 16)

    def without_tiles(g):
        pixels = sky[:, group_rows(g), :].reshape(CH * 16, SIDE)
        there = model[:, group_rows(g), :].reshape(CH * 16, SIDE)
        return pixels - (totals * scale) * there

    def wait_tiles(i, carry):
        landed(arrived.at[2 + i], tile_recv.at[2 + i]).wait_recv()
        return carry

    def with_sources(g, first, last):
        held = arrived[2 * first : 2 * last, group_rows(g), :].reshape((last - first) * 32, SIDE)
        before = without_tiles(g) if first == 0 else partial[g]
        return before + scale * dot(kron[:, first * 32 : last * 32], held)

    for first, last in ((0, 8), (8, 12)):
        lax.fori_loop(max(2 * first - 2, 0), 2 * last - 2, wait_tiles, 0)

        def add_sources(q, carry):
            for i in range(4):
                partial[q * 4 + i] = with_sources(q * 4 + i, first, last)
            return carry

        if first == 0:
            for k in range(2):
                forward(jnp.int32(len(IN_ORDER) - 2 + k), 0)
                lax.fori_loop(2 * k, 2 * k + 2, add_sources, 0)
        else:
            lax.fori_loop(0, SIDE // 64, add_sources, 0)
    lax.fori_loop(22, 2 * len(PLACES), wait_tiles, 0)

    def combine(g):
        rows = group_rows(g)
        new = with_sources(g, 12, 16).reshape(CH, 16, SIDE)
        extended[:, rows, :SIDE] = new.astype(BF)
        for k in range(PACKS):
            parts = [new[min(3 * k + m, CH - 1), :, :128] for m in range(3)]
            parts = [pltpu.roll(part, m * REACH, 1) if m else part for m, part in enumerate(parts)]
            columns[k, rows, :] = three_beside(*parts).astype(BF)

    chunks = 8
    deep = SIDE // chunks

    def columns_copy(q):
        rows = pl.ds(pl.multiple_of(q * deep, deep), deep)
        return pltpu.make_async_remote_copy(
            src_ref=columns.at[:, rows, :],
            dst_ref=beside.at[:, rows, :],
            send_sem=columns_send.at[q],
            recv_sem=columns_recv.at[q],
            device_id={"fx": prev},
            device_id_type=pl.DeviceIdType.MESH,
        )

    def halo_copy(i):
        source = (extended.at[:, :HALO, :SIDE], columns.at[:, :HALO, :])[i]
        target = (extended.at[:, SIDE:, :SIDE], corner)[i]
        where = ({"fy": up}, {"fy": up, "fx": prev})[i]
        return pltpu.make_async_remote_copy(
            src_ref=source,
            dst_ref=target,
            send_sem=halo_send.at[i],
            recv_sem=halo_recv.at[i],
            device_id=where,
            device_id_type=pl.DeviceIdType.MESH,
        )

    def make_chunk(q, carry):
        for i in range(deep // 16):
            combine(q * (deep // 16) + i)
        columns_copy(q).start()

        @pl.when(q == (HALO - 1) // deep)
        def _():
            for i in range(2):
                halo_copy(i).start()

        return carry

    lax.fori_loop(0, chunks, make_chunk, 0)

    def place(source, begin, end):
        for c in range(CH):
            values = turned(source[c // 3].astype(F32), c % 3)
            extended[c, begin:end, SIDE:] = values.astype(BF)

    halo_copy(1).wait_recv()
    place(corner, SIDE, TALL)
    for q in range(chunks):
        columns_copy(q).wait_recv()
        place(beside.at[:, q * deep : (q + 1) * deep, :], q * deep, (q + 1) * deep)
    halo_copy(0).wait_recv()

    def finish_shares(i, carry):
        share_copy(i).wait_send()
        return carry

    def finish_sent(i, carry):
        for r in range(2):
            hop_copy(sending.at[i, r], tile_send.at[2 * i + r], jnp.int32(0), False).wait_send()
        return carry

    def finish_forwards(f, carry):
        hop_copy(relay.at[f], relay_send.at[f], jnp.int32(0), False).wait_send()
        return carry

    lax.fori_loop(0, len(PLACES), finish_shares, 0)
    lax.fori_loop(0, len(PLACES), finish_sent, 0)
    lax.fori_loop(0, len(IN_ORDER), finish_forwards, 0)
    for i in range(2):
        halo_copy(i).wait_send()
    for q in range(chunks):
        columns_copy(q).wait_send()


def spill_kernel(
    n_fy,
    n_fx,
    cells,
    left,
    above,
    corner,
    side,
    bottom,
    to_right,
    to_below,
    to_corner,
    load_sem,
    send_sem,
    recv_sem,
):
    threes = [(3 * k, min(3 * k + 3, CH)) for k in range(PACKS)]
    loads = [
        pltpu.make_async_copy(cells.at[a:e, :, SIDE:], side.at[a:e], load_sem.at[k])
        for k, (a, e) in enumerate(threes)
    ]
    load_bottom = pltpu.make_async_copy(cells.at[:, SIDE:, :SIDE], bottom, load_sem.at[PACKS])
    for load in loads:
        load.start()
    load_bottom.start()
    fy = lax.axis_index("fy")
    fx = lax.axis_index("fx")
    up, down = (fy + n_fy - 1) % n_fy, (fy + 1) % n_fy
    prev, nxt = (fx + n_fx - 1) % n_fx, (fx + 1) % n_fx
    barrier = pltpu.get_barrier_semaphore()
    for where in (
        {"fy": up},
        {"fy": down},
        {"fx": prev},
        {"fx": nxt},
        {"fy": up, "fx": prev},
        {"fy": down, "fx": nxt},
    ):
        pl.semaphore_signal(barrier, inc=1, device_id=where, device_id_type=pl.DeviceIdType.MESH)
    pl.semaphore_wait(barrier, 6)

    def spill_copy(source, target, where, sem):
        return pltpu.make_async_remote_copy(
            src_ref=source,
            dst_ref=target,
            send_sem=send_sem.at[sem],
            recv_sem=recv_sem.at[sem],
            device_id=where,
            device_id_type=pl.DeviceIdType.MESH,
        )

    copies = []
    for k in range(PACKS):
        loads[k].wait()
        packed = three_beside(*[side[min(3 * k + m, CH - 1)] for m in range(3)]).astype(BF)
        to_right[k] = packed[:SIDE]
        to_corner[k] = packed[SIDE:]
        copies.append(spill_copy(to_right.at[k], left.at[k], {"fx": nxt}, k))
        copies[-1].start()
    copies.append(spill_copy(to_corner, corner, {"fy": down, "fx": nxt}, PACKS))
    copies[-1].start()
    load_bottom.wait()
    to_below[...] = bottom[...].astype(BF)
    copies.append(spill_copy(to_below, above, {"fy": down}, PACKS + 1))
    copies[-1].start()
    for copy in copies:
        copy.wait()


def add_kernel(cells, left, above, corner, out):
    for h in range(4):

        channel = 4 * pl.program_id(0) + h

        def columns(packed):
            values = packed[channel // 3].astype(F32)
            for m in range(1, 3):
                values = jnp.where(channel % 3 == m, turned(packed[channel // 3].astype(F32), m), values)
            lane = lax.broadcasted_iota(jnp.int32, values.shape, 1)
            return jnp.where(lane < REACH, values, 0.0)

        def finished(total):
            return jnp.maximum(total * (1.0 / BASES), 0.0)

        from_left = columns(left)
        from_above = above[h].astype(F32)
        first = from_left[:HALO] + from_above[:, :128] + columns(corner)
        out[h, :HALO, :128] = finished(cells[h, :HALO, :128] + first)
        out[h, :HALO, 128:] = finished(cells[h, :HALO, 128:] + from_above[:, 128:])
        out[h, HALO:, :128] = finished(cells[h, HALO:, :128] + from_left[HALO:])
        out[h, HALO:, 128:] = finished(cells[h, HALO:, 128:])


def per_device(n_fy, n_fx, sky_image, vis_tiles, tile_dest, tile_chan, tile_count, thresholds):
    made = {name: jnp.asarray(table) for name, table in tables().items()}
    smem = pl.BlockSpec(memory_space=pltpu.SMEM)
    vmem = pl.BlockSpec(memory_space=pltpu.VMEM)
    anywhere = pl.BlockSpec(memory_space=pl.ANY)
    dma = pltpu.SemaphoreType.DMA
    tiles = vis_tiles.shape[0]
    extended = pl.pallas_call(
        functools.partial(exchange_kernel, n_fy, n_fx),
        out_shape=pltpu.VMEM((CH, TALL, WIDE), BF),
        in_specs=[smem] * 3 + [anywhere] * 5,
        scratch_shapes=[
            pltpu.VMEM((2 * SIDE, 2 * SIDE), BF),
            pltpu.VMEM((SIDE, 2 * SIDE), BF),
            pltpu.VMEM((SIDE, SIDE), BF),
            pltpu.VMEM((tiles, 2, SIDE, SIDE), BF),
            pltpu.VMEM((CH, SIDE, SIDE), F32),
            pltpu.VMEM((CH, SIDE, SIDE), F32),
            pltpu.VMEM((SIDE // 16, CH * 16, SIDE), F32),
            pltpu.VMEM((n_fx, 2, SIDE, SIDE), BF),
            pltpu.VMEM((2 * n_fx, SIDE, SIDE), BF),
            pltpu.VMEM((len(IN_ORDER), SIDE, SIDE), BF),
            pltpu.VMEM((2, 2 * SIDE, SIDE), BF),
            pltpu.VMEM((n_fx, 8, 128), F32),
            pltpu.VMEM((n_fx, 8, 128), F32),
            pltpu.VMEM((CH * 16, n_fx * 32), BF),
            pltpu.VMEM((PACKS, SIDE, 128), BF),
            pltpu.VMEM((PACKS, SIDE, 128), BF),
            pltpu.VMEM((PACKS, HALO, 128), BF),
            dma((5,)),
            dma((2 * len(PLACES),)),
            dma((2 * n_fx,)),
            dma((len(IN_ORDER),)),
            dma((len(IN_ORDER),)),
            dma((n_fx,)),
            dma((n_fx,)),
            dma((2,)),
            dma((2,)),
            dma((8,)),
            dma((8,)),
        ],
        compiler_params=pltpu.CompilerParams(
            collective_id=0, has_side_effects=True, vmem_limit_bytes=58 * 1024 * 1024
        ),
    )(
        tile_dest.reshape(tiles),
        tile_chan,
        tile_count,
        made["fourier"],
        made["back"],
        made["excess"],
        sky_image,
        vis_tiles,
    )
    rows, columns = made["rows"], made["columns"]
    row_sec = jnp.einsum("bkn,cnx->bckx", rows, extended, preferred_element_type=F32).astype(BF)
    row_sec = lax.optimization_barrier(row_sec)
    coefficient = jnp.einsum("bcyx,bkx->bcyk", row_sec, columns, preferred_element_type=F32)
    limits = thresholds.astype(F32)
    shrunk = (coefficient - jnp.clip(coefficient, -limits, limits)).astype(BF)
    row_sec = jnp.einsum("bjy,bcjk->bcyk", rows, shrunk, preferred_element_type=F32).astype(BF)
    cells = jnp.einsum("bcyk,bkx->cyx", row_sec, made["spread"], preferred_element_type=F32)
    left, above, corner = pl.pallas_call(
        functools.partial(spill_kernel, n_fy, n_fx),
        out_shape=(
            pltpu.VMEM((PACKS, SIDE, 128), BF),
            pltpu.VMEM((CH, HALO, SIDE), BF),
            pltpu.VMEM((PACKS, HALO, 128), BF),
        ),
        in_specs=[anywhere],
        scratch_shapes=[
            pltpu.VMEM((CH, TALL, 128), F32),
            pltpu.VMEM((CH, HALO, SIDE), F32),
            pltpu.VMEM((PACKS, SIDE, 128), BF),
            pltpu.VMEM((CH, HALO, SIDE), BF),
            pltpu.VMEM((PACKS, HALO, 128), BF),
            dma((PACKS + 1,)),
            dma((PACKS + 2,)),
            dma((PACKS + 2,)),
        ],
        compiler_params=pltpu.CompilerParams(
            collective_id=1, has_side_effects=True, vmem_limit_bytes=58 * 1024 * 1024
        ),
    )(cells)
    return pl.pallas_call(
        add_kernel,
        out_shape=jax.ShapeDtypeStruct((CH, SIDE, SIDE), F32),
        grid=(CH // 4,),
        in_specs=[
            pl.BlockSpec((4, SIDE, SIDE), lambda p: (p, 0, 0)),
            pl.BlockSpec((PACKS, SIDE, 128), lambda p: (0, 0, 0)),
            pl.BlockSpec((4, HALO, SIDE), lambda p: (p, 0, 0)),
            pl.BlockSpec((PACKS, HALO, 128), lambda p: (0, 0, 0)),
        ],
        out_specs=pl.BlockSpec((4, SIDE, SIDE), lambda p: (p, 0, 0)),
        compiler_params=pltpu.CompilerParams(vmem_limit_bytes=16 * 1024 * 1024),
    )(cells, left, above, corner)


def solution(mesh):
    in_specs = (
        P(None, "fy", "fx"),
        P(("fy", "fx"), None, None, None),
        P(("fy", "fx"), None),
        P(("fy", "fx")),
        P(("fy", "fx")),
        P(None, None, "fy", "fx"),
    )
    out_specs = P(None, "fy", "fx")
    return jax.shard_map(
        functools.partial(per_device, mesh.shape["fy"], mesh.shape["fx"]),
        mesh=mesh,
        in_specs=in_specs,
        out_specs=out_specs,
        check_vma=False,
    )
```
